32 devices in a mesh: rows: 8 (over z, core), seq: 4 (over y, x).
Axes of the slice: x: 2, y: 2, z: 4, core: 2. Of those that a mesh axis runs over, the one named last changes fastest.
Arguments:
- frames: bfloat16 [16, 1024, 1024], P('rows', 'seq'), may hold values from -6 to 6
- text_states: bfloat16 [16, 256, 768], P('rows', 'seq'), may hold values from -6 to 6
- clip_lengths: int32 [16, 4], P('rows'), may hold values from 1 to 1021, as said below
- text_lengths: int32 [16, 4], P('rows'), may hold values from 1 to 253, as said below
- self_gain: float32 [1024], replicated, may hold values from 0.5 to 1.5
- self_shift: float32 [1024], replicated, may hold values from -3 to 3
- self_qkv: bfloat16 [1024, 3072], replicated, may hold values from -0.1875 to 0.1875
- self_out: bfloat16 [1024, 1024], replicated, may hold values from -2 to 2
- cross_gain: float32 [1024], replicated, may hold values from 0.5 to 1.5
- cross_shift: float32 [1024], replicated, may hold values from -3 to 3
- cross_query: bfloat16 [1024, 1024], replicated, may hold values from -0.1875 to 0.1875
- text_proj: bfloat16 [768, 1024], replicated, may hold values from -0.21875 to 0.21875
- text_bias: float32 [1024], replicated, may hold values from -3 to 3
- cross_kv: bfloat16 [1024, 2048], replicated, may hold values from -0.1875 to 0.1875
- cross_out: bfloat16 [1024, 1024], replicated, may hold values from -1.5 to 1.5
- feed_gain: float32 [1024], replicated, may hold values from 0.5 to 1.5
- feed_shift: float32 [1024], replicated, may hold values from -3 to 3
- feed_in: bfloat16 [1024, 4096], replicated, may hold values from -0.1875 to 0.1875
- feed_out: bfloat16 [4096, 1024], replicated, may hold values from -0.09375 to 0.09375
- grad_out: bfloat16 [16, 1024, 1024], P('rows', 'seq'), may hold values from -6 to 6
Outputs:
- result: bfloat16 [16, 1024, 1024], P('rows', 'seq')
- grad_frames: float32 [16, 1024, 1024], P('rows', 'seq')
- grad_text: float32 [16, 256, 768], P('rows', 'seq')
- grad_self_gain: float32 [1024], P('seq')
- grad_self_shift: float32 [1024], P('seq')
- grad_self_qkv: float32 [1024, 3072], P('rows', 'seq')
- grad_self_out: float32 [1024, 1024], P('rows', 'seq')
- grad_cross_gain: float32 [1024], P('seq')
- grad_cross_shift: float32 [1024], P('seq')
- grad_cross_query: float32 [1024, 1024], P('rows', 'seq')
- grad_text_proj: float32 [768, 1024], P('rows', 'seq')
- grad_text_bias: float32 [1024], P('seq')
- grad_cross_kv: float32 [1024, 2048], P('rows', 'seq')
- grad_cross_out: float32 [1024, 1024], P('rows', 'seq')
- grad_feed_gain: float32 [1024], P('seq')
- grad_feed_shift: float32 [1024], P('seq')
- grad_feed_in: float32 [1024, 4096], P('rows', 'seq')
- grad_feed_out: float32 [4096, 1024], P('seq', 'rows')
The draws below stay inside these ranges and needn't reach their ends.
Inputs may be any that keep to these rules, and one draw needn't show every extreme that they name: `clip_lengths`: the 4 clip lengths of a row sum to 1024; among the rows of one index of rows, one has a clip of exactly 1021 frames. `text_lengths`: the 4 text lengths of a row sum to 256; clip c of a row reads the text tokens of its clip c; among the rows of one index of rows, one has a clip of exactly 253 text tokens.
All inputs are finite; a program needn't handle non-finite values.
Results may differ from the reference program's by a relative error of at most 0.014.
Values may be sent and summed in bfloat16 or wider, within the bound.
A program may use at most 256 MiB of HBM per device.

```python
import jax
import jax.numpy as jnp
from jax import lax

D = 1024
H = 16
HD = 64
FF = 4096
E = 768
TEXT = 256
CLIPS = 4
FRAMES = 1024
ROWS_DEV = 2
ROWS = 16
N_ROWS = 8


def random_cuts(row_key, total_count):
    chosen = jax.random.permutation(row_key, total_count - 1)[:CLIPS - 1] + 1
    edges = jnp.concatenate([jnp.zeros((1,), jnp.int32), jnp.sort(chosen).astype(jnp.int32), jnp.full((1,), total_count, jnp.int32)])
    return edges[1:] - edges[:-1]


def draw_clip_lengths(key, part):
    key = jax.random.fold_in(key, 11)
    pick_key, cut_key, place_key = jax.random.split(key, 3)
    regular = jax.vmap(lambda row_key: random_cuts(row_key, FRAMES))(jax.random.split(cut_key, ROWS))
    placed = jax.random.randint(place_key, (ROWS, 1), 0, CLIPS)
    columns = jnp.arange(CLIPS, dtype=jnp.int32)[None, :]
    spanning = jnp.where(columns == placed, FRAMES - CLIPS + 1, 1)
    chosen_row = jax.random.randint(pick_key, (N_ROWS, 1), 0, ROWS_DEV)
    row_in_group = jnp.arange(ROWS_DEV, dtype=jnp.int32)[None, :]
    is_long = (row_in_group == chosen_row).reshape(ROWS, 1)
    return jnp.where(is_long, spanning, regular).astype(jnp.int32)


def draw_text_lengths(key, part):
    key = jax.random.fold_in(key, 12)
    cut_key, place_key = jax.random.split(key, 2)
    regular = jax.vmap(lambda row_key: random_cuts(row_key, TEXT))(jax.random.split(cut_key, ROWS))
    placed = jax.random.randint(place_key, (ROWS, 1), 0, CLIPS)
    columns = jnp.arange(CLIPS, dtype=jnp.int32)[None, :]
    longest = jnp.where(columns == placed, TEXT - CLIPS + 1, 1)
    row_in_group = (jnp.arange(ROWS, dtype=jnp.int32) % ROWS_DEV).reshape(ROWS, 1)
    return jnp.where(row_in_group == 0, longest, regular).astype(jnp.int32)


def strengthened(result, stream_key, source, target, parts, factor):
    def block_of(dim):
        return (jnp.arange(result.shape[dim]) // (result.shape[dim] // parts)).reshape((-1,) + (1,) * (result.ndim - 1 - dim))

    near = jax.random.permutation(stream_key, parts)[block_of(target)]
    second = (block_of(target) + parts // 2) % parts
    return jnp.where((block_of(source) == near) | (block_of(source) == second), factor * result, result)


def level_of(rng, extent, pieces, least, largest):
    loudness = 1.0
    for position, shards_of in pieces:
        draws = jax.random.uniform(jax.random.fold_in(jax.random.fold_in(rng, 6), position), (shards_of,), jnp.float32, least / len(pieces), largest / len(pieces))
        loudness = loudness * jnp.repeat(jnp.exp(draws), extent[position] // shards_of).reshape((-1,) + (1,) * (len(extent) - 1 - position))
    return loudness


def bell_draw(own_key, shape, spread, bound, cuts=(), kind=jnp.bfloat16):
    entries = jax.random.normal(own_key, shape, jnp.float32) * spread
    if len(cuts) > 0:
        entries = level_of(own_key, shape, cuts, -0.22, 0.18) * entries
    return jnp.clip(entries, min=-bound, max=bound).astype(kind)


def gaussian_with(own_key, dims, spread, bound, shards, heavy, held_as=jnp.bfloat16):
    values = spread * jax.random.normal(own_key, dims, jnp.float32)
    if shards:
        values = values * level_of(own_key, dims, shards, -0.22, 0.18)
    return jnp.clip(strengthened(values, jax.random.fold_in(own_key, 3), *heavy), -bound, bound).astype(held_as)


def setup_inputs(seed: int = 0) -> dict:
    keys = jax.random.split(jax.random.key(seed), 21)
    frames = gaussian_with(keys[0], (ROWS, FRAMES, D), 1.0, 6.0, ((0, 8), (1, 4)), (1, 2, 4, 2.0))
    text_states = bell_draw(keys[1], (ROWS, TEXT, E), 1.0, 6.0, ((0, 8), (1, 4)))
    clip_lengths = draw_clip_lengths(jax.random.fold_in(keys[20], 71), 0)
    text_lengths = draw_text_lengths(jax.random.fold_in(keys[20], 71), 0)
    self_gain = jnp.clip(1.0 + 0.1 * jax.random.normal(keys[4], (D,), jnp.float32), 0.5, 1.5)
    self_shift = bell_draw(keys[5], (D,), 0.5, 3.0, (), jnp.float32)
    self_qkv = bell_draw(keys[6], (D, 3 * D), D ** -0.5, 0.1875)
    self_out = bell_draw(keys[7], (D, D), (max(D // 128, 1)) ** -0.5, 2.0)
    cross_gain = jnp.clip(1.0 + 0.1 * jax.random.normal(keys[8], (D,), jnp.float32), 0.5, 1.5)
    cross_shift = bell_draw(keys[9], (D,), 0.5, 3.0, (), jnp.float32)
    cross_query = bell_draw(keys[10], (D, D), D ** -0.5, 0.1875)
    text_proj = bell_draw(keys[11], (E, D), E ** -0.5, 0.21875)
    text_bias = bell_draw(keys[12], (D,), 0.5, 3.0, (), jnp.float32)
    cross_kv = bell_draw(keys[13], (D, 2 * D), D ** -0.5, 0.1875)
    cross_out = bell_draw(keys[14], (D, D), (max(D // 64, 1)) ** -0.5, 1.5)
    feed_gain = jnp.clip(1.0 + 0.1 * jax.random.normal(keys[15], (D,), jnp.float32), 0.5, 1.5)
    feed_shift = bell_draw(keys[16], (D,), 0.5, 3.0, (), jnp.float32)
    feed_in = bell_draw(keys[17], (D, FF), D ** -0.5, 0.1875)
    feed_out = bell_draw(keys[18], (FF, D), FF ** -0.5, 0.09375)
    grad_out = gaussian_with(keys[19], (ROWS, FRAMES, D), 1.0, 6.0, ((0, 8), (1, 4)), (0, 2, 8, 2.0))
    return dict(frames=frames, text_states=text_states, clip_lengths=clip_lengths, text_lengths=text_lengths, self_gain=self_gain, self_shift=self_shift, self_qkv=self_qkv, self_out=self_out, cross_gain=cross_gain, cross_shift=cross_shift, cross_query=cross_query, text_proj=text_proj, text_bias=text_bias, cross_kv=cross_kv, cross_out=cross_out, feed_gain=feed_gain, feed_shift=feed_shift, feed_in=feed_in, feed_out=feed_out, grad_out=grad_out)


HIGHEST_PRECISION = lax.Precision.HIGHEST
EPSILON = 1e-05
MASKED = -1e+30

@jax.custom_vjp
def low(v):
    return lax.optimization_barrier(v.astype(jnp.bfloat16)).astype(jnp.float32)

@jax.custom_vjp
def low_back(v):
    return v

def low_keep(v):
    return (low(v), None)

def low_pass(kept, grad):
    return (grad,)

def back_keep(v):
    return (v, None)

def back_low(kept, grad):
    return (low(grad),)
low.defvjp(low_keep, low_pass)
low_back.defvjp(back_keep, back_low)

def both_ways(values):
    return low_back(low(values))

def matmul(left_side, right_side):
    return jnp.matmul(left_side, right_side, precision=HIGHEST_PRECISION)

def layer_norm(values, gain_vector, shift_vector):
    centered = values - lax.optimization_barrier(jnp.mean(values, axis=-1, keepdims=True))
    variance = lax.optimization_barrier(jnp.mean(centered * centered, axis=-1, keepdims=True))
    return centered * lax.rsqrt(variance + EPSILON) * gain_vector + shift_vector

def segment_ids(lengths, total_count):
    boundaries = jnp.cumsum(lengths).astype(jnp.int32)
    positions = jnp.arange(total_count, dtype=jnp.int32)
    return lax.optimization_barrier(jnp.sum((positions[:, None] >= boundaries[None, :]).astype(jnp.int32), axis=1)).astype(jnp.int32)

def attention(queries, key_rows, value_rows, allowed):
    query_count = queries.shape[0]
    key_count = key_rows.shape[0]
    query_split = queries.reshape(query_count, H, HD)
    key_split = key_rows.reshape(key_count, H, HD)
    value_split = value_rows.reshape(key_count, H, HD)
    scores = low_back(jnp.einsum('qhd,khd->hqk', query_split, key_split, precision=HIGHEST_PRECISION) * HD ** (-0.5))
    scores = jnp.where(allowed[None], scores, MASKED)
    highest = lax.optimization_barrier(jnp.max(scores, axis=-1, keepdims=True))
    exponent = jnp.exp(scores - highest)
    softmax_weights = low(exponent / lax.optimization_barrier(jnp.sum(exponent, axis=-1, keepdims=True)))
    mixture = jnp.einsum('hqk,khd->qhd', softmax_weights, value_split, precision=HIGHEST_PRECISION)
    return mixture.reshape(query_count, H * HD)

def layer_row(inputs, params):
    frames_row, text_row, clip_row, text_row_lengths = inputs
    self_gain, self_shift, self_qkv, self_out, cross_gain, cross_shift, cross_query, text_proj, text_bias, cross_kv, cross_out, feed_gain, feed_shift, feed_in, feed_out = params
    frame_segs = segment_ids(clip_row, FRAMES)
    text_segs = segment_ids(text_row_lengths, TEXT)
    positions = jnp.arange(FRAMES, dtype=jnp.int32)
    self_allowed = (frame_segs[:, None] == frame_segs[None, :]) & (positions[None, :] <= positions[:, None])
    cross_allowed = frame_segs[:, None] == text_segs[None, :]
    normed_self = low(layer_norm(frames_row, self_gain, self_shift))
    packed = both_ways(matmul(normed_self, self_qkv))
    self_mix = both_ways(attention(packed[:, :D], packed[:, D:2 * D], packed[:, 2 * D:], self_allowed))
    first = frames_row + low_back(matmul(self_mix, self_out))
    normed_cross = low(layer_norm(first, cross_gain, cross_shift))
    cross_queries = both_ways(matmul(normed_cross, cross_query))
    projected = both_ways(matmul(text_row, text_proj) + text_bias)
    text_pair = both_ways(matmul(projected, cross_kv))
    cross_mix = both_ways(attention(cross_queries, text_pair[:, :D], text_pair[:, D:], cross_allowed))
    second = first + low_back(matmul(cross_mix, cross_out))
    normed_feed = low(layer_norm(second, feed_gain, feed_shift))
    pre_act = low_back(matmul(normed_feed, feed_in))
    activated = low(jax.nn.gelu(pre_act, approximate=False))
    return second + low_back(matmul(activated, feed_out))

def reference(frames, text_states, clip_lengths, text_lengths, self_gain, self_shift, self_qkv, self_out, cross_gain, cross_shift, cross_query, text_proj, text_bias, cross_kv, cross_out, feed_gain, feed_shift, feed_in, feed_out, grad_out):
    params = tuple((item.astype(jnp.float32) for item in (self_gain, self_shift, self_qkv, self_out, cross_gain, cross_shift, cross_query, text_proj, text_bias, cross_kv, cross_out, feed_gain, feed_shift, feed_in, feed_out)))

    def whole_batch(frames_float, text_float, weights):

        def per_row(inputs):
            return layer_row(inputs, weights)
        return lax.map(jax.checkpoint(per_row), (frames_float, text_float, clip_lengths, text_lengths))
    outputs, pullback = jax.vjp(whole_batch, frames.astype(jnp.float32), text_states.astype(jnp.float32), params)
    grad_input, grad_states, grads = pullback(grad_out.astype(jnp.float32))
    return (outputs.astype(jnp.bfloat16), grad_input, grad_states, grads[0], grads[1], grads[2], grads[3], grads[4], grads[5], grads[6], grads[7], grads[8], grads[9], grads[10], grads[11], grads[12], grads[13], grads[14])
```

```python
import functools
import math

import jax
import jax.numpy as jnp
from jax import lax
from jax.experimental import pallas as pl
from jax.experimental.pallas import tpu as pltpu
from jax.sharding import PartitionSpec as P

HD = 64
PAIR = 2 * HD
EPSILON = 1e-05
MASKED = -1e30
ROWS = "rows"
SEQ = "seq"
BF = jnp.bfloat16
F32 = jnp.float32
VMEM_LIMIT = 48 * 1024 * 1024


def dot(left, right, left_dim=1, right_dim=0):
    return lax.dot_general(
        left, right, (((left_dim,), (right_dim,)), ((), ())), preferred_element_type=F32
    )


def pick(array, index, axis):
    return lax.dynamic_index_in_dim(array, index, axis, keepdims=False)


def after(value, *others):
    return lax.optimization_barrier((value,) + others)[0]


class Place:
    def __init__(self):
        self.rows, self.seq = lax.axis_size(ROWS), lax.axis_size(SEQ)
        self.nz = self.rows // 2
        self.nx = math.isqrt(self.seq)
        self.ny = self.seq // self.nx
        row, self.spot = lax.axis_index(ROWS), lax.axis_index(SEQ)
        self.core, self.z = row % 2, row // 2
        self.x, self.y = self.spot % self.nx, self.spot // self.nx
        self.owner = [0 if 4 * s // self.seq in (0, 3) else 1 for s in range(self.seq)]
        self.members = [[s for s in range(self.seq) if self.owner[s] == c] for c in (0, 1)]
        self.rank = [self.members[self.owner[s]].index(s) for s in range(self.seq)]

    def permute(self, value, target):
        pairs = []
        for z in range(self.nz):
            for c in range(2):
                for s in range(self.seq):
                    tz, tc, ts = target(z, c, s)
                    pairs.append(((2 * z + c) * self.seq + s, (2 * tz + tc) * self.seq + ts))
        return lax.ppermute(value, (ROWS, SEQ), pairs)

    def swap_core(self, value):
        return self.permute(value, lambda z, c, s: (z, 1 - c, s))

    def next_z(self, value):
        return self.permute(value, lambda z, c, s: ((z + 1) % self.nz, c, s))

    def next_x(self, value):
        nx = self.nx
        return self.permute(value, lambda z, c, s: (z, c, s // nx * nx + (s % nx + 1) % nx))

    def next_y(self, value):
        return self.permute(value, lambda z, c, s: (z, c, (s + self.nx) % self.seq))

    def to_rows(self, value):
        count = value.shape[0]
        my_rank = jnp.array(self.rank, jnp.int32)[self.spot]
        got = []
        for t in range(count):

            def target(z, c, s, t=t):
                return z, self.owner[s], c * count + (t + self.rank[s]) % count

            got.append(self.permute(pick(value, (t + my_rank) % count, 0), target))
        stacked = jnp.stack(got)
        here = self.spot % count
        return jnp.concatenate([pick(stacked, (here - k) % count, 0) for k in range(count)], axis=0)

    def from_rows(self, value, count):
        my_rank = jnp.array(self.rank, jnp.int32)[self.spot]
        slots = value.reshape(count, value.shape[0] // count, value.shape[1])
        here = self.spot % count
        got = []
        for t in range(count):

            def target(z, c, s, t=t):
                return z, s // count, self.members[c][(s % count - t) % count]

            got.append(self.permute(pick(slots, (here - t) % count, 0), target))
        stacked = jnp.stack(got)
        return jnp.stack([pick(stacked, (i - my_rank) % count, 0) for i in range(count)])

    def positions(self, total, core):
        quarter = total // 4
        inner = jnp.arange(quarter, dtype=jnp.int32)
        return jnp.concatenate([inner + core * quarter, inner + (3 - core) * quarter])

    def offset(self, i, j):
        return (self.y + 1 + i) % self.ny * self.nx + (self.x + 1 + j) % self.nx

    def relative_columns(self, value, outer_x):
        blocks = value.reshape(value.shape[0], self.seq, -1)
        if outer_x:
            order = [self.offset(i, j) for j in range(self.nx) for i in range(self.ny)]
        else:
            order = [self.offset(i, j) for i in range(self.ny) for j in range(self.nx)]
        return jnp.concatenate([pick(blocks, place, 1) for place in order], axis=1)


    def vector_sum(self, value):
        bit = 1
        while bit < self.rows:
            value = value + self.permute(
                value,
                lambda z, c, s: ((2 * z + c ^ bit) // 2, (2 * z + c ^ bit) % 2, s),
            )
            bit *= 2
        bit = 1
        while bit < self.seq:
            value = value + self.permute(value, lambda z, c, s: (z, c, s ^ bit))
            bit *= 2
        return value


def ring_order(count):
    return list(range(count - 2, -1, -1)) + [count - 1]


def ring_sum(pieces, send):
    order = ring_order(len(pieces))
    value = pieces[order[0]]()
    for k in order[1:]:
        value = pieces[k]() + send(value.astype(BF)).astype(F32)
    return value


def normalize(values):
    centered = values - jnp.mean(values, axis=-1, keepdims=True)
    scale = lax.rsqrt(jnp.mean(centered * centered, axis=-1, keepdims=True) + EPSILON)
    return centered * scale, scale


def layer_norm(values, gain, shift):
    return (normalize(values)[0] * gain + shift).astype(BF)


def norm_backward(values, gain, cotangent):
    normal, scale = normalize(values)
    grown = cotangent * gain
    inner = jnp.mean(grown, axis=-1, keepdims=True)
    along = jnp.mean(grown * normal, axis=-1, keepdims=True)
    grad = scale * (grown - inner - normal * along)
    return grad, jnp.sum(cotangent * normal, axis=0), jnp.sum(cotangent, axis=0)


def nt(left, right):
    return dot(left, right, 1, 1)


def head_lanes(values, head):
    lane = lax.broadcasted_iota(jnp.int32, values.shape, 1)
    return jnp.where((lane < HD) == (head == 0), values, jnp.zeros_like(values))


def turned(values):
    return jnp.swapaxes(values.astype(F32), 0, 1).astype(BF)


def segment_bias(key_segment, query_segment, causal):
    allowed = key_segment == query_segment
    if causal:
        key = lax.broadcasted_iota(jnp.int32, allowed.shape, 0)
        query = lax.broadcasted_iota(jnp.int32, allowed.shape, 1)
        allowed = allowed & (key <= query)
    return jnp.where(allowed, 0.0, MASKED).astype(F32)


def forward_heads(queries, blocks, lse_ref, at):
    parts = []
    for head in range(2):
        query = head_lanes(queries, head)
        scores = [nt(keys, query) + bias() for keys, _, bias in blocks]
        highest = functools.reduce(
            jnp.maximum, [jnp.max(s, axis=0, keepdims=True) for s in scores]
        )
        weights = [jnp.exp(s - highest) for s in scores]
        total = sum(jnp.sum(w, axis=0, keepdims=True) for w in weights)
        mixed = sum(
            dot(values[head * HD : (head + 1) * HD], w.astype(BF))
            for (_, values, _), w in zip(blocks, weights)
        )
        parts.append(mixed * (1.0 / total))
        lse_ref[0, head : head + 1, at] = highest + jnp.log(total)
    return jnp.swapaxes(jnp.concatenate(parts, axis=0), 0, 1).astype(BF)


def backward_heads(queries, grads, mixed, blocks, lse_ref, at):
    product = jnp.swapaxes(grads.astype(F32) * mixed.astype(F32), 0, 1)
    parts = []
    for head in range(2):
        query, grad = head_lanes(queries, head), head_lanes(grads, head)
        rows = slice(head * HD, (head + 1) * HD)
        inner = jnp.sum(product[rows], axis=0, keepdims=True)
        totals = lse_ref[0, head : head + 1, at]
        grad_query = None
        for keys, turned_keys, values, bias, sums in blocks:
            weights = jnp.exp(nt(keys, query) + bias() - totals)
            scores = (weights * (nt(values, grad) - inner)).astype(BF)
            add_to(sums, 0, dot(scores, query))
            add_to(sums, 1, dot(weights.astype(BF), grad))
            term = dot(turned_keys[rows], scores)
            grad_query = term if grad_query is None else grad_query + term
        parts.append(grad_query)
    return (jnp.swapaxes(jnp.concatenate(parts, axis=0), 0, 1) * HD**-0.5).astype(BF)


def add_to(sums, index, term):
    sums[index] = term if sums[index] is None else sums[index] + term


def scaled(values):
    return values * jnp.array(HD**-0.5, BF)


def self_plan(core):
    if core == 0:
        return [(0, 0, 0)], [(0, 0, 1), (0, 1, 2), (1, 0, 3), (1, 1, 4)]
    return [(0, 0, 0), (1, 0, 4)], [(0, 0, 1), (0, 1, 2), (1, 0, 3)]


def self_biases(core, qseg_ref, kseg_refs, bias_ref):
    length = bias_ref.shape[1]
    low, high = slice(0, length), slice(length, 2 * length)
    own, other = kseg_refs
    bias_ref[0] = segment_bias(own[low], qseg_ref[:, low], True)
    bias_ref[1] = segment_bias(own[low], qseg_ref[:, high], False)
    bias_ref[2] = segment_bias(own[high], qseg_ref[:, high], True)
    bias_ref[3] = segment_bias(other[low], qseg_ref[:, high], False)

    @pl.when(core == 0)
    def _():
        bias_ref[4] = segment_bias(other[high], qseg_ref[:, high], False)

    @pl.when(core != 0)
    def _():
        bias_ref[4] = segment_bias(other[low], qseg_ref[:, low], False)


def self_forward_kernel(
    core_ref, qseg_ref, own_ref, other_ref, q_ref, k_ref, v_ref, ko_ref, vo_ref, o_ref, lse_ref, bias_ref
):
    core = core_ref[0]
    length = bias_ref.shape[1]

    @pl.when(pl.program_id(0) == 0)
    def _():
        self_biases(core, qseg_ref, (own_ref, other_ref), bias_ref)

    keys, values = (k_ref, ko_ref), (v_ref, vo_ref)
    for which in range(2):

        @pl.when((core == 0) == (which == 0))
        def _(which=which):
            for half, plan in enumerate(self_plan(which)):
                at = slice(half * length, (half + 1) * length)
                blocks = []
                for source, part, number in plan:
                    where = slice(part * length, (part + 1) * length)
                    blocks.append(
                        (
                            keys[source][where],
                            turned(values[source][where]),
                            functools.partial(bias_ref.__getitem__, number),
                        )
                    )
                o_ref[at] = forward_heads(scaled(q_ref[at]), blocks, lse_ref, at)


def self_backward_kernel(
    core_ref,
    qseg_ref,
    own_ref,
    other_ref,
    q_ref,
    k_ref,
    v_ref,
    ko_ref,
    vo_ref,
    g_ref,
    o_ref,
    lse_ref,
    dq_ref,
    dk_ref,
    dv_ref,
    dko_ref,
    dvo_ref,
    bias_ref,
):
    core = core_ref[0]
    length = bias_ref.shape[1]

    @pl.when(pl.program_id(0) == 0)
    def _():
        self_biases(core, qseg_ref, (own_ref, other_ref), bias_ref)

    keys, values = (k_ref, ko_ref), (v_ref, vo_ref)
    for which in range(2):

        @pl.when((core == 0) == (which == 0))
        def _(which=which):
            sums = {(s, p): [None, None] for s in range(2) for p in range(2)}
            for half, plan in enumerate(self_plan(which)):
                at = slice(half * length, (half + 1) * length)
                blocks = []
                for source, part, number in plan:
                    where = slice(part * length, (part + 1) * length)
                    blocks.append(
                        (
                            keys[source][where],
                            turned(keys[source][where]),
                            values[source][where],
                            functools.partial(bias_ref.__getitem__, number),
                            sums[source, part],
                        )
                    )
                dq_ref[at] = backward_heads(
                    scaled(q_ref[at]), g_ref[at], o_ref[at], blocks, lse_ref, at
                )
            for (source, part), pair in sums.items():
                where = slice(part * length, (part + 1) * length)
                for ref, value in zip(((dk_ref, dv_ref), (dko_ref, dvo_ref))[source], pair):
                    if value is None:
                        ref[where] = jnp.zeros((length, PAIR), BF)
                    else:
                        ref[where] = value.astype(BF)


def cross_forward_kernel(qseg_ref, kseg_ref, q_ref, k_ref, v_ref, o_ref, lse_ref, bias_ref):
    length = q_ref.shape[0] // 2

    @pl.when(pl.program_id(0) == 0)
    def _():
        bias_ref[...] = segment_bias(kseg_ref[...], qseg_ref[...], False)

    turned_values = turned(v_ref[...])
    for half in range(2):
        at = slice(half * length, (half + 1) * length)
        blocks = [(k_ref[...], turned_values, lambda at=at: bias_ref[:, at])]
        o_ref[at] = forward_heads(scaled(q_ref[at]), blocks, lse_ref, at)


def cross_backward_kernel(
    qseg_ref,
    kseg_ref,
    q_ref,
    k_ref,
    v_ref,
    g_ref,
    o_ref,
    lse_ref,
    dq_ref,
    dk_ref,
    dv_ref,
    bias_ref,
):
    length = q_ref.shape[0] // 2

    @pl.when(pl.program_id(0) == 0)
    def _():
        bias_ref[...] = segment_bias(kseg_ref[...], qseg_ref[...], False)

    turned_keys = turned(k_ref[...])
    sums = [None, None]
    for half in range(2):
        at = slice(half * length, (half + 1) * length)
        blocks = [(k_ref[...], turned_keys, v_ref[...], lambda at=at: bias_ref[:, at], sums)]
        dq_ref[at] = backward_heads(scaled(q_ref[at]), g_ref[at], o_ref[at], blocks, lse_ref, at)
    dk_ref[...] = sums[0].astype(BF)
    dv_ref[...] = sums[1].astype(BF)


def column(rows, first=0):
    return pl.BlockSpec((rows, PAIR), lambda i: (0, first + i))


def whole(array):
    return pl.BlockSpec(array.shape, lambda i: (0,) * array.ndim)


SMEM_SPEC = pl.BlockSpec(memory_space=pltpu.SMEM)


def without(kernel, first, count):
    def run(*refs):
        kernel(*refs[:first], *refs[first + count :])

    return run


ANY_SPEC = pl.BlockSpec(memory_space=pl.ANY)
WHOLE_SPEC = pl.BlockSpec(memory_space=pltpu.VMEM)


def attention_call(kernel, heads, in_specs, outs, bias_shape, flops, arguments, before=()):
    pairs = heads // 2
    kernel = without(kernel, len(arguments), len(before))
    in_specs = list(in_specs) + [ANY_SPEC] * len(before)
    arguments = tuple(arguments) + tuple(before)
    out_shape, out_specs = [], []
    for rows in outs:
        if rows is None:
            queries = outs[0]
            out_shape.append(jax.ShapeDtypeStruct((pairs, 8, queries), F32))
            out_specs.append(pl.BlockSpec((1, 8, queries), lambda i: (i, 0, 0)))
        else:
            out_shape.append(jax.ShapeDtypeStruct((rows, pairs * PAIR), BF))
            out_specs.append(column(rows))
    return pl.pallas_call(
        kernel,
        grid=(pairs,),
        in_specs=in_specs,
        out_specs=out_specs,
        out_shape=out_shape,
        scratch_shapes=[pltpu.VMEM(bias_shape, F32)],
        compiler_params=pltpu.CompilerParams(vmem_limit_bytes=VMEM_LIMIT),
        cost_estimate=pl.CostEstimate(flops=flops, bytes_accessed=8 << 20, transcendentals=flops >> 8),
    )(*arguments)


def lse_spec(queries):
    return pl.BlockSpec((1, 8, queries), lambda i: (i, 0, 0))


def self_forward(core, qseg, own, other, queries, pair, pair_other):
    rows, width = queries.shape
    heads = width // HD
    length = rows // 2
    half = heads // 2
    return attention_call(
        self_forward_kernel,
        heads,
        [
            SMEM_SPEC,
            whole(qseg),
            whole(own),
            whole(other),
            column(rows),
            column(rows),
            column(rows, half),
            column(rows),
            column(rows, half),
        ],
        (rows, None),
        (5, length, length),
        heads * 5 * 4 * length * length * PAIR * 2,
        (core, qseg, own, other, queries, pair, pair, pair_other, pair_other),
    )


def self_backward(core, qseg, own, other, queries, pair, pair_other, grads, mixed, lse, before=()):
    rows, width = queries.shape
    heads = width // HD
    length = rows // 2
    half = heads // 2
    return attention_call(
        self_backward_kernel,
        heads,
        [
            SMEM_SPEC,
            whole(qseg),
            whole(own),
            whole(other),
            column(rows),
            column(rows),
            column(rows, half),
            column(rows),
            column(rows, half),
            column(rows),
            column(rows),
            lse_spec(rows),
        ],
        (rows,) * 5,
        (5, length, length),
        heads * 5 * 10 * length * length * PAIR * 2,
        (core, qseg, own, other, queries, pair, pair, pair_other, pair_other, grads, mixed, lse),
        before,
    )


def cross_forward(qseg, kseg, queries, pair):
    rows, width = queries.shape
    heads = width // HD
    count = pair.shape[0]
    return attention_call(
        cross_forward_kernel,
        heads,
        [whole(qseg), whole(kseg), column(rows), column(count), column(count, heads // 2)],
        (rows, None),
        (count, rows),
        heads * 4 * rows * count * PAIR * 2,
        (qseg, kseg, queries, pair, pair),
    )


def cross_backward(qseg, kseg, queries, pair, grads, mixed, lse, before=()):
    rows, width = queries.shape
    heads = width // HD
    count = pair.shape[0]
    return attention_call(
        cross_backward_kernel,
        heads,
        [
            whole(qseg),
            whole(kseg),
            column(rows),
            column(count),
            column(count, heads // 2),
            column(rows),
            column(rows),
            lse_spec(rows),
        ],
        (rows, count, count),
        (count, rows),
        heads * 10 * rows * count * PAIR * 2,
        (qseg, kseg, queries, pair, pair, grads, mixed, lse),
        before,
    )


def gelu_and_slope(values):
    inside = 0.5 * (1.0 + lax.erf(values * (0.5**0.5)))
    bell = jnp.exp(-0.5 * values * values) * ((2.0 * math.pi) ** -0.5)
    return values * inside, inside + values * bell

def feed_kernel(shape, meta_ref, own_ref, other_ref, gown_ref, gother_ref, win_ref, wout_ref, *refs):
    nx, ny, nz, chunk = shape
    res_ref, res_other_ref, grad_ref, grad_other_ref = refs[:4]
    gin_refs, gout_refs = refs[4 : 4 + nx], refs[4 + nx : 4 + nx + ny]
    act_ref, pre_ref, turned_ref, gturned_ref, res_acc, grad_acc = refs[4 + nx + ny :]
    j, i = pl.program_id(0), pl.program_id(1)
    z = meta_ref[3]
    tokens = own_ref.shape[0]
    sources = ((own_ref, gown_ref, res_ref, grad_ref), (other_ref, gother_ref, res_acc, grad_acc))

    @pl.when((i == 0) & (j == 0))
    def _():
        for side, (values, grads, res, grad) in enumerate(sources):
            at = slice(side * tokens, (side + 1) * tokens)
            turned_ref[:, at] = turned(values[...])
            gturned_ref[:, at] = turned(grads[...])
            res[...] = jnp.zeros_like(res)
            grad[...] = jnp.zeros_like(grad)

    for side, (values, grads, res, grad) in enumerate(sources):
        for m in range(tokens // chunk):
            at = slice(m * chunk, (m + 1) * chunk)
            activated, slope = gelu_and_slope(dot(values[at], win_ref[...]))
            activated = activated.astype(BF)
            before = (nt(grads[at], wout_ref[...]) * slope).astype(BF)
            to = slice(side * tokens + m * chunk, side * tokens + (m + 1) * chunk)
            act_ref[to] = activated
            pre_ref[to] = before
            res[at] += dot(activated, wout_ref[...])
            grad[at] += nt(before, win_ref[...])

    rows = turned_ref.shape[0] // nz
    for k in range(nz):
        source = pl.ds(pl.multiple_of((z + 1 + k) % nz * rows, rows), rows)
        to = slice(k * rows, (k + 1) * rows)
        gin = dot(turned_ref[source], pre_ref[...]).astype(BF)
        gout = dot(gturned_ref[source], act_ref[...]).astype(BF)
        for number, ref in enumerate(gin_refs):

            @pl.when(j == number)
            def _(ref=ref):
                ref[0, to] = gin

        for number, ref in enumerate(gout_refs):

            @pl.when(i == number)
            def _(ref=ref):
                ref[0, to] = gout

    @pl.when((i == ny - 1) & (j == nx - 1))
    def _():
        res_other_ref[...] = res_acc[...].astype(BF)
        grad_other_ref[...] = grad_acc[...].astype(BF)


def feed(place, meta, own, other, gown, gother, feed_in, feed_out):
    nx, ny, nz = place.nx, place.ny, place.nz
    tokens, width = own.shape
    part = feed_in.shape[1] // place.seq // 2
    chunk = min(256, tokens)

    def unit(j, i, meta):
        return 2 * ((meta[2] + 1 + i) % ny * nx + (meta[1] + 1 + j) % nx) + meta[0]

    def gin_spec(number):
        def index(j, i, meta):
            return jnp.where(j == number, i, jnp.where(j < number, 0, ny - 1)), 0, 0

        return pl.BlockSpec((1, width, part), index)

    gout_spec = pl.BlockSpec((1, width, part), lambda j, i, meta: (j, 0, 0))
    total = 2 * tokens
    return pl.pallas_call(
        functools.partial(feed_kernel, (nx, ny, nz, chunk)),
        grid_spec=pltpu.PrefetchScalarGridSpec(
            num_scalar_prefetch=1,
            grid=(nx, ny),
            in_specs=[WHOLE_SPEC] * 4
            + [
                pl.BlockSpec((width, part), lambda j, i, meta: (0, unit(j, i, meta))),
                pl.BlockSpec((part, width), lambda j, i, meta: (unit(j, i, meta), 0)),
            ],
            out_specs=[WHOLE_SPEC] * 4 + [gin_spec(n) for n in range(nx)] + [gout_spec] * ny,
            scratch_shapes=[
                pltpu.VMEM((total, part), BF),
                pltpu.VMEM((total, part), BF),
                pltpu.VMEM((width, total), BF),
                pltpu.VMEM((width, total), BF),
                pltpu.VMEM((tokens, width), F32),
                pltpu.VMEM((tokens, width), F32),
            ],
        ),
        out_shape=[
            jax.ShapeDtypeStruct((tokens, width), F32),
            jax.ShapeDtypeStruct((tokens, width), BF),
            jax.ShapeDtypeStruct((tokens, width), F32),
            jax.ShapeDtypeStruct((tokens, width), BF),
        ]
        + [jax.ShapeDtypeStruct((ny, width, part), BF)] * nx
        + [jax.ShapeDtypeStruct((nx, width, part), BF)] * ny,
        compiler_params=pltpu.CompilerParams(vmem_limit_bytes=60 * 1024 * 1024),
        cost_estimate=pl.CostEstimate(
            flops=12 * total * width * part * place.seq,
            bytes_accessed=40 << 20,
            transcendentals=2 * total * part * place.seq,
        ),
    )(meta, own, other, gown, gother, feed_in, feed_out)


def weight_kernel(shape, meta_ref, *refs):
    count, nz = shape
    lefts, rights = refs[:count], refs[count : 2 * count]
    own_ref, other_ref, turned_ref = refs[2 * count :]
    core, z = meta_ref[0], meta_ref[3]
    block = own_ref.shape[1] // nz
    for number in range(count):

        @pl.when(pl.program_id(0) == number)
        def _(left=lefts[number], right=rights[number]):
            tokens = left.shape[0]
            turned_ref[:, :tokens] = turned(left[...])
            for k in range(nz):
                start = (z + 1 + k) % nz * 2
                to = slice(k * block, (k + 1) * block)
                for which, ref in ((core, own_ref), (1 - core, other_ref)):
                    at = pl.ds(pl.multiple_of((start + which) * block, block), block)
                    ref[0, to] = dot(turned_ref[at, :tokens], right[...]).astype(BF)


def weight_parts(place, meta, lefts, rights, before=()):
    count = len(lefts)
    depth, width = lefts[0].shape[1], rights[0].shape[1]
    tokens = max(left.shape[0] for left in lefts)
    out = jax.ShapeDtypeStruct((count, depth // 2, width), BF)
    spec = pl.BlockSpec((1, depth // 2, width), lambda u: (u, 0, 0))
    return pl.pallas_call(
        without(functools.partial(weight_kernel, (count, place.nz)), 1 + 2 * count, len(before)),
        grid=(count,),
        in_specs=[SMEM_SPEC] + [WHOLE_SPEC] * (2 * count) + [ANY_SPEC] * len(before),
        out_specs=[spec, spec],
        out_shape=[out, out],
        scratch_shapes=[pltpu.VMEM((depth, tokens), BF)],
        compiler_params=pltpu.CompilerParams(vmem_limit_bytes=VMEM_LIMIT),
        cost_estimate=pl.CostEstimate(
            flops=2 * count * tokens * depth * width,
            bytes_accessed=count * depth * width * 4,
            transcendentals=0,
        ),
    )(meta, *lefts, *rights, *before)


def shards(
    frames,
    text_states,
    clip_lengths,
    text_lengths,
    self_gain,
    self_shift,
    self_qkv,
    self_out,
    cross_gain,
    cross_shift,
    cross_query,
    text_proj,
    text_bias,
    cross_kv,
    cross_out,
    feed_gain,
    feed_shift,
    feed_in,
    feed_out,
    grad_out,
):
    place = Place()
    count = frames.shape[0]
    width = frames.shape[2]
    frame_total = frames.shape[1] * place.seq
    text_total = text_states.shape[1] * place.seq

    lengths = jnp.concatenate([clip_lengths, text_lengths], axis=1)
    lengths_other = place.swap_core(lengths)
    mine = place.spot // count == place.core
    row_lengths = pick(jnp.where(mine, lengths, lengths_other), place.spot % count, 0)
    clips = clip_lengths.shape[1]
    frame_ends = jnp.cumsum(row_lengths[:clips])
    text_ends = jnp.cumsum(row_lengths[clips:])

    def segments(positions, ends):
        return jnp.sum((positions[:, None] >= ends[None, :]).astype(jnp.int32), axis=1)

    own_segment = segments(place.positions(frame_total, place.core), frame_ends)
    other_segment = segments(place.positions(frame_total, 1 - place.core), frame_ends)
    text_positions = jnp.concatenate(
        [place.positions(text_total, place.core), place.positions(text_total, 1 - place.core)]
    )
    text_segment = segments(text_positions, text_ends)
    query_segment = own_segment[None, :]
    own_segment, other_segment = own_segment[:, None], other_segment[:, None]
    text_segment = text_segment[:, None]
    core = place.core.reshape(1).astype(jnp.int32)

    text_half = place.to_rows(text_states)
    layer_raw = place.to_rows(frames)
    text_input = jnp.concatenate([text_half, place.swap_core(text_half)], axis=0)
    cotangent = place.to_rows(after(grad_out, layer_raw))
    cotangent_other = place.swap_core(cotangent)
    projected = (dot(text_input, text_proj) + text_bias).astype(BF)
    text_pair = dot(projected, cross_kv).astype(BF)

    layer_input = layer_raw.astype(F32)
    normed_self = layer_norm(layer_input, self_gain, self_shift)
    pair = dot(normed_self, self_qkv[:, width:]).astype(BF)
    pair_other = place.swap_core(pair)
    queries = dot(normed_self, self_qkv[:, :width]).astype(BF)
    self_mix, self_lse = self_forward(
        core, query_segment, own_segment, other_segment, queries, pair, pair_other
    )
    first = layer_input + dot(self_mix, self_out)
    normed_cross = layer_norm(first, cross_gain, cross_shift)
    cross_queries = dot(normed_cross, cross_query).astype(BF)
    cross_mix, cross_lse = cross_forward(query_segment, text_segment, cross_queries, text_pair)
    second = first + dot(cross_mix, cross_out)
    normed_feed = layer_norm(second, feed_gain, feed_shift)

    nx, ny, nz, seq = place.nx, place.ny, place.nz, place.seq
    meta = jnp.stack([place.core, place.x, place.y, place.z]).astype(jnp.int32)
    normed_other = place.swap_core(normed_feed)
    fed = feed(
        place, meta, normed_feed, normed_other, cotangent, cotangent_other, feed_in, feed_out
    )
    result, result_away, grad_normed_feed, grad_away = fed[:4]
    grad_in, grad_out_parts = fed[4 : 4 + nx], fed[4 + nx :]
    grad_normed_feed = grad_normed_feed + place.swap_core(grad_away).astype(F32)

    def x_piece(k):
        return lambda: grad_in[k].astype(F32)

    def y_piece(k):
        return lambda: grad_out_parts[k].astype(F32)

    in_half = ring_sum([x_piece(k) for k in range(nx)], place.next_x).astype(BF)
    out_half = ring_sum([y_piece(k) for k in range(ny)], place.next_y).astype(BF)

    grad_part, grad_feed_gain, grad_feed_shift = norm_backward(second, feed_gain, grad_normed_feed)
    grad_second = cotangent.astype(F32) + grad_part
    grad_second_branch = grad_second.astype(BF)
    grad_cross_mix = dot(grad_second_branch, cross_out, 1, 1).astype(BF)
    grad_cross_queries, grad_text_keys, grad_text_values = cross_backward(
        query_segment,
        text_segment,
        cross_queries,
        text_pair,
        grad_cross_mix,
        cross_mix,
        cross_lse,
    )
    result = (second + result + place.swap_core(after(result_away, grad_cross_mix)).astype(F32)).astype(BF)
    result = place.from_rows(result, count)
    grad_normed_cross = dot(grad_cross_queries, cross_query, 1, 1)
    grad_part, grad_cross_gain, grad_cross_shift = norm_backward(first, cross_gain, grad_normed_cross)
    grad_first = grad_second + grad_part
    grad_first_branch = grad_first.astype(BF)
    grad_self_mix = dot(grad_first_branch, self_out, 1, 1).astype(BF)

    grad_pair = jnp.concatenate([grad_text_keys, grad_text_values], axis=1)
    grad_projected = dot(grad_pair, cross_kv, 1, 1).astype(BF)
    text_blocks = text_input.reshape(text_total, place.rows, -1)
    padding = width // place.rows - text_blocks.shape[2]
    text_padded = jnp.pad(text_blocks, ((0, 0), (0, 0), (0, padding))).reshape(text_total, width)
    middle_own, middle_away = weight_parts(
        place,
        meta,
        [cross_mix, normed_cross, projected, projected, text_padded],
        [grad_second_branch, grad_cross_queries, grad_text_keys, grad_text_values, grad_projected],
    )
    out_own, out_away = weight_parts(place, meta, [self_mix], [grad_first_branch])
    middle_got = place.swap_core(middle_away)
    out_got = place.swap_core(out_away)
    grad_text_bias = jnp.sum(grad_projected.astype(F32), axis=0)
    grad_text = dot(grad_projected, text_proj, 1, 1)

    grad_queries, grad_keys, grad_values, keys_away, values_away = self_backward(
        core,
        query_segment,
        own_segment,
        other_segment,
        queries,
        pair,
        pair_other,
        grad_self_mix,
        self_mix,
        self_lse,
        before=(in_half, out_half, middle_got, out_got),
    )
    grad_keys = (grad_keys.astype(F32) + place.swap_core(keys_away).astype(F32)).astype(BF)
    grad_values = (grad_values.astype(F32) + place.swap_core(values_away).astype(F32)).astype(BF)
    grad_packed = jnp.concatenate([grad_queries, grad_keys, grad_values], axis=1)

    in_quarter = ring_sum([lambda k=k: in_half[k].astype(F32) for k in range(ny)], place.next_y)
    out_quarter = ring_sum([lambda k=k: out_half[k].astype(F32) for k in range(nx)], place.next_x)
    feed_quarter = jnp.stack([in_quarter, out_quarter]).astype(BF)
    feed_quarter = feed_quarter.reshape(2, nz, -1, feed_quarter.shape[2])
    feed_own = ring_sum([lambda k=k: feed_quarter[:, k].astype(F32) for k in range(nz)], place.next_z)
    block = width // place.rows
    feed_own = feed_own.reshape(2, 2, block, -1)
    feed_got = place.swap_core(pick(feed_own, 1 - place.core, 1))
    feed_own = pick(feed_own, place.core, 1)
    low = jnp.where(place.core == 0, feed_own, feed_got)
    high = jnp.where(place.core == 0, feed_got, feed_own)
    sum_feed = jnp.concatenate([low, high], axis=2)

    def middle_piece(k):
        at = slice(k * block, (k + 1) * block)
        return lambda: middle_own[:, at].astype(F32) + middle_got[:, at].astype(F32)

    middle = ring_sum([middle_piece(k) for k in range(nz)], place.next_z).astype(BF)
    spread = jnp.concatenate(
        [
            middle[0].reshape(block, seq, -1),
            middle[1].reshape(block, seq, -1),
            jnp.concatenate([middle[2], middle[3]], axis=1).reshape(block, seq, -1),
            middle[4].reshape(block, seq, -1),
        ],
        axis=2,
    ).reshape(block, ny, nx, -1)

    def shifted(array, index, number, length, axis):
        return lambda: pick(array, (index + 1 + number) % length, axis).astype(F32)

    spread = ring_sum([shifted(spread, place.x, k, nx, 2) for k in range(nx)], place.next_x).astype(BF)
    spread = ring_sum([shifted(spread, place.y, k, ny, 1) for k in range(ny)], place.next_y)
    piece = width // seq
    sum_cross_out, sum_cross_query = spread[:, :piece], spread[:, piece : 2 * piece]
    sum_cross_kv, sum_text_proj = spread[:, 2 * piece : 4 * piece], spread[:, 4 * piece :]
    sum_text_proj = sum_text_proj[: block - padding]

    relative_parts = place.relative_columns(grad_packed, True)
    qkv_own, qkv_away = weight_parts(place, meta, [normed_self], [relative_parts])
    qkv_got = place.swap_core(qkv_away)

    def columns(array):
        return array[0].reshape(array.shape[1], nx, ny, -1)

    def natural(array):
        return jnp.stack(
            [
                jnp.stack(
                    [
                        pick(array[0].reshape(array.shape[1], seq, -1), place.offset(i, j), 1)
                        for i in range(ny)
                    ],
                    axis=1,
                )
                for j in range(nx)
            ],
            axis=1,
        )

    last_own = jnp.concatenate([columns(qkv_own), natural(out_own)], axis=3)
    last_got = jnp.concatenate([columns(qkv_got), natural(out_got)], axis=3)
    last = (last_own.astype(F32) + last_got.astype(F32)).astype(BF)
    last = last.reshape(nz, 2, block // 2, nx, ny, -1)
    upper = ring_sum([lambda k=k: last[:, 0, :, k].astype(F32) for k in range(nx)], place.next_x).astype(BF)
    lower = ring_sum([lambda k=k: last[:, 1, :, :, k].astype(F32) for k in range(ny)], place.next_y).astype(BF)
    upper = ring_sum([lambda a=upper[:, :, k]: a.astype(F32) for k in range(ny)], place.next_y)
    lower = ring_sum([lambda a=lower[:, :, k]: a.astype(F32) for k in range(nx)], place.next_x)
    last = jnp.stack([upper, lower], axis=1).astype(BF)
    last = ring_sum([lambda a=last[k]: a.astype(F32) for k in range(nz)], place.next_z)
    last = last.reshape(block, -1)
    sum_self_qkv, sum_self_out = last[:, : 3 * piece], last[:, 3 * piece :]

    grad_normed_self = dot(grad_packed, self_qkv, 1, 1)
    grad_part, grad_self_gain, grad_self_shift = norm_backward(layer_input, self_gain, grad_normed_self)
    grad_frames = place.from_rows((grad_first + grad_part).astype(BF), count)
    half = grad_text.shape[0] // 2
    text_away = place.swap_core(grad_text[half:].astype(BF))
    grad_text = place.from_rows((grad_text[:half] + text_away.astype(F32)).astype(BF), count)

    vectors = place.vector_sum(
        jnp.stack(
            [
                grad_self_gain,
                grad_self_shift,
                grad_cross_gain,
                grad_cross_shift,
                grad_text_bias,
                grad_feed_gain,
                grad_feed_shift,
            ]
        )
    )
    vectors = pick(vectors.reshape(7, seq, width // seq), place.spot, 1)
    return (
        result,
        grad_frames.astype(F32),
        grad_text.astype(F32),
        vectors[0],
        vectors[1],
        sum_self_qkv,
        sum_self_out,
        vectors[2],
        vectors[3],
        sum_cross_query,
        sum_text_proj,
        vectors[4],
        sum_cross_kv,
        sum_cross_out,
        vectors[5],
        vectors[6],
        sum_feed[0],
        jnp.swapaxes(sum_feed[1], 0, 1),
    )


def solution(mesh):
    split, copied, table = P(ROWS, SEQ, None), P(), P(ROWS, None)
    vector, matrix = P(SEQ), P(ROWS, SEQ)
    return jax.shard_map(
        shards,
        mesh=mesh,
        in_specs=(split, split, table, table) + (copied,) * 15 + (split,),
        out_specs=(
            (split,) * 3
            + (vector, vector, matrix, matrix)
            + (vector, vector, matrix, matrix)
            + (vector, matrix, matrix)
            + (vector, vector, matrix, P(SEQ, ROWS))
        ),
        check_vma=False,
    )
```

```python
import functools
import math

import jax
import jax.numpy as jnp
from jax import lax
from jax.experimental import pallas as pl
from jax.experimental.pallas import tpu as pltpu
from jax.sharding import PartitionSpec as P

HD = 64
PAIR = 2 * HD
EPSILON = 1e-05
MASKED = -1e30
ROWS = "rows"
SEQ = "seq"
BF = jnp.bfloat16
F32 = jnp.float32
VMEM_LIMIT = 48 * 1024 * 1024


def dot(left, right, left_dim=1, right_dim=0):
    return lax.dot_general(
        left, right, (((left_dim,), (right_dim,)), ((), ())), preferred_element_type=F32
    )


def pick(array, index, axis):
    return lax.dynamic_index_in_dim(array, index, axis, keepdims=False)


def after(value, *others):
    return lax.optimization_barrier((value,) + others)[0]


class Place:
    def __init__(self):
        self.rows, self.seq = lax.axis_size(ROWS), lax.axis_size(SEQ)
        self.nz = self.rows // 2
        self.nx = math.isqrt(self.seq)
        self.ny = self.seq // self.nx
        row, self.spot = lax.axis_index(ROWS), lax.axis_index(SEQ)
        self.core, self.z = row % 2, row // 2
        self.x, self.y = self.spot % self.nx, self.spot // self.nx
        self.owner = [0 if 4 * s // self.seq in (0, 3) else 1 for s in range(self.seq)]
        self.members = [[s for s in range(self.seq) if self.owner[s] == c] for c in (0, 1)]
        self.rank = [self.members[self.owner[s]].index(s) for s in range(self.seq)]

    def permute(self, value, target):
        pairs = []
        for z in range(self.nz):
            for c in range(2):
                for s in range(self.seq):
                    tz, tc, ts = target(z, c, s)
                    pairs.append(((2 * z + c) * self.seq + s, (2 * tz + tc) * self.seq + ts))
        return lax.ppermute(value, (ROWS, SEQ), pairs)

    def swap_core(self, value):
        return self.permute(value, lambda z, c, s: (z, 1 - c, s))

    def next_z(self, value):
        return self.permute(value, lambda z, c, s: ((z + 1) % self.nz, c, s))

    def next_x(self, value):
        nx = self.nx
        return self.permute(value, lambda z, c, s: (z, c, s // nx * nx + (s % nx + 1) % nx))

    def next_y(self, value):
        return self.permute(value, lambda z, c, s: (z, c, (s + self.nx) % self.seq))

    def to_rows(self, value):
        count = value.shape[0]
        my_rank = jnp.array(self.rank, jnp.int32)[self.spot]
        got = []
        for t in range(count):

            def target(z, c, s, t=t):
                return z, self.owner[s], c * count + (t + self.rank[s]) % count

            got.append(self.permute(pick(value, (t + my_rank) % count, 0), target))
        stacked = jnp.stack(got)
        here = self.spot % count
        return jnp.concatenate([pick(stacked, (here - k) % count, 0) for k in range(count)], axis=0)

    def from_rows(self, value, count):
        my_rank = jnp.array(self.rank, jnp.int32)[self.spot]
        slots = value.reshape(count, value.shape[0] // count, value.shape[1])
        here = self.spot % count
        got = []
        for t in range(count):

            def target(z, c, s, t=t):
                return z, s // count, self.members[c][(s % count - t) % count]

            got.append(self.permute(pick(slots, (here - t) % count, 0), target))
        stacked = jnp.stack(got)
        return jnp.stack([pick(stacked, (i - my_rank) % count, 0) for i in range(count)])

    def positions(self, total, core):
        quarter = total // 4
        inner = jnp.arange(quarter, dtype=jnp.int32)
        return jnp.concatenate([inner + core * quarter, inner + (3 - core) * quarter])

    def offset(self, i, j):
        return (self.y + 1 + i) % self.ny * self.nx + (self.x + 1 + j) % self.nx

    def relative_columns(self, value, outer_x):
        blocks = value.reshape(value.shape[0], self.seq, -1)
        if outer_x:
            order = [self.offset(i, j) for j in range(self.nx) for i in range(self.ny)]
        else:
            order = [self.offset(i, j) for i in range(self.ny) for j in range(self.nx)]
        return jnp.concatenate([pick(blocks, place, 1) for place in order], axis=1)


    def vector_sum(self, value):
        bit = 1
        while bit < self.rows:
            value = value + self.permute(
                value,
                lambda z, c, s: ((2 * z + c ^ bit) // 2, (2 * z + c ^ bit) % 2, s),
            )
            bit *= 2
        bit = 1
        while bit < self.seq:
            value = value + self.permute(value, lambda z, c, s: (z, c, s ^ bit))
            bit *= 2
        return value


def ring_order(count):
    return list(range(count - 2, -1, -1)) + [count - 1]


def ring_sum(pieces, send):
    order = ring_order(len(pieces))
    value = pieces[order[0]]()
    for k in order[1:]:
        value = pieces[k]() + send(value.astype(BF)).astype(F32)
    return value


def normalize(values):
    centered = values - jnp.mean(values, axis=-1, keepdims=True)
    scale = lax.rsqrt(jnp.mean(centered * centered, axis=-1, keepdims=True) + EPSILON)
    return centered * scale, scale


def layer_norm(values, gain, shift):
    return (normalize(values)[0] * gain + shift).astype(BF)


def norm_backward(values, gain, cotangent):
    normal, scale = normalize(values)
    grown = cotangent * gain
    inner = jnp.mean(grown, axis=-1, keepdims=True)
    along = jnp.mean(grown * normal, axis=-1, keepdims=True)
    grad = scale * (grown - inner - normal * along)
    return grad, jnp.sum(cotangent * normal, axis=0), jnp.sum(cotangent, axis=0)


def nt(left, right):
    return dot(left, right, 1, 1)


def head_lanes(values, head):
    lane = lax.broadcasted_iota(jnp.int32, values.shape, 1)
    return jnp.where((lane < HD) == (head == 0), values, jnp.zeros_like(values))


def turned(values):
    return jnp.swapaxes(values.astype(F32), 0, 1).astype(BF)


def segment_bias(key_segment, query_segment, causal):
    allowed = key_segment == query_segment
    if causal:
        key = lax.broadcasted_iota(jnp.int32, allowed.shape, 0)
        query = lax.broadcasted_iota(jnp.int32, allowed.shape, 1)
        allowed = allowed & (key <= query)
    return jnp.where(allowed, 0.0, MASKED).astype(F32)


def forward_heads(queries, blocks, lse_ref, at):
    parts = []
    for head in range(2):
        query = head_lanes(queries, head)
        scores = [nt(keys, query) + bias() for keys, _, bias in blocks]
        highest = functools.reduce(
            jnp.maximum, [jnp.max(s, axis=0, keepdims=True) for s in scores]
        )
        weights = [jnp.exp(s - highest) for s in scores]
        total = sum(jnp.sum(w, axis=0, keepdims=True) for w in weights)
        mixed = sum(
            dot(values[head * HD : (head + 1) * HD], w.astype(BF))
            for (_, values, _), w in zip(blocks, weights)
        )
        parts.append(mixed * (1.0 / total))
        lse_ref[0, head : head + 1, at] = highest + jnp.log(total)
    return jnp.swapaxes(jnp.concatenate(parts, axis=0), 0, 1).astype(BF)


def backward_heads(queries, grads, mixed, blocks, lse_ref, at):
    product = jnp.swapaxes(grads.astype(F32) * mixed.astype(F32), 0, 1)
    parts = []
    for head in range(2):
        query, grad = head_lanes(queries, head), head_lanes(grads, head)
        rows = slice(head * HD, (head + 1) * HD)
        inner = jnp.sum(product[rows], axis=0, keepdims=True)
        totals = lse_ref[0, head : head + 1, at]
        grad_query = None
        for keys, turned_keys, values, bias, sums in blocks:
            weights = jnp.exp(nt(keys, query) + bias() - totals)
            scores = (weights * (nt(values, grad) - inner)).astype(BF)
            add_to(sums, 0, dot(scores, query))
            add_to(sums, 1, dot(weights.astype(BF), grad))
            term = dot(turned_keys[rows], scores)
            grad_query = term if grad_query is None else grad_query + term
        parts.append(grad_query)
    return (jnp.swapaxes(jnp.concatenate(parts, axis=0), 0, 1) * HD**-0.5).astype(BF)


def add_to(sums, index, term):
    sums[index] = term if sums[index] is None else sums[index] + term


def scaled(values):
    return values * jnp.array(HD**-0.5, BF)


def self_plan(core):
    if core == 0:
        return [(0, 0, 0)], [(0, 0, 1), (0, 1, 2), (1, 0, 3), (1, 1, 4)]
    return [(0, 0, 0), (1, 0, 4)], [(0, 0, 1), (0, 1, 2), (1, 0, 3)]


def self_biases(core, qseg_ref, kseg_refs, bias_ref):
    length = bias_ref.shape[1]
    low, high = slice(0, length), slice(length, 2 * length)
    own, other = kseg_refs
    bias_ref[0] = segment_bias(own[low], qseg_ref[:, low], True)
    bias_ref[1] = segment_bias(own[low], qseg_ref[:, high], False)
    bias_ref[2] = segment_bias(own[high], qseg_ref[:, high], True)
    bias_ref[3] = segment_bias(other[low], qseg_ref[:, high], False)

    @pl.when(core == 0)
    def _():
        bias_ref[4] = segment_bias(other[high], qseg_ref[:, high], False)

    @pl.when(core != 0)
    def _():
        bias_ref[4] = segment_bias(other[low], qseg_ref[:, low], False)


def self_forward_kernel(
    core_ref, qseg_ref, own_ref, other_ref, q_ref, k_ref, v_ref, ko_ref, vo_ref, o_ref, lse_ref, bias_ref
):
    core = core_ref[0]
    length = bias_ref.shape[1]

    @pl.when(pl.program_id(0) == 0)
    def _():
        self_biases(core, qseg_ref, (own_ref, other_ref), bias_ref)

    keys, values = (k_ref, ko_ref), (v_ref, vo_ref)
    for which in range(2):

        @pl.when((core == 0) == (which == 0))
        def _(which=which):
            for half, plan in enumerate(self_plan(which)):
                at = slice(half * length, (half + 1) * length)
                blocks = []
                for source, part, number in plan:
                    where = slice(part * length, (part + 1) * length)
                    blocks.append(
                        (
                            keys[source][where],
                            turned(values[source][where]),
                            functools.partial(bias_ref.__getitem__, number),
                        )
                    )
                o_ref[at] = forward_heads(scaled(q_ref[at]), blocks, lse_ref, at)


def self_backward_kernel(
    core_ref,
    qseg_ref,
    own_ref,
    other_ref,
    q_ref,
    k_ref,
    v_ref,
    ko_ref,
    vo_ref,
    g_ref,
    o_ref,
    lse_ref,
    dq_ref,
    dk_ref,
    dv_ref,
    dko_ref,
    dvo_ref,
    bias_ref,
):
    core = core_ref[0]
    length = bias_ref.shape[1]

    @pl.when(pl.program_id(0) == 0)
    def _():
        self_biases(core, qseg_ref, (own_ref, other_ref), bias_ref)

    keys, values = (k_ref, ko_ref), (v_ref, vo_ref)
    for which in range(2):

        @pl.when((core == 0) == (which == 0))
        def _(which=which):
            sums = {(s, p): [None, None] for s in range(2) for p in range(2)}
            for half, plan in enumerate(self_plan(which)):
                at = slice(half * length, (half + 1) * length)
                blocks = []
                for source, part, number in plan:
                    where = slice(part * length, (part + 1) * length)
                    blocks.append(
                        (
                            keys[source][where],
                            turned(keys[source][where]),
                            values[source][where],
                            functools.partial(bias_ref.__getitem__, number),
                            sums[source, part],
                        )
                    )
                dq_ref[at] = backward_heads(
                    scaled(q_ref[at]), g_ref[at], o_ref[at], blocks, lse_ref, at
                )
            for (source, part), pair in sums.items():
                where = slice(part * length, (part + 1) * length)
                for ref, value in zip(((dk_ref, dv_ref), (dko_ref, dvo_ref))[source], pair):
                    if value is None:
                        ref[where] = jnp.zeros((length, PAIR), BF)
                    else:
                        ref[where] = value.astype(BF)


def cross_forward_kernel(qseg_ref, kseg_ref, q_ref, k_ref, v_ref, o_ref, lse_ref, bias_ref):
    length = q_ref.shape[0] // 2

    @pl.when(pl.program_id(0) == 0)
    def _():
        bias_ref[...] = segment_bias(kseg_ref[...], qseg_ref[...], False)

    turned_values = turned(v_ref[...])
    for half in range(2):
        at = slice(half * length, (half + 1) * length)
        blocks = [(k_ref[...], turned_values, lambda at=at: bias_ref[:, at])]
        o_ref[at] = forward_heads(scaled(q_ref[at]), blocks, lse_ref, at)


def cross_backward_kernel(
    qseg_ref,
    kseg_ref,
    q_ref,
    k_ref,
    v_ref,
    g_ref,
    o_ref,
    lse_ref,
    dq_ref,
    dk_ref,
    dv_ref,
    bias_ref,
):
    length = q_ref.shape[0] // 2

    @pl.when(pl.program_id(0) == 0)
    def _():
        bias_ref[...] = segment_bias(kseg_ref[...], qseg_ref[...], False)

    turned_keys = turned(k_ref[...])
    sums = [None, None]
    for half in range(2):
        at = slice(half * length, (half + 1) * length)
        blocks = [(k_ref[...], turned_keys, v_ref[...], lambda at=at: bias_ref[:, at], sums)]
        dq_ref[at] = backward_heads(scaled(q_ref[at]), g_ref[at], o_ref[at], blocks, lse_ref, at)
    dk_ref[...] = sums[0].astype(BF)
    dv_ref[...] = sums[1].astype(BF)


def column(rows, first=0):
    return pl.BlockSpec((rows, PAIR), lambda i: (0, first + i))


def whole(array):
    return pl.BlockSpec(array.shape, lambda i: (0,) * array.ndim)


SMEM_SPEC = pl.BlockSpec(memory_space=pltpu.SMEM)


def without(kernel, first, count):
    def run(*refs):
        kernel(*refs[:first], *refs[first + count :])

    return run


ANY_SPEC = pl.BlockSpec(memory_space=pl.ANY)
WHOLE_SPEC = pl.BlockSpec(memory_space=pltpu.VMEM)


def attention_call(kernel, heads, in_specs, outs, bias_shape, flops, arguments, before=()):
    pairs = heads // 2
    kernel = without(kernel, len(arguments), len(before))
    in_specs = list(in_specs) + [ANY_SPEC] * len(before)
    arguments = tuple(arguments) + tuple(before)
    out_shape, out_specs = [], []
    for rows in outs:
        if rows is None:
            queries = outs[0]
            out_shape.append(jax.ShapeDtypeStruct((pairs, 8, queries), F32))
            out_specs.append(pl.BlockSpec((1, 8, queries), lambda i: (i, 0, 0)))
        else:
            out_shape.append(jax.ShapeDtypeStruct((rows, pairs * PAIR), BF))
            out_specs.append(column(rows))
    return pl.pallas_call(
        kernel,
        grid=(pairs,),
        in_specs=in_specs,
        out_specs=out_specs,
        out_shape=out_shape,
        scratch_shapes=[pltpu.VMEM(bias_shape, F32)],
        compiler_params=pltpu.CompilerParams(vmem_limit_bytes=VMEM_LIMIT),
        cost_estimate=pl.CostEstimate(flops=flops, bytes_accessed=8 << 20, transcendentals=flops >> 8),
    )(*arguments)


def lse_spec(queries):
    return pl.BlockSpec((1, 8, queries), lambda i: (i, 0, 0))


def self_forward(core, qseg, own, other, queries, pair, pair_other):
    rows, width = queries.shape
    heads = width // HD
    length = rows // 2
    half = heads // 2
    return attention_call(
        self_forward_kernel,
        heads,
        [
            SMEM_SPEC,
            whole(qseg),
            whole(own),
            whole(other),
            column(rows),
            column(rows),
            column(rows, half),
            column(rows),
            column(rows, half),
        ],
        (rows, None),
        (5, length, length),
        heads * 5 * 4 * length * length * PAIR * 2,
        (core, qseg, own, other, queries, pair, pair, pair_other, pair_other),
    )


def self_backward(core, qseg, own, other, queries, pair, pair_other, grads, mixed, lse, before=()):
    rows, width = queries.shape
    heads = width // HD
    length = rows // 2
    half = heads // 2
    return attention_call(
        self_backward_kernel,
        heads,
        [
            SMEM_SPEC,
            whole(qseg),
            whole(own),
            whole(other),
            column(rows),
            column(rows),
            column(rows, half),
            column(rows),
            column(rows, half),
            column(rows),
            column(rows),
            lse_spec(rows),
        ],
        (rows,) * 5,
        (5, length, length),
        heads * 5 * 10 * length * length * PAIR * 2,
        (core, qseg, own, other, queries, pair, pair, pair_other, pair_other, grads, mixed, lse),
        before,
    )


def cross_forward(qseg, kseg, queries, pair):
    rows, width = queries.shape
    heads = width // HD
    count = pair.shape[0]
    return attention_call(
        cross_forward_kernel,
        heads,
        [whole(qseg), whole(kseg), column(rows), column(count), column(count, heads // 2)],
        (rows, None),
        (count, rows),
        heads * 4 * rows * count * PAIR * 2,
        (qseg, kseg, queries, pair, pair),
    )


def cross_backward(qseg, kseg, queries, pair, grads, mixed, lse, before=()):
    rows, width = queries.shape
    heads = width // HD
    count = pair.shape[0]
    return attention_call(
        cross_backward_kernel,
        heads,
        [
            whole(qseg),
            whole(kseg),
            column(rows),
            column(count),
            column(count, heads // 2),
            column(rows),
            column(rows),
            lse_spec(rows),
        ],
        (rows, count, count),
        (count, rows),
        heads * 10 * rows * count * PAIR * 2,
        (qseg, kseg, queries, pair, pair, grads, mixed, lse),
        before,
    )


def gelu_and_slope(values):
    inside = 0.5 * (1.0 + lax.erf(values * (0.5**0.5)))
    bell = jnp.exp(-0.5 * values * values) * ((2.0 * math.pi) ** -0.5)
    return values * inside, inside + values * bell

def feed_kernel(shape, meta_ref, own_ref, other_ref, gown_ref, gother_ref, win_ref, wout_ref, *refs):
    nx, ny, nz, chunk = shape
    res_ref, res_other_ref, grad_ref, grad_other_ref = refs[:4]
    gin_refs, gout_refs = refs[4 : 4 + nx], refs[4 + nx : 4 + nx + ny]
    act_ref, pre_ref, turned_ref, gturned_ref, res_acc, grad_acc = refs[4 + nx + ny :]
    j, i = pl.program_id(0), pl.program_id(1)
    z = meta_ref[3]
    tokens = own_ref.shape[0]
    sources = ((own_ref, gown_ref, res_ref, grad_ref), (other_ref, gother_ref, res_acc, grad_acc))

    @pl.when((i == 0) & (j == 0))
    def _():
        for side, (values, grads, res, grad) in enumerate(sources):
            at = slice(side * tokens, (side + 1) * tokens)
            turned_ref[:, at] = turned(values[...])
            gturned_ref[:, at] = turned(grads[...])
            res[...] = jnp.zeros_like(res)
            grad[...] = jnp.zeros_like(grad)

    for side, (values, grads, res, grad) in enumerate(sources):
        for m in range(tokens // chunk):
            at = slice(m * chunk, (m + 1) * chunk)
            activated, slope = gelu_and_slope(dot(values[at], win_ref[...]))
            activated = activated.astype(BF)
            before = (nt(grads[at], wout_ref[...]) * slope).astype(BF)
            to = slice(side * tokens + m * chunk, side * tokens + (m + 1) * chunk)
            act_ref[to] = activated
            pre_ref[to] = before
            res[at] += dot(activated, wout_ref[...])
            grad[at] += nt(before, win_ref[...])

    rows = turned_ref.shape[0] // nz
    for k in range(nz):
        source = pl.ds(pl.multiple_of((z + 1 + k) % nz * rows, rows), rows)
        to = slice(k * rows, (k + 1) * rows)
        gin = dot(turned_ref[source], pre_ref[...]).astype(BF)
        gout = dot(gturned_ref[source], act_ref[...]).astype(BF)
        for number, ref in enumerate(gin_refs):

            @pl.when(j == number)
            def _(ref=ref):
                ref[0, to] = gin

        for number, ref in enumerate(gout_refs):

            @pl.when(i == number)
            def _(ref=ref):
                ref[0, to] = gout

    @pl.when((i == ny - 1) & (j == nx - 1))
    def _():
        res_other_ref[...] = res_acc[...].astype(BF)
        grad_other_ref[...] = grad_acc[...].astype(BF)


def feed(place, meta, own, other, gown, gother, feed_in, feed_out):
    nx, ny, nz = place.nx, place.ny, place.nz
    tokens, width = own.shape
    part = feed_in.shape[1] // place.seq // 2
    chunk = min(256, tokens)

    def unit(j, i, meta):
        return 2 * ((meta[2] + 1 + i) % ny * nx + (meta[1] + 1 + j) % nx) + meta[0]

    def gin_spec(number):
        def index(j, i, meta):
            return jnp.where(j == number, i, jnp.where(j < number, 0, ny - 1)), 0, 0

        return pl.BlockSpec((1, width, part), index)

    gout_spec = pl.BlockSpec((1, width, part), lambda j, i, meta: (j, 0, 0))
    total = 2 * tokens
    return pl.pallas_call(
        functools.partial(feed_kernel, (nx, ny, nz, chunk)),
        grid_spec=pltpu.PrefetchScalarGridSpec(
            num_scalar_prefetch=1,
            grid=(nx, ny),
            in_specs=[WHOLE_SPEC] * 4
            + [
                pl.BlockSpec((width, part), lambda j, i, meta: (0, unit(j, i, meta))),
                pl.BlockSpec((part, width), lambda j, i, meta: (unit(j, i, meta), 0)),
            ],
            out_specs=[WHOLE_SPEC] * 4 + [gin_spec(n) for n in range(nx)] + [gout_spec] * ny,
            scratch_shapes=[
                pltpu.VMEM((total, part), BF),
                pltpu.VMEM((total, part), BF),
                pltpu.VMEM((width, total), BF),
                pltpu.VMEM((width, total), BF),
                pltpu.VMEM((tokens, width), F32),
                pltpu.VMEM((tokens, width), F32),
            ],
        ),
        out_shape=[
            jax.ShapeDtypeStruct((tokens, width), F32),
            jax.ShapeDtypeStruct((tokens, width), BF),
            jax.ShapeDtypeStruct((tokens, width), F32),
            jax.ShapeDtypeStruct((tokens, width), BF),
        ]
        + [jax.ShapeDtypeStruct((ny, width, part), BF)] * nx
        + [jax.ShapeDtypeStruct((nx, width, part), BF)] * ny,
        compiler_params=pltpu.CompilerParams(vmem_limit_bytes=60 * 1024 * 1024),
        cost_estimate=pl.CostEstimate(
            flops=12 * total * width * part * place.seq,
            bytes_accessed=40 << 20,
            transcendentals=2 * total * part * place.seq,
        ),
    )(meta, own, other, gown, gother, feed_in, feed_out)


def weight_kernel(shape, meta_ref, *refs):
    count, nz = shape
    lefts, rights = refs[:count], refs[count : 2 * count]
    own_ref, other_ref, turned_ref = refs[2 * count :]
    core, z = meta_ref[0], meta_ref[3]
    block = own_ref.shape[1] // nz
    for number in range(count):

        @pl.when(pl.program_id(0) == number)
        def _(left=lefts[number], right=rights[number]):
            tokens = left.shape[0]
            turned_ref[:, :tokens] = turned(left[...])
            for k in range(nz):
                start = (z + 1 + k) % nz * 2
                to = slice(k * block, (k + 1) * block)
                for which, ref in ((core, own_ref), (1 - core, other_ref)):
                    at = pl.ds(pl.multiple_of((start + which) * block, block), block)
                    ref[0, to] = dot(turned_ref[at, :tokens], right[...]).astype(BF)


def weight_parts(place, meta, lefts, rights, before=()):
    count = len(lefts)
    depth, width = lefts[0].shape[1], rights[0].shape[1]
    tokens = max(left.shape[0] for left in lefts)
    out = jax.ShapeDtypeStruct((count, depth // 2, width), BF)
    spec = pl.BlockSpec((1, depth // 2, width), lambda u: (u, 0, 0))
    return pl.pallas_call(
        without(functools.partial(weight_kernel, (count, place.nz)), 1 + 2 * count, len(before)),
        grid=(count,),
        in_specs=[SMEM_SPEC] + [WHOLE_SPEC] * (2 * count) + [ANY_SPEC] * len(before),
        out_specs=[spec, spec],
        out_shape=[out, out],
        scratch_shapes=[pltpu.VMEM((depth, tokens), BF)],
        compiler_params=pltpu.CompilerParams(vmem_limit_bytes=VMEM_LIMIT),
        cost_estimate=pl.CostEstimate(
            flops=2 * count * tokens * depth * width,
            bytes_accessed=count * depth * width * 4,
            transcendentals=0,
        ),
    )(meta, *lefts, *rights, *before)


MESH = pl.DeviceIdType.MESH


class Mail:
    def __init__(self, send_sems, recv_sems):
        self.send_sems, self.recv_sems, self.sent = send_sems, recv_sems, []

    def send(self, source, target, device):
        number = len(self.sent)
        copy = pltpu.make_async_remote_copy(
            src_ref=source,
            dst_ref=target,
            send_sem=self.send_sems.at[number],
            recv_sem=self.recv_sems.at[number],
            device_id=device,
            device_id_type=MESH,
        )
        copy.start()
        self.sent.append(copy)
        return copy

    def finish(self):
        for copy in self.sent:
            copy.wait_send()


class Ways:
    def __init__(self, nz):
        self.row, self.spot = lax.axis_index(ROWS), lax.axis_index(SEQ)
        self.core, self.z = self.row % 2, self.row // 2
        self.x, self.y = self.spot % 2, self.spot // 2
        self.nz = nz
        self.sibling = (self.row + 1 - 2 * self.core, self.spot)
        self.across_x = (self.row, self.spot + 1 - 2 * self.x)
        self.across_y = (self.row, self.y * -2 + 2 + self.x)
        self.above = ((self.row + 2) % (2 * nz), self.spot)
        self.below = ((self.row + 2 * nz - 2) % (2 * nz), self.spot)

    def plane(self):
        devices = []
        for other in range(2):
            row = self.row if other == 0 else self.sibling[0]
            devices += [(row, (self.spot + s) % 4) for s in range(4) if other or s]
        return devices

    def meet(self, devices):
        barrier = pltpu.get_barrier_semaphore()
        for device in devices:
            pl.semaphore_signal(barrier, inc=1, device_id=device, device_id_type=MESH)
        pl.semaphore_wait(barrier, len(devices))

    def place(self, q):
        return (self.y + 1 + q % 2) % 2 * 2 + (self.x + 1 + q // 2) % 2

    def rows(self, k, which, block):
        start = ((self.z + 1 + k) % self.nz * 2 + which) * block
        return pl.ds(pl.multiple_of(start, block), block)


class Home:
    def __init__(self, ways, out_ref, send_sems, recv_sems):
        self.ways, self.out_ref = ways, out_ref
        self.send_sems, self.recv_sems = send_sems, recv_sems
        self.started = []

    def send(self, source, slot):
        ways = self.ways
        spot = jnp.where(ways.core == 0, 3 * slot, 1 + slot)
        row = 2 * ways.z + ways.spot // 2
        stays = (spot == ways.spot) & (row == ways.row)
        to = self.out_ref.at[ways.spot % 2]
        copy = pltpu.make_async_remote_copy(
            src_ref=source,
            dst_ref=to,
            send_sem=self.send_sems.at[slot],
            recv_sem=self.recv_sems.at[ways.spot % 2],
            device_id=(row, spot),
            device_id_type=MESH,
        )
        local = pltpu.make_async_copy(source, to, self.recv_sems.at[ways.spot % 2])

        @pl.when(stays)
        def _():
            local.start()

        @pl.when(jnp.logical_not(stays))
        def _():
            copy.start()

        self.started.append((stays, copy))

    def finish(self):
        for r in range(2):
            to = self.out_ref.at[r]
            pltpu.make_async_copy(to, to, self.recv_sems.at[r]).wait()
        for stays, copy in self.started:

            @pl.when(jnp.logical_not(stays))
            def _(copy=copy):
                copy.wait_send()


def middle_kernel(
    shape,
    mixed_ref,
    normed_ref,
    projected_ref,
    text_ref,
    self_ref,
    g_second_ref,
    g_query_ref,
    g_keys_ref,
    g_values_ref,
    g_projected_ref,
    g_first_ref,
    send_up_ref,
    send_low_ref,
    keep_up_ref,
    keep_low_ref,
    mixed_t,
    normed_t,
    projected_t,
    text_t,
    self_t,
    own_ref,
    away_ref,
    got_ref,
    send_sems,
    recv_sems,
):
    nz, piece = shape
    ways = Ways(nz)
    ways.meet([ways.sibling])
    mail = Mail(send_sems, recv_sems)
    for left, to in ((mixed_ref, mixed_t), (normed_ref, normed_t), (projected_ref, projected_t), (self_ref, self_t)):
        to[...] = turned(left[...])
    turned_text = turned(text_ref[...])
    block = own_ref.shape[2]
    count = 2 * nz
    part = turned_text.shape[0] // count
    text_t[...] = jnp.zeros_like(text_t)
    for b in range(count):
        text_t[b * block : b * block + part] = turned_text[b * part : (b + 1) * part]
    half = block // 2
    up, low = slice(0, half), slice(half, block)
    homes = (
        (send_up_ref.at[0], send_low_ref.at[0]),
        (send_up_ref.at[1], keep_low_ref.at[0]),
        (keep_up_ref.at[0], send_low_ref.at[1]),
        (keep_up_ref.at[1], keep_low_ref.at[1]),
    )
    copies = []

    def settle(q):
        copies[q].wait_recv()
        total = own_ref[q] + got_ref[q]
        homes[q][0][...] = total[:, up]
        homes[q][1][...] = total[:, low]

    for q in range(4):
        place = ways.place(q)
        columns = pl.ds(pl.multiple_of(place * piece, piece), piece)
        twice = pl.ds(pl.multiple_of(place % 2 * 2 * piece, piece), 2 * piece)
        pair = jnp.where(place < 2, g_keys_ref[:, twice], g_values_ref[:, twice])
        units = (
            (mixed_t, g_second_ref[:, columns]),
            (normed_t, g_query_ref[:, columns]),
            (projected_t, pair),
            (text_t, g_projected_ref[:, columns]),
            (self_t, g_first_ref[:, columns]),
        )
        for which, ref in ((1 - ways.core, away_ref), (ways.core, own_ref)):
            first = 0
            for left, right in units:
                to = slice(first, first + right.shape[1])
                first += right.shape[1]
                for k in range(nz):
                    ref[q, k, :, to] = dot(left[ways.rows(k, which, block)], right).astype(BF)
            if ref is away_ref:
                copies.append(mail.send(away_ref.at[q], got_ref.at[q], ways.sibling))
        if q > 0:
            settle(q - 1)
    settle(3)
    mail.finish()


def middle_parts(place, lefts, rights):
    nz = place.nz
    depth, width = lefts[0].shape[1], rights[0].shape[1]
    piece, block = width // place.seq, depth // place.rows
    columns = piece * len(rights)
    out = jax.ShapeDtypeStruct((2, nz, block // 2, columns), BF)
    big = pltpu.VMEM((4, nz, block, columns), BF)
    return pl.pallas_call(
        functools.partial(middle_kernel, (nz, piece)),
        in_specs=[WHOLE_SPEC] * 11,
        out_specs=[WHOLE_SPEC] * 4,
        out_shape=[out] * 4,
        scratch_shapes=[pltpu.VMEM((depth, left.shape[0]), BF) for left in lefts]
        + [big] * 3
        + [pltpu.SemaphoreType.DMA((4,))] * 2,
        compiler_params=pltpu.CompilerParams(
            collective_id=2, has_side_effects=True, vmem_limit_bytes=VMEM_LIMIT
        ),
        cost_estimate=pl.CostEstimate(
            flops=2 * 8 * 512 * depth * width, bytes_accessed=24 << 20, transcendentals=0
        ),
    )(*lefts, *rights)


def final_kernel(nz, *refs):
    (
        normed_ref,
        input_ref,
        first_ref,
        gain_ref,
        weight_ref,
        gq_ref,
        gk_ref,
        gv_ref,
        k_away_ref,
        v_away_ref,
        upper_ref,
        upper_got_ref,
        lower_ref,
        lower_got_ref,
        in_keep_ref,
        in_got_ref,
        out_keep_ref,
        out_got_ref,
        vector_ref,
        result_ref,
        result_away_ref,
        text_ref,
    ) = refs[:22]
    (qkv_ref, middle_ref, feed_ref, sum_ref, result_out, frames_out, text_out) = refs[22:29]
    (
        packed_ref,
        k_got_ref,
        v_got_ref,
        acc_ref,
        turned_ref,
        own_ref,
        away_ref,
        got_ref,
        first_x_ref,
        first_y_ref,
        second_y_ref,
        second_x_ref,
        mid_up_ref,
        mid_low_ref,
        mid_ref,
        mid_ring_ref,
        qkv_ring_ref,
        feed_send_ref,
        feed_ring_ref,
        feed_away_ref,
        feed_other_ref,
        vector_out_ref,
        vector_in_ref,
        result_got_ref,
        text_away_ref,
        text_got_ref,
        send_sems,
        recv_sems,
        home_sends,
        home_recvs,
    ) = refs[29:]
    ways = Ways(nz)
    core, z = ways.core, ways.z
    sibling, across_x, across_y, above = ways.sibling, ways.across_x, ways.across_y, ways.above
    ways.meet(ways.plane() + [ways.above, ways.below])
    mail = Mail(send_sems, recv_sems)
    ring = ring_order(nz)
    half = upper_ref.shape[2]
    feed_rows = feed_ring_ref.shape[2]
    tokens, width = normed_ref.shape

    k_copy = mail.send(k_away_ref, k_got_ref, sibling)
    v_copy = mail.send(v_away_ref, v_got_ref, sibling)

    def feed_piece(kind, k):
        keep, got = ((in_keep_ref, in_got_ref), (out_keep_ref, out_got_ref))[kind]
        at = slice(k * feed_rows, (k + 1) * feed_rows)
        return keep[at].astype(F32) + got[at].astype(F32)

    def feed_send(t, kind):
        return mail.send(feed_send_ref.at[kind, t], feed_ring_ref.at[kind, t], above)

    feed_copies = {}
    for kind in range(2):
        feed_send_ref[kind, 0] = feed_piece(kind, ring[0]).astype(BF)
        feed_copies[kind, 0] = feed_send(0, kind)

    mid_copies = {}
    for k in ring:
        mid_ref[k, :half] = upper_ref[0, k] + upper_got_ref[0, k]
        mid_ref[k, half:] = lower_ref[0, k] + lower_got_ref[0, k]
        mid_copies[k] = (
            mail.send(mid_ref.at[k, :half], mid_up_ref.at[k], across_y),
            mail.send(mid_ref.at[k, half:], mid_low_ref.at[k], across_x),
        )
    result_copy = mail.send(result_away_ref, result_got_ref, sibling)
    text_rows = text_ref.shape[0] // 2
    text_away_ref[...] = text_ref[text_rows:].astype(BF)
    text_copy = mail.send(text_away_ref, text_got_ref, sibling)

    turned_ref[...] = turned(normed_ref[...])
    packed_ref[:, :width] = gq_ref[...]
    k_copy.wait_recv()
    packed_ref[:, width : 2 * width] = gk_ref[...] + k_got_ref[...]
    v_copy.wait_recv()
    packed_ref[:, 2 * width :] = gv_ref[...] + v_got_ref[...]

    block = own_ref.shape[2]
    columns = own_ref.shape[3]
    core_copies = []
    for q in range(4):
        right = packed_ref[:, pl.ds(pl.multiple_of(ways.place(q) * columns, columns), columns)]
        for which, ref in ((1 - core, away_ref), (core, own_ref)):
            for k in range(nz):
                ref[q, k] = dot(turned_ref[ways.rows(k, which, block)], right).astype(BF)
            if ref is away_ref:
                core_copies.append(mail.send(away_ref.at[q], got_ref.at[q], sibling))

    def feed_step(t):
        for kind in range(2):
            feed_copies[kind, t - 1].wait_recv()
            total = feed_piece(kind, ring[t]) + feed_ring_ref[kind, t - 1].astype(F32)
            if t < nz - 1:
                feed_send_ref[kind, t] = total.astype(BF)
                feed_copies[kind, t] = feed_send(t, kind)
            else:
                feed_finish(kind, total)

    def feed_finish(kind, total):
        rows = total.shape[0] // 2
        away = jnp.where(core == 0, total[rows:], total[:rows])
        own = jnp.where(core == 0, total[:rows], total[rows:])
        across = total.shape[1]
        feed_away_ref[kind] = away
        feed_copies[kind, nz] = mail.send(feed_away_ref.at[kind], feed_other_ref.at[kind], sibling)
        at = pl.ds(pl.multiple_of(core * across, across), across)
        feed_ref[kind, :, at] = own

    def feed_last(kind):
        feed_copies[kind, nz].wait_recv()
        across = feed_other_ref.shape[2]
        at = pl.ds(pl.multiple_of((1 - core) * across, across), across)
        feed_ref[kind, :, at] = feed_other_ref[kind]

    def core_step(q):
        core_copies[q].wait_recv()
        own_ref[q] = own_ref[q] + got_ref[q]

    mid_ring = {}

    def mid_send(t):
        k = ring[t]
        up, low = mid_copies[k]
        up.wait()
        low.wait()
        mid_ref[k, :half] = upper_ref[1, k] + upper_got_ref[1, k] + mid_up_ref[k]
        mid_ref[k, half:] = lower_ref[1, k] + lower_got_ref[1, k] + mid_low_ref[k]
        if t > 0:
            mid_ring[t - 1].wait_recv()
        if t == nz - 1:
            middle_ref[...] = mid_ref[k].astype(F32) + mid_ring_ref[t - 1].astype(F32)
            return
        if t > 0:
            mid_ref[k] = mid_ref[k] + mid_ring_ref[t - 1]
        mid_ring[t] = mail.send(mid_ref.at[k], mid_ring_ref.at[t], above)

    qkv_ring = {}

    def qkv_send(t):
        k = ring[t]
        if t > 0:
            qkv_ring[t - 1].wait_recv()
        if t == nz - 1:
            qkv_ref[...] = own_ref[3, k].astype(F32) + qkv_ring_ref[t - 1].astype(F32)
            return
        if t > 0:
            own_ref[3, k] = own_ref[3, k] + qkv_ring_ref[t - 1]
        qkv_ring[t] = mail.send(own_ref.at[3, k], qkv_ring_ref.at[t], above)

    up, low = slice(0, half), slice(half, 2 * half)
    core_step(0)
    upper_first = [mail.send(own_ref.at[0, :, up], first_x_ref.at[0], across_x)]
    lower_first = [mail.send(own_ref.at[0, :, low], first_y_ref.at[0], across_y)]
    core_step(1)
    upper_first.append(mail.send(own_ref.at[1, :, up], first_x_ref.at[1], across_x))
    core_step(2)
    lower_first.append(mail.send(own_ref.at[2, :, low], first_y_ref.at[1], across_y))
    core_step(3)

    result_copy.wait_recv()
    slots = tokens // 2
    result_got_ref[...] = (result_ref[...] + result_got_ref[...].astype(F32)).astype(BF)
    result_home = Home(ways, result_out, home_sends.at[0], home_recvs.at[0])
    for slot in range(2):
        result_home.send(result_got_ref.at[slot * slots : (slot + 1) * slots], slot)
    text_copy.wait_recv()
    text_got_ref[...] = (text_ref[:text_rows] + text_got_ref[...].astype(F32)).astype(BF)
    text_home = Home(ways, text_out, home_sends.at[1], home_recvs.at[1])
    for slot in range(2):
        at = slice(slot * text_rows // 2, (slot + 1) * text_rows // 2)
        text_home.send(text_got_ref.at[at], slot)

    acc_ref[...] = nt(packed_ref[:, :width], weight_ref[:, :width])
    acc_ref[...] += nt(packed_ref[:, width : 2 * width], weight_ref[:, width : 2 * width])
    mid_send(0)
    feed_step(1)
    acc_ref[...] += nt(packed_ref[:, 2 * width :], weight_ref[:, 2 * width :])
    gain_sum = jnp.zeros((1, width), F32)
    shift_sum = jnp.zeros((1, width), F32)
    chunk = min(128, tokens)
    for m in range(tokens // chunk):
        at = slice(m * chunk, (m + 1) * chunk)
        grad, gain_part, shift_part = norm_backward(
            input_ref[at].astype(F32), gain_ref[...], acc_ref[at]
        )
        k_got_ref[at] = (first_ref[at] + grad).astype(BF)
        gain_sum += gain_part[None]
        shift_sum += shift_part[None]
    frames_home = Home(ways, frames_out, home_sends.at[2], home_recvs.at[2])
    for slot in range(2):
        frames_home.send(k_got_ref.at[slot * slots : (slot + 1) * slots], slot)
    vector_out_ref[0] = vector_ref[...]
    vector_out_ref[0, 0:1] = gain_sum
    vector_out_ref[0, 1:2] = shift_sum
    vector_copy = mail.send(vector_out_ref.at[0], vector_in_ref.at[0], sibling)
    mid_send(1)

    vector_copy.wait_recv()
    vector_out_ref[1] = vector_out_ref[0] + vector_in_ref[0]
    vector_copy = mail.send(vector_out_ref.at[1], vector_in_ref.at[1], across_x)
    for t in range(2, nz):
        feed_step(t)
        if t < nz - 1:
            mid_send(t)
    vector_copy.wait_recv()
    vector_out_ref[2] = vector_out_ref[1] + vector_in_ref[1]
    vector_copy = mail.send(vector_out_ref.at[2], vector_in_ref.at[2], across_y)

    upper_first[0].wait_recv()
    own_ref[2, :, up] = own_ref[2, :, up] + first_x_ref[0]
    upper_second = mail.send(own_ref.at[2, :, up], second_y_ref, across_y)
    lower_first[0].wait_recv()
    own_ref[1, :, low] = own_ref[1, :, low] + first_y_ref[0]
    lower_second = mail.send(own_ref.at[1, :, low], second_x_ref, across_x)
    vector_copy.wait_recv()
    vector_out_ref[3] = vector_out_ref[2] + vector_in_ref[2]
    vector_copy = mail.send(vector_out_ref.at[3], vector_in_ref.at[3], above)
    upper_first[1].wait_recv()
    own_ref[3, :, up] = own_ref[3, :, up] + first_x_ref[1]
    lower_first[1].wait_recv()
    own_ref[3, :, low] = own_ref[3, :, low] + first_y_ref[1]
    mid_send(nz - 1)
    for kind in range(2):
        feed_last(kind)
    total = vector_out_ref[3]
    for t in range(nz - 1):
        vector_copy.wait_recv()
        total = total + vector_in_ref[3 + t]
        if t < nz - 2:
            vector_copy = mail.send(vector_in_ref.at[3 + t], vector_in_ref.at[4 + t], above)
    sum_ref[...] = total
    upper_second.wait_recv()
    own_ref[3, :, up] = own_ref[3, :, up] + second_y_ref[...]
    lower_second.wait_recv()
    own_ref[3, :, low] = own_ref[3, :, low] + second_x_ref[...]
    for t in range(nz):
        qkv_send(t)
    result_home.finish()
    text_home.finish()
    frames_home.finish()
    for number, copy in enumerate(mail.sent):
        if not any(copy is c for pair in mid_copies.values() for c in pair):
            copy.wait_send()


def final_sums(place, count, *operands):
    nz = place.nz
    normed, weight, upper, in_keep = operands[0], operands[4], operands[10], operands[14]
    vectors, text = operands[18], operands[21]
    tokens, width = normed.shape
    block, piece = width // place.rows, weight.shape[1] // place.seq
    half, middle = block // 2, upper.shape[3]
    feed_width = in_keep.shape[1]
    feed_rows = width // nz
    copies = 2 + 2 * nz + 2 * nz + 2 + 4 + 3 + nz - 1 + 4 + 2 + 2 * (nz - 1)
    vmem = pltpu.VMEM
    return pl.pallas_call(
        functools.partial(final_kernel, nz),
        in_specs=[WHOLE_SPEC] * 22,
        out_specs=[WHOLE_SPEC] * 4 + [ANY_SPEC] * 3,
        out_shape=[
            jax.ShapeDtypeStruct((block, piece), F32),
            jax.ShapeDtypeStruct((block, middle), F32),
            jax.ShapeDtypeStruct((2, block, 2 * feed_width), F32),
            jax.ShapeDtypeStruct(vectors.shape, F32),
            jax.ShapeDtypeStruct((count, tokens // count, width), BF),
            jax.ShapeDtypeStruct((count, tokens // count, width), BF),
            jax.ShapeDtypeStruct((count, text.shape[0] // 2 // count, text.shape[1]), BF),
        ],
        scratch_shapes=[
            vmem((tokens, 3 * width), BF),
            vmem((tokens, width), BF),
            vmem((tokens, width), BF),
            vmem((tokens, width), F32),
            vmem((width, tokens), BF),
            vmem((4, nz, block, piece), BF),
            vmem((4, nz, block, piece), BF),
            vmem((4, nz, block, piece), BF),
            vmem((2, nz, half, piece), BF),
            vmem((2, nz, half, piece), BF),
            vmem((nz, half, piece), BF),
            vmem((nz, half, piece), BF),
            vmem((nz, half, middle), BF),
            vmem((nz, half, middle), BF),
            vmem((nz, block, middle), BF),
            vmem((nz - 1, block, middle), BF),
            vmem((nz - 1, block, piece), BF),
            vmem((2, nz - 1, feed_rows, feed_width), BF),
            vmem((2, nz - 1, feed_rows, feed_width), BF),
            vmem((2, feed_rows // 2, feed_width), F32),
            vmem((2, feed_rows // 2, feed_width), F32),
            vmem((4,) + vectors.shape, F32),
            vmem((2 + nz,) + vectors.shape, F32),
            vmem((tokens, width), BF),
            vmem((text.shape[0] // 2, text.shape[1]), BF),
            vmem((text.shape[0] // 2, text.shape[1]), BF),
            pltpu.SemaphoreType.DMA((copies,)),
            pltpu.SemaphoreType.DMA((copies,)),
            pltpu.SemaphoreType.DMA((3, 2)),
            pltpu.SemaphoreType.DMA((3, 2)),
        ],
        compiler_params=pltpu.CompilerParams(
            collective_id=1, has_side_effects=True, vmem_limit_bytes=63 * 1024 * 1024
        ),
        cost_estimate=pl.CostEstimate(
            flops=60 * tokens * width * weight.shape[1], bytes_accessed=40 << 20, transcendentals=0
        ),
    )(*operands)


def permuted_sums(place, meta, in_half, out_half, lefts, rights, normed_self, backward_self):
    nx, ny, nz, seq = place.nx, place.ny, place.nz, place.seq
    width = normed_self.shape[1]
    block, piece = width // place.rows, width // seq
    middle_own, middle_away = weight_parts(
        place, meta, lefts[:3] + lefts[2:4], rights[:5]
    )
    out_own, out_away = weight_parts(place, meta, lefts[4:], rights[5:])
    middle_got = place.swap_core(middle_away)
    out_got = place.swap_core(out_away)
    grad_packed = backward_self(in_half, out_half, middle_got, out_got)
    in_quarter = ring_sum([lambda k=k: in_half[k].astype(F32) for k in range(ny)], place.next_y)
    out_quarter = ring_sum([lambda k=k: out_half[k].astype(F32) for k in range(nx)], place.next_x)
    feed_quarter = jnp.stack([in_quarter, out_quarter]).astype(BF)
    feed_quarter = feed_quarter.reshape(2, nz, -1, feed_quarter.shape[2])
    feed_own = ring_sum([lambda k=k: feed_quarter[:, k].astype(F32) for k in range(nz)], place.next_z)
    feed_own = feed_own.reshape(2, 2, block, -1)
    feed_got = place.swap_core(pick(feed_own, 1 - place.core, 1))
    feed_own = pick(feed_own, place.core, 1)
    low = jnp.where(place.core == 0, feed_own, feed_got)
    high = jnp.where(place.core == 0, feed_got, feed_own)
    sum_feed = jnp.concatenate([low, high], axis=2)

    def middle_piece(k):
        at = slice(k * block, (k + 1) * block)
        return lambda: middle_own[:, at].astype(F32) + middle_got[:, at].astype(F32)

    middle = ring_sum([middle_piece(k) for k in range(nz)], place.next_z).astype(BF)
    spread = jnp.concatenate(
        [
            middle[0].reshape(block, seq, -1),
            middle[1].reshape(block, seq, -1),
            jnp.concatenate([middle[2], middle[3]], axis=1).reshape(block, seq, -1),
            middle[4].reshape(block, seq, -1),
        ],
        axis=2,
    ).reshape(block, ny, nx, -1)

    def shifted(array, index, number, length, axis):
        return lambda: pick(array, (index + 1 + number) % length, axis).astype(F32)

    spread = ring_sum([shifted(spread, place.x, k, nx, 2) for k in range(nx)], place.next_x).astype(BF)
    spread = ring_sum([shifted(spread, place.y, k, ny, 1) for k in range(ny)], place.next_y)
    relative_parts = place.relative_columns(grad_packed, True)
    qkv_own, qkv_away = weight_parts(place, meta, [normed_self], [relative_parts])
    qkv_got = place.swap_core(qkv_away)

    def columns(array):
        return array[0].reshape(array.shape[1], nx, ny, -1)

    def natural(array):
        return jnp.stack(
            [
                jnp.stack(
                    [
                        pick(array[0].reshape(array.shape[1], seq, -1), place.offset(i, j), 1)
                        for i in range(ny)
                    ],
                    axis=1,
                )
                for j in range(nx)
            ],
            axis=1,
        )

    last_own = jnp.concatenate([columns(qkv_own), natural(out_own)], axis=3)
    last_got = jnp.concatenate([columns(qkv_got), natural(out_got)], axis=3)
    last = (last_own.astype(F32) + last_got.astype(F32)).astype(BF)
    last = last.reshape(nz, 2, block // 2, nx, ny, -1)
    upper = ring_sum([lambda k=k: last[:, 0, :, k].astype(F32) for k in range(nx)], place.next_x).astype(BF)
    lower = ring_sum([lambda k=k: last[:, 1, :, :, k].astype(F32) for k in range(ny)], place.next_y).astype(BF)
    upper = ring_sum([lambda a=upper[:, :, k]: a.astype(F32) for k in range(ny)], place.next_y)
    lower = ring_sum([lambda a=lower[:, :, k]: a.astype(F32) for k in range(nx)], place.next_x)
    last = jnp.stack([upper, lower], axis=1).astype(BF)
    last = ring_sum([lambda a=last[k]: a.astype(F32) for k in range(nz)], place.next_z)
    last = last.reshape(block, -1)
    sum_self_qkv, sum_self_out = last[:, : 3 * piece], last[:, 3 * piece :]

    return sum_feed, spread, sum_self_qkv, sum_self_out, grad_packed


def shards(
    frames,
    text_states,
    clip_lengths,
    text_lengths,
    self_gain,
    self_shift,
    self_qkv,
    self_out,
    cross_gain,
    cross_shift,
    cross_query,
    text_proj,
    text_bias,
    cross_kv,
    cross_out,
    feed_gain,
    feed_shift,
    feed_in,
    feed_out,
    grad_out,
):
    place = Place()
    count = frames.shape[0]
    width = frames.shape[2]
    frame_total = frames.shape[1] * place.seq
    text_total = text_states.shape[1] * place.seq

    lengths = jnp.concatenate([clip_lengths, text_lengths], axis=1)
    lengths_other = place.swap_core(lengths)
    mine = place.spot // count == place.core
    row_lengths = pick(jnp.where(mine, lengths, lengths_other), place.spot % count, 0)
    clips = clip_lengths.shape[1]
    frame_ends = jnp.cumsum(row_lengths[:clips])
    text_ends = jnp.cumsum(row_lengths[clips:])

    def segments(positions, ends):
        return jnp.sum((positions[:, None] >= ends[None, :]).astype(jnp.int32), axis=1)

    own_segment = segments(place.positions(frame_total, place.core), frame_ends)
    other_segment = segments(place.positions(frame_total, 1 - place.core), frame_ends)
    text_positions = jnp.concatenate(
        [place.positions(text_total, place.core), place.positions(text_total, 1 - place.core)]
    )
    text_segment = segments(text_positions, text_ends)
    query_segment = own_segment[None, :]
    own_segment, other_segment = own_segment[:, None], other_segment[:, None]
    text_segment = text_segment[:, None]
    core = place.core.reshape(1).astype(jnp.int32)

    text_half = place.to_rows(text_states)
    layer_raw = place.to_rows(frames)
    text_input = jnp.concatenate([text_half, place.swap_core(text_half)], axis=0)
    cotangent = place.to_rows(after(grad_out, layer_raw))
    cotangent_other = place.swap_core(cotangent)
    projected = (dot(text_input, text_proj) + text_bias).astype(BF)
    text_pair = dot(projected, cross_kv).astype(BF)

    layer_input = layer_raw.astype(F32)
    normed_self = layer_norm(layer_input, self_gain, self_shift)
    pair = dot(normed_self, self_qkv[:, width:]).astype(BF)
    pair_other = place.swap_core(pair)
    queries = dot(normed_self, self_qkv[:, :width]).astype(BF)
    self_mix, self_lse = self_forward(
        core, query_segment, own_segment, other_segment, queries, pair, pair_other
    )
    first = layer_input + dot(self_mix, self_out)
    normed_cross = layer_norm(first, cross_gain, cross_shift)
    cross_queries = dot(normed_cross, cross_query).astype(BF)
    cross_mix, cross_lse = cross_forward(query_segment, text_segment, cross_queries, text_pair)
    second = first + dot(cross_mix, cross_out)
    normed_feed = layer_norm(second, feed_gain, feed_shift)

    nx, ny, nz, seq = place.nx, place.ny, place.nz, place.seq
    meta = jnp.stack([place.core, place.x, place.y, place.z]).astype(jnp.int32)
    normed_other = place.swap_core(normed_feed)
    fed = feed(
        place, meta, normed_feed, normed_other, cotangent, cotangent_other, feed_in, feed_out
    )
    result, result_away, grad_normed_feed, grad_away = fed[:4]
    grad_in, grad_out_parts = fed[4 : 4 + nx], fed[4 + nx :]
    grad_normed_feed = grad_normed_feed + place.swap_core(grad_away).astype(F32)

    def x_piece(k):
        return lambda: grad_in[k].astype(F32)

    def y_piece(k):
        return lambda: grad_out_parts[k].astype(F32)

    in_half = ring_sum([x_piece(k) for k in range(nx)], place.next_x).astype(BF)
    out_half = ring_sum([y_piece(k) for k in range(ny)], place.next_y).astype(BF)

    grad_part, grad_feed_gain, grad_feed_shift = norm_backward(second, feed_gain, grad_normed_feed)
    grad_second = cotangent.astype(F32) + grad_part
    grad_second_branch = grad_second.astype(BF)
    grad_cross_mix = dot(grad_second_branch, cross_out, 1, 1).astype(BF)
    grad_cross_queries, grad_text_keys, grad_text_values = cross_backward(
        query_segment,
        text_segment,
        cross_queries,
        text_pair,
        grad_cross_mix,
        cross_mix,
        cross_lse,
    )
    grad_normed_cross = dot(grad_cross_queries, cross_query, 1, 1)
    grad_part, grad_cross_gain, grad_cross_shift = norm_backward(first, cross_gain, grad_normed_cross)
    grad_first = grad_second + grad_part
    grad_first_branch = grad_first.astype(BF)
    grad_self_mix = dot(grad_first_branch, self_out, 1, 1).astype(BF)

    grad_pair = jnp.concatenate([grad_text_keys, grad_text_values], axis=1)
    grad_projected = dot(grad_pair, cross_kv, 1, 1).astype(BF)
    grad_text_bias = jnp.sum(grad_projected.astype(F32), axis=0)
    grad_text = dot(grad_projected, text_proj, 1, 1)
    block, piece = width // place.rows, width // seq
    padding = block - text_input.shape[1] // place.rows
    lefts = [cross_mix, normed_cross, projected, text_input, self_mix]
    rights = [
        grad_second_branch,
        grad_cross_queries,
        grad_text_keys,
        grad_text_values,
        grad_projected,
        grad_first_branch,
    ]
    result = second + result

    def backward_self(*before):
        return self_backward(
            core,
            query_segment,
            own_segment,
            other_segment,
            queries,
            pair,
            pair_other,
            grad_self_mix,
            self_mix,
            self_lse,
            before=before,
        )

    def vector_list(grad_gain, grad_shift):
        return jnp.stack(
            [
                grad_gain,
                grad_shift,
                grad_cross_gain,
                grad_cross_shift,
                grad_text_bias,
                grad_feed_gain,
                grad_feed_shift,
                jnp.zeros_like(grad_feed_shift),
            ]
        )

    if nx == 2 and ny == 2 and piece % 128 == 0:
        send_up, send_low, keep_up, keep_low = middle_parts(place, lefts, rights)
        up_got, low_got = place.next_x(send_up), place.next_y(send_low)
        in_got, out_got = place.next_y(in_half[0]), place.next_x(out_half[0])
        grads = backward_self(in_half[0], out_half[0])
        nothing = jnp.zeros_like(grad_feed_shift)
        sum_self_qkv, spread, sum_feed, vectors, result, grad_frames, grad_text = final_sums(
            place,
            count,
            normed_self,
            layer_raw,
            grad_first,
            self_gain[None],
            self_qkv,
            *grads,
            keep_up,
            up_got,
            keep_low,
            low_got,
            in_half[1],
            in_got,
            out_half[1],
            out_got,
            vector_list(nothing, nothing),
            result,
            result_away,
            grad_text,
        )
        sum_self_out = spread[:, 5 * piece :]
    else:

        def packed_self(*before):
            grads = backward_self(*before)
            keys = (grads[1].astype(F32) + place.swap_core(grads[3]).astype(F32)).astype(BF)
            values = (grads[2].astype(F32) + place.swap_core(grads[4]).astype(F32)).astype(BF)
            return jnp.concatenate([grads[0], keys, values], axis=1)

        text_blocks = text_input.reshape(text_total, place.rows, -1)
        text_padded = jnp.pad(text_blocks, ((0, 0), (0, 0), (0, padding))).reshape(text_total, width)
        lefts[3] = text_padded
        sum_feed, spread, sum_self_qkv, sum_self_out, grad_packed = permuted_sums(
            place, meta, in_half, out_half, lefts, rights, normed_self, packed_self
        )
        result = (result + place.swap_core(result_away).astype(F32)).astype(BF)
        result = place.from_rows(result, count)
        grad_normed_self = dot(grad_packed, self_qkv, 1, 1)
        grad_part, grad_gain, grad_shift = norm_backward(layer_input, self_gain, grad_normed_self)
        grad_frames = place.from_rows((grad_first + grad_part).astype(BF), count)
        half = grad_text.shape[0] // 2
        text_away = place.swap_core(grad_text[half:].astype(BF))
        grad_text = (grad_text[:half] + text_away.astype(F32)).astype(BF)
        grad_text = place.from_rows(grad_text, count)
        vectors = place.vector_sum(vector_list(grad_gain, grad_shift))
    sum_cross_out, sum_cross_query = spread[:, :piece], spread[:, piece : 2 * piece]
    sum_cross_kv, sum_text_proj = spread[:, 2 * piece : 4 * piece], spread[:, 4 * piece : 5 * piece]
    sum_text_proj = sum_text_proj[: block - padding]
    vectors = pick(vectors.reshape(8, seq, width // seq), place.spot, 1)
    return (
        result,
        grad_frames.astype(F32),
        grad_text.astype(F32),
        vectors[0],
        vectors[1],
        sum_self_qkv,
        sum_self_out,
        vectors[2],
        vectors[3],
        sum_cross_query,
        sum_text_proj,
        vectors[4],
        sum_cross_kv,
        sum_cross_out,
        vectors[5],
        vectors[6],
        sum_feed[0],
        jnp.swapaxes(sum_feed[1], 0, 1),
    )


def solution(mesh):
    split, copied, table = P(ROWS, SEQ, None), P(), P(ROWS, None)
    vector, matrix = P(SEQ), P(ROWS, SEQ)
    return jax.shard_map(
        shards,
        mesh=mesh,
        in_specs=(split, split, table, table) + (copied,) * 15 + (split,),
        out_specs=(
            (split,) * 3
            + (vector, vector, matrix, matrix)
            + (vector, vector, matrix, matrix)
            + (vector, matrix, matrix)
            + (vector, vector, matrix, P(SEQ, ROWS))
        ),
        check_vma=False,
    )
```

```python
import functools
import math

import jax
import jax.numpy as jnp
from jax import lax
from jax.experimental import pallas as pl
from jax.experimental.pallas import tpu as pltpu
from jax.sharding import PartitionSpec as P

HD = 64
PAIR = 2 * HD
EPSILON = 1e-05
MASKED = -1e30
CLIPS = 4
ROWS = "rows"
SEQ = "seq"
BF = jnp.bfloat16
F32 = jnp.float32
VMEM_LIMIT = 48 * 1024 * 1024


def dot(left, right, left_dim=1, right_dim=0):
    return lax.dot_general(
        left, right, (((left_dim,), (right_dim,)), ((), ())), preferred_element_type=F32
    )


def pick(array, index, axis):
    return lax.dynamic_index_in_dim(array, index, axis, keepdims=False)


def after(value, *others):
    return lax.optimization_barrier((value,) + others)[0]


class Place:
    def __init__(self):
        self.rows, self.seq = lax.axis_size(ROWS), lax.axis_size(SEQ)
        self.nz = self.rows // 2
        self.nx = math.isqrt(self.seq)
        self.ny = self.seq // self.nx
        row, self.spot = lax.axis_index(ROWS), lax.axis_index(SEQ)
        self.core, self.z = row % 2, row // 2
        self.x, self.y = self.spot % self.nx, self.spot // self.nx
        self.owner = [0 if 4 * s // self.seq in (0, 3) else 1 for s in range(self.seq)]
        self.members = [[s for s in range(self.seq) if self.owner[s] == c] for c in (0, 1)]
        self.rank = [self.members[self.owner[s]].index(s) for s in range(self.seq)]

    def permute(self, value, target):
        pairs = []
        for z in range(self.nz):
            for c in range(2):
                for s in range(self.seq):
                    tz, tc, ts = target(z, c, s)
                    pairs.append(((2 * z + c) * self.seq + s, (2 * tz + tc) * self.seq + ts))
        return lax.ppermute(value, (ROWS, SEQ), pairs)

    def swap_core(self, value):
        return self.permute(value, lambda z, c, s: (z, 1 - c, s))

    def next_z(self, value):
        return self.permute(value, lambda z, c, s: ((z + 1) % self.nz, c, s))

    def next_x(self, value):
        nx = self.nx
        return self.permute(value, lambda z, c, s: (z, c, s // nx * nx + (s % nx + 1) % nx))

    def next_y(self, value):
        return self.permute(value, lambda z, c, s: (z, c, (s + self.nx) % self.seq))

    def to_rows(self, value):
        count = value.shape[0]
        my_rank = jnp.array(self.rank, jnp.int32)[self.spot]
        got = []
        for t in range(count):

            def target(z, c, s, t=t):
                return z, self.owner[s], c * count + (t + self.rank[s]) % count

            got.append(self.permute(pick(value, (t + my_rank) % count, 0), target))
        stacked = jnp.stack(got)
        here = self.spot % count
        return jnp.concatenate([pick(stacked, (here - k) % count, 0) for k in range(count)], axis=0)

    def from_rows(self, value, count):
        my_rank = jnp.array(self.rank, jnp.int32)[self.spot]
        slots = value.reshape(count, value.shape[0] // count, value.shape[1])
        here = self.spot % count
        got = []
        for t in range(count):

            def target(z, c, s, t=t):
                return z, s // count, self.members[c][(s % count - t) % count]

            got.append(self.permute(pick(slots, (here - t) % count, 0), target))
        stacked = jnp.stack(got)
        return jnp.stack([pick(stacked, (i - my_rank) % count, 0) for i in range(count)])

    def positions(self, total, core):
        quarter = total // 4
        inner = jnp.arange(quarter, dtype=jnp.int32)
        return jnp.concatenate([inner + core * quarter, inner + (3 - core) * quarter])

    def offset(self, i, j):
        return (self.y + 1 + i) % self.ny * self.nx + (self.x + 1 + j) % self.nx

    def relative_columns(self, value, outer_x):
        blocks = value.reshape(value.shape[0], self.seq, -1)
        if outer_x:
            order = [self.offset(i, j) for j in range(self.nx) for i in range(self.ny)]
        else:
            order = [self.offset(i, j) for i in range(self.ny) for j in range(self.nx)]
        return jnp.concatenate([pick(blocks, place, 1) for place in order], axis=1)


    def vector_sum(self, value):
        bit = 1
        while bit < self.rows:
            value = value + self.permute(
                value,
                lambda z, c, s: ((2 * z + c ^ bit) // 2, (2 * z + c ^ bit) % 2, s),
            )
            bit *= 2
        bit = 1
        while bit < self.seq:
            value = value + self.permute(value, lambda z, c, s: (z, c, s ^ bit))
            bit *= 2
        return value


def ring_order(count):
    return list(range(count - 2, -1, -1)) + [count - 1]


def ring_sum(pieces, send):
    order = ring_order(len(pieces))
    value = pieces[order[0]]()
    for k in order[1:]:
        value = pieces[k]() + send(value.astype(BF)).astype(F32)
    return value


def normalize(values):
    centered = values - jnp.mean(values, axis=-1, keepdims=True)
    scale = lax.rsqrt(jnp.mean(centered * centered, axis=-1, keepdims=True) + EPSILON)
    return centered * scale, scale


def layer_norm(values, gain, shift):
    return (normalize(values)[0] * gain + shift).astype(BF)


def norm_backward(values, gain, cotangent):
    normal, scale = normalize(values)
    grown = cotangent * gain
    inner = jnp.mean(grown, axis=-1, keepdims=True)
    along = jnp.mean(grown * normal, axis=-1, keepdims=True)
    grad = scale * (grown - inner - normal * along)
    return grad, jnp.sum(cotangent * normal, axis=0), jnp.sum(cotangent, axis=0)


def nt(left, right):
    return dot(left, right, 1, 1)


def head_lanes(values, head):
    lane = lax.broadcasted_iota(jnp.int32, values.shape, 1)
    return jnp.where((lane < HD) == (head == 0), values, jnp.zeros_like(values))


def turned(values):
    return jnp.swapaxes(values.astype(F32), 0, 1).astype(BF)


def running(lengths_ref, first):
    ends, total = [], 0
    for c in range(CLIPS):
        total = total + lengths_ref[first + c]
        ends.append(total)
    return ends


def spans(start, length, axis, ends):
    shape = (length, 1) if axis == 0 else (1, length)
    positions = lax.broadcasted_iota(jnp.int32, shape, axis) + start
    return sum((positions >= end).astype(jnp.int32) for end in ends)


def segment_bias(key_segment, query_segment, causal):
    allowed = key_segment == query_segment
    if causal:
        key = lax.broadcasted_iota(jnp.int32, allowed.shape, 0)
        query = lax.broadcasted_iota(jnp.int32, allowed.shape, 1)
        allowed = allowed & (key <= query)
    return jnp.where(allowed, 0.0, MASKED).astype(F32)


def forward_heads(queries, blocks, lse_ref, at):
    parts = []
    for head in range(2):
        query = head_lanes(queries, head)
        scores = [nt(keys, query) + bias() for keys, _, bias in blocks]
        highest = functools.reduce(
            jnp.maximum, [jnp.max(s, axis=0, keepdims=True) for s in scores]
        )
        weights = [jnp.exp(s - highest) for s in scores]
        total = sum(jnp.sum(w, axis=0, keepdims=True) for w in weights)
        mixed = sum(
            dot(values[head * HD : (head + 1) * HD], w.astype(BF))
            for (_, values, _), w in zip(blocks, weights)
        )
        parts.append(mixed * (1.0 / total))
        lse_ref[0, head : head + 1, at] = highest + jnp.log(total)
    return jnp.swapaxes(jnp.concatenate(parts, axis=0), 0, 1).astype(BF)


def backward_heads(queries, grads, mixed, blocks, lse_ref, at):
    product = jnp.swapaxes(grads.astype(F32) * mixed.astype(F32), 0, 1)
    parts = []
    for head in range(2):
        query, grad = head_lanes(queries, head), head_lanes(grads, head)
        rows = slice(head * HD, (head + 1) * HD)
        inner = jnp.sum(product[rows], axis=0, keepdims=True)
        totals = lse_ref[0, head : head + 1, at]
        grad_query = None
        for keys, turned_keys, values, bias, sums in blocks:
            weights = jnp.exp(nt(keys, query) + bias() - totals)
            scores = (weights * (nt(values, grad) - inner)).astype(BF)
            add_to(sums, 0, dot(scores, query))
            add_to(sums, 1, dot(weights.astype(BF), grad))
            term = dot(turned_keys[rows], scores)
            grad_query = term if grad_query is None else grad_query + term
        parts.append(grad_query)
    return (jnp.swapaxes(jnp.concatenate(parts, axis=0), 0, 1) * HD**-0.5).astype(BF)


def add_to(sums, index, term):
    sums[index] = term if sums[index] is None else sums[index] + term


def scaled(values):
    return values * jnp.array(HD**-0.5, BF)


def self_plan(core):
    if core == 0:
        return [(0, 0, 0)], [(0, 0, 1), (0, 1, 2), (1, 0, 3), (1, 1, 4)]
    return [(0, 0, 0), (1, 0, 4)], [(0, 0, 1), (0, 1, 2), (1, 0, 3)]


def self_biases(core, lengths_ref, bias_ref):
    length = bias_ref.shape[1]
    ends = running(lengths_ref, 0)
    quarters = (core, 3 - core)
    keys = [spans(q * length, length, 0, ends) for q in quarters]
    queries = [spans(q * length, length, 1, ends) for q in quarters]
    others = [spans(q * length, length, 0, ends) for q in (1 - core, 2 + core)]
    bias_ref[0] = segment_bias(keys[0], queries[0], True)
    bias_ref[1] = segment_bias(keys[0], queries[1], False)
    bias_ref[2] = segment_bias(keys[1], queries[1], True)
    bias_ref[3] = segment_bias(others[0], queries[1], False)
    last_key = jnp.where(core == 0, others[1], others[0])
    last_query = jnp.where(core == 0, queries[1], queries[0])
    bias_ref[4] = segment_bias(last_key, last_query, False)


def cross_bias(lengths_ref, bias_ref):
    core = lax.axis_index(ROWS) % 2
    count, rows = bias_ref.shape
    for n, token in enumerate((core, 3 - core, 1 - core, 2 + core)):
        keys = spans(token * (count // 4), count // 4, 0, running(lengths_ref, CLIPS))
        for m, frame in enumerate((core, 3 - core)):
            queries = spans(frame * (rows // 2), rows // 2, 1, running(lengths_ref, 0))
            at = slice(n * (count // 4), (n + 1) * (count // 4))
            bias_ref[at, m * (rows // 2) : (m + 1) * (rows // 2)] = segment_bias(keys, queries, False)


def self_forward_kernel(
    lengths_ref, q_ref, k_ref, v_ref, ko_ref, vo_ref, o_ref, lse_ref, bias_ref
):
    core = lax.axis_index(ROWS) % 2
    length = bias_ref.shape[1]

    @pl.when(pl.program_id(0) == 0)
    def _():
        self_biases(core, lengths_ref, bias_ref)

    keys, values = (k_ref, ko_ref), (v_ref, vo_ref)
    for which in range(2):

        @pl.when((core == 0) == (which == 0))
        def _(which=which):
            for half, plan in enumerate(self_plan(which)):
                at = slice(half * length, (half + 1) * length)
                blocks = []
                for source, part, number in plan:
                    where = slice(part * length, (part + 1) * length)
                    blocks.append(
                        (
                            keys[source][where],
                            turned(values[source][where]),
                            functools.partial(bias_ref.__getitem__, number),
                        )
                    )
                o_ref[at] = forward_heads(scaled(q_ref[at]), blocks, lse_ref, at)


def self_backward_kernel(
    lengths_ref,
    q_ref,
    k_ref,
    v_ref,
    ko_ref,
    vo_ref,
    g_ref,
    o_ref,
    lse_ref,
    dq_ref,
    dk_ref,
    dv_ref,
    dko_ref,
    dvo_ref,
    bias_ref,
):
    core = lax.axis_index(ROWS) % 2
    length = bias_ref.shape[1]

    @pl.when(pl.program_id(0) == 0)
    def _():
        self_biases(core, lengths_ref, bias_ref)

    keys, values = (k_ref, ko_ref), (v_ref, vo_ref)
    for which in range(2):

        @pl.when((core == 0) == (which == 0))
        def _(which=which):
            sums = {(s, p): [None, None] for s in range(2) for p in range(2)}
            for half, plan in enumerate(self_plan(which)):
                at = slice(half * length, (half + 1) * length)
                blocks = []
                for source, part, number in plan:
                    where = slice(part * length, (part + 1) * length)
                    blocks.append(
                        (
                            keys[source][where],
                            turned(keys[source][where]),
                            values[source][where],
                            functools.partial(bias_ref.__getitem__, number),
                            sums[source, part],
                        )
                    )
                dq_ref[at] = backward_heads(
                    scaled(q_ref[at]), g_ref[at], o_ref[at], blocks, lse_ref, at
                )
            for (source, part), pair in sums.items():
                where = slice(part * length, (part + 1) * length)
                for ref, value in zip(((dk_ref, dv_ref), (dko_ref, dvo_ref))[source], pair):
                    if value is None:
                        ref[where] = jnp.zeros((length, PAIR), BF)
                    else:
                        ref[where] = value.astype(BF)


def cross_forward_kernel(lengths_ref, q_ref, k_ref, v_ref, o_ref, lse_ref, bias_ref):
    length = q_ref.shape[0] // 2

    @pl.when(pl.program_id(0) == 0)
    def _():
        cross_bias(lengths_ref, bias_ref)

    turned_values = turned(v_ref[...])
    for half in range(2):
        at = slice(half * length, (half + 1) * length)
        blocks = [(k_ref[...], turned_values, lambda at=at: bias_ref[:, at])]
        o_ref[at] = forward_heads(scaled(q_ref[at]), blocks, lse_ref, at)


def cross_backward_kernel(
    lengths_ref,
    q_ref,
    k_ref,
    v_ref,
    g_ref,
    o_ref,
    lse_ref,
    dq_ref,
    dk_ref,
    dv_ref,
    bias_ref,
):
    length = q_ref.shape[0] // 2

    @pl.when(pl.program_id(0) == 0)
    def _():
        cross_bias(lengths_ref, bias_ref)

    turned_keys = turned(k_ref[...])
    sums = [None, None]
    for half in range(2):
        at = slice(half * length, (half + 1) * length)
        blocks = [(k_ref[...], turned_keys, v_ref[...], lambda at=at: bias_ref[:, at], sums)]
        dq_ref[at] = backward_heads(scaled(q_ref[at]), g_ref[at], o_ref[at], blocks, lse_ref, at)
    dk_ref[...] = sums[0].astype(BF)
    dv_ref[...] = sums[1].astype(BF)


def column(rows, first=0):
    return pl.BlockSpec((rows, PAIR), lambda i: (0, first + i))


SMEM_SPEC = pl.BlockSpec(memory_space=pltpu.SMEM)


def without(kernel, first, count):
    def run(*refs):
        kernel(*refs[:first], *refs[first + count :])

    return run


ANY_SPEC = pl.BlockSpec(memory_space=pl.ANY)
WHOLE_SPEC = pl.BlockSpec(memory_space=pltpu.VMEM)


MARK = jax.ShapeDtypeStruct((8, 128), F32)


def marked(kernel, at):
    def run(*refs):
        refs[at][...] = jnp.zeros((8, 128), F32)
        kernel(*refs[:at], *refs[at + 1 :])

    return run


def attention_call(kernel, heads, in_specs, outs, bias_shape, flops, arguments, before=()):
    pairs = heads // 2
    kernel = marked(kernel, len(arguments) + len(outs))
    kernel = without(kernel, len(arguments), len(before))
    in_specs = list(in_specs) + [ANY_SPEC] * len(before)
    arguments = tuple(arguments) + tuple(before)
    out_shape, out_specs = [], []
    for rows in outs:
        if rows is None:
            queries = outs[0]
            out_shape.append(jax.ShapeDtypeStruct((pairs, 8, queries), F32))
            out_specs.append(pl.BlockSpec((1, 8, queries), lambda i: (i, 0, 0)))
        else:
            out_shape.append(jax.ShapeDtypeStruct((rows, pairs * PAIR), BF))
            out_specs.append(column(rows))
    out_shape.append(MARK)
    out_specs.append(pl.BlockSpec((8, 128), lambda i: (0, 0)))
    return pl.pallas_call(
        kernel,
        grid=(pairs,),
        in_specs=in_specs,
        out_specs=out_specs,
        out_shape=out_shape,
        scratch_shapes=[pltpu.VMEM(bias_shape, F32)],
        compiler_params=pltpu.CompilerParams(vmem_limit_bytes=VMEM_LIMIT),
        cost_estimate=pl.CostEstimate(flops=flops, bytes_accessed=8 << 20, transcendentals=flops >> 8),
    )(*arguments)


def lse_spec(queries):
    return pl.BlockSpec((1, 8, queries), lambda i: (i, 0, 0))


def self_forward(lengths, queries, pair, pair_other):
    rows, width = queries.shape
    heads = width // HD
    length = rows // 2
    half = heads // 2
    return attention_call(
        self_forward_kernel,
        heads,
        [
            SMEM_SPEC,
            column(rows),
            column(rows),
            column(rows, half),
            column(rows),
            column(rows, half),
        ],
        (rows, None),
        (5, length, length),
        heads * 5 * 4 * length * length * PAIR * 2,
        (lengths, queries, pair, pair, pair_other, pair_other),
    )


def self_backward(lengths, queries, pair, pair_other, grads, mixed, lse, before=()):
    rows, width = queries.shape
    heads = width // HD
    length = rows // 2
    half = heads // 2
    return attention_call(
        self_backward_kernel,
        heads,
        [
            SMEM_SPEC,
            column(rows),
            column(rows),
            column(rows, half),
            column(rows),
            column(rows, half),
            column(rows),
            column(rows),
            lse_spec(rows),
        ],
        (rows,) * 5,
        (5, length, length),
        heads * 5 * 10 * length * length * PAIR * 2,
        (lengths, queries, pair, pair, pair_other, pair_other, grads, mixed, lse),
        before,
    )


def cross_forward(lengths, queries, pair):
    rows, width = queries.shape
    heads = width // HD
    count = pair.shape[0]
    return attention_call(
        cross_forward_kernel,
        heads,
        [SMEM_SPEC, column(rows), column(count), column(count, heads // 2)],
        (rows, None),
        (count, rows),
        heads * 4 * rows * count * PAIR * 2,
        (lengths, queries, pair, pair),
    )


def cross_backward(lengths, queries, pair, grads, mixed, lse, before=()):
    rows, width = queries.shape
    heads = width // HD
    count = pair.shape[0]
    return attention_call(
        cross_backward_kernel,
        heads,
        [
            SMEM_SPEC,
            column(rows),
            column(count),
            column(count, heads // 2),
            column(rows),
            column(rows),
            lse_spec(rows),
        ],
        (rows, count, count),
        (count, rows),
        heads * 10 * rows * count * PAIR * 2,
        (lengths, queries, pair, pair, grads, mixed, lse),
        before,
    )


def gelu_and_slope(values):
    inside = 0.5 * (1.0 + lax.erf(values * (0.5**0.5)))
    bell = jnp.exp(-0.5 * values * values) * ((2.0 * math.pi) ** -0.5)
    return values * inside, inside + values * bell


def feed_kernel(shape, meta_ref, own_ref, other_ref, gown_ref, gother_ref, win_ref, wout_ref, *refs):
    nx, ny, nz, chunk = shape
    res_ref, res_other_ref, grad_ref, grad_other_ref = refs[:4]
    up_refs, low_refs, gout_refs = refs[4 : 4 + nx], refs[4 + nx : 4 + nx + ny], refs[4 + nx + ny : 4 + nx + ny + nz]
    act_ref, pre_ref, turned_ref, gturned_ref, res_acc, grad_acc = refs[4 + nx + ny + nz :]
    j, i = pl.program_id(0), pl.program_id(1)
    z = meta_ref[3]
    tokens = own_ref.shape[0]
    sources = ((own_ref, gown_ref, res_ref, grad_ref), (other_ref, gother_ref, res_acc, grad_acc))

    @pl.when((i == 0) & (j == 0))
    def _():
        for side, (values, grads, res, grad) in enumerate(sources):
            at = slice(side * tokens, (side + 1) * tokens)
            turned_ref[:, at] = turned(values[...])
            gturned_ref[:, at] = turned(grads[...])
            res[...] = jnp.zeros_like(res)
            grad[...] = jnp.zeros_like(grad)

    for side, (values, grads, res, grad) in enumerate(sources):
        for m in range(tokens // chunk):
            at = slice(m * chunk, (m + 1) * chunk)
            activated, slope = gelu_and_slope(dot(values[at], win_ref[...]))
            activated = activated.astype(BF)
            before = (nt(grads[at], wout_ref[...]) * slope).astype(BF)
            to = slice(side * tokens + m * chunk, side * tokens + (m + 1) * chunk)
            act_ref[to] = activated
            pre_ref[to] = before
            res[at] += dot(activated, wout_ref[...])
            grad[at] += nt(before, win_ref[...])

    rows = turned_ref.shape[0] // nz
    half = rows // 2
    for k in range(nz):
        source = pl.ds(pl.multiple_of((z + 1 + k) % nz * rows, rows), rows)
        gin = dot(turned_ref[source], pre_ref[...]).astype(BF)
        gout_refs[k][0] = dot(gturned_ref[source], act_ref[...]).astype(BF)
        to = slice(k * half, (k + 1) * half)
        for number, ref in enumerate(up_refs):

            @pl.when(j == number)
            def _(ref=ref):
                ref[0, to] = gin[:half]

        for number, ref in enumerate(low_refs):

            @pl.when(i == number)
            def _(ref=ref):
                ref[0, to] = gin[half:]

    @pl.when((i == ny - 1) & (j == nx - 1))
    def _():
        res_other_ref[...] = res_acc[...].astype(BF)
        grad_other_ref[...] = grad_acc[...].astype(BF)


def feed(place, meta, own, other, gown, gother, feed_in, feed_out):
    nx, ny, nz = place.nx, place.ny, place.nz
    tokens, width = own.shape
    part = feed_in.shape[1] // place.seq // 2
    chunk = min(256, tokens)

    def unit(j, i, meta):
        return 2 * ((meta[2] + 1 + i) % ny * nx + (meta[1] + 1 + j) % nx) + meta[0]

    def up_spec(number):
        def index(j, i, meta):
            return jnp.where(j == number, i, jnp.where(j < number, 0, ny - 1)), 0, 0

        return pl.BlockSpec((1, width // 2, part), index)

    low_spec = pl.BlockSpec((1, width // 2, part), lambda j, i, meta: (j, 0, 0))
    gout_spec = pl.BlockSpec((1, width // nz, part), lambda j, i, meta: (j * ny + i, 0, 0))
    total = 2 * tokens
    shape = jax.ShapeDtypeStruct
    return pl.pallas_call(
        functools.partial(feed_kernel, (nx, ny, nz, chunk)),
        grid_spec=pltpu.PrefetchScalarGridSpec(
            num_scalar_prefetch=1,
            grid=(nx, ny),
            in_specs=[WHOLE_SPEC] * 4
            + [
                pl.BlockSpec((width, part), lambda j, i, meta: (0, unit(j, i, meta))),
                pl.BlockSpec((part, width), lambda j, i, meta: (unit(j, i, meta), 0)),
            ],
            out_specs=[WHOLE_SPEC] * 4
            + [up_spec(n) for n in range(nx)]
            + [low_spec] * ny
            + [gout_spec] * nz,
            scratch_shapes=[
                pltpu.VMEM((total, part), BF),
                pltpu.VMEM((total, part), BF),
                pltpu.VMEM((width, total), BF),
                pltpu.VMEM((width, total), BF),
                pltpu.VMEM((tokens, width), F32),
                pltpu.VMEM((tokens, width), F32),
            ],
        ),
        out_shape=[
            shape((tokens, width), F32),
            shape((tokens, width), BF),
            shape((tokens, width), F32),
            shape((tokens, width), BF),
        ]
        + [shape((ny, width // 2, part), BF)] * nx
        + [shape((nx, width // 2, part), BF)] * ny
        + [shape((place.seq, width // nz, part), BF)] * nz,
        compiler_params=pltpu.CompilerParams(vmem_limit_bytes=60 * 1024 * 1024),
        cost_estimate=pl.CostEstimate(
            flops=12 * total * width * part * place.seq,
            bytes_accessed=40 << 20,
            transcendentals=2 * total * part * place.seq,
        ),
    )(meta, own, other, gown, gother, feed_in, feed_out)


def weight_kernel(shape, meta_ref, *refs):
    count, nz = shape
    lefts, rights = refs[:count], refs[count : 2 * count]
    own_ref, other_ref, turned_ref = refs[2 * count :]
    core, z = meta_ref[0], meta_ref[3]
    block = own_ref.shape[1] // nz
    for number in range(count):

        @pl.when(pl.program_id(0) == number)
        def _(left=lefts[number], right=rights[number]):
            tokens = left.shape[0]
            turned_ref[:, :tokens] = turned(left[...])
            for k in range(nz):
                start = (z + 1 + k) % nz * 2
                to = slice(k * block, (k + 1) * block)
                for which, ref in ((core, own_ref), (1 - core, other_ref)):
                    at = pl.ds(pl.multiple_of((start + which) * block, block), block)
                    ref[0, to] = dot(turned_ref[at, :tokens], right[...]).astype(BF)


def weight_parts(place, meta, lefts, rights, before=()):
    count = len(lefts)
    depth, width = lefts[0].shape[1], rights[0].shape[1]
    tokens = max(left.shape[0] for left in lefts)
    out = jax.ShapeDtypeStruct((count, depth // 2, width), BF)
    spec = pl.BlockSpec((1, depth // 2, width), lambda u: (u, 0, 0))
    return pl.pallas_call(
        without(functools.partial(weight_kernel, (count, place.nz)), 1 + 2 * count, len(before)),
        grid=(count,),
        in_specs=[SMEM_SPEC] + [WHOLE_SPEC] * (2 * count) + [ANY_SPEC] * len(before),
        out_specs=[spec, spec],
        out_shape=[out, out],
        scratch_shapes=[pltpu.VMEM((depth, tokens), BF)],
        compiler_params=pltpu.CompilerParams(vmem_limit_bytes=VMEM_LIMIT),
        cost_estimate=pl.CostEstimate(
            flops=2 * count * tokens * depth * width,
            bytes_accessed=count * depth * width * 4,
            transcendentals=0,
        ),
    )(meta, *lefts, *rights, *before)


MESH = pl.DeviceIdType.MESH


class Mail:
    def __init__(self, send_sems, recv_sems):
        self.send_sems, self.recv_sems, self.sent = send_sems, recv_sems, []

    def send(self, source, target, device):
        number = len(self.sent)
        copy = pltpu.make_async_remote_copy(
            src_ref=source,
            dst_ref=target,
            send_sem=self.send_sems.at[number],
            recv_sem=self.recv_sems.at[number],
            device_id=device,
            device_id_type=MESH,
        )
        copy.start()
        self.sent.append(copy)
        return copy

    def finish(self):
        for copy in self.sent:
            copy.wait_send()


class Ways:
    def __init__(self, nz):
        self.row, self.spot = lax.axis_index(ROWS), lax.axis_index(SEQ)
        self.core, self.z = self.row % 2, self.row // 2
        self.x, self.y = self.spot % 2, self.spot // 2
        self.nz = nz
        self.sibling = (self.row + 1 - 2 * self.core, self.spot)
        self.across_x = (self.row, self.spot + 1 - 2 * self.x)
        self.across_y = (self.row, self.y * -2 + 2 + self.x)
        self.above = ((self.row + 2) % (2 * nz), self.spot)
        self.below = ((self.row + 2 * nz - 2) % (2 * nz), self.spot)

    def plane(self):
        devices = []
        for other in range(2):
            row = self.row if other == 0 else self.sibling[0]
            devices += [(row, (self.spot + s) % 4) for s in range(4) if other or s]
        return devices

    def meet(self, devices):
        barrier = pltpu.get_barrier_semaphore()
        for device in devices:
            pl.semaphore_signal(barrier, inc=1, device_id=device, device_id_type=MESH)
        pl.semaphore_wait(barrier, len(devices))

    def place(self, q):
        return (self.y + 1 + q % 2) % 2 * 2 + (self.x + 1 + q // 2) % 2

    def rows(self, k, which, block):
        start = ((self.z + 1 + k) % self.nz * 2 + which) * block
        return pl.ds(pl.multiple_of(start, block), block)


class Home:
    def __init__(self, ways, out_ref, send_sems, recv_sems):
        self.ways, self.out_ref = ways, out_ref
        self.send_sems, self.recv_sems = send_sems, recv_sems
        self.started = []

    def send(self, source, slot):
        ways = self.ways
        spot = jnp.where(ways.core == 0, 3 * slot, 1 + slot)
        row = 2 * ways.z + ways.spot // 2
        stays = (spot == ways.spot) & (row == ways.row)
        to = self.out_ref.at[ways.spot % 2]
        copy = pltpu.make_async_remote_copy(
            src_ref=source,
            dst_ref=to,
            send_sem=self.send_sems.at[slot],
            recv_sem=self.recv_sems.at[ways.spot % 2],
            device_id=(row, spot),
            device_id_type=MESH,
        )
        local = pltpu.make_async_copy(source, to, self.recv_sems.at[ways.spot % 2])

        @pl.when(stays)
        def _():
            local.start()

        @pl.when(jnp.logical_not(stays))
        def _():
            copy.start()

        self.started.append((stays, copy))

    def finish(self):
        for r in range(2):
            to = self.out_ref.at[r]
            pltpu.make_async_copy(to, to, self.recv_sems.at[r]).wait()
        for stays, copy in self.started:

            @pl.when(jnp.logical_not(stays))
            def _(copy=copy):
                copy.wait_send()


class Gathering:
    def __init__(self, ways, source_ref, target_ref, send_sems, recv_sems):
        self.ways, self.source_ref, self.target_ref = ways, source_ref, target_ref
        self.send_sems, self.recv_sems = send_sems, recv_sems
        self.block = source_ref.shape[1]
        self.started = []

    def start(self):
        ways = self.ways
        owner = jnp.where((ways.spot == 0) | (ways.spot == 3), 0, 1)
        slot = ways.spot // 2
        to = self.target_ref.at[pl.ds(pl.multiple_of(slot * self.block, self.block), self.block)]
        for r in range(2):
            row, spot = 2 * ways.z + owner, 2 * ways.core + r
            stays = (spot == ways.spot) & (row == ways.row)
            copy = pltpu.make_async_remote_copy(
                src_ref=self.source_ref.at[r],
                dst_ref=to,
                send_sem=self.send_sems.at[r],
                recv_sem=self.recv_sems.at[slot],
                device_id=(row, spot),
                device_id_type=MESH,
            )
            local = pltpu.make_async_copy(self.source_ref.at[r], to, self.recv_sems.at[slot])

            @pl.when(stays)
            def _(local=local):
                local.start()

            @pl.when(jnp.logical_not(stays))
            def _(copy=copy):
                copy.start()

            self.started.append((stays, copy))

    def arrived(self, slot):
        to = self.target_ref.at[slot * self.block : (slot + 1) * self.block]
        pltpu.make_async_copy(to, to, self.recv_sems.at[slot]).wait()

    def finish(self):
        for stays, copy in self.started:

            @pl.when(jnp.logical_not(stays))
            def _(copy=copy):
                copy.wait_send()


def entry_kernel(
    nz,
    frames_ref,
    text_ref,
    grad_ref,
    lengths_ref,
    gain_ref,
    shift_ref,
    qkv_ref,
    proj_ref,
    bias_ref,
    kv_ref,
    input_ref,
    normed_ref,
    queries_ref,
    pair_ref,
    pair_other_ref,
    cotangent_ref,
    words_ref,
    projected_ref,
    text_pair_ref,
    lengths_other_ref,
    qkv_here,
    proj_here,
    kv_here,
    load_sems,
    send_sems,
    recv_sems,
    gather_sends,
    gather_recvs,
):
    loads = [
        pltpu.make_async_copy(source, target, load_sems.at[number])
        for number, (source, target) in enumerate(
            ((proj_ref, proj_here), (kv_ref, kv_here), (qkv_ref, qkv_here))
        )
    ]
    for load in loads:
        load.start()
    ways = Ways(nz)
    ways.meet(ways.plane())
    mail = Mail(send_sems, recv_sems)
    words = Gathering(ways, text_ref, words_ref, gather_sends.at[0], gather_recvs.at[0])
    frames = Gathering(ways, frames_ref, input_ref, gather_sends.at[1], gather_recvs.at[1])
    grads = Gathering(ways, grad_ref, cotangent_ref, gather_sends.at[2], gather_recvs.at[2])
    words.start()
    frames.start()
    lengths_copy = mail.send(lengths_ref, lengths_other_ref, ways.sibling)
    half = words_ref.shape[0] // 2
    for slot in range(2):
        words.arrived(slot)
    words_copy = mail.send(words_ref.at[:half], words_ref.at[half:], ways.sibling)
    for load in loads:
        load.wait()
    words_copy.wait_recv()
    projected = (dot(words_ref[...], proj_here[...]) + bias_ref[...]).astype(BF)
    projected_ref[...] = projected
    text_pair_ref[...] = dot(projected, kv_here[...]).astype(BF)
    width = input_ref.shape[1]
    block = input_ref.shape[0] // 2
    copies = []
    for slot in range(2):
        frames.arrived(slot)
        if slot == 1:
            grads.start()
        at = slice(slot * block, (slot + 1) * block)
        normed_ref[at] = layer_norm(input_ref[at].astype(F32), gain_ref[...], shift_ref[...])
        pair_ref[at] = dot(normed_ref[at], qkv_here[:, width:]).astype(BF)
        copies.append(mail.send(pair_ref.at[at], pair_other_ref.at[at], ways.sibling))
    queries_ref[...] = dot(normed_ref[...], qkv_here[:, :width]).astype(BF)
    lengths_copy.wait_recv()
    for copy in copies:
        copy.wait_recv()
    for slot in range(2):
        grads.arrived(slot)
    mail.finish()
    for gathering in (words, frames, grads):
        gathering.finish()


def entry(place, frames, text, grads, lengths, gain, shift, qkv, proj, bias, kv):
    count, block, width = frames.shape
    tokens, words = count * block, 2 * count * text.shape[1]
    shape, vmem = jax.ShapeDtypeStruct, pltpu.VMEM
    return pl.pallas_call(
        functools.partial(entry_kernel, place.nz),
        in_specs=[ANY_SPEC] * 3 + [WHOLE_SPEC] * 3 + [ANY_SPEC] * 2 + [WHOLE_SPEC, ANY_SPEC],
        out_specs=[WHOLE_SPEC] * 10,
        out_shape=[
            shape((tokens, width), BF),
            shape((tokens, width), BF),
            shape((tokens, width), BF),
            shape((tokens, 2 * width), BF),
            shape((tokens, 2 * width), BF),
            shape((tokens, width), BF),
            shape((words, text.shape[2]), BF),
            shape((words, width), BF),
            shape((words, 2 * width), BF),
            shape(lengths.shape, jnp.int32),
        ],
        scratch_shapes=[
            vmem(qkv.shape, BF),
            vmem(proj.shape, BF),
            vmem(kv.shape, BF),
            pltpu.SemaphoreType.DMA((3,)),
            pltpu.SemaphoreType.DMA((4,)),
            pltpu.SemaphoreType.DMA((4,)),
            pltpu.SemaphoreType.DMA((3, 2)),
            pltpu.SemaphoreType.DMA((3, 2)),
        ],
        compiler_params=pltpu.CompilerParams(
            collective_id=3, has_side_effects=True, vmem_limit_bytes=VMEM_LIMIT
        ),
        cost_estimate=pl.CostEstimate(
            flops=20 * tokens * width * width, bytes_accessed=20 << 20, transcendentals=0
        ),
    )(frames, text, grads, lengths, gain[None], shift[None], qkv, proj, bias[None], kv)


def middle_kernel(
    shape,
    mixed_ref,
    normed_ref,
    projected_ref,
    text_ref,
    self_ref,
    g_second_ref,
    g_query_ref,
    g_keys_ref,
    g_values_ref,
    g_projected_ref,
    g_first_ref,
    result_ref,
    result_away_ref,
    send_up_ref,
    send_low_ref,
    keep_up_ref,
    keep_low_ref,
    result_out,
    mixed_t,
    normed_t,
    projected_t,
    text_t,
    self_t,
    own_ref,
    away_ref,
    got_ref,
    result_got_ref,
    send_sems,
    recv_sems,
    home_sends,
    home_recvs,
):
    nz, piece = shape
    ways = Ways(nz)
    ways.meet(ways.plane())
    mail = Mail(send_sems, recv_sems)
    result_copy = mail.send(result_away_ref, result_got_ref, ways.sibling)
    home = Home(ways, result_out, home_sends, home_recvs)
    for left, to in ((mixed_ref, mixed_t), (normed_ref, normed_t), (projected_ref, projected_t), (self_ref, self_t)):
        to[...] = turned(left[...])
    turned_text = turned(text_ref[...])
    block = own_ref.shape[2]
    count = 2 * nz
    part = turned_text.shape[0] // count
    text_t[...] = jnp.zeros_like(text_t)
    for b in range(count):
        text_t[b * block : b * block + part] = turned_text[b * part : (b + 1) * part]
    half = block // 2
    up, low = slice(0, half), slice(half, block)
    homes = (
        (send_up_ref.at[0], send_low_ref.at[0]),
        (send_up_ref.at[1], keep_low_ref.at[0]),
        (keep_up_ref.at[0], send_low_ref.at[1]),
        (keep_up_ref.at[1], keep_low_ref.at[1]),
    )
    copies = []

    def settle(q):
        copies[q].wait_recv()
        total = own_ref[q] + got_ref[q]
        homes[q][0][...] = total[:, up]
        homes[q][1][...] = total[:, low]

    for q in range(4):
        place = ways.place(q)
        columns = pl.ds(pl.multiple_of(place * piece, piece), piece)
        twice = pl.ds(pl.multiple_of(place % 2 * 2 * piece, piece), 2 * piece)
        pair = jnp.where(place < 2, g_keys_ref[:, twice], g_values_ref[:, twice])
        units = (
            (mixed_t, g_second_ref[:, columns]),
            (normed_t, g_query_ref[:, columns]),
            (projected_t, pair),
            (text_t, g_projected_ref[:, columns]),
            (self_t, g_first_ref[:, columns]),
        )
        for which, ref in ((1 - ways.core, away_ref), (ways.core, own_ref)):
            first = 0
            for left, right in units:
                to = slice(first, first + right.shape[1])
                first += right.shape[1]
                for k in range(nz):
                    ref[q, k, :, to] = dot(left[ways.rows(k, which, block)], right).astype(BF)
            if ref is away_ref:
                copies.append(mail.send(away_ref.at[q], got_ref.at[q], ways.sibling))
        if q == 0:
            result_copy.wait_recv()
            result_got_ref[...] = (result_ref[...] + result_got_ref[...].astype(F32)).astype(BF)
            slots = result_ref.shape[0] // 2
            for slot in range(2):
                home.send(result_got_ref.at[slot * slots : (slot + 1) * slots], slot)
        else:
            settle(q - 1)
    settle(3)
    mail.finish()
    home.finish()


def middle_parts(place, count, lefts, rights, result, result_away, before):
    nz = place.nz
    depth, width = lefts[0].shape[1], rights[0].shape[1]
    piece, block = width // place.seq, depth // place.rows
    columns = piece * len(rights)
    out = jax.ShapeDtypeStruct((2, nz, block // 2, columns), BF)
    big = pltpu.VMEM((4, nz, block, columns), BF)
    return pl.pallas_call(
        without(marked(functools.partial(middle_kernel, (nz, piece)), 18), 13, len(before)),
        in_specs=[WHOLE_SPEC] * 12 + [ANY_SPEC] * (1 + len(before)),
        out_specs=[WHOLE_SPEC] * 4 + [ANY_SPEC, WHOLE_SPEC],
        out_shape=[out] * 4
        + [jax.ShapeDtypeStruct((count, result.shape[0] // count, width), BF), MARK],
        scratch_shapes=[pltpu.VMEM((depth, left.shape[0]), BF) for left in lefts]
        + [big] * 3
        + [pltpu.VMEM(result.shape, BF)]
        + [pltpu.SemaphoreType.DMA((5,))] * 2
        + [pltpu.SemaphoreType.DMA((2,))] * 2,
        compiler_params=pltpu.CompilerParams(
            collective_id=2, has_side_effects=True, vmem_limit_bytes=60 * 1024 * 1024
        ),
        cost_estimate=pl.CostEstimate(
            flops=2 * 8 * 512 * depth * width, bytes_accessed=24 << 20, transcendentals=0
        ),
    )(*lefts, *rights, result, result_away, *before)


def final_kernel(nz, *refs):
    (
        normed_ref,
        input_ref,
        first_ref,
        gain_ref,
        weight_ref,
        gq_ref,
        gk_ref,
        gv_ref,
        k_away_ref,
        v_away_ref,
        upper_ref,
        upper_got_ref,
        lower_ref,
        lower_got_ref,
        in_up_ref,
        in_up_got_ref,
        in_low_ref,
        in_low_got_ref,
        out_ref,
        vector_ref,
        text_ref,
    ) = refs[:21]
    (qkv_ref, middle_ref, feed_ref, sum_ref, frames_out, text_out) = refs[21:27]
    (
        weight_here,
        first_here,
        load_sems,
        packed_ref,
        k_got_ref,
        v_got_ref,
        acc_ref,
        turned_ref,
        own_ref,
        away_ref,
        got_ref,
        first_x_ref,
        first_y_ref,
        second_y_ref,
        second_x_ref,
        mid_up_ref,
        mid_low_ref,
        mid_ref,
        mid_ring_ref,
        qkv_ring_ref,
        feed_send_ref,
        feed_ring_ref,
        out_x_ref,
        out_own_ref,
        out_y_ref,
        feed_away_ref,
        feed_other_ref,
        vector_out_ref,
        vector_in_ref,
        text_away_ref,
        text_got_ref,
        send_sems,
        recv_sems,
        home_sends,
        home_recvs,
    ) = refs[27:]
    loads = [
        pltpu.make_async_copy(source, target, load_sems.at[number])
        for number, (source, target) in enumerate(
            ((weight_ref, weight_here), (first_ref, first_here))
        )
    ]
    for load in loads:
        load.start()
    weight_ref, first_ref = weight_here, first_here
    ways = Ways(nz)
    core, z = ways.core, ways.z
    sibling, across_x, across_y, above = ways.sibling, ways.across_x, ways.across_y, ways.above
    ways.meet(ways.plane() + [ways.above, ways.below])
    mail = Mail(send_sems, recv_sems)
    ring = ring_order(nz)
    half = upper_ref.shape[2]
    feed_half = feed_ring_ref.shape[1] // 2
    tokens, width = normed_ref.shape

    k_copy = mail.send(k_away_ref, k_got_ref, sibling)
    v_copy = mail.send(v_away_ref, v_got_ref, sibling)

    out_copies = [mail.send(out_ref.at[q], out_x_ref.at[q], across_x) for q in range(2)]
    feed_copies, feed_last_copies = [], {}

    def feed_piece(t):
        at = slice(ring[t] * feed_half, (ring[t] + 1) * feed_half)
        return (
            in_up_ref[at].astype(F32) + in_up_got_ref[at].astype(F32),
            in_low_ref[at].astype(F32) + in_low_got_ref[at].astype(F32),
        )

    def feed_step(t):
        upper_part, lower_part = feed_piece(t)
        if t > 0:
            feed_copies[t - 1].wait_recv()
            upper_part += feed_ring_ref[t - 1, :feed_half].astype(F32)
            lower_part += feed_ring_ref[t - 1, feed_half:].astype(F32)
        if t == nz - 1:
            feed_finish(0, upper_part, lower_part)
            return
        feed_send_ref[t, :feed_half] = upper_part.astype(BF)
        feed_send_ref[t, feed_half:] = lower_part.astype(BF)
        feed_copies.append(mail.send(feed_send_ref.at[t], feed_ring_ref.at[t], above))

    feed_step(0)

    mid_copies = {}
    for k in ring:
        mid_ref[k, :half] = upper_ref[0, k] + upper_got_ref[0, k]
        mid_ref[k, half:] = lower_ref[0, k] + lower_got_ref[0, k]
        mid_copies[k] = (
            mail.send(mid_ref.at[k, :half], mid_up_ref.at[k], across_y),
            mail.send(mid_ref.at[k, half:], mid_low_ref.at[k], across_x),
        )
    text_rows = text_ref.shape[0] // 2
    text_away_ref[...] = text_ref[text_rows:].astype(BF)
    text_copy = mail.send(text_away_ref, text_got_ref, sibling)

    turned_ref[...] = turned(normed_ref[...])
    packed_ref[:, :width] = gq_ref[...]
    k_copy.wait_recv()
    packed_ref[:, width : 2 * width] = gk_ref[...] + k_got_ref[...]
    v_copy.wait_recv()
    packed_ref[:, 2 * width :] = gv_ref[...] + v_got_ref[...]

    block = own_ref.shape[2]
    columns = own_ref.shape[3]
    core_copies = []
    for q in range(4):
        right = packed_ref[:, pl.ds(pl.multiple_of(ways.place(q) * columns, columns), columns)]
        for which, ref in ((1 - core, away_ref), (core, own_ref)):
            for k in range(nz):
                ref[q, k] = dot(turned_ref[ways.rows(k, which, block)], right).astype(BF)
            if ref is away_ref:
                core_copies.append(mail.send(away_ref.at[q], got_ref.at[q], sibling))

    def out_step():
        for q in range(2):
            out_copies[q].wait_recv()
            out_own_ref[q] = out_ref[2 + q] + out_x_ref[q]
            if q == 0:
                out_copies.append(mail.send(out_own_ref.at[0], out_y_ref, across_y))

    def out_last():
        out_copies[2].wait_recv()
        total = out_own_ref[1].astype(F32) + out_y_ref[...].astype(F32)
        feed_finish(1, total[:feed_half], total[feed_half:])

    def feed_finish(kind, even, odd):
        away = jnp.where(core == 0, odd, even)
        own = jnp.where(core == 0, even, odd)
        across = own.shape[1]
        feed_away_ref[kind] = away
        feed_last_copies[kind] = mail.send(feed_away_ref.at[kind], feed_other_ref.at[kind], sibling)
        at = pl.ds(pl.multiple_of(core * across, across), across)
        feed_ref[kind, :, at] = own

    def feed_last(kind):
        feed_last_copies[kind].wait_recv()
        across = feed_other_ref.shape[2]
        at = pl.ds(pl.multiple_of((1 - core) * across, across), across)
        feed_ref[kind, :, at] = feed_other_ref[kind]

    def core_step(q):
        core_copies[q].wait_recv()
        own_ref[q] = own_ref[q] + got_ref[q]

    mid_ring = {}

    def mid_send(t):
        k = ring[t]
        up, low = mid_copies[k]
        up.wait()
        low.wait()
        mid_ref[k, :half] = upper_ref[1, k] + upper_got_ref[1, k] + mid_up_ref[k]
        mid_ref[k, half:] = lower_ref[1, k] + lower_got_ref[1, k] + mid_low_ref[k]
        if t > 0:
            mid_ring[t - 1].wait_recv()
        if t == nz - 1:
            middle_ref[...] = mid_ref[k].astype(F32) + mid_ring_ref[t - 1].astype(F32)
            return
        if t > 0:
            mid_ref[k] = mid_ref[k] + mid_ring_ref[t - 1]
        mid_ring[t] = mail.send(mid_ref.at[k], mid_ring_ref.at[t], above)

    qkv_ring = {}

    def qkv_send(t):
        k = ring[t]
        second[k][0].wait_recv()
        own_ref[3, k, up] = own_ref[3, k, up] + second_y_ref[k]
        second[k][1].wait_recv()
        own_ref[3, k, low] = own_ref[3, k, low] + second_x_ref[k]
        if t > 0:
            qkv_ring[t - 1].wait_recv()
        if t == nz - 1:
            qkv_ref[...] = own_ref[3, k].astype(F32) + qkv_ring_ref[t - 1].astype(F32)
            return
        if t > 0:
            own_ref[3, k] = own_ref[3, k] + qkv_ring_ref[t - 1]
        qkv_ring[t] = mail.send(own_ref.at[3, k], qkv_ring_ref.at[t], above)

    up, low = slice(0, half), slice(half, 2 * half)
    core_step(0)
    upper_first = [mail.send(own_ref.at[0, :, up], first_x_ref.at[0], across_x)]
    lower_first = [mail.send(own_ref.at[0, :, low], first_y_ref.at[0], across_y)]
    core_step(1)
    upper_first.append(mail.send(own_ref.at[1, :, up], first_x_ref.at[1], across_x))
    core_step(2)
    lower_first.append(mail.send(own_ref.at[2, :, low], first_y_ref.at[1], across_y))
    core_step(3)
    out_step()

    for load in loads:
        load.wait()
    slots = tokens // 2
    text_copy.wait_recv()
    text_got_ref[...] = (text_ref[:text_rows] + text_got_ref[...].astype(F32)).astype(BF)
    text_home = Home(ways, text_out, home_sends.at[0], home_recvs.at[0])
    for slot in range(2):
        at = slice(slot * text_rows // 2, (slot + 1) * text_rows // 2)
        text_home.send(text_got_ref.at[at], slot)

    acc_ref[...] = nt(packed_ref[:, :width], weight_ref[:, :width])
    acc_ref[...] += nt(packed_ref[:, width : 2 * width], weight_ref[:, width : 2 * width])
    mid_send(0)
    feed_step(1)
    acc_ref[...] += nt(packed_ref[:, 2 * width :], weight_ref[:, 2 * width :])
    gain_sum = jnp.zeros((1, width), F32)
    shift_sum = jnp.zeros((1, width), F32)
    chunk = min(128, tokens)
    for m in range(tokens // chunk):
        at = slice(m * chunk, (m + 1) * chunk)
        grad, gain_part, shift_part = norm_backward(
            input_ref[at].astype(F32), gain_ref[...], acc_ref[at]
        )
        k_got_ref[at] = (first_ref[at] + grad).astype(BF)
        gain_sum += gain_part[None]
        shift_sum += shift_part[None]
    vector_out_ref[0] = vector_ref[...]
    vector_out_ref[0, 0:1] = gain_sum
    vector_out_ref[0, 1:2] = shift_sum
    vector_copy = mail.send(vector_out_ref.at[0], vector_in_ref.at[0], sibling)
    mid_send(1)

    vector_copy.wait_recv()
    vector_out_ref[1] = vector_out_ref[0] + vector_in_ref[0]
    vector_copy = mail.send(vector_out_ref.at[1], vector_in_ref.at[1], across_x)
    for t in range(2, nz):
        feed_step(t)
        if t < nz - 1:
            mid_send(t)
    vector_copy.wait_recv()
    vector_out_ref[2] = vector_out_ref[1] + vector_in_ref[1]
    vector_copy = mail.send(vector_out_ref.at[2], vector_in_ref.at[2], across_y)
    out_last()

    upper_first[0].wait_recv()
    own_ref[2, :, up] = own_ref[2, :, up] + first_x_ref[0]
    lower_first[0].wait_recv()
    own_ref[1, :, low] = own_ref[1, :, low] + first_y_ref[0]
    second = {}
    for k in ring:
        second[k] = (
            mail.send(own_ref.at[2, k, up], second_y_ref.at[k], across_y),
            mail.send(own_ref.at[1, k, low], second_x_ref.at[k], across_x),
        )
    frames_home = Home(ways, frames_out, home_sends.at[1], home_recvs.at[1])
    for slot in range(2):
        frames_home.send(k_got_ref.at[slot * slots : (slot + 1) * slots], slot)
    vector_copy.wait_recv()
    vector_out_ref[3] = vector_out_ref[2] + vector_in_ref[2]
    vector_copy = mail.send(vector_out_ref.at[3], vector_in_ref.at[3], above)
    upper_first[1].wait_recv()
    own_ref[3, :, up] = own_ref[3, :, up] + first_x_ref[1]
    lower_first[1].wait_recv()
    own_ref[3, :, low] = own_ref[3, :, low] + first_y_ref[1]
    mid_send(nz - 1)
    for kind in range(2):
        feed_last(kind)
    total = vector_out_ref[3]
    for t in range(nz - 1):
        vector_copy.wait_recv()
        total = total + vector_in_ref[3 + t]
        if t < nz - 2:
            vector_copy = mail.send(vector_in_ref.at[3 + t], vector_in_ref.at[4 + t], above)
    sum_ref[...] = total
    for t in range(nz):
        qkv_send(t)
    text_home.finish()
    frames_home.finish()
    for number, copy in enumerate(mail.sent):
        if not any(copy is c for pair in mid_copies.values() for c in pair):
            copy.wait_send()


FINAL_IN_PLACE = (2, 4, 8, 9)


def final_sums(place, count, *operands):
    nz = place.nz
    normed, weight, upper, in_up = operands[0], operands[4], operands[10], operands[14]
    vectors, text = operands[19], operands[20]
    tokens, width = normed.shape
    block, piece = width // place.rows, weight.shape[1] // place.seq
    half, middle = block // 2, upper.shape[3]
    feed_width = in_up.shape[1]
    feed_rows = width // nz
    copies = 2 + 3 + nz - 1 + 2 + 2 * nz + 1 + 4 + 3 + nz - 1 + 4 + 2 * nz + 2 * (nz - 1)
    vmem = pltpu.VMEM
    return pl.pallas_call(
        functools.partial(final_kernel, nz),
        in_specs=[
            ANY_SPEC if n in FINAL_IN_PLACE else WHOLE_SPEC for n in range(len(operands))
        ],
        out_specs=[WHOLE_SPEC] * 4 + [ANY_SPEC] * 2,
        out_shape=[
            jax.ShapeDtypeStruct((block, piece), F32),
            jax.ShapeDtypeStruct((block, middle), F32),
            jax.ShapeDtypeStruct((2, block, 2 * feed_width), F32),
            jax.ShapeDtypeStruct(vectors.shape, F32),
            jax.ShapeDtypeStruct((count, tokens // count, width), BF),
            jax.ShapeDtypeStruct((count, text.shape[0] // 2 // count, text.shape[1]), BF),
        ],
        scratch_shapes=[
            vmem(weight.shape, BF),
            vmem((tokens, width), F32),
            pltpu.SemaphoreType.DMA((2,)),
            vmem((tokens, 3 * width), BF),
            vmem((tokens, width), BF),
            vmem((tokens, width), BF),
            vmem((tokens, width), F32),
            vmem((width, tokens), BF),
            vmem((4, nz, block, piece), BF),
            vmem((4, nz, block, piece), BF),
            vmem((4, nz, block, piece), BF),
            vmem((2, nz, half, piece), BF),
            vmem((2, nz, half, piece), BF),
            vmem((nz, half, piece), BF),
            vmem((nz, half, piece), BF),
            vmem((nz, half, middle), BF),
            vmem((nz, half, middle), BF),
            vmem((nz, block, middle), BF),
            vmem((nz - 1, block, middle), BF),
            vmem((nz - 1, block, piece), BF),
            vmem((nz - 1, feed_rows, feed_width), BF),
            vmem((nz - 1, feed_rows, feed_width), BF),
            vmem((2, feed_rows, feed_width), BF),
            vmem((2, feed_rows, feed_width), BF),
            vmem((feed_rows, feed_width), BF),
            vmem((2, feed_rows // 2, feed_width), F32),
            vmem((2, feed_rows // 2, feed_width), F32),
            vmem((4,) + vectors.shape, F32),
            vmem((2 + nz,) + vectors.shape, F32),
            vmem((text.shape[0] // 2, text.shape[1]), BF),
            vmem((text.shape[0] // 2, text.shape[1]), BF),
            pltpu.SemaphoreType.DMA((copies,)),
            pltpu.SemaphoreType.DMA((copies,)),
            pltpu.SemaphoreType.DMA((2, 2)),
            pltpu.SemaphoreType.DMA((2, 2)),
        ],
        compiler_params=pltpu.CompilerParams(
            collective_id=1, has_side_effects=True, vmem_limit_bytes=63 * 1024 * 1024
        ),
        cost_estimate=pl.CostEstimate(
            flops=60 * tokens * width * weight.shape[1], bytes_accessed=40 << 20, transcendentals=0
        ),
    )(*operands)


def permuted_sums(place, meta, in_up, in_low, out_sum, lefts, rights, normed_self, backward_self):
    nx, ny, nz, seq = place.nx, place.ny, place.nz, place.seq
    width = normed_self.shape[1]
    block, piece = width // place.rows, width // seq
    middle_own, middle_away = weight_parts(
        place, meta, lefts[:3] + lefts[2:4], rights[:5]
    )
    out_own, out_away = weight_parts(place, meta, lefts[4:], rights[5:])
    middle_got = place.swap_core(middle_away)
    out_got = place.swap_core(out_away)
    grad_packed = backward_self(middle_got, out_got)
    in_up = ring_sum([lambda a=in_up[k]: a.astype(F32) for k in range(ny)], place.next_y)
    in_low = ring_sum([lambda a=in_low[k]: a.astype(F32) for k in range(nx)], place.next_x)
    in_both = jnp.stack([in_up, in_low]).astype(BF).reshape(2, nz, block, -1)
    in_both = ring_sum([lambda a=in_both[:, k]: a.astype(F32) for k in range(nz)], place.next_z)
    out_sum = out_sum.reshape((nx, ny) + out_sum.shape[1:])
    out_sum = ring_sum([lambda a=out_sum[k]: a.astype(F32) for k in range(nx)], place.next_x)
    out_sum = out_sum.astype(BF)
    out_sum = ring_sum([lambda a=out_sum[k]: a.astype(F32) for k in range(ny)], place.next_y)
    feed_own = jnp.stack([in_both, out_sum.reshape(2, block, -1)])
    feed_got = place.swap_core(pick(feed_own, 1 - place.core, 1))
    feed_own = pick(feed_own, place.core, 1)
    low = jnp.where(place.core == 0, feed_own, feed_got)
    high = jnp.where(place.core == 0, feed_got, feed_own)
    sum_feed = jnp.concatenate([low, high], axis=2)

    def middle_piece(k):
        at = slice(k * block, (k + 1) * block)
        return lambda: middle_own[:, at].astype(F32) + middle_got[:, at].astype(F32)

    middle = ring_sum([middle_piece(k) for k in range(nz)], place.next_z).astype(BF)
    spread = jnp.concatenate(
        [
            middle[0].reshape(block, seq, -1),
            middle[1].reshape(block, seq, -1),
            jnp.concatenate([middle[2], middle[3]], axis=1).reshape(block, seq, -1),
            middle[4].reshape(block, seq, -1),
        ],
        axis=2,
    ).reshape(block, ny, nx, -1)

    def shifted(array, index, number, length, axis):
        return lambda: pick(array, (index + 1 + number) % length, axis).astype(F32)

    spread = ring_sum([shifted(spread, place.x, k, nx, 2) for k in range(nx)], place.next_x).astype(BF)
    spread = ring_sum([shifted(spread, place.y, k, ny, 1) for k in range(ny)], place.next_y)
    relative_parts = place.relative_columns(grad_packed, True)
    qkv_own, qkv_away = weight_parts(place, meta, [normed_self], [relative_parts])
    qkv_got = place.swap_core(qkv_away)

    def columns(array):
        return array[0].reshape(array.shape[1], nx, ny, -1)

    def natural(array):
        return jnp.stack(
            [
                jnp.stack(
                    [
                        pick(array[0].reshape(array.shape[1], seq, -1), place.offset(i, j), 1)
                        for i in range(ny)
                    ],
                    axis=1,
                )
                for j in range(nx)
            ],
            axis=1,
        )

    last_own = jnp.concatenate([columns(qkv_own), natural(out_own)], axis=3)
    last_got = jnp.concatenate([columns(qkv_got), natural(out_got)], axis=3)
    last = (last_own.astype(F32) + last_got.astype(F32)).astype(BF)
    last = last.reshape(nz, 2, block // 2, nx, ny, -1)
    upper = ring_sum([lambda k=k: last[:, 0, :, k].astype(F32) for k in range(nx)], place.next_x).astype(BF)
    lower = ring_sum([lambda k=k: last[:, 1, :, :, k].astype(F32) for k in range(ny)], place.next_y).astype(BF)
    upper = ring_sum([lambda a=upper[:, :, k]: a.astype(F32) for k in range(ny)], place.next_y)
    lower = ring_sum([lambda a=lower[:, :, k]: a.astype(F32) for k in range(nx)], place.next_x)
    last = jnp.stack([upper, lower], axis=1).astype(BF)
    last = ring_sum([lambda a=last[k]: a.astype(F32) for k in range(nz)], place.next_z)
    last = last.reshape(block, -1)
    sum_self_qkv, sum_self_out = last[:, : 3 * piece], last[:, 3 * piece :]

    return sum_feed, spread, sum_self_qkv, sum_self_out, grad_packed


def shards(
    frames,
    text_states,
    clip_lengths,
    text_lengths,
    self_gain,
    self_shift,
    self_qkv,
    self_out,
    cross_gain,
    cross_shift,
    cross_query,
    text_proj,
    text_bias,
    cross_kv,
    cross_out,
    feed_gain,
    feed_shift,
    feed_in,
    feed_out,
    grad_out,
):
    place = Place()
    count = frames.shape[0]
    width = frames.shape[2]
    text_total = text_states.shape[1] * place.seq

    nx, ny, nz, seq = place.nx, place.ny, place.nz, place.seq
    block, piece = width // place.rows, width // seq
    kernels = nx == 2 and ny == 2 and piece % 128 == 0
    lengths = jnp.concatenate([clip_lengths, text_lengths], axis=1)
    if kernels:
        padded = jnp.zeros((8, 128), jnp.int32).at[:count, : 2 * CLIPS].set(lengths)
        (
            layer_raw,
            normed_self,
            queries,
            pair,
            pair_other,
            cotangent,
            text_input,
            projected,
            text_pair,
            lengths_other,
        ) = entry(
            place,
            frames,
            text_states,
            grad_out,
            padded,
            self_gain,
            self_shift,
            self_qkv,
            text_proj,
            text_bias,
            cross_kv,
        )
        lengths_other = lengths_other[:count, : 2 * CLIPS]
        layer_input = layer_raw.astype(F32)
    else:
        lengths_other = place.swap_core(lengths)
        text_half = place.to_rows(text_states)
        layer_raw = place.to_rows(frames)
        text_input = jnp.concatenate([text_half, place.swap_core(text_half)], axis=0)
        cotangent = place.to_rows(grad_out)
        projected = (dot(text_input, text_proj) + text_bias).astype(BF)
        text_pair = dot(projected, cross_kv).astype(BF)
        layer_input = layer_raw.astype(F32)
        normed_self = layer_norm(layer_input, self_gain, self_shift)
        pair = dot(normed_self, self_qkv[:, width:]).astype(BF)
        pair_other = place.swap_core(pair)
        queries = dot(normed_self, self_qkv[:, :width]).astype(BF)
    cotangent_other = place.swap_core(cotangent)
    mine = place.spot // count == place.core
    row_lengths = pick(jnp.where(mine, lengths, lengths_other), place.spot % count, 0)

    self_mix, self_lse, _ = self_forward(row_lengths, queries, pair, pair_other)
    first = layer_input + dot(self_mix, self_out)
    normed_cross = layer_norm(first, cross_gain, cross_shift)
    cross_queries = dot(normed_cross, cross_query).astype(BF)
    cross_mix, cross_lse, _ = cross_forward(row_lengths, cross_queries, text_pair)
    second = first + dot(cross_mix, cross_out)
    normed_feed = layer_norm(second, feed_gain, feed_shift)

    meta = jnp.stack([place.core, place.x, place.y, place.z]).astype(jnp.int32)
    normed_other = place.swap_core(normed_feed)
    fed = feed(
        place, meta, normed_feed, normed_other, cotangent, cotangent_other, feed_in, feed_out
    )
    result, result_away, grad_normed_feed, grad_away = fed[:4]
    up_parts, low_parts, out_parts = fed[4 : 4 + nx], fed[4 + nx : 4 + nx + ny], fed[4 + nx + ny :]
    grad_normed_feed = grad_normed_feed + place.swap_core(grad_away).astype(F32)

    grad_part, grad_feed_gain, grad_feed_shift = norm_backward(second, feed_gain, grad_normed_feed)
    grad_second = cotangent.astype(F32) + grad_part
    grad_second_branch = grad_second.astype(BF)
    grad_cross_mix = dot(grad_second_branch, cross_out, 1, 1).astype(BF)
    grad_cross_queries, grad_text_keys, grad_text_values, cross_mark = cross_backward(
        row_lengths,
        cross_queries,
        text_pair,
        grad_cross_mix,
        cross_mix,
        cross_lse,
    )
    late = cross_mark[0, 0]
    in_up = ring_sum([lambda a=a: a.astype(F32) for a in up_parts], place.next_x)
    in_low = ring_sum([lambda a=a: a.astype(F32) for a in low_parts], place.next_y)
    in_up, in_low = (in_up + late).astype(BF), (in_low + late).astype(BF)
    order = ring_order(nz)

    def out_step(sent, t, mark):
        return (out_parts[order[t]].astype(F32) + place.next_z(sent).astype(F32) + mark).astype(BF)

    out_sum = out_step(out_parts[order[0]], 1, late)

    grad_normed_cross = dot(grad_cross_queries, cross_query, 1, 1)
    grad_part, grad_cross_gain, grad_cross_shift = norm_backward(first, cross_gain, grad_normed_cross)
    grad_first = grad_second + grad_part
    grad_first_branch = grad_first.astype(BF)
    grad_self_mix = dot(grad_first_branch, self_out, 1, 1).astype(BF)

    grad_pair = jnp.concatenate([grad_text_keys, grad_text_values], axis=1)
    grad_projected = dot(grad_pair, cross_kv, 1, 1).astype(BF)
    grad_text_bias = jnp.sum(grad_projected.astype(F32), axis=0)
    grad_text = dot(grad_projected, text_proj, 1, 1)
    padding = block - text_input.shape[1] // place.rows
    lefts = [cross_mix, normed_cross, projected, text_input, self_mix]
    rights = [
        grad_second_branch,
        grad_cross_queries,
        grad_text_keys,
        grad_text_values,
        grad_projected,
        grad_first_branch,
    ]
    result = second + result

    def backward_self(*before):
        return self_backward(
            row_lengths,
            queries,
            pair,
            pair_other,
            grad_self_mix,
            self_mix,
            self_lse,
            before=before,
        )[:5]

    def vector_list(grad_gain, grad_shift):
        return jnp.stack(
            [
                grad_gain,
                grad_shift,
                grad_cross_gain,
                grad_cross_shift,
                grad_text_bias,
                grad_feed_gain,
                grad_feed_shift,
                jnp.zeros_like(grad_feed_shift),
            ]
        )

    if kernels:
        send_up, send_low, keep_up, keep_low, result, middle_mark = middle_parts(
            place, count, lefts, rights, result, result_away, (in_up[0], in_low[0], out_sum)
        )
        up_got, low_got = place.next_x(send_up), place.next_y(send_low)
        in_up_got, in_low_got = place.next_y(in_up[0]), place.next_x(in_low[0])
        out_sum = out_step(out_sum, 2, middle_mark[0, 0])
        grads = backward_self(out_sum)
        for t in range(3, nz):
            out_sum = out_step(out_sum, t, 0.0)
        nothing = jnp.zeros_like(grad_feed_shift)
        sum_self_qkv, spread, sum_feed, vectors, grad_frames, grad_text = final_sums(
            place,
            count,
            normed_self,
            layer_raw,
            grad_first,
            self_gain[None],
            self_qkv,
            *grads,
            keep_up,
            up_got,
            keep_low,
            low_got,
            in_up[1],
            in_up_got,
            in_low[1],
            in_low_got,
            out_sum,
            vector_list(nothing, nothing),
            grad_text,
        )
        sum_self_out = spread[:, 5 * piece :]
    else:

        def packed_self(*before):
            grads = backward_self(*before)
            keys = (grads[1].astype(F32) + place.swap_core(grads[3]).astype(F32)).astype(BF)
            values = (grads[2].astype(F32) + place.swap_core(grads[4]).astype(F32)).astype(BF)
            return jnp.concatenate([grads[0], keys, values], axis=1)

        for t in range(2, nz):
            out_sum = out_step(out_sum, t, 0.0)
        text_blocks = text_input.reshape(text_total, place.rows, -1)
        text_padded = jnp.pad(text_blocks, ((0, 0), (0, 0), (0, padding))).reshape(text_total, width)
        lefts[3] = text_padded
        sum_feed, spread, sum_self_qkv, sum_self_out, grad_packed = permuted_sums(
            place, meta, in_up, in_low, out_sum, lefts, rights, normed_self, packed_self
        )
        result = (result + place.swap_core(result_away).astype(F32)).astype(BF)
        result = place.from_rows(result, count)
        grad_normed_self = dot(grad_packed, self_qkv, 1, 1)
        grad_part, grad_gain, grad_shift = norm_backward(layer_input, self_gain, grad_normed_self)
        grad_frames = place.from_rows((grad_first + grad_part).astype(BF), count)
        half = grad_text.shape[0] // 2
        text_away = place.swap_core(grad_text[half:].astype(BF))
        grad_text = (grad_text[:half] + text_away.astype(F32)).astype(BF)
        grad_text = place.from_rows(grad_text, count)
        vectors = place.vector_sum(vector_list(grad_gain, grad_shift))
    sum_cross_out, sum_cross_query = spread[:, :piece], spread[:, piece : 2 * piece]
    sum_cross_kv, sum_text_proj = spread[:, 2 * piece : 4 * piece], spread[:, 4 * piece : 5 * piece]
    sum_text_proj = sum_text_proj[: block - padding]
    vectors = pick(vectors.reshape(8, seq, width // seq), place.spot, 1)
    return (
        result,
        grad_frames.astype(F32),
        grad_text.astype(F32),
        vectors[0],
        vectors[1],
        sum_self_qkv,
        sum_self_out,
        vectors[2],
        vectors[3],
        sum_cross_query,
        sum_text_proj,
        vectors[4],
        sum_cross_kv,
        sum_cross_out,
        vectors[5],
        vectors[6],
        sum_feed[0],
        jnp.swapaxes(sum_feed[1], 0, 1),
    )


def solution(mesh):
    split, copied, table = P(ROWS, SEQ, None), P(), P(ROWS, None)
    vector, matrix = P(SEQ), P(ROWS, SEQ)
    return jax.shard_map(
        shards,
        mesh=mesh,
        in_specs=(split, split, table, table) + (copied,) * 15 + (split,),
        out_specs=(
            (split,) * 3
            + (vector, vector, matrix, matrix)
            + (vector, vector, matrix, matrix)
            + (vector, matrix, matrix)
            + (vector, vector, matrix, P(SEQ, ROWS))
        ),
        check_vma=False,
    )
```

```python
import functools
import math

import jax
import jax.numpy as jnp
from jax import lax
from jax.experimental import pallas as pl
from jax.experimental.pallas import tpu as pltpu
from jax.sharding import PartitionSpec as P

HD = 64
PAIR = 2 * HD
EPSILON = 1e-05
MASKED = -1e30
CLIPS = 4
ROWS = "rows"
SEQ = "seq"
BF = jnp.bfloat16
F32 = jnp.float32
VMEM_LIMIT = 48 * 1024 * 1024
MOST_VMEM = 62 * 1024 * 1024


def dot(left, right, left_dim=1, right_dim=0):
    return lax.dot_general(
        left, right, (((left_dim,), (right_dim,)), ((), ())), preferred_element_type=F32
    )


def pick(array, index, axis):
    return lax.dynamic_index_in_dim(array, index, axis, keepdims=False)


def after(value, *others):
    return lax.optimization_barrier((value,) + others)[0]


class Place:
    def __init__(self):
        self.rows, self.seq = lax.axis_size(ROWS), lax.axis_size(SEQ)
        self.nz = self.rows // 2
        self.nx = math.isqrt(self.seq)
        self.ny = self.seq // self.nx
        row, self.spot = lax.axis_index(ROWS), lax.axis_index(SEQ)
        self.core, self.z = row % 2, row // 2
        self.x, self.y = self.spot % self.nx, self.spot // self.nx
        self.owner = [0 if 4 * s // self.seq in (0, 3) else 1 for s in range(self.seq)]
        self.members = [[s for s in range(self.seq) if self.owner[s] == c] for c in (0, 1)]
        self.rank = [self.members[self.owner[s]].index(s) for s in range(self.seq)]

    def permute(self, value, target):
        pairs = []
        for z in range(self.nz):
            for c in range(2):
                for s in range(self.seq):
                    tz, tc, ts = target(z, c, s)
                    pairs.append(((2 * z + c) * self.seq + s, (2 * tz + tc) * self.seq + ts))
        return lax.ppermute(value, (ROWS, SEQ), pairs)

    def swap_core(self, value):
        return self.permute(value, lambda z, c, s: (z, 1 - c, s))

    def next_z(self, value):
        return self.permute(value, lambda z, c, s: ((z + 1) % self.nz, c, s))

    def next_x(self, value):
        nx = self.nx
        return self.permute(value, lambda z, c, s: (z, c, s // nx * nx + (s % nx + 1) % nx))

    def next_y(self, value):
        return self.permute(value, lambda z, c, s: (z, c, (s + self.nx) % self.seq))

    def to_rows(self, value):
        count = value.shape[0]
        my_rank = jnp.array(self.rank, jnp.int32)[self.spot]
        got = []
        for t in range(count):

            def target(z, c, s, t=t):
                return z, self.owner[s], c * count + (t + self.rank[s]) % count

            got.append(self.permute(pick(value, (t + my_rank) % count, 0), target))
        stacked = jnp.stack(got)
        here = self.spot % count
        return jnp.concatenate([pick(stacked, (here - k) % count, 0) for k in range(count)], axis=0)

    def from_rows(self, value, count):
        my_rank = jnp.array(self.rank, jnp.int32)[self.spot]
        slots = value.reshape(count, value.shape[0] // count, value.shape[1])
        here = self.spot % count
        got = []
        for t in range(count):

            def target(z, c, s, t=t):
                return z, s // count, self.members[c][(s % count - t) % count]

            got.append(self.permute(pick(slots, (here - t) % count, 0), target))
        stacked = jnp.stack(got)
        return jnp.stack([pick(stacked, (i - my_rank) % count, 0) for i in range(count)])

    def positions(self, total, core):
        quarter = total // 4
        inner = jnp.arange(quarter, dtype=jnp.int32)
        return jnp.concatenate([inner + core * quarter, inner + (3 - core) * quarter])

    def offset(self, i, j):
        return (self.y + 1 + i) % self.ny * self.nx + (self.x + 1 + j) % self.nx

    def relative_columns(self, value, outer_x):
        blocks = value.reshape(value.shape[0], self.seq, -1)
        if outer_x:
            order = [self.offset(i, j) for j in range(self.nx) for i in range(self.ny)]
        else:
            order = [self.offset(i, j) for i in range(self.ny) for j in range(self.nx)]
        return jnp.concatenate([pick(blocks, place, 1) for place in order], axis=1)


    def vector_sum(self, value):
        bit = 1
        while bit < self.rows:
            value = value + self.permute(
                value,
                lambda z, c, s: ((2 * z + c ^ bit) // 2, (2 * z + c ^ bit) % 2, s),
            )
            bit *= 2
        bit = 1
        while bit < self.seq:
            value = value + self.permute(value, lambda z, c, s: (z, c, s ^ bit))
            bit *= 2
        return value


def ring_order(count):
    return list(range(count - 2, -1, -1)) + [count - 1]


def ring_sum(pieces, send):
    order = ring_order(len(pieces))
    value = pieces[order[0]]()
    for k in order[1:]:
        value = pieces[k]() + send(value.astype(BF)).astype(F32)
    return value


def normalize(values):
    centered = values - jnp.mean(values, axis=-1, keepdims=True)
    scale = lax.rsqrt(jnp.mean(centered * centered, axis=-1, keepdims=True) + EPSILON)
    return centered * scale, scale


def layer_norm(values, gain, shift):
    return (normalize(values)[0] * gain + shift).astype(BF)


def norm_backward(values, gain, cotangent):
    normal, scale = normalize(values)
    grown = cotangent * gain
    inner = jnp.mean(grown, axis=-1, keepdims=True)
    along = jnp.mean(grown * normal, axis=-1, keepdims=True)
    grad = scale * (grown - inner - normal * along)
    return grad, jnp.sum(cotangent * normal, axis=0), jnp.sum(cotangent, axis=0)


def nt(left, right):
    return dot(left, right, 1, 1)


def head_lanes(values, head):
    lane = lax.broadcasted_iota(jnp.int32, values.shape, 1)
    return jnp.where((lane < HD) == (head == 0), values, jnp.zeros_like(values))


def turned(values):
    return jnp.swapaxes(values.astype(F32), 0, 1).astype(BF)


def running(lengths_ref, first):
    ends, total = [], 0
    for c in range(CLIPS):
        total = total + lengths_ref[first + c]
        ends.append(total)
    return ends


def spans(start, length, axis, ends):
    shape = (length, 1) if axis == 0 else (1, length)
    positions = lax.broadcasted_iota(jnp.int32, shape, axis) + start
    return sum((positions >= end).astype(jnp.int32) for end in ends)


def segment_bias(key_segment, query_segment, causal):
    allowed = key_segment == query_segment
    if causal:
        key = lax.broadcasted_iota(jnp.int32, allowed.shape, 0)
        query = lax.broadcasted_iota(jnp.int32, allowed.shape, 1)
        allowed = allowed & (key <= query)
    return jnp.where(allowed, 0.0, MASKED).astype(F32)


def forward_heads(queries, blocks, lse_ref, at):
    parts = []
    for head in range(2):
        query = head_lanes(queries, head)
        scores = [nt(keys, query) + bias() for keys, _, bias in blocks]
        highest = functools.reduce(
            jnp.maximum, [jnp.max(s, axis=0, keepdims=True) for s in scores]
        )
        weights = [jnp.exp(s - highest) for s in scores]
        total = sum(jnp.sum(w, axis=0, keepdims=True) for w in weights)
        mixed = sum(
            dot(values[head * HD : (head + 1) * HD], w.astype(BF))
            for (_, values, _), w in zip(blocks, weights)
        )
        parts.append(mixed * (1.0 / total))
        lse_ref[0, head : head + 1, at] = highest + jnp.log(total)
    return jnp.swapaxes(jnp.concatenate(parts, axis=0), 0, 1).astype(BF)


def backward_heads(queries, grads, mixed, blocks, lse_ref, at):
    product = jnp.swapaxes(grads.astype(F32) * mixed.astype(F32), 0, 1)
    parts = []
    for head in range(2):
        query, grad = head_lanes(queries, head), head_lanes(grads, head)
        rows = slice(head * HD, (head + 1) * HD)
        inner = jnp.sum(product[rows], axis=0, keepdims=True)
        totals = lse_ref[0, head : head + 1, at]
        grad_query = None
        for keys, turned_keys, values, bias, sums in blocks:
            weights = jnp.exp(nt(keys, query) + bias() - totals)
            scores = (weights * (nt(values, grad) - inner)).astype(BF)
            add_to(sums, 0, dot(scores, query))
            add_to(sums, 1, dot(weights.astype(BF), grad))
            term = dot(turned_keys[rows], scores)
            grad_query = term if grad_query is None else grad_query + term
        parts.append(grad_query)
    return (jnp.swapaxes(jnp.concatenate(parts, axis=0), 0, 1) * HD**-0.5).astype(BF)


def add_to(sums, index, term):
    sums[index] = term if sums[index] is None else sums[index] + term


def scaled(values):
    return values * jnp.array(HD**-0.5, BF)


def self_plan(core):
    if core == 0:
        return [(0, 0, 0)], [(0, 0, 1), (0, 1, 2), (1, 0, 3), (1, 1, 4)]
    return [(0, 0, 0), (1, 0, 4)], [(0, 0, 1), (0, 1, 2), (1, 0, 3)]


def self_biases(core, lengths_ref, bias_ref):
    length = bias_ref.shape[1]
    ends = running(lengths_ref, 0)
    quarters = (core, 3 - core)
    keys = [spans(q * length, length, 0, ends) for q in quarters]
    queries = [spans(q * length, length, 1, ends) for q in quarters]
    others = [spans(q * length, length, 0, ends) for q in (1 - core, 2 + core)]
    bias_ref[0] = segment_bias(keys[0], queries[0], True)
    bias_ref[1] = segment_bias(keys[0], queries[1], False)
    bias_ref[2] = segment_bias(keys[1], queries[1], True)
    bias_ref[3] = segment_bias(others[0], queries[1], False)
    last_key = jnp.where(core == 0, others[1], others[0])
    last_query = jnp.where(core == 0, queries[1], queries[0])
    bias_ref[4] = segment_bias(last_key, last_query, False)


def cross_bias(lengths_ref, bias_ref):
    core = lax.axis_index(ROWS) % 2
    count, rows = bias_ref.shape
    for n, token in enumerate((core, 3 - core, 1 - core, 2 + core)):
        keys = spans(token * (count // 4), count // 4, 0, running(lengths_ref, CLIPS))
        for m, frame in enumerate((core, 3 - core)):
            queries = spans(frame * (rows // 2), rows // 2, 1, running(lengths_ref, 0))
            at = slice(n * (count // 4), (n + 1) * (count // 4))
            bias_ref[at, m * (rows // 2) : (m + 1) * (rows // 2)] = segment_bias(keys, queries, False)


def self_forward_kernel(
    lengths_ref, q_ref, k_ref, v_ref, ko_ref, vo_ref, o_ref, lse_ref, bias_ref
):
    core = lax.axis_index(ROWS) % 2
    length = bias_ref.shape[1]

    @pl.when(pl.program_id(0) == 0)
    def _():
        self_biases(core, lengths_ref, bias_ref)

    keys, values = (k_ref, ko_ref), (v_ref, vo_ref)
    for which in range(2):

        @pl.when((core == 0) == (which == 0))
        def _(which=which):
            for half, plan in enumerate(self_plan(which)):
                at = slice(half * length, (half + 1) * length)
                blocks = []
                for source, part, number in plan:
                    where = slice(part * length, (part + 1) * length)
                    blocks.append(
                        (
                            keys[source][where],
                            turned(values[source][where]),
                            functools.partial(bias_ref.__getitem__, number),
                        )
                    )
                o_ref[at] = forward_heads(scaled(q_ref[at]), blocks, lse_ref, at)


def self_backward_kernel(
    lengths_ref,
    q_ref,
    k_ref,
    v_ref,
    ko_ref,
    vo_ref,
    g_ref,
    o_ref,
    lse_ref,
    dq_ref,
    dk_ref,
    dv_ref,
    dko_ref,
    dvo_ref,
    bias_ref,
):
    core = lax.axis_index(ROWS) % 2
    length = bias_ref.shape[1]

    @pl.when(pl.program_id(0) == 0)
    def _():
        self_biases(core, lengths_ref, bias_ref)

    keys, values = (k_ref, ko_ref), (v_ref, vo_ref)
    for which in range(2):

        @pl.when((core == 0) == (which == 0))
        def _(which=which):
            sums = {(s, p): [None, None] for s in range(2) for p in range(2)}
            for half, plan in enumerate(self_plan(which)):
                at = slice(half * length, (half + 1) * length)
                blocks = []
                for source, part, number in plan:
                    where = slice(part * length, (part + 1) * length)
                    blocks.append(
                        (
                            keys[source][where],
                            turned(keys[source][where]),
                            values[source][where],
                            functools.partial(bias_ref.__getitem__, number),
                            sums[source, part],
                        )
                    )
                dq_ref[at] = backward_heads(
                    scaled(q_ref[at]), g_ref[at], o_ref[at], blocks, lse_ref, at
                )
            for (source, part), pair in sums.items():
                where = slice(part * length, (part + 1) * length)
                for ref, value in zip(((dk_ref, dv_ref), (dko_ref, dvo_ref))[source], pair):
                    if value is None:
                        ref[where] = jnp.zeros((length, PAIR), BF)
                    else:
                        ref[where] = value.astype(BF)


def cross_forward_kernel(lengths_ref, q_ref, k_ref, v_ref, o_ref, lse_ref, bias_ref):
    length = q_ref.shape[0] // 2

    @pl.when(pl.program_id(0) == 0)
    def _():
        cross_bias(lengths_ref, bias_ref)

    turned_values = turned(v_ref[...])
    for half in range(2):
        at = slice(half * length, (half + 1) * length)
        blocks = [(k_ref[...], turned_values, lambda at=at: bias_ref[:, at])]
        o_ref[at] = forward_heads(scaled(q_ref[at]), blocks, lse_ref, at)


def cross_backward_kernel(
    lengths_ref,
    q_ref,
    k_ref,
    v_ref,
    g_ref,
    o_ref,
    lse_ref,
    dq_ref,
    dk_ref,
    dv_ref,
    bias_ref,
):
    length = q_ref.shape[0] // 2

    @pl.when(pl.program_id(0) == 0)
    def _():
        cross_bias(lengths_ref, bias_ref)

    turned_keys = turned(k_ref[...])
    sums = [None, None]
    for half in range(2):
        at = slice(half * length, (half + 1) * length)
        blocks = [(k_ref[...], turned_keys, v_ref[...], lambda at=at: bias_ref[:, at], sums)]
        dq_ref[at] = backward_heads(scaled(q_ref[at]), g_ref[at], o_ref[at], blocks, lse_ref, at)
    dk_ref[...] = sums[0].astype(BF)
    dv_ref[...] = sums[1].astype(BF)


def column(rows, first=0):
    return pl.BlockSpec((rows, PAIR), lambda i: (0, first + i))


SMEM_SPEC = pl.BlockSpec(memory_space=pltpu.SMEM)


def without(kernel, first, count):
    def run(*refs):
        kernel(*refs[:first], *refs[first + count :])

    return run


ANY_SPEC = pl.BlockSpec(memory_space=pl.ANY)
WHOLE_SPEC = pl.BlockSpec(memory_space=pltpu.VMEM)


MARK = jax.ShapeDtypeStruct((8, 128), F32)


def marked(kernel, at):
    def run(*refs):
        refs[at][...] = jnp.zeros((8, 128), F32)
        kernel(*refs[:at], *refs[at + 1 :])

    return run


def attention_call(
    kernel, heads, in_specs, outs, bias_shape, flops, arguments, before=(), limit=VMEM_LIMIT
):
    pairs = heads // 2
    kernel = marked(kernel, len(arguments) + len(outs))
    kernel = without(kernel, len(arguments), len(before))
    in_specs = list(in_specs) + [ANY_SPEC] * len(before)
    arguments = tuple(arguments) + tuple(before)
    out_shape, out_specs = [], []
    for rows in outs:
        if rows is None:
            queries = outs[0]
            out_shape.append(jax.ShapeDtypeStruct((pairs, 8, queries), F32))
            out_specs.append(pl.BlockSpec((1, 8, queries), lambda i: (i, 0, 0)))
        else:
            out_shape.append(jax.ShapeDtypeStruct((rows, pairs * PAIR), BF))
            out_specs.append(column(rows))
    out_shape.append(MARK)
    out_specs.append(pl.BlockSpec((8, 128), lambda i: (0, 0)))
    return pl.pallas_call(
        kernel,
        grid=(pairs,),
        in_specs=in_specs,
        out_specs=out_specs,
        out_shape=out_shape,
        scratch_shapes=[pltpu.VMEM(bias_shape, F32)],
        compiler_params=pltpu.CompilerParams(vmem_limit_bytes=limit),
        cost_estimate=pl.CostEstimate(flops=flops, bytes_accessed=8 << 20, transcendentals=flops >> 8),
    )(*arguments)


def lse_spec(queries):
    return pl.BlockSpec((1, 8, queries), lambda i: (i, 0, 0))


def self_forward(lengths, queries, pair, pair_other):
    rows, width = queries.shape
    heads = width // HD
    length = rows // 2
    half = heads // 2
    return attention_call(
        self_forward_kernel,
        heads,
        [
            SMEM_SPEC,
            column(rows),
            column(rows),
            column(rows, half),
            column(rows),
            column(rows, half),
        ],
        (rows, None),
        (5, length, length),
        heads * 5 * 4 * length * length * PAIR * 2,
        (lengths, queries, pair, pair, pair_other, pair_other),
    )


def self_backward(lengths, queries, pair, pair_other, grads, mixed, lse, before=()):
    rows, width = queries.shape
    heads = width // HD
    length = rows // 2
    half = heads // 2
    return attention_call(
        self_backward_kernel,
        heads,
        [
            SMEM_SPEC,
            column(rows),
            column(rows),
            column(rows, half),
            column(rows),
            column(rows, half),
            column(rows),
            column(rows),
            lse_spec(rows),
        ],
        (rows,) * 5,
        (5, length, length),
        heads * 5 * 10 * length * length * PAIR * 2,
        (lengths, queries, pair, pair, pair_other, pair_other, grads, mixed, lse),
        before,
        MOST_VMEM,
    )


def cross_forward(lengths, queries, pair):
    rows, width = queries.shape
    heads = width // HD
    count = pair.shape[0]
    return attention_call(
        cross_forward_kernel,
        heads,
        [SMEM_SPEC, column(rows), column(count), column(count, heads // 2)],
        (rows, None),
        (count, rows),
        heads * 4 * rows * count * PAIR * 2,
        (lengths, queries, pair, pair),
    )


def cross_backward(lengths, queries, pair, grads, mixed, lse, before=()):
    rows, width = queries.shape
    heads = width // HD
    count = pair.shape[0]
    return attention_call(
        cross_backward_kernel,
        heads,
        [
            SMEM_SPEC,
            column(rows),
            column(count),
            column(count, heads // 2),
            column(rows),
            column(rows),
            lse_spec(rows),
        ],
        (rows, count, count),
        (count, rows),
        heads * 10 * rows * count * PAIR * 2,
        (lengths, queries, pair, pair, grads, mixed, lse),
        before,
    )


def gelu_and_slope(values):
    inside = 0.5 * (1.0 + lax.erf(values * (0.5**0.5)))
    bell = jnp.exp(-0.5 * values * values) * ((2.0 * math.pi) ** -0.5)
    return values * inside, inside + values * bell


def feed_kernel(shape, meta_ref, own_ref, other_ref, gown_ref, gother_ref, win_ref, wout_ref, *refs):
    nx, ny, nz, chunk = shape
    res_out, res_other_out, grad_out, grad_other_out = refs[:4]
    up_refs, low_refs, gout_refs = refs[4 : 4 + nx], refs[4 + nx : 4 + nx + ny], refs[4 + nx + ny : 4 + nx + ny + nz]
    (act_ref, pre_ref, turned_ref, gturned_ref, res_acc, grad_acc) = refs[4 + nx + ny + nz : 10 + nx + ny + nz]
    res_ref, grad_ref, res_other_ref, grad_other_ref, store_sems = refs[10 + nx + ny + nz :]
    stores = [
        pltpu.make_async_copy(source, target, store_sems.at[number])
        for number, (source, target) in enumerate(
            (
                (res_ref, res_out),
                (res_other_ref, res_other_out),
                (grad_ref, grad_out),
                (grad_other_ref, grad_other_out),
            )
        )
    ]
    j, i = pl.program_id(0), pl.program_id(1)
    z = meta_ref[3]
    tokens = own_ref.shape[0]
    sources = ((own_ref, gown_ref, res_ref, grad_ref), (other_ref, gother_ref, res_acc, grad_acc))

    @pl.when((i == 0) & (j == 0))
    def _():
        for side, (values, grads, res, grad) in enumerate(sources):
            at = slice(side * tokens, (side + 1) * tokens)
            turned_ref[:, at] = turned(values[...])
            gturned_ref[:, at] = turned(grads[...])
            res[...] = jnp.zeros_like(res)
            grad[...] = jnp.zeros_like(grad)

    for side, (values, grads, res, grad) in enumerate(sources):
        for m in range(tokens // chunk):
            at = slice(m * chunk, (m + 1) * chunk)
            activated, slope = gelu_and_slope(dot(values[at], win_ref[...]))
            activated = activated.astype(BF)
            before = (nt(grads[at], wout_ref[...]) * slope).astype(BF)
            to = slice(side * tokens + m * chunk, side * tokens + (m + 1) * chunk)
            act_ref[to] = activated
            pre_ref[to] = before
            res[at] += dot(activated, wout_ref[...])
            grad[at] += nt(before, win_ref[...])

    @pl.when((i == ny - 1) & (j == nx - 1))
    def _():
        res_other_ref[...] = res_acc[...].astype(BF)
        grad_other_ref[...] = grad_acc[...].astype(BF)
        for copy in stores:
            copy.start()

    rows = turned_ref.shape[0] // nz
    half = rows // 2
    for k in range(nz):
        source = pl.ds(pl.multiple_of((z + 1 + k) % nz * rows, rows), rows)
        gin = dot(turned_ref[source], pre_ref[...]).astype(BF)
        gout_refs[k][0] = dot(gturned_ref[source], act_ref[...]).astype(BF)
        to = slice(k * half, (k + 1) * half)
        for number, ref in enumerate(up_refs):

            @pl.when(j == number)
            def _(ref=ref):
                ref[0, to] = gin[:half]

        for number, ref in enumerate(low_refs):

            @pl.when(i == number)
            def _(ref=ref):
                ref[0, to] = gin[half:]

    @pl.when((i == ny - 1) & (j == nx - 1))
    def _():
        for copy in stores:
            copy.wait()


def feed(place, meta, own, other, gown, gother, feed_in, feed_out):
    nx, ny, nz = place.nx, place.ny, place.nz
    tokens, width = own.shape
    part = feed_in.shape[1] // place.seq // 2
    chunk = min(256, tokens)

    def unit(j, i, meta):
        return 2 * ((meta[2] + 1 + i) % ny * nx + (meta[1] + 1 + j) % nx) + meta[0]

    def up_spec(number):
        def index(j, i, meta):
            return jnp.where(j == number, i, jnp.where(j < number, 0, ny - 1)), 0, 0

        return pl.BlockSpec((1, width // 2, part), index)

    low_spec = pl.BlockSpec((1, width // 2, part), lambda j, i, meta: (j, 0, 0))
    gout_spec = pl.BlockSpec((1, width // nz, part), lambda j, i, meta: (j * ny + i, 0, 0))
    total = 2 * tokens
    shape = jax.ShapeDtypeStruct
    return pl.pallas_call(
        functools.partial(feed_kernel, (nx, ny, nz, chunk)),
        grid_spec=pltpu.PrefetchScalarGridSpec(
            num_scalar_prefetch=1,
            grid=(nx, ny),
            in_specs=[WHOLE_SPEC] * 4
            + [
                pl.BlockSpec((width, part), lambda j, i, meta: (0, unit(j, i, meta))),
                pl.BlockSpec((part, width), lambda j, i, meta: (unit(j, i, meta), 0)),
            ],
            out_specs=[ANY_SPEC] * 4
            + [up_spec(n) for n in range(nx)]
            + [low_spec] * ny
            + [gout_spec] * nz,
            scratch_shapes=[
                pltpu.VMEM((total, part), BF),
                pltpu.VMEM((total, part), BF),
                pltpu.VMEM((width, total), BF),
                pltpu.VMEM((width, total), BF),
                pltpu.VMEM((tokens, width), F32),
                pltpu.VMEM((tokens, width), F32),
                pltpu.VMEM((tokens, width), F32),
                pltpu.VMEM((tokens, width), F32),
                pltpu.VMEM((tokens, width), BF),
                pltpu.VMEM((tokens, width), BF),
                pltpu.SemaphoreType.DMA((4,)),
            ],
        ),
        out_shape=[
            shape((tokens, width), F32),
            shape((tokens, width), BF),
            shape((tokens, width), F32),
            shape((tokens, width), BF),
        ]
        + [shape((ny, width // 2, part), BF)] * nx
        + [shape((nx, width // 2, part), BF)] * ny
        + [shape((place.seq, width // nz, part), BF)] * nz,
        compiler_params=pltpu.CompilerParams(vmem_limit_bytes=60 * 1024 * 1024),
        cost_estimate=pl.CostEstimate(
            flops=12 * total * width * part * place.seq,
            bytes_accessed=40 << 20,
            transcendentals=2 * total * part * place.seq,
        ),
    )(meta, own, other, gown, gother, feed_in, feed_out)


def weight_kernel(shape, meta_ref, *refs):
    count, nz = shape
    lefts, rights = refs[:count], refs[count : 2 * count]
    own_ref, other_ref, turned_ref = refs[2 * count :]
    core, z = meta_ref[0], meta_ref[3]
    block = own_ref.shape[1] // nz
    for number in range(count):

        @pl.when(pl.program_id(0) == number)
        def _(left=lefts[number], right=rights[number]):
            tokens = left.shape[0]
            turned_ref[:, :tokens] = turned(left[...])
            for k in range(nz):
                start = (z + 1 + k) % nz * 2
                to = slice(k * block, (k + 1) * block)
                for which, ref in ((core, own_ref), (1 - core, other_ref)):
                    at = pl.ds(pl.multiple_of((start + which) * block, block), block)
                    ref[0, to] = dot(turned_ref[at, :tokens], right[...]).astype(BF)


def weight_parts(place, meta, lefts, rights, before=()):
    count = len(lefts)
    depth, width = lefts[0].shape[1], rights[0].shape[1]
    tokens = max(left.shape[0] for left in lefts)
    out = jax.ShapeDtypeStruct((count, depth // 2, width), BF)
    spec = pl.BlockSpec((1, depth // 2, width), lambda u: (u, 0, 0))
    return pl.pallas_call(
        without(functools.partial(weight_kernel, (count, place.nz)), 1 + 2 * count, len(before)),
        grid=(count,),
        in_specs=[SMEM_SPEC] + [WHOLE_SPEC] * (2 * count) + [ANY_SPEC] * len(before),
        out_specs=[spec, spec],
        out_shape=[out, out],
        scratch_shapes=[pltpu.VMEM((depth, tokens), BF)],
        compiler_params=pltpu.CompilerParams(vmem_limit_bytes=VMEM_LIMIT),
        cost_estimate=pl.CostEstimate(
            flops=2 * count * tokens * depth * width,
            bytes_accessed=count * depth * width * 4,
            transcendentals=0,
        ),
    )(meta, *lefts, *rights, *before)


MESH = pl.DeviceIdType.MESH


class Mail:
    def __init__(self, send_sems, recv_sems):
        self.send_sems, self.recv_sems, self.sent = send_sems, recv_sems, []

    def send(self, source, target, device):
        number = len(self.sent)
        copy = pltpu.make_async_remote_copy(
            src_ref=source,
            dst_ref=target,
            send_sem=self.send_sems.at[number],
            recv_sem=self.recv_sems.at[number],
            device_id=device,
            device_id_type=MESH,
        )
        copy.start()
        self.sent.append(copy)
        return copy

    def finish(self):
        for copy in self.sent:
            copy.wait_send()


class Ways:
    def __init__(self, nz):
        self.row, self.spot = lax.axis_index(ROWS), lax.axis_index(SEQ)
        self.core, self.z = self.row % 2, self.row // 2
        self.x, self.y = self.spot % 2, self.spot // 2
        self.nz = nz
        self.sibling = (self.row + 1 - 2 * self.core, self.spot)
        self.across_x = (self.row, self.spot + 1 - 2 * self.x)
        self.across_y = (self.row, self.y * -2 + 2 + self.x)
        self.above = ((self.row + 2) % (2 * nz), self.spot)
        self.below = ((self.row + 2 * nz - 2) % (2 * nz), self.spot)

    def plane(self):
        devices = []
        for other in range(2):
            row = self.row if other == 0 else self.sibling[0]
            devices += [(row, (self.spot + s) % 4) for s in range(4) if other or s]
        return devices

    def meet(self, devices):
        barrier = pltpu.get_barrier_semaphore()
        for device in devices:
            pl.semaphore_signal(barrier, inc=1, device_id=device, device_id_type=MESH)
        pl.semaphore_wait(barrier, len(devices))

    def place(self, q):
        return (self.y + 1 + q % 2) % 2 * 2 + (self.x + 1 + q // 2) % 2

    def rows(self, k, which, block):
        start = ((self.z + 1 + k) % self.nz * 2 + which) * block
        return pl.ds(pl.multiple_of(start, block), block)


class Home:
    def __init__(self, ways, out_ref, send_sems, recv_sems):
        self.ways, self.out_ref = ways, out_ref
        self.send_sems, self.recv_sems = send_sems, recv_sems
        self.started = []

    def send(self, source, slot):
        ways = self.ways
        spot = jnp.where(ways.core == 0, 3 * slot, 1 + slot)
        row = 2 * ways.z + ways.spot // 2
        stays = (spot == ways.spot) & (row == ways.row)
        to = self.out_ref.at[ways.spot % 2]
        copy = pltpu.make_async_remote_copy(
            src_ref=source,
            dst_ref=to,
            send_sem=self.send_sems.at[slot],
            recv_sem=self.recv_sems.at[ways.spot % 2],
            device_id=(row, spot),
            device_id_type=MESH,
        )
        local = pltpu.make_async_copy(source, to, self.recv_sems.at[ways.spot % 2])

        @pl.when(stays)
        def _():
            local.start()

        @pl.when(jnp.logical_not(stays))
        def _():
            copy.start()

        self.started.append((stays, copy))

    def finish(self):
        for r in range(2):
            to = self.out_ref.at[r]
            pltpu.make_async_copy(to, to, self.recv_sems.at[r]).wait()
        for stays, copy in self.started:

            @pl.when(jnp.logical_not(stays))
            def _(copy=copy):
                copy.wait_send()


class Gathering:
    def __init__(self, ways, source_ref, target_ref, send_sems, recv_sems):
        self.ways, self.source_ref, self.target_ref = ways, source_ref, target_ref
        self.send_sems, self.recv_sems = send_sems, recv_sems
        self.block = source_ref.shape[1]
        self.copies = []
        owner = jnp.where((ways.spot == 0) | (ways.spot == 3), 0, 1)
        slot = ways.spot // 2
        to = target_ref.at[pl.ds(pl.multiple_of(slot * self.block, self.block), self.block)]
        for r in range(2):
            row, spot = 2 * ways.z + owner, 2 * ways.core + r
            stays = (spot == ways.spot) & (row == ways.row)
            copy = pltpu.make_async_remote_copy(
                src_ref=source_ref.at[r],
                dst_ref=to,
                send_sem=send_sems.at[r],
                recv_sem=recv_sems.at[slot],
                device_id=(row, spot),
                device_id_type=MESH,
            )
            local = pltpu.make_async_copy(source_ref.at[r], to, recv_sems.at[slot])
            self.copies.append((stays, copy, local))

    def start(self):
        for stays, copy, local in self.copies:

            @pl.when(stays)
            def _(local=local):
                local.start()

            @pl.when(jnp.logical_not(stays))
            def _(copy=copy):
                copy.start()

    def arrived(self, slot):
        to = self.target_ref.at[slot * self.block : (slot + 1) * self.block]
        pltpu.make_async_copy(to, to, self.recv_sems.at[slot]).wait()

    def finish(self):
        for stays, copy, _ in self.copies:

            @pl.when(jnp.logical_not(stays))
            def _(copy=copy):
                copy.wait_send()


def self_forward_carrying(nz, lengths_ref, *refs):
    grads_ref, cotangent_ref = refs[5], refs[8]
    bias_ref, sends, recvs = refs[9:]
    gathering = Gathering(Ways(nz), grads_ref, cotangent_ref, sends, recvs)

    @pl.when(pl.program_id(0) == 0)
    def _():
        gathering.ways.meet(gathering.ways.plane())
        gathering.start()

    self_forward_kernel(lengths_ref, *refs[:5], *refs[6:8], bias_ref)

    @pl.when(pl.program_id(0) == pl.num_programs(0) - 1)
    def _():
        for slot in range(2):
            gathering.arrived(slot)
        gathering.finish()


def self_forward_and_gather(place, lengths, queries, pair, pair_other, grads):
    rows, width = queries.shape
    half = width // HD // 2
    length = rows // 2
    return pl.pallas_call(
        functools.partial(self_forward_carrying, place.nz),
        grid=(half,),
        in_specs=[
            SMEM_SPEC,
            column(rows),
            column(rows),
            column(rows, half),
            column(rows),
            column(rows, half),
            ANY_SPEC,
        ],
        out_specs=[column(rows), lse_spec(rows), ANY_SPEC],
        out_shape=[
            jax.ShapeDtypeStruct((rows, width), BF),
            jax.ShapeDtypeStruct((half, 8, rows), F32),
            jax.ShapeDtypeStruct((rows, width), BF),
        ],
        scratch_shapes=[pltpu.VMEM((5, length, length), F32)]
        + [pltpu.SemaphoreType.DMA((2,))] * 2,
        compiler_params=pltpu.CompilerParams(
            collective_id=4, has_side_effects=True, vmem_limit_bytes=VMEM_LIMIT
        ),
        cost_estimate=pl.CostEstimate(
            flops=40 * rows * length * width, bytes_accessed=8 << 20, transcendentals=0
        ),
    )(lengths, queries, pair, pair, pair_other, pair_other, grads)


def entry_kernel(
    nz,
    frames_ref,
    text_ref,
    lengths_ref,
    gain_ref,
    shift_ref,
    qkv_ref,
    proj_ref,
    bias_ref,
    kv_ref,
    input_out,
    normed_out,
    queries_out,
    pair_out,
    pair_other_ref,
    words_out,
    projected_out,
    text_pair_out,
    lengths_other_ref,
    input_ref,
    normed_ref,
    queries_ref,
    pair_ref,
    words_ref,
    projected_ref,
    text_pair_ref,
    store_sems,
    qkv_here,
    proj_here,
    kv_here,
    load_sems,
    send_sems,
    recv_sems,
    gather_sends,
    gather_recvs,
):
    loads = [
        pltpu.make_async_copy(source, target, load_sems.at[number])
        for number, (source, target) in enumerate(
            ((proj_ref, proj_here), (kv_ref, kv_here), (qkv_ref, qkv_here))
        )
    ]
    for load in loads:
        load.start()
    stores = []

    def store(source, target):
        copy = pltpu.make_async_copy(source, target, store_sems.at[len(stores)])
        copy.start()
        stores.append(copy)

    ways = Ways(nz)
    ways.meet(ways.plane())
    mail = Mail(send_sems, recv_sems)
    words = Gathering(ways, text_ref, words_ref, gather_sends.at[0], gather_recvs.at[0])
    frames = Gathering(ways, frames_ref, input_ref, gather_sends.at[1], gather_recvs.at[1])
    words.start()
    frames.start()
    lengths_copy = mail.send(lengths_ref, lengths_other_ref, ways.sibling)
    half = words_ref.shape[0] // 2
    for slot in range(2):
        words.arrived(slot)
    words_copy = mail.send(words_ref.at[:half], words_ref.at[half:], ways.sibling)
    loads[0].wait()
    loads[1].wait()
    words_copy.wait_recv()
    store(words_ref, words_out)
    projected = (dot(words_ref[...], proj_here[...]) + bias_ref[...]).astype(BF)
    projected_ref[...] = projected
    store(projected_ref, projected_out)
    text_pair_ref[...] = dot(projected, kv_here[...]).astype(BF)
    store(text_pair_ref, text_pair_out)
    loads[2].wait()
    width = input_ref.shape[1]
    block = input_ref.shape[0] // 2
    copies = []
    for slot in range(2):
        frames.arrived(slot)
        at = slice(slot * block, (slot + 1) * block)
        normed_ref[at] = layer_norm(input_ref[at].astype(F32), gain_ref[...], shift_ref[...])
        store(input_ref.at[at], input_out.at[at])
        store(normed_ref.at[at], normed_out.at[at])
        pair_ref[at] = dot(normed_ref[at], qkv_here[:, width:]).astype(BF)
        store(pair_ref.at[at], pair_out.at[at])
        copies.append(mail.send(pair_ref.at[at], pair_other_ref.at[at], ways.sibling))
    queries_ref[...] = dot(normed_ref[...], qkv_here[:, :width]).astype(BF)
    store(queries_ref, queries_out)
    lengths_copy.wait_recv()
    for copy in copies:
        copy.wait_recv()
    mail.finish()
    for gathering in (words, frames):
        gathering.finish()
    for copy in stores:
        copy.wait()


def entry(place, frames, text, lengths, gain, shift, qkv, proj, bias, kv):
    count, block, width = frames.shape
    tokens, words = count * block, 2 * count * text.shape[1]
    shape, vmem = jax.ShapeDtypeStruct, pltpu.VMEM
    return pl.pallas_call(
        functools.partial(entry_kernel, place.nz),
        in_specs=[ANY_SPEC] * 2 + [WHOLE_SPEC] * 3 + [ANY_SPEC] * 2 + [WHOLE_SPEC, ANY_SPEC],
        out_specs=[ANY_SPEC] * 8 + [WHOLE_SPEC],
        out_shape=[
            shape((tokens, width), BF),
            shape((tokens, width), BF),
            shape((tokens, width), BF),
            shape((tokens, 2 * width), BF),
            shape((tokens, 2 * width), BF),
            shape((words, text.shape[2]), BF),
            shape((words, width), BF),
            shape((words, 2 * width), BF),
            shape(lengths.shape, jnp.int32),
        ],
        scratch_shapes=[
            vmem((tokens, width), BF),
            vmem((tokens, width), BF),
            vmem((tokens, width), BF),
            vmem((tokens, 2 * width), BF),
            vmem((words, text.shape[2]), BF),
            vmem((words, width), BF),
            vmem((words, 2 * width), BF),
            pltpu.SemaphoreType.DMA((10,)),
            vmem(qkv.shape, BF),
            vmem(proj.shape, BF),
            vmem(kv.shape, BF),
            pltpu.SemaphoreType.DMA((3,)),
            pltpu.SemaphoreType.DMA((4,)),
            pltpu.SemaphoreType.DMA((4,)),
            pltpu.SemaphoreType.DMA((2, 2)),
            pltpu.SemaphoreType.DMA((2, 2)),
        ],
        compiler_params=pltpu.CompilerParams(
            collective_id=3, has_side_effects=True, vmem_limit_bytes=MOST_VMEM
        ),
        cost_estimate=pl.CostEstimate(
            flops=20 * tokens * width * width, bytes_accessed=20 << 20, transcendentals=0
        ),
    )(frames, text, lengths, gain[None], shift[None], qkv, proj, bias[None], kv)


def with_loads(kernel, count, late):
    def run(*refs):
        inputs, rest = list(refs[:count]), refs[count:]
        here, sems = rest[-len(late) - 1 : -1], rest[-1]
        copies = []
        for number, which in enumerate(late):
            copy = pltpu.make_async_copy(inputs[which], here[number], sems.at[number])
            copy.start()
            inputs[which] = here[number]
            copies.append(copy)
        open_copies = dict(zip(map(id, here), copies))

        def wait(*wanted):
            for ref in wanted:
                open_copies.pop(id(ref)).wait()

        kernel(wait, *inputs, *rest[: -len(late) - 1])

    return run


def load_scratch(operands, late):
    return [pltpu.VMEM(operands[n].shape, operands[n].dtype) for n in late] + [
        pltpu.SemaphoreType.DMA((len(late),))
    ]


def middle_kernel(
    shape,
    wait,
    mixed_ref,
    normed_ref,
    projected_ref,
    text_ref,
    self_ref,
    g_second_ref,
    g_query_ref,
    g_keys_ref,
    g_values_ref,
    g_projected_ref,
    g_first_ref,
    result_ref,
    result_away_ref,
    in_up_ref,
    in_up_got_ref,
    in_low_ref,
    in_low_got_ref,
    out_one_ref,
    out_one_got_ref,
    out_zero_ref,
    self_weight_ref,
    send_up_ref,
    send_low_ref,
    keep_up_ref,
    keep_low_ref,
    result_out,
    in_up_keep,
    in_up_next,
    in_low_keep,
    in_low_next,
    out_next,
    g_mix_ref,
    mixed_t,
    normed_t,
    projected_t,
    text_t,
    self_t,
    own_ref,
    away_ref,
    got_ref,
    result_got_ref,
    in_send_ref,
    out_send_ref,
    out_came_ref,
    send_sems,
    recv_sems,
    home_sends,
    home_recvs,
):
    nz, piece = shape
    ways = Ways(nz)
    ways.meet(ways.plane() + [ways.above, ways.below])
    mail = Mail(send_sems, recv_sems)
    result_copy = mail.send(result_away_ref, result_got_ref, ways.sibling)
    wait(out_one_ref, out_one_got_ref)
    out_send_ref[...] = out_one_ref[...] + out_one_got_ref[...]
    out_copy = mail.send(out_send_ref, out_came_ref, ways.above)
    wait(in_up_ref, in_up_got_ref, in_low_ref, in_low_got_ref)
    in_send_ref[0] = in_up_ref[0] + in_up_got_ref[0]
    in_send_ref[1] = in_low_ref[0] + in_low_got_ref[0]
    in_copies = [
        mail.send(in_send_ref.at[0], in_up_next, ways.across_y),
        mail.send(in_send_ref.at[1], in_low_next, ways.across_x),
    ]
    in_up_keep[...] = in_up_ref[1] + in_up_got_ref[1]
    in_low_keep[...] = in_low_ref[1] + in_low_got_ref[1]
    home = Home(ways, result_out, home_sends, home_recvs)
    for left, to in ((mixed_ref, mixed_t), (normed_ref, normed_t), (projected_ref, projected_t), (self_ref, self_t)):
        wait(left)
        to[...] = turned(left[...])
    wait(text_ref)
    turned_text = turned(text_ref[...])
    block = own_ref.shape[2]
    count = 2 * nz
    part = turned_text.shape[0] // count
    text_t[...] = jnp.zeros_like(text_t)
    for b in range(count):
        text_t[b * block : b * block + part] = turned_text[b * part : (b + 1) * part]
    half = block // 2
    up, low = slice(0, half), slice(half, block)
    homes = (
        (send_up_ref.at[0], send_low_ref.at[0]),
        (send_up_ref.at[1], keep_low_ref.at[0]),
        (keep_up_ref.at[0], send_low_ref.at[1]),
        (keep_up_ref.at[1], keep_low_ref.at[1]),
    )
    copies = []
    wait(g_second_ref, g_query_ref, g_keys_ref, g_values_ref, g_projected_ref, g_first_ref)

    def settle(q):
        copies[q].wait_recv()
        total = own_ref[q] + got_ref[q]
        homes[q][0][...] = total[:, up]
        homes[q][1][...] = total[:, low]

    for q in range(4):
        place = ways.place(q)
        columns = pl.ds(pl.multiple_of(place * piece, piece), piece)
        twice = pl.ds(pl.multiple_of(place % 2 * 2 * piece, piece), 2 * piece)
        pair = jnp.where(place < 2, g_keys_ref[:, twice], g_values_ref[:, twice])
        units = (
            (mixed_t, g_second_ref[:, columns]),
            (normed_t, g_query_ref[:, columns]),
            (projected_t, pair),
            (text_t, g_projected_ref[:, columns]),
            (self_t, g_first_ref[:, columns]),
        )
        for which, ref in ((1 - ways.core, away_ref), (ways.core, own_ref)):
            first = 0
            for left, right in units:
                to = slice(first, first + right.shape[1])
                first += right.shape[1]
                for k in range(nz):
                    ref[q, k, :, to] = dot(left[ways.rows(k, which, block)], right).astype(BF)
            if ref is away_ref:
                copies.append(mail.send(away_ref.at[q], got_ref.at[q], ways.sibling))
        if q == 0:
            wait(result_ref)
            result_copy.wait_recv()
            result_got_ref[...] = (result_ref[...] + result_got_ref[...].astype(F32)).astype(BF)
            slots = result_ref.shape[0] // 2
            for slot in range(2):
                home.send(result_got_ref.at[slot * slots : (slot + 1) * slots], slot)
        else:
            settle(q - 1)
    wait(self_weight_ref)
    g_mix_ref[...] = nt(g_first_ref[...], self_weight_ref[...]).astype(BF)
    settle(3)
    for copy in in_copies:
        copy.wait_recv()
    out_copy.wait_recv()
    wait(out_zero_ref)
    out_next[...] = out_zero_ref[...] + out_came_ref[...]
    mail.finish()
    home.finish()


def middle_parts(place, count, lefts, rights, result, result_away, feeds, weight):
    nz = place.nz
    depth, width = lefts[0].shape[1], rights[0].shape[1]
    piece, block = width // place.seq, depth // place.rows
    columns = piece * len(rights)
    out = jax.ShapeDtypeStruct((2, nz, block // 2, columns), BF)
    big = pltpu.VMEM((4, nz, block, columns), BF)
    operands = [*lefts, *rights, result, result_away, *feeds, weight]
    late = (17, 18, 13, 14, 15, 16, 0, 1, 2, 4, 3, 5, 6, 7, 8, 9, 10, 11, 20, 19)
    return pl.pallas_call(
        with_loads(functools.partial(middle_kernel, (nz, piece)), len(operands), late),
        in_specs=[ANY_SPEC] * len(operands),
        out_specs=[WHOLE_SPEC] * 4
        + [ANY_SPEC, WHOLE_SPEC, ANY_SPEC, WHOLE_SPEC, ANY_SPEC, WHOLE_SPEC, WHOLE_SPEC],
        out_shape=[out] * 4
        + [jax.ShapeDtypeStruct((count, result.shape[0] // count, width), BF)]
        + [jax.ShapeDtypeStruct(feeds[0].shape[1:], BF)] * 4
        + [jax.ShapeDtypeStruct(feeds[4].shape, BF), jax.ShapeDtypeStruct(result.shape, BF)],
        scratch_shapes=[pltpu.VMEM((depth, left.shape[0]), BF) for left in lefts]
        + [big] * 3
        + [pltpu.VMEM(result.shape, BF), pltpu.VMEM(feeds[0].shape, BF)]
        + [pltpu.VMEM(feeds[4].shape, BF)] * 2
        + [pltpu.SemaphoreType.DMA((8,))] * 2
        + [pltpu.SemaphoreType.DMA((2,))] * 2
        + load_scratch(operands, late),
        compiler_params=pltpu.CompilerParams(
            collective_id=2, has_side_effects=True, vmem_limit_bytes=63 * 1024 * 1024
        ),
        cost_estimate=pl.CostEstimate(
            flops=2 * 8 * 512 * depth * width, bytes_accessed=24 << 20, transcendentals=0
        ),
    )(*operands)


def final_kernel(nz, wait, *refs):
    (
        normed_ref,
        input_ref,
        first_ref,
        gain_ref,
        weight_ref,
        gq_ref,
        gk_ref,
        gv_ref,
        k_away_ref,
        v_away_ref,
        upper_ref,
        upper_got_ref,
        lower_ref,
        lower_got_ref,
        in_up_ref,
        in_up_got_ref,
        in_low_ref,
        in_low_got_ref,
        out_last_ref,
        out_got_ref,
        vector_ref,
        projected_ref,
        proj_ref,
    ) = refs[:23]
    (qkv_ref, middle_ref, feed_ref, sum_ref, frames_out, text_out) = refs[23:29]
    (
        out_ref,
        text_ref,
        packed_ref,
        k_got_ref,
        v_got_ref,
        acc_ref,
        turned_ref,
        own_ref,
        away_ref,
        got_ref,
        first_x_ref,
        first_y_ref,
        second_y_ref,
        second_x_ref,
        mid_up_ref,
        mid_low_ref,
        mid_ref,
        mid_ring_ref,
        qkv_ring_ref,
        feed_send_ref,
        feed_ring_ref,
        out_x_ref,
        out_own_ref,
        out_y_ref,
        feed_away_ref,
        feed_other_ref,
        vector_out_ref,
        vector_in_ref,
        text_away_ref,
        text_got_ref,
        send_sems,
        recv_sems,
        home_sends,
        home_recvs,
    ) = refs[29:]
    ways = Ways(nz)
    core, z = ways.core, ways.z
    sibling, across_x, across_y, above = ways.sibling, ways.across_x, ways.across_y, ways.above
    ways.meet(ways.plane() + [ways.above, ways.below])
    mail = Mail(send_sems, recv_sems)
    ring = ring_order(nz)
    half = upper_ref.shape[2]
    feed_half = feed_ring_ref.shape[1] // 2
    tokens, width = normed_ref.shape

    k_copy = mail.send(k_away_ref, k_got_ref, sibling)
    v_copy = mail.send(v_away_ref, v_got_ref, sibling)

    wait(out_last_ref, out_got_ref)
    out_ref[...] = out_last_ref[...] + out_got_ref[...]
    out_copies = [mail.send(out_ref.at[q], out_x_ref.at[q], across_x) for q in range(2)]
    feed_copies, feed_last_copies = [], {}

    def feed_piece(t):
        at = slice(ring[t] * feed_half, (ring[t] + 1) * feed_half)
        return (
            in_up_ref[at].astype(F32) + in_up_got_ref[at].astype(F32),
            in_low_ref[at].astype(F32) + in_low_got_ref[at].astype(F32),
        )

    def feed_step(t):
        upper_part, lower_part = feed_piece(t)
        if t > 0:
            feed_copies[t - 1].wait_recv()
            upper_part += feed_ring_ref[t - 1, :feed_half].astype(F32)
            lower_part += feed_ring_ref[t - 1, feed_half:].astype(F32)
        if t == nz - 1:
            feed_finish(0, upper_part, lower_part)
            return
        feed_send_ref[t, :feed_half] = upper_part.astype(BF)
        feed_send_ref[t, feed_half:] = lower_part.astype(BF)
        feed_copies.append(mail.send(feed_send_ref.at[t], feed_ring_ref.at[t], above))

    wait(in_up_ref, in_up_got_ref, in_low_ref, in_low_got_ref)
    feed_step(0)

    mid_copies = {}
    wait(upper_ref, upper_got_ref, lower_ref, lower_got_ref)
    for k in ring:
        mid_ref[k, :half] = upper_ref[0, k] + upper_got_ref[0, k]
        mid_ref[k, half:] = lower_ref[0, k] + lower_got_ref[0, k]
        mid_copies[k] = (
            mail.send(mid_ref.at[k, :half], mid_up_ref.at[k], across_y),
            mail.send(mid_ref.at[k, half:], mid_low_ref.at[k], across_x),
        )
    wait(normed_ref, gq_ref, gk_ref, gv_ref)
    turned_ref[...] = turned(normed_ref[...])
    packed_ref[:, :width] = gq_ref[...]
    k_copy.wait_recv()
    packed_ref[:, width : 2 * width] = gk_ref[...] + k_got_ref[...]
    v_copy.wait_recv()
    packed_ref[:, 2 * width :] = gv_ref[...] + v_got_ref[...]

    block = own_ref.shape[2]
    columns = own_ref.shape[3]
    core_copies = []
    for q in range(4):
        right = packed_ref[:, pl.ds(pl.multiple_of(ways.place(q) * columns, columns), columns)]
        for which, ref in ((1 - core, away_ref), (core, own_ref)):
            for k in range(nz):
                ref[q, k] = dot(turned_ref[ways.rows(k, which, block)], right).astype(BF)
            if ref is away_ref:
                core_copies.append(mail.send(away_ref.at[q], got_ref.at[q], sibling))

    def out_step():
        for q in range(2):
            out_copies[q].wait_recv()
            out_own_ref[q] = out_ref[2 + q] + out_x_ref[q]
            if q == 0:
                out_copies.append(mail.send(out_own_ref.at[0], out_y_ref, across_y))

    def out_last():
        out_copies[2].wait_recv()
        total = out_own_ref[1].astype(F32) + out_y_ref[...].astype(F32)
        feed_finish(1, total[:feed_half], total[feed_half:])

    def feed_finish(kind, even, odd):
        away = jnp.where(core == 0, odd, even)
        own = jnp.where(core == 0, even, odd)
        across = own.shape[1]
        feed_away_ref[kind] = away
        feed_last_copies[kind] = mail.send(feed_away_ref.at[kind], feed_other_ref.at[kind], sibling)
        at = pl.ds(pl.multiple_of(core * across, across), across)
        feed_ref[kind, :, at] = own

    def feed_last(kind):
        feed_last_copies[kind].wait_recv()
        across = feed_other_ref.shape[2]
        at = pl.ds(pl.multiple_of((1 - core) * across, across), across)
        feed_ref[kind, :, at] = feed_other_ref[kind]

    wait(projected_ref, proj_ref)
    text_ref[...] = nt(projected_ref[...], proj_ref[...])
    text_rows = text_ref.shape[0] // 2
    text_away_ref[...] = text_ref[text_rows:].astype(BF)
    text_copy = mail.send(text_away_ref, text_got_ref, sibling)

    def core_step(q):
        core_copies[q].wait_recv()
        own_ref[q] = own_ref[q] + got_ref[q]

    mid_ring = {}

    def mid_send(t):
        k = ring[t]
        up, low = mid_copies[k]
        up.wait()
        low.wait()
        mid_ref[k, :half] = upper_ref[1, k] + upper_got_ref[1, k] + mid_up_ref[k]
        mid_ref[k, half:] = lower_ref[1, k] + lower_got_ref[1, k] + mid_low_ref[k]
        if t > 0:
            mid_ring[t - 1].wait_recv()
        if t == nz - 1:
            middle_ref[...] = mid_ref[k].astype(F32) + mid_ring_ref[t - 1].astype(F32)
            return
        if t > 0:
            mid_ref[k] = mid_ref[k] + mid_ring_ref[t - 1]
        mid_ring[t] = mail.send(mid_ref.at[k], mid_ring_ref.at[t], above)

    qkv_ring = {}

    def qkv_send(t):
        k = ring[t]
        second[k][0].wait_recv()
        own_ref[3, k, up] = own_ref[3, k, up] + second_y_ref[k]
        second[k][1].wait_recv()
        own_ref[3, k, low] = own_ref[3, k, low] + second_x_ref[k]
        if t > 0:
            qkv_ring[t - 1].wait_recv()
        if t == nz - 1:
            qkv_ref[...] = own_ref[3, k].astype(F32) + qkv_ring_ref[t - 1].astype(F32)
            return
        if t > 0:
            own_ref[3, k] = own_ref[3, k] + qkv_ring_ref[t - 1]
        qkv_ring[t] = mail.send(own_ref.at[3, k], qkv_ring_ref.at[t], above)

    up, low = slice(0, half), slice(half, 2 * half)
    core_step(0)
    upper_first = [mail.send(own_ref.at[0, :, up], first_x_ref.at[0], across_x)]
    lower_first = [mail.send(own_ref.at[0, :, low], first_y_ref.at[0], across_y)]
    core_step(1)
    upper_first.append(mail.send(own_ref.at[1, :, up], first_x_ref.at[1], across_x))
    core_step(2)
    lower_first.append(mail.send(own_ref.at[2, :, low], first_y_ref.at[1], across_y))
    core_step(3)
    out_step()

    slots = tokens // 2
    text_copy.wait_recv()
    text_got_ref[...] = (text_ref[:text_rows] + text_got_ref[...].astype(F32)).astype(BF)
    text_home = Home(ways, text_out, home_sends.at[0], home_recvs.at[0])
    for slot in range(2):
        at = slice(slot * text_rows // 2, (slot + 1) * text_rows // 2)
        text_home.send(text_got_ref.at[at], slot)

    wait(weight_ref)
    acc_ref[...] = nt(packed_ref[:, :width], weight_ref[:, :width])
    acc_ref[...] += nt(packed_ref[:, width : 2 * width], weight_ref[:, width : 2 * width])
    mid_send(0)
    feed_step(1)
    acc_ref[...] += nt(packed_ref[:, 2 * width :], weight_ref[:, 2 * width :])
    wait(input_ref, first_ref, gain_ref)
    gain_sum = jnp.zeros((1, width), F32)
    shift_sum = jnp.zeros((1, width), F32)
    chunk = min(128, tokens)
    for m in range(tokens // chunk):
        at = slice(m * chunk, (m + 1) * chunk)
        grad, gain_part, shift_part = norm_backward(
            input_ref[at].astype(F32), gain_ref[...], acc_ref[at]
        )
        k_got_ref[at] = (first_ref[at] + grad).astype(BF)
        gain_sum += gain_part[None]
        shift_sum += shift_part[None]
    wait(vector_ref)
    vector_out_ref[0] = vector_ref[...]
    vector_out_ref[0, 0:1] = gain_sum
    vector_out_ref[0, 1:2] = shift_sum
    vector_copy = mail.send(vector_out_ref.at[0], vector_in_ref.at[0], sibling)
    mid_send(1)

    vector_copy.wait_recv()
    vector_out_ref[1] = vector_out_ref[0] + vector_in_ref[0]
    vector_copy = mail.send(vector_out_ref.at[1], vector_in_ref.at[1], across_x)
    for t in range(2, nz):
        feed_step(t)
        if t < nz - 1:
            mid_send(t)
    vector_copy.wait_recv()
    vector_out_ref[2] = vector_out_ref[1] + vector_in_ref[1]
    vector_copy = mail.send(vector_out_ref.at[2], vector_in_ref.at[2], across_y)
    out_last()

    upper_first[0].wait_recv()
    own_ref[2, :, up] = own_ref[2, :, up] + first_x_ref[0]
    lower_first[0].wait_recv()
    own_ref[1, :, low] = own_ref[1, :, low] + first_y_ref[0]
    second = {}
    for k in ring:
        second[k] = (
            mail.send(own_ref.at[2, k, up], second_y_ref.at[k], across_y),
            mail.send(own_ref.at[1, k, low], second_x_ref.at[k], across_x),
        )
    frames_home = Home(ways, frames_out, home_sends.at[1], home_recvs.at[1])
    for slot in range(2):
        frames_home.send(k_got_ref.at[slot * slots : (slot + 1) * slots], slot)
    vector_copy.wait_recv()
    vector_out_ref[3] = vector_out_ref[2] + vector_in_ref[2]
    vector_copy = mail.send(vector_out_ref.at[3], vector_in_ref.at[3], above)
    upper_first[1].wait_recv()
    own_ref[3, :, up] = own_ref[3, :, up] + first_x_ref[1]
    lower_first[1].wait_recv()
    own_ref[3, :, low] = own_ref[3, :, low] + first_y_ref[1]
    mid_send(nz - 1)
    for kind in range(2):
        feed_last(kind)
    total = vector_out_ref[3]
    for t in range(nz - 1):
        vector_copy.wait_recv()
        total = total + vector_in_ref[3 + t]
        if t < nz - 2:
            vector_copy = mail.send(vector_in_ref.at[3 + t], vector_in_ref.at[4 + t], above)
    sum_ref[...] = total
    for t in range(nz):
        qkv_send(t)
    text_home.finish()
    frames_home.finish()
    for number, copy in enumerate(mail.sent):
        if not any(copy is c for pair in mid_copies.values() for c in pair):
            copy.wait_send()


FINAL_LOADS = (18, 19, 14, 15, 16, 17, 10, 11, 12, 13, 0, 5, 6, 7, 21, 22, 4, 1, 2, 3, 20)


def final_sums(place, count, *operands):
    nz = place.nz
    normed, weight, upper, in_up = operands[0], operands[4], operands[10], operands[14]
    vectors, projected, proj = operands[20], operands[21], operands[22]
    words, text_width = projected.shape[0], proj.shape[0]
    tokens, width = normed.shape
    block, piece = width // place.rows, weight.shape[1] // place.seq
    half, middle = block // 2, upper.shape[3]
    feed_width = in_up.shape[1]
    feed_rows = width // nz
    copies = 2 + 3 + nz - 1 + 2 + 2 * nz + 1 + 4 + 3 + nz - 1 + 4 + 2 * nz + 2 * (nz - 1)
    vmem = pltpu.VMEM
    return pl.pallas_call(
        with_loads(functools.partial(final_kernel, nz), len(operands), FINAL_LOADS),
        in_specs=[ANY_SPEC] * len(operands),
        out_specs=[WHOLE_SPEC] * 4 + [ANY_SPEC] * 2,
        out_shape=[
            jax.ShapeDtypeStruct((block, piece), F32),
            jax.ShapeDtypeStruct((block, middle), F32),
            jax.ShapeDtypeStruct((2, block, 2 * feed_width), F32),
            jax.ShapeDtypeStruct(vectors.shape, F32),
            jax.ShapeDtypeStruct((count, tokens // count, width), BF),
            jax.ShapeDtypeStruct((count, words // 2 // count, text_width), BF),
        ],
        scratch_shapes=[
            vmem((4, feed_rows, feed_width), BF),
            vmem((words, text_width), F32),
            vmem((tokens, 3 * width), BF),
            vmem((tokens, width), BF),
            vmem((tokens, width), BF),
            vmem((tokens, width), F32),
            vmem((width, tokens), BF),
            vmem((4, nz, block, piece), BF),
            vmem((4, nz, block, piece), BF),
            vmem((4, nz, block, piece), BF),
            vmem((2, nz, half, piece), BF),
            vmem((2, nz, half, piece), BF),
            vmem((nz, half, piece), BF),
            vmem((nz, half, piece), BF),
            vmem((nz, half, middle), BF),
            vmem((nz, half, middle), BF),
            vmem((nz, block, middle), BF),
            vmem((nz - 1, block, middle), BF),
            vmem((nz - 1, block, piece), BF),
            vmem((nz - 1, feed_rows, feed_width), BF),
            vmem((nz - 1, feed_rows, feed_width), BF),
            vmem((2, feed_rows, feed_width), BF),
            vmem((2, feed_rows, feed_width), BF),
            vmem((feed_rows, feed_width), BF),
            vmem((2, feed_rows // 2, feed_width), F32),
            vmem((2, feed_rows // 2, feed_width), F32),
            vmem((4,) + vectors.shape, F32),
            vmem((2 + nz,) + vectors.shape, F32),
            vmem((words // 2, text_width), BF),
            vmem((words // 2, text_width), BF),
            pltpu.SemaphoreType.DMA((copies,)),
            pltpu.SemaphoreType.DMA((copies,)),
            pltpu.SemaphoreType.DMA((2, 2)),
            pltpu.SemaphoreType.DMA((2, 2)),
        ]
        + load_scratch(operands, FINAL_LOADS),
        compiler_params=pltpu.CompilerParams(
            collective_id=1, has_side_effects=True, vmem_limit_bytes=63 * 1024 * 1024
        ),
        cost_estimate=pl.CostEstimate(
            flops=60 * tokens * width * weight.shape[1], bytes_accessed=40 << 20, transcendentals=0
        ),
    )(*operands)


def last_kernel(padding, qkv_ref, middle_ref, feed_ref, frames_ref, text_ref, *outs):
    frames_out, text_out, qkv_out, self_out, query_out, proj_out, kv_out, cross_out, in_out, out_out = outs
    piece = self_out.shape[1]
    frames_out[...] = frames_ref[...].astype(F32)
    text_out[...] = text_ref[...].astype(F32)
    qkv_out[...] = qkv_ref[...]
    cross_out[...] = middle_ref[:, :piece]
    query_out[...] = middle_ref[:, piece : 2 * piece]
    kv_out[...] = middle_ref[:, 2 * piece : 4 * piece]
    proj_out[...] = middle_ref[: proj_out.shape[0], 4 * piece : 5 * piece]
    self_out[...] = middle_ref[:, 5 * piece :]
    in_out[...] = feed_ref[0]
    out_out[...] = jnp.swapaxes(feed_ref[1], 0, 1)


def last_step(padding, piece, qkv, middle, feed_sums, frames, text):
    block, across = qkv.shape[0], feed_sums.shape[2]
    shapes = [
        frames.shape,
        text.shape,
        qkv.shape,
        (block, piece),
        (block, piece),
        (block - padding, piece),
        (block, 2 * piece),
        (block, piece),
        (block, across),
        (across, block),
    ]
    return pl.pallas_call(
        functools.partial(last_kernel, padding),
        in_specs=[WHOLE_SPEC] * 5,
        out_specs=[WHOLE_SPEC] * len(shapes),
        out_shape=[jax.ShapeDtypeStruct(shape, F32) for shape in shapes],
        compiler_params=pltpu.CompilerParams(vmem_limit_bytes=MOST_VMEM),
    )(qkv, middle, feed_sums, frames, text)


def permuted_sums(place, meta, in_up, in_low, out_sum, lefts, rights, normed_self, backward_self):
    nx, ny, nz, seq = place.nx, place.ny, place.nz, place.seq
    width = normed_self.shape[1]
    block, piece = width // place.rows, width // seq
    middle_own, middle_away = weight_parts(
        place, meta, lefts[:3] + lefts[2:4], rights[:5]
    )
    out_own, out_away = weight_parts(place, meta, lefts[4:], rights[5:])
    middle_got = place.swap_core(middle_away)
    out_got = place.swap_core(out_away)
    grad_packed = backward_self(middle_got, out_got)
    in_up = ring_sum([lambda a=in_up[k]: a.astype(F32) for k in range(ny)], place.next_y)
    in_low = ring_sum([lambda a=in_low[k]: a.astype(F32) for k in range(nx)], place.next_x)
    in_both = jnp.stack([in_up, in_low]).astype(BF).reshape(2, nz, block, -1)
    in_both = ring_sum([lambda a=in_both[:, k]: a.astype(F32) for k in range(nz)], place.next_z)
    out_sum = out_sum.reshape((nx, ny) + out_sum.shape[1:])
    out_sum = ring_sum([lambda a=out_sum[k]: a.astype(F32) for k in range(nx)], place.next_x)
    out_sum = out_sum.astype(BF)
    out_sum = ring_sum([lambda a=out_sum[k]: a.astype(F32) for k in range(ny)], place.next_y)
    feed_own = jnp.stack([in_both, out_sum.reshape(2, block, -1)])
    feed_got = place.swap_core(pick(feed_own, 1 - place.core, 1))
    feed_own = pick(feed_own, place.core, 1)
    low = jnp.where(place.core == 0, feed_own, feed_got)
    high = jnp.where(place.core == 0, feed_got, feed_own)
    sum_feed = jnp.concatenate([low, high], axis=2)

    def middle_piece(k):
        at = slice(k * block, (k + 1) * block)
        return lambda: middle_own[:, at].astype(F32) + middle_got[:, at].astype(F32)

    middle = ring_sum([middle_piece(k) for k in range(nz)], place.next_z).astype(BF)
    spread = jnp.concatenate(
        [
            middle[0].reshape(block, seq, -1),
            middle[1].reshape(block, seq, -1),
            jnp.concatenate([middle[2], middle[3]], axis=1).reshape(block, seq, -1),
            middle[4].reshape(block, seq, -1),
        ],
        axis=2,
    ).reshape(block, ny, nx, -1)

    def shifted(array, index, number, length, axis):
        return lambda: pick(array, (index + 1 + number) % length, axis).astype(F32)

    spread = ring_sum([shifted(spread, place.x, k, nx, 2) for k in range(nx)], place.next_x).astype(BF)
    spread = ring_sum([shifted(spread, place.y, k, ny, 1) for k in range(ny)], place.next_y)
    relative_parts = place.relative_columns(grad_packed, True)
    qkv_own, qkv_away = weight_parts(place, meta, [normed_self], [relative_parts])
    qkv_got = place.swap_core(qkv_away)

    def columns(array):
        return array[0].reshape(array.shape[1], nx, ny, -1)

    def natural(array):
        return jnp.stack(
            [
                jnp.stack(
                    [
                        pick(array[0].reshape(array.shape[1], seq, -1), place.offset(i, j), 1)
                        for i in range(ny)
                    ],
                    axis=1,
                )
                for j in range(nx)
            ],
            axis=1,
        )

    last_own = jnp.concatenate([columns(qkv_own), natural(out_own)], axis=3)
    last_got = jnp.concatenate([columns(qkv_got), natural(out_got)], axis=3)
    last = (last_own.astype(F32) + last_got.astype(F32)).astype(BF)
    last = last.reshape(nz, 2, block // 2, nx, ny, -1)
    upper = ring_sum([lambda k=k: last[:, 0, :, k].astype(F32) for k in range(nx)], place.next_x).astype(BF)
    lower = ring_sum([lambda k=k: last[:, 1, :, :, k].astype(F32) for k in range(ny)], place.next_y).astype(BF)
    upper = ring_sum([lambda a=upper[:, :, k]: a.astype(F32) for k in range(ny)], place.next_y)
    lower = ring_sum([lambda a=lower[:, :, k]: a.astype(F32) for k in range(nx)], place.next_x)
    last = jnp.stack([upper, lower], axis=1).astype(BF)
    last = ring_sum([lambda a=last[k]: a.astype(F32) for k in range(nz)], place.next_z)
    last = last.reshape(block, -1)
    sum_self_qkv, sum_self_out = last[:, : 3 * piece], last[:, 3 * piece :]

    return sum_feed, spread, sum_self_qkv, sum_self_out, grad_packed


def shards(
    frames,
    text_states,
    clip_lengths,
    text_lengths,
    self_gain,
    self_shift,
    self_qkv,
    self_out,
    cross_gain,
    cross_shift,
    cross_query,
    text_proj,
    text_bias,
    cross_kv,
    cross_out,
    feed_gain,
    feed_shift,
    feed_in,
    feed_out,
    grad_out,
):
    place = Place()
    count = frames.shape[0]
    width = frames.shape[2]
    text_total = text_states.shape[1] * place.seq

    nx, ny, nz, seq = place.nx, place.ny, place.nz, place.seq
    block, piece = width // place.rows, width // seq
    kernels = nx == 2 and ny == 2 and nz == 4 and piece % 128 == 0
    lengths = jnp.concatenate([clip_lengths, text_lengths], axis=1)
    if kernels:
        padded = jnp.zeros((8, 128), jnp.int32).at[:count, : 2 * CLIPS].set(lengths)
        (
            layer_raw,
            normed_self,
            queries,
            pair,
            pair_other,
            text_input,
            projected,
            text_pair,
            lengths_other,
        ) = entry(
            place,
            frames,
            text_states,
            padded,
            self_gain,
            self_shift,
            self_qkv,
            text_proj,
            text_bias,
            cross_kv,
        )
        lengths_other = lengths_other[:count, : 2 * CLIPS]
        layer_input = layer_raw.astype(F32)
    else:
        lengths_other = place.swap_core(lengths)
        text_half = place.to_rows(text_states)
        layer_raw = place.to_rows(frames)
        text_input = jnp.concatenate([text_half, place.swap_core(text_half)], axis=0)
        cotangent = place.to_rows(grad_out)
        projected = (dot(text_input, text_proj) + text_bias).astype(BF)
        text_pair = dot(projected, cross_kv).astype(BF)
        layer_input = layer_raw.astype(F32)
        normed_self = layer_norm(layer_input, self_gain, self_shift)
        pair = dot(normed_self, self_qkv[:, width:]).astype(BF)
        pair_other = place.swap_core(pair)
        queries = dot(normed_self, self_qkv[:, :width]).astype(BF)
    mine = place.spot // count == place.core
    row_lengths = pick(jnp.where(mine, lengths, lengths_other), place.spot % count, 0)

    if kernels:
        self_mix, self_lse, cotangent = self_forward_and_gather(
            place, row_lengths, queries, pair, pair_other, grad_out
        )
    else:
        self_mix, self_lse, _ = self_forward(row_lengths, queries, pair, pair_other)
    cotangent_other = place.swap_core(cotangent)
    first = layer_input + dot(self_mix, self_out)
    normed_cross = layer_norm(first, cross_gain, cross_shift)
    cross_queries = dot(normed_cross, cross_query).astype(BF)
    cross_mix, cross_lse, _ = cross_forward(row_lengths, cross_queries, text_pair)
    second = first + dot(cross_mix, cross_out)
    normed_feed = layer_norm(second, feed_gain, feed_shift)

    meta = jnp.stack([place.core, place.x, place.y, place.z]).astype(jnp.int32)
    normed_other = place.swap_core(normed_feed)
    fed = feed(
        place, meta, normed_feed, normed_other, cotangent, cotangent_other, feed_in, feed_out
    )
    result, result_away, grad_normed_feed, grad_away = fed[:4]
    up_parts, low_parts, out_parts = fed[4 : 4 + nx], fed[4 + nx : 4 + nx + ny], fed[4 + nx + ny :]
    grad_normed_feed = grad_normed_feed + place.swap_core(grad_away).astype(F32)

    grad_part, grad_feed_gain, grad_feed_shift = norm_backward(second, feed_gain, grad_normed_feed)
    grad_second = cotangent.astype(F32) + grad_part
    grad_second_branch = grad_second.astype(BF)
    grad_cross_mix = dot(grad_second_branch, cross_out, 1, 1).astype(BF)
    grad_cross_queries, grad_text_keys, grad_text_values, _ = cross_backward(
        row_lengths,
        cross_queries,
        text_pair,
        grad_cross_mix,
        cross_mix,
        cross_lse,
    )
    grad_normed_cross = dot(grad_cross_queries, cross_query, 1, 1)
    grad_part, grad_cross_gain, grad_cross_shift = norm_backward(first, cross_gain, grad_normed_cross)
    grad_first = grad_second + grad_part
    grad_first_branch = grad_first.astype(BF)

    grad_pair = jnp.concatenate([grad_text_keys, grad_text_values], axis=1)
    grad_projected = dot(grad_pair, cross_kv, 1, 1).astype(BF)
    grad_text_bias = jnp.sum(grad_projected.astype(F32), axis=0)
    padding = block - text_input.shape[1] // place.rows
    lefts = [cross_mix, normed_cross, projected, text_input, self_mix]
    rights = [
        grad_second_branch,
        grad_cross_queries,
        grad_text_keys,
        grad_text_values,
        grad_projected,
        grad_first_branch,
    ]
    result = second + result

    def backward_self(grad_self_mix, *before):
        return self_backward(
            row_lengths,
            queries,
            pair,
            pair_other,
            grad_self_mix,
            self_mix,
            self_lse,
            before=before,
        )[:5]

    def vector_list(grad_gain, grad_shift):
        return jnp.stack(
            [
                grad_gain,
                grad_shift,
                grad_cross_gain,
                grad_cross_shift,
                grad_text_bias,
                grad_feed_gain,
                grad_feed_shift,
                jnp.zeros_like(grad_feed_shift),
            ]
        )

    if kernels:
        (
            send_up,
            send_low,
            keep_up,
            keep_low,
            result,
            in_up,
            in_up_got,
            in_low,
            in_low_got,
            out_sum,
            grad_self_mix,
        ) = middle_parts(
            place,
            count,
            lefts,
            rights,
            result,
            result_away,
            (
                up_parts[1],
                place.next_x(up_parts[0]),
                low_parts[1],
                place.next_y(low_parts[0]),
                out_parts[1],
                place.next_z(out_parts[2]),
                out_parts[0],
            ),
            self_out,
        )
        up_got, low_got = place.next_x(send_up), place.next_y(send_low)
        out_got = place.next_z(out_sum)
        grads = backward_self(grad_self_mix)
        nothing = jnp.zeros_like(grad_feed_shift)
        sum_self_qkv, spread, sum_feed, vectors, grad_frames, grad_text = final_sums(
            place,
            count,
            normed_self,
            layer_raw,
            grad_first,
            self_gain[None],
            self_qkv,
            *grads,
            keep_up,
            up_got,
            keep_low,
            low_got,
            in_up,
            in_up_got,
            in_low,
            in_low_got,
            out_parts[3],
            out_got,
            vector_list(nothing, nothing),
            grad_projected,
            text_proj,
        )
        (
            grad_frames,
            grad_text,
            sum_self_qkv,
            sum_self_out,
            sum_cross_query,
            sum_text_proj,
            sum_cross_kv,
            sum_cross_out,
            sum_feed_in,
            sum_feed_out,
        ) = last_step(padding, piece, sum_self_qkv, spread, sum_feed, grad_frames, grad_text)
    else:

        def packed_self(*before):
            grads = backward_self(dot(grad_first_branch, self_out, 1, 1).astype(BF), *before)
            keys = (grads[1].astype(F32) + place.swap_core(grads[3]).astype(F32)).astype(BF)
            values = (grads[2].astype(F32) + place.swap_core(grads[4]).astype(F32)).astype(BF)
            return jnp.concatenate([grads[0], keys, values], axis=1)

        in_up = ring_sum([lambda a=a: a.astype(F32) for a in up_parts], place.next_x).astype(BF)
        in_low = ring_sum([lambda a=a: a.astype(F32) for a in low_parts], place.next_y).astype(BF)
        out_sum = ring_sum([lambda a=a: a.astype(F32) for a in out_parts], place.next_z).astype(BF)
        grad_text = dot(grad_projected, text_proj, 1, 1)
        text_blocks = text_input.reshape(text_total, place.rows, -1)
        text_padded = jnp.pad(text_blocks, ((0, 0), (0, 0), (0, padding))).reshape(text_total, width)
        lefts[3] = text_padded
        sum_feed, spread, sum_self_qkv, sum_self_out, grad_packed = permuted_sums(
            place, meta, in_up, in_low, out_sum, lefts, rights, normed_self, packed_self
        )
        result = (result + place.swap_core(result_away).astype(F32)).astype(BF)
        result = place.from_rows(result, count)
        grad_normed_self = dot(grad_packed, self_qkv, 1, 1)
        grad_part, grad_gain, grad_shift = norm_backward(layer_input, self_gain, grad_normed_self)
        grad_frames = place.from_rows((grad_first + grad_part).astype(BF), count)
        half = grad_text.shape[0] // 2
        text_away = place.swap_core(grad_text[half:].astype(BF))
        grad_text = (grad_text[:half] + text_away.astype(F32)).astype(BF)
        grad_text = place.from_rows(grad_text, count)
        vectors = place.vector_sum(vector_list(grad_gain, grad_shift))
        sum_cross_out, sum_cross_query = spread[:, :piece], spread[:, piece : 2 * piece]
        sum_cross_kv, sum_text_proj = spread[:, 2 * piece : 4 * piece], spread[:, 4 * piece : 5 * piece]
        sum_text_proj = sum_text_proj[: block - padding]
        sum_feed_in, sum_feed_out = sum_feed[0], jnp.swapaxes(sum_feed[1], 0, 1)
        grad_frames, grad_text = grad_frames.astype(F32), grad_text.astype(F32)
    vectors = pick(vectors.reshape(8, seq, width // seq), place.spot, 1)
    return (
        result,
        grad_frames,
        grad_text,
        vectors[0],
        vectors[1],
        sum_self_qkv,
        sum_self_out,
        vectors[2],
        vectors[3],
        sum_cross_query,
        sum_text_proj,
        vectors[4],
        sum_cross_kv,
        sum_cross_out,
        vectors[5],
        vectors[6],
        sum_feed_in,
        sum_feed_out,
    )


def solution(mesh):
    split, copied, table = P(ROWS, SEQ, None), P(), P(ROWS, None)
    vector, matrix = P(SEQ), P(ROWS, SEQ)
    return jax.shard_map(
        shards,
        mesh=mesh,
        in_specs=(split, split, table, table) + (copied,) * 15 + (split,),
        out_specs=(
            (split,) * 3
            + (vector, vector, matrix, matrix)
            + (vector, vector, matrix, matrix)
            + (vector, matrix, matrix)
            + (vector, vector, matrix, P(SEQ, ROWS))
        ),
        check_vma=False,
    )
```

```python
import functools
import math

import jax
import jax.numpy as jnp
from jax import lax
from jax.experimental import pallas as pl
from jax.experimental.pallas import tpu as pltpu
from jax.sharding import PartitionSpec as P

HD = 64
PAIR = 2 * HD
EPSILON = 1e-05
MASKED = -1e30
CLIPS = 4
ROWS = "rows"
SEQ = "seq"
BF = jnp.bfloat16
F32 = jnp.float32
VMEM_LIMIT = 48 * 1024 * 1024
MOST_VMEM = 62 * 1024 * 1024


def dot(left, right, left_dim=1, right_dim=0):
    return lax.dot_general(
        left, right, (((left_dim,), (right_dim,)), ((), ())), preferred_element_type=F32
    )


def pick(array, index, axis):
    return lax.dynamic_index_in_dim(array, index, axis, keepdims=False)


def after(value, *others):
    return lax.optimization_barrier((value,) + others)[0]


class Place:
    def __init__(self):
        self.rows, self.seq = lax.axis_size(ROWS), lax.axis_size(SEQ)
        self.nz = self.rows // 2
        self.nx = math.isqrt(self.seq)
        self.ny = self.seq // self.nx
        row, self.spot = lax.axis_index(ROWS), lax.axis_index(SEQ)
        self.core, self.z = row % 2, row // 2
        self.x, self.y = self.spot % self.nx, self.spot // self.nx
        self.owner = [0 if 4 * s // self.seq in (0, 3) else 1 for s in range(self.seq)]
        self.members = [[s for s in range(self.seq) if self.owner[s] == c] for c in (0, 1)]
        self.rank = [self.members[self.owner[s]].index(s) for s in range(self.seq)]

    def permute(self, value, target):
        pairs = []
        for z in range(self.nz):
            for c in range(2):
                for s in range(self.seq):
                    tz, tc, ts = target(z, c, s)
                    pairs.append(((2 * z + c) * self.seq + s, (2 * tz + tc) * self.seq + ts))
        return lax.ppermute(value, (ROWS, SEQ), pairs)

    def swap_core(self, value):
        return self.permute(value, lambda z, c, s: (z, 1 - c, s))

    def next_z(self, value):
        return self.permute(value, lambda z, c, s: ((z + 1) % self.nz, c, s))

    def next_x(self, value):
        nx = self.nx
        return self.permute(value, lambda z, c, s: (z, c, s // nx * nx + (s % nx + 1) % nx))

    def next_y(self, value):
        return self.permute(value, lambda z, c, s: (z, c, (s + self.nx) % self.seq))

    def to_rows(self, value):
        count = value.shape[0]
        my_rank = jnp.array(self.rank, jnp.int32)[self.spot]
        got = []
        for t in range(count):

            def target(z, c, s, t=t):
                return z, self.owner[s], c * count + (t + self.rank[s]) % count

            got.append(self.permute(pick(value, (t + my_rank) % count, 0), target))
        stacked = jnp.stack(got)
        here = self.spot % count
        return jnp.concatenate([pick(stacked, (here - k) % count, 0) for k in range(count)], axis=0)

    def from_rows(self, value, count):
        my_rank = jnp.array(self.rank, jnp.int32)[self.spot]
        slots = value.reshape(count, value.shape[0] // count, value.shape[1])
        here = self.spot % count
        got = []
        for t in range(count):

            def target(z, c, s, t=t):
                return z, s // count, self.members[c][(s % count - t) % count]

            got.append(self.permute(pick(slots, (here - t) % count, 0), target))
        stacked = jnp.stack(got)
        return jnp.stack([pick(stacked, (i - my_rank) % count, 0) for i in range(count)])

    def positions(self, total, core):
        quarter = total // 4
        inner = jnp.arange(quarter, dtype=jnp.int32)
        return jnp.concatenate([inner + core * quarter, inner + (3 - core) * quarter])

    def offset(self, i, j):
        return (self.y + 1 + i) % self.ny * self.nx + (self.x + 1 + j) % self.nx

    def relative_columns(self, value, outer_x):
        blocks = value.reshape(value.shape[0], self.seq, -1)
        if outer_x:
            order = [self.offset(i, j) for j in range(self.nx) for i in range(self.ny)]
        else:
            order = [self.offset(i, j) for i in range(self.ny) for j in range(self.nx)]
        return jnp.concatenate([pick(blocks, place, 1) for place in order], axis=1)


    def vector_sum(self, value):
        bit = 1
        while bit < self.rows:
            value = value + self.permute(
                value,
                lambda z, c, s: ((2 * z + c ^ bit) // 2, (2 * z + c ^ bit) % 2, s),
            )
            bit *= 2
        bit = 1
        while bit < self.seq:
            value = value + self.permute(value, lambda z, c, s: (z, c, s ^ bit))
            bit *= 2
        return value


def ring_order(count):
    return list(range(count - 2, -1, -1)) + [count - 1]


def ring_sum(pieces, send):
    order = ring_order(len(pieces))
    value = pieces[order[0]]()
    for k in order[1:]:
        value = pieces[k]() + send(value.astype(BF)).astype(F32)
    return value


def normalize(values):
    centered = values - jnp.mean(values, axis=-1, keepdims=True)
    scale = lax.rsqrt(jnp.mean(centered * centered, axis=-1, keepdims=True) + EPSILON)
    return centered * scale, scale


def layer_norm(values, gain, shift):
    return (normalize(values)[0] * gain + shift).astype(BF)


def norm_backward(values, gain, cotangent):
    normal, scale = normalize(values)
    grown = cotangent * gain
    inner = jnp.mean(grown, axis=-1, keepdims=True)
    along = jnp.mean(grown * normal, axis=-1, keepdims=True)
    grad = scale * (grown - inner - normal * along)
    return grad, jnp.sum(cotangent * normal, axis=0), jnp.sum(cotangent, axis=0)


def nt(left, right):
    return dot(left, right, 1, 1)


def head_lanes(values, head):
    lane = lax.broadcasted_iota(jnp.int32, values.shape, 1)
    return jnp.where((lane < HD) == (head == 0), values, jnp.zeros_like(values))


def turned(values):
    return jnp.swapaxes(values.astype(F32), 0, 1).astype(BF)


def running(lengths_ref, first):
    ends, total = [], 0
    for c in range(CLIPS):
        total = total + lengths_ref[first + c]
        ends.append(total)
    return ends


def spans(start, length, axis, ends):
    shape = (length, 1) if axis == 0 else (1, length)
    positions = lax.broadcasted_iota(jnp.int32, shape, axis) + start
    return sum((positions >= end).astype(jnp.int32) for end in ends)


def segment_bias(key_segment, query_segment, causal):
    allowed = key_segment == query_segment
    if causal:
        key = lax.broadcasted_iota(jnp.int32, allowed.shape, 0)
        query = lax.broadcasted_iota(jnp.int32, allowed.shape, 1)
        allowed = allowed & (key <= query)
    return jnp.where(allowed, 0.0, MASKED).astype(F32)


def forward_heads(queries, blocks, lse_ref, at):
    parts = []
    for head in range(2):
        query = head_lanes(queries, head)
        scores = [nt(keys, query) + bias() for keys, _, bias in blocks]
        highest = functools.reduce(
            jnp.maximum, [jnp.max(s, axis=0, keepdims=True) for s in scores]
        )
        weights = [jnp.exp(s - highest) for s in scores]
        total = sum(jnp.sum(w, axis=0, keepdims=True) for w in weights)
        mixed = sum(
            dot(values[head * HD : (head + 1) * HD], w.astype(BF))
            for (_, values, _), w in zip(blocks, weights)
        )
        parts.append(mixed * (1.0 / total))
        lse_ref[0, head : head + 1, at] = highest + jnp.log(total)
    return jnp.swapaxes(jnp.concatenate(parts, axis=0), 0, 1).astype(BF)


def backward_heads(queries, grads, mixed, blocks, lse_ref, at):
    product = jnp.swapaxes(grads.astype(F32) * mixed.astype(F32), 0, 1)
    parts = []
    for head in range(2):
        query, grad = head_lanes(queries, head), head_lanes(grads, head)
        rows = slice(head * HD, (head + 1) * HD)
        inner = jnp.sum(product[rows], axis=0, keepdims=True)
        totals = lse_ref[0, head : head + 1, at]
        grad_query = None
        for keys, turned_keys, values, bias, sums in blocks:
            weights = jnp.exp(nt(keys, query) + bias() - totals)
            scores = (weights * (nt(values, grad) - inner)).astype(BF)
            add_to(sums, 0, dot(scores, query))
            add_to(sums, 1, dot(weights.astype(BF), grad))
            term = dot(turned_keys[rows], scores)
            grad_query = term if grad_query is None else grad_query + term
        parts.append(grad_query)
    return (jnp.swapaxes(jnp.concatenate(parts, axis=0), 0, 1) * HD**-0.5).astype(BF)


def add_to(sums, index, term):
    sums[index] = term if sums[index] is None else sums[index] + term


def scaled(values):
    return values * jnp.array(HD**-0.5, BF)


def self_plan(core):
    if core == 0:
        return [(0, 0, 0)], [(0, 0, 1), (0, 1, 2), (1, 0, 3), (1, 1, 4)]
    return [(0, 0, 0), (1, 0, 4)], [(0, 0, 1), (0, 1, 2), (1, 0, 3)]


def self_biases(core, lengths_ref, bias_ref):
    length = bias_ref.shape[1]
    ends = running(lengths_ref, 0)
    quarters = (core, 3 - core)
    keys = [spans(q * length, length, 0, ends) for q in quarters]
    queries = [spans(q * length, length, 1, ends) for q in quarters]
    others = [spans(q * length, length, 0, ends) for q in (1 - core, 2 + core)]
    bias_ref[0] = segment_bias(keys[0], queries[0], True)
    bias_ref[1] = segment_bias(keys[0], queries[1], False)
    bias_ref[2] = segment_bias(keys[1], queries[1], True)
    bias_ref[3] = segment_bias(others[0], queries[1], False)
    last_key = jnp.where(core == 0, others[1], others[0])
    last_query = jnp.where(core == 0, queries[1], queries[0])
    bias_ref[4] = segment_bias(last_key, last_query, False)


def cross_bias(lengths_ref, bias_ref):
    core = lax.axis_index(ROWS) % 2
    count, rows = bias_ref.shape
    for n, token in enumerate((core, 3 - core, 1 - core, 2 + core)):
        keys = spans(token * (count // 4), count // 4, 0, running(lengths_ref, CLIPS))
        for m, frame in enumerate((core, 3 - core)):
            queries = spans(frame * (rows // 2), rows // 2, 1, running(lengths_ref, 0))
            at = slice(n * (count // 4), (n + 1) * (count // 4))
            bias_ref[at, m * (rows // 2) : (m + 1) * (rows // 2)] = segment_bias(keys, queries, False)


def self_forward_kernel(
    lengths_ref, q_ref, k_ref, v_ref, ko_ref, vo_ref, o_ref, lse_ref, bias_ref, fresh=True
):
    core = lax.axis_index(ROWS) % 2
    length = bias_ref.shape[1]

    @pl.when((pl.program_id(0) == 0) & fresh)
    def _():
        self_biases(core, lengths_ref, bias_ref)

    keys, values = (k_ref, ko_ref), (v_ref, vo_ref)
    for which in range(2):

        @pl.when((core == 0) == (which == 0))
        def _(which=which):
            for half, plan in enumerate(self_plan(which)):
                at = slice(half * length, (half + 1) * length)
                blocks = []
                for source, part, number in plan:
                    where = slice(part * length, (part + 1) * length)
                    blocks.append(
                        (
                            keys[source][where],
                            turned(values[source][where]),
                            functools.partial(bias_ref.__getitem__, number),
                        )
                    )
                o_ref[at] = forward_heads(scaled(q_ref[at]), blocks, lse_ref, at)


def self_backward_kernel(
    lengths_ref,
    q_ref,
    k_ref,
    v_ref,
    ko_ref,
    vo_ref,
    g_ref,
    o_ref,
    lse_ref,
    dq_ref,
    dk_ref,
    dv_ref,
    dko_ref,
    dvo_ref,
    bias_ref,
    fresh=True,
):
    core = lax.axis_index(ROWS) % 2
    length = bias_ref.shape[1]

    @pl.when((pl.program_id(0) == 0) & fresh)
    def _():
        self_biases(core, lengths_ref, bias_ref)

    keys, values = (k_ref, ko_ref), (v_ref, vo_ref)
    for which in range(2):

        @pl.when((core == 0) == (which == 0))
        def _(which=which):
            sums = {(s, p): [None, None] for s in range(2) for p in range(2)}
            for half, plan in enumerate(self_plan(which)):
                at = slice(half * length, (half + 1) * length)
                blocks = []
                for source, part, number in plan:
                    where = slice(part * length, (part + 1) * length)
                    blocks.append(
                        (
                            keys[source][where],
                            turned(keys[source][where]),
                            values[source][where],
                            functools.partial(bias_ref.__getitem__, number),
                            sums[source, part],
                        )
                    )
                dq_ref[at] = backward_heads(
                    scaled(q_ref[at]), g_ref[at], o_ref[at], blocks, lse_ref, at
                )
            for (source, part), pair in sums.items():
                where = slice(part * length, (part + 1) * length)
                for ref, value in zip(((dk_ref, dv_ref), (dko_ref, dvo_ref))[source], pair):
                    if value is None:
                        ref[where] = jnp.zeros((length, PAIR), BF)
                    else:
                        ref[where] = value.astype(BF)


def cross_forward_kernel(lengths_ref, q_ref, k_ref, v_ref, o_ref, lse_ref, bias_ref, fresh=True):
    length = q_ref.shape[0] // 2

    @pl.when((pl.program_id(0) == 0) & fresh)
    def _():
        cross_bias(lengths_ref, bias_ref)

    turned_values = turned(v_ref[...])
    for half in range(2):
        at = slice(half * length, (half + 1) * length)
        blocks = [(k_ref[...], turned_values, lambda at=at: bias_ref[:, at])]
        o_ref[at] = forward_heads(scaled(q_ref[at]), blocks, lse_ref, at)


def cross_backward_kernel(
    lengths_ref,
    q_ref,
    k_ref,
    v_ref,
    g_ref,
    o_ref,
    lse_ref,
    dq_ref,
    dk_ref,
    dv_ref,
    bias_ref,
    fresh=True,
):
    length = q_ref.shape[0] // 2

    @pl.when((pl.program_id(0) == 0) & fresh)
    def _():
        cross_bias(lengths_ref, bias_ref)

    turned_keys = turned(k_ref[...])
    sums = [None, None]
    for half in range(2):
        at = slice(half * length, (half + 1) * length)
        blocks = [(k_ref[...], turned_keys, v_ref[...], lambda at=at: bias_ref[:, at], sums)]
        dq_ref[at] = backward_heads(scaled(q_ref[at]), g_ref[at], o_ref[at], blocks, lse_ref, at)
    dk_ref[...] = sums[0].astype(BF)
    dv_ref[...] = sums[1].astype(BF)


GROUP = 2


def column(rows, first=0):
    return pl.BlockSpec((rows, GROUP * PAIR), lambda i: (0, first // GROUP + i))


def grouped(kernel):
    def part(ref, pair):
        if len(ref.shape) == 2 and ref.shape[1] == GROUP * PAIR and ref.dtype == BF:
            return ref.at[:, pair * PAIR : (pair + 1) * PAIR]
        if len(ref.shape) == 3 and ref.shape[:2] == (GROUP, 8):
            return ref.at[pair : pair + 1]
        return ref

    def run(*refs):
        for pair in range(GROUP):
            kernel(*[part(ref, pair) for ref in refs], fresh=pair == 0)

    return run


SMEM_SPEC = pl.BlockSpec(memory_space=pltpu.SMEM)


def without(kernel, first, count):
    def run(*refs):
        kernel(*refs[:first], *refs[first + count :])

    return run


ANY_SPEC = pl.BlockSpec(memory_space=pl.ANY)
WHOLE_SPEC = pl.BlockSpec(memory_space=pltpu.VMEM)


MARK = jax.ShapeDtypeStruct((8, 128), F32)


def marked(kernel, at):
    def run(*refs):
        refs[at][...] = jnp.zeros((8, 128), F32)
        kernel(*refs[:at], *refs[at + 1 :])

    return run


def attention_call(
    kernel, heads, in_specs, outs, bias_shape, flops, arguments, before=(), limit=VMEM_LIMIT
):
    pairs = heads // 2
    kernel = marked(grouped(kernel), len(arguments) + len(outs))
    kernel = without(kernel, len(arguments), len(before))
    in_specs = list(in_specs) + [ANY_SPEC] * len(before)
    arguments = tuple(arguments) + tuple(before)
    out_shape, out_specs = [], []
    for rows in outs:
        if rows is None:
            queries = outs[0]
            out_shape.append(jax.ShapeDtypeStruct((pairs, 8, queries), F32))
            out_specs.append(lse_spec(queries))
        else:
            out_shape.append(jax.ShapeDtypeStruct((rows, pairs * PAIR), BF))
            out_specs.append(column(rows))
    out_shape.append(MARK)
    out_specs.append(pl.BlockSpec((8, 128), lambda i: (0, 0)))
    return pl.pallas_call(
        kernel,
        grid=(pairs // GROUP,),
        in_specs=in_specs,
        out_specs=out_specs,
        out_shape=out_shape,
        scratch_shapes=[pltpu.VMEM(bias_shape, F32)],
        compiler_params=pltpu.CompilerParams(vmem_limit_bytes=limit),
        cost_estimate=pl.CostEstimate(flops=flops, bytes_accessed=8 << 20, transcendentals=flops >> 8),
    )(*arguments)


def lse_spec(queries):
    return pl.BlockSpec((GROUP, 8, queries), lambda i: (i, 0, 0))


def self_forward(lengths, queries, pair, pair_other):
    rows, width = queries.shape
    heads = width // HD
    length = rows // 2
    half = heads // 2
    return attention_call(
        self_forward_kernel,
        heads,
        [
            SMEM_SPEC,
            column(rows),
            column(rows),
            column(rows, half),
            column(rows),
            column(rows, half),
        ],
        (rows, None),
        (5, length, length),
        heads * 5 * 4 * length * length * PAIR * 2,
        (lengths, queries, pair, pair, pair_other, pair_other),
    )


def self_backward(lengths, queries, pair, pair_other, grads, mixed, lse, before=()):
    rows, width = queries.shape
    heads = width // HD
    length = rows // 2
    half = heads // 2
    return attention_call(
        self_backward_kernel,
        heads,
        [
            SMEM_SPEC,
            column(rows),
            column(rows),
            column(rows, half),
            column(rows),
            column(rows, half),
            column(rows),
            column(rows),
            lse_spec(rows),
        ],
        (rows,) * 5,
        (5, length, length),
        heads * 5 * 10 * length * length * PAIR * 2,
        (lengths, queries, pair, pair, pair_other, pair_other, grads, mixed, lse),
        before,
        MOST_VMEM,
    )


def cross_forward(lengths, queries, pair):
    rows, width = queries.shape
    heads = width // HD
    count = pair.shape[0]
    return attention_call(
        cross_forward_kernel,
        heads,
        [SMEM_SPEC, column(rows), column(count), column(count, heads // 2)],
        (rows, None),
        (count, rows),
        heads * 4 * rows * count * PAIR * 2,
        (lengths, queries, pair, pair),
    )


def cross_backward(lengths, queries, pair, grads, mixed, lse, before=()):
    rows, width = queries.shape
    heads = width // HD
    count = pair.shape[0]
    return attention_call(
        cross_backward_kernel,
        heads,
        [
            SMEM_SPEC,
            column(rows),
            column(count),
            column(count, heads // 2),
            column(rows),
            column(rows),
            lse_spec(rows),
        ],
        (rows, count, count),
        (count, rows),
        heads * 10 * rows * count * PAIR * 2,
        (lengths, queries, pair, pair, grads, mixed, lse),
        before,
    )


def gelu_and_slope(values):
    inside = 0.5 * (1.0 + lax.erf(values * (0.5**0.5)))
    bell = jnp.exp(-0.5 * values * values) * ((2.0 * math.pi) ** -0.5)
    return values * inside, inside + values * bell


def feed_kernel(shape, meta_ref, own_in, other_in, gown_in, gother_in, win_ref, wout_ref, *refs):
    nx, ny, nz, chunk = shape
    res_out, res_other_out, grad_out, grad_other_out = refs[:4]
    up_refs, low_refs, gout_refs = refs[4 : 4 + nx], refs[4 + nx : 4 + nx + ny], refs[4 + nx + ny : 4 + nx + ny + nz]
    scratch = refs[4 + nx + ny + nz :]
    act_ref, pre_ref, own_ref, other_ref, gown_ref, gother_ref, res_acc, grad_acc = scratch[:8]
    res_ref, grad_ref, res_other_ref, grad_other_ref, load_sems, store_sems = scratch[8:]
    loads = [
        pltpu.make_async_copy(source, target, load_sems.at[number])
        for number, (source, target) in enumerate(
            (
                (own_in, own_ref),
                (gown_in, gown_ref),
                (other_in, other_ref),
                (gother_in, gother_ref),
            )
        )
    ]
    stores = [
        pltpu.make_async_copy(source, target, store_sems.at[number])
        for number, (source, target) in enumerate(
            (
                (res_ref, res_out),
                (res_other_ref, res_other_out),
                (grad_ref, grad_out),
                (grad_other_ref, grad_other_out),
            )
        )
    ]
    j, i = pl.program_id(0), pl.program_id(1)
    z = meta_ref[3]
    tokens = own_ref.shape[0]
    sources = ((own_ref, gown_ref, res_ref, grad_ref), (other_ref, gother_ref, res_acc, grad_acc))

    first = (i == 0) & (j == 0)

    @pl.when(first)
    def _():
        for load in loads:
            load.start()
        for _, _, res, grad in sources:
            res[...] = jnp.zeros_like(res)
            grad[...] = jnp.zeros_like(grad)

    for side, (values, grads, res, grad) in enumerate(sources):

        @pl.when(first)
        def _(side=side):
            loads[2 * side].wait()
            loads[2 * side + 1].wait()

        for m in range(tokens // chunk):
            at = slice(m * chunk, (m + 1) * chunk)
            activated, slope = gelu_and_slope(dot(values[at], win_ref[...]))
            activated = activated.astype(BF)
            before = (nt(grads[at], wout_ref[...]) * slope).astype(BF)
            to = slice(side * tokens + m * chunk, side * tokens + (m + 1) * chunk)
            act_ref[to] = activated
            pre_ref[to] = before
            res[at] += dot(activated, wout_ref[...])
            grad[at] += nt(before, win_ref[...])

    @pl.when((i == ny - 1) & (j == nx - 1))
    def _():
        res_other_ref[...] = res_acc[...].astype(BF)
        grad_other_ref[...] = grad_acc[...].astype(BF)
        for copy in stores:
            copy.start()

    rows = own_ref.shape[1] // nz
    half = rows // 2

    def both(one, two, right):
        low, high = right[:tokens], right[tokens:]
        return (dot(one, low, 0, 0) + dot(two, high, 0, 0)).astype(BF)

    for k in range(nz):
        at = pl.ds(pl.multiple_of((z + 1 + k) % nz * rows, rows), rows)
        gin = both(own_ref[:, at], other_ref[:, at], pre_ref)
        gout_refs[k][0] = both(gown_ref[:, at], gother_ref[:, at], act_ref)
        to = slice(k * half, (k + 1) * half)
        for number, ref in enumerate(up_refs):

            @pl.when(j == number)
            def _(ref=ref):
                ref[0, to] = gin[:half]

        for number, ref in enumerate(low_refs):

            @pl.when(i == number)
            def _(ref=ref):
                ref[0, to] = gin[half:]

    @pl.when((i == ny - 1) & (j == nx - 1))
    def _():
        for copy in stores:
            copy.wait()


def feed(place, meta, own, other, gown, gother, feed_in, feed_out):
    nx, ny, nz = place.nx, place.ny, place.nz
    tokens, width = own.shape
    part = feed_in.shape[1] // place.seq // 2
    chunk = min(256, tokens)

    def unit(j, i, meta):
        return 2 * ((meta[2] + 1 + i) % ny * nx + (meta[1] + 1 + j) % nx) + meta[0]

    def up_spec(number):
        def index(j, i, meta):
            return jnp.where(j == number, i, jnp.where(j < number, 0, ny - 1)), 0, 0

        return pl.BlockSpec((1, width // 2, part), index)

    low_spec = pl.BlockSpec((1, width // 2, part), lambda j, i, meta: (j, 0, 0))
    gout_spec = pl.BlockSpec((1, width // nz, part), lambda j, i, meta: (j * ny + i, 0, 0))
    total = 2 * tokens
    shape = jax.ShapeDtypeStruct
    return pl.pallas_call(
        functools.partial(feed_kernel, (nx, ny, nz, chunk)),
        grid_spec=pltpu.PrefetchScalarGridSpec(
            num_scalar_prefetch=1,
            grid=(nx, ny),
            in_specs=[ANY_SPEC] * 4
            + [
                pl.BlockSpec((width, part), lambda j, i, meta: (0, unit(j, i, meta))),
                pl.BlockSpec((part, width), lambda j, i, meta: (unit(j, i, meta), 0)),
            ],
            out_specs=[ANY_SPEC] * 4
            + [up_spec(n) for n in range(nx)]
            + [low_spec] * ny
            + [gout_spec] * nz,
            scratch_shapes=[
                pltpu.VMEM((total, part), BF),
                pltpu.VMEM((total, part), BF),
                pltpu.VMEM((tokens, width), BF),
                pltpu.VMEM((tokens, width), BF),
                pltpu.VMEM((tokens, width), BF),
                pltpu.VMEM((tokens, width), BF),
                pltpu.VMEM((tokens, width), F32),
                pltpu.VMEM((tokens, width), F32),
                pltpu.VMEM((tokens, width), F32),
                pltpu.VMEM((tokens, width), F32),
                pltpu.VMEM((tokens, width), BF),
                pltpu.VMEM((tokens, width), BF),
                pltpu.SemaphoreType.DMA((4,)),
                pltpu.SemaphoreType.DMA((4,)),
            ],
        ),
        out_shape=[
            shape((tokens, width), F32),
            shape((tokens, width), BF),
            shape((tokens, width), F32),
            shape((tokens, width), BF),
        ]
        + [shape((ny, width // 2, part), BF)] * nx
        + [shape((nx, width // 2, part), BF)] * ny
        + [shape((place.seq, width // nz, part), BF)] * nz,
        compiler_params=pltpu.CompilerParams(vmem_limit_bytes=60 * 1024 * 1024),
        cost_estimate=pl.CostEstimate(
            flops=12 * total * width * part * place.seq,
            bytes_accessed=40 << 20,
            transcendentals=2 * total * part * place.seq,
        ),
    )(meta, own, other, gown, gother, feed_in, feed_out)


def weight_kernel(shape, meta_ref, *refs):
    count, nz = shape
    lefts, rights = refs[:count], refs[count : 2 * count]
    own_ref, other_ref, turned_ref = refs[2 * count :]
    core, z = meta_ref[0], meta_ref[3]
    block = own_ref.shape[1] // nz
    for number in range(count):

        @pl.when(pl.program_id(0) == number)
        def _(left=lefts[number], right=rights[number]):
            tokens = left.shape[0]
            turned_ref[:, :tokens] = turned(left[...])
            for k in range(nz):
                start = (z + 1 + k) % nz * 2
                to = slice(k * block, (k + 1) * block)
                for which, ref in ((core, own_ref), (1 - core, other_ref)):
                    at = pl.ds(pl.multiple_of((start + which) * block, block), block)
                    ref[0, to] = dot(turned_ref[at, :tokens], right[...]).astype(BF)


def weight_parts(place, meta, lefts, rights, before=()):
    count = len(lefts)
    depth, width = lefts[0].shape[1], rights[0].shape[1]
    tokens = max(left.shape[0] for left in lefts)
    out = jax.ShapeDtypeStruct((count, depth // 2, width), BF)
    spec = pl.BlockSpec((1, depth // 2, width), lambda u: (u, 0, 0))
    return pl.pallas_call(
        without(functools.partial(weight_kernel, (count, place.nz)), 1 + 2 * count, len(before)),
        grid=(count,),
        in_specs=[SMEM_SPEC] + [WHOLE_SPEC] * (2 * count) + [ANY_SPEC] * len(before),
        out_specs=[spec, spec],
        out_shape=[out, out],
        scratch_shapes=[pltpu.VMEM((depth, tokens), BF)],
        compiler_params=pltpu.CompilerParams(vmem_limit_bytes=VMEM_LIMIT),
        cost_estimate=pl.CostEstimate(
            flops=2 * count * tokens * depth * width,
            bytes_accessed=count * depth * width * 4,
            transcendentals=0,
        ),
    )(meta, *lefts, *rights, *before)


MESH = pl.DeviceIdType.MESH


class Mail:
    def __init__(self, send_sems, recv_sems):
        self.send_sems, self.recv_sems, self.sent = send_sems, recv_sems, []

    def send(self, source, target, device):
        number = len(self.sent)
        copy = pltpu.make_async_remote_copy(
            src_ref=source,
            dst_ref=target,
            send_sem=self.send_sems.at[number],
            recv_sem=self.recv_sems.at[number],
            device_id=device,
            device_id_type=MESH,
        )
        copy.start()
        self.sent.append(copy)
        return copy

    def finish(self):
        for copy in self.sent:
            copy.wait_send()


class Ways:
    def __init__(self, nz):
        self.row, self.spot = lax.axis_index(ROWS), lax.axis_index(SEQ)
        self.core, self.z = self.row % 2, self.row // 2
        self.x, self.y = self.spot % 2, self.spot // 2
        self.nz = nz
        self.sibling = (self.row + 1 - 2 * self.core, self.spot)
        self.across_x = (self.row, self.spot + 1 - 2 * self.x)
        self.across_y = (self.row, self.y * -2 + 2 + self.x)
        self.above = ((self.row + 2) % (2 * nz), self.spot)
        self.below = ((self.row + 2 * nz - 2) % (2 * nz), self.spot)

    def plane(self):
        devices = []
        for other in range(2):
            row = self.row if other == 0 else self.sibling[0]
            devices += [(row, (self.spot + s) % 4) for s in range(4) if other or s]
        return devices

    def meet(self, devices):
        barrier = pltpu.get_barrier_semaphore()
        for device in devices:
            pl.semaphore_signal(barrier, inc=1, device_id=device, device_id_type=MESH)
        pl.semaphore_wait(barrier, len(devices))

    def place(self, q):
        return (self.y + 1 + q % 2) % 2 * 2 + (self.x + 1 + q // 2) % 2

    def rows(self, k, which, block):
        start = ((self.z + 1 + k) % self.nz * 2 + which) * block
        return pl.ds(pl.multiple_of(start, block), block)


class Home:
    def __init__(self, ways, out_ref, send_sems, recv_sems):
        self.ways, self.out_ref = ways, out_ref
        self.send_sems, self.recv_sems = send_sems, recv_sems
        self.started = []

    def send(self, source, slot):
        ways = self.ways
        spot = jnp.where(ways.core == 0, 3 * slot, 1 + slot)
        row = 2 * ways.z + ways.spot // 2
        stays = (spot == ways.spot) & (row == ways.row)
        to = self.out_ref.at[ways.spot % 2]
        copy = pltpu.make_async_remote_copy(
            src_ref=source,
            dst_ref=to,
            send_sem=self.send_sems.at[slot],
            recv_sem=self.recv_sems.at[ways.spot % 2],
            device_id=(row, spot),
            device_id_type=MESH,
        )
        local = pltpu.make_async_copy(source, to, self.recv_sems.at[ways.spot % 2])

        @pl.when(stays)
        def _():
            local.start()

        @pl.when(jnp.logical_not(stays))
        def _():
            copy.start()

        self.started.append((stays, copy))

    def finish(self):
        for r in range(2):
            to = self.out_ref.at[r]
            pltpu.make_async_copy(to, to, self.recv_sems.at[r]).wait()
        for stays, copy in self.started:

            @pl.when(jnp.logical_not(stays))
            def _(copy=copy):
                copy.wait_send()


class Gathering:
    def __init__(self, ways, source_ref, target_ref, send_sems, recv_sems):
        self.ways, self.source_ref, self.target_ref = ways, source_ref, target_ref
        self.send_sems, self.recv_sems = send_sems, recv_sems
        self.block = source_ref.shape[1]
        self.copies = []
        owner = jnp.where((ways.spot == 0) | (ways.spot == 3), 0, 1)
        slot = ways.spot // 2
        to = target_ref.at[pl.ds(pl.multiple_of(slot * self.block, self.block), self.block)]
        for r in range(2):
            row, spot = 2 * ways.z + owner, 2 * ways.core + r
            stays = (spot == ways.spot) & (row == ways.row)
            copy = pltpu.make_async_remote_copy(
                src_ref=source_ref.at[r],
                dst_ref=to,
                send_sem=send_sems.at[r],
                recv_sem=recv_sems.at[slot],
                device_id=(row, spot),
                device_id_type=MESH,
            )
            local = pltpu.make_async_copy(source_ref.at[r], to, recv_sems.at[slot])
            self.copies.append((stays, copy, local))

    def start(self):
        for stays, copy, local in self.copies:

            @pl.when(stays)
            def _(local=local):
                local.start()

            @pl.when(jnp.logical_not(stays))
            def _(copy=copy):
                copy.start()

    def arrived(self, slot):
        to = self.target_ref.at[slot * self.block : (slot + 1) * self.block]
        pltpu.make_async_copy(to, to, self.recv_sems.at[slot]).wait()

    def finish(self):
        for stays, copy, _ in self.copies:

            @pl.when(jnp.logical_not(stays))
            def _(copy=copy):
                copy.wait_send()


def self_forward_carrying(nz, lengths_ref, *refs):
    grads_ref, cotangent_ref = refs[5], refs[8]
    bias_ref, sends, recvs = refs[9:]
    gathering = Gathering(Ways(nz), grads_ref, cotangent_ref, sends, recvs)

    @pl.when(pl.program_id(0) == 0)
    def _():
        gathering.ways.meet(gathering.ways.plane())
        gathering.start()

    grouped(self_forward_kernel)(lengths_ref, *refs[:5], *refs[6:8], bias_ref)

    @pl.when(pl.program_id(0) == pl.num_programs(0) - 1)
    def _():
        for slot in range(2):
            gathering.arrived(slot)
        gathering.finish()


def self_forward_and_gather(place, lengths, queries, pair, pair_other, grads):
    rows, width = queries.shape
    half = width // HD // 2
    length = rows // 2
    return pl.pallas_call(
        functools.partial(self_forward_carrying, place.nz),
        grid=(half // GROUP,),
        in_specs=[
            SMEM_SPEC,
            column(rows),
            column(rows),
            column(rows, half),
            column(rows),
            column(rows, half),
            ANY_SPEC,
        ],
        out_specs=[column(rows), lse_spec(rows), ANY_SPEC],
        out_shape=[
            jax.ShapeDtypeStruct((rows, width), BF),
            jax.ShapeDtypeStruct((half, 8, rows), F32),
            jax.ShapeDtypeStruct((rows, width), BF),
        ],
        scratch_shapes=[pltpu.VMEM((5, length, length), F32)]
        + [pltpu.SemaphoreType.DMA((2,))] * 2,
        compiler_params=pltpu.CompilerParams(
            collective_id=4, has_side_effects=True, vmem_limit_bytes=VMEM_LIMIT
        ),
        cost_estimate=pl.CostEstimate(
            flops=40 * rows * length * width, bytes_accessed=8 << 20, transcendentals=0
        ),
    )(lengths, queries, pair, pair, pair_other, pair_other, grads)


def entry_kernel(
    nz,
    frames_ref,
    text_ref,
    lengths_ref,
    gain_ref,
    shift_ref,
    qkv_ref,
    proj_ref,
    bias_ref,
    kv_ref,
    input_out,
    normed_out,
    queries_out,
    pair_out,
    pair_other_ref,
    words_out,
    projected_out,
    text_pair_out,
    lengths_other_ref,
    input_ref,
    normed_ref,
    queries_ref,
    pair_ref,
    words_ref,
    projected_ref,
    text_pair_ref,
    store_sems,
    qkv_here,
    proj_here,
    kv_here,
    load_sems,
    send_sems,
    recv_sems,
    gather_sends,
    gather_recvs,
):
    loads = [
        pltpu.make_async_copy(source, target, load_sems.at[number])
        for number, (source, target) in enumerate(
            ((proj_ref, proj_here), (kv_ref, kv_here), (qkv_ref, qkv_here))
        )
    ]
    for load in loads:
        load.start()
    stores = []

    def store(source, target):
        copy = pltpu.make_async_copy(source, target, store_sems.at[len(stores)])
        copy.start()
        stores.append(copy)

    ways = Ways(nz)
    ways.meet(ways.plane())
    mail = Mail(send_sems, recv_sems)
    words = Gathering(ways, text_ref, words_ref, gather_sends.at[0], gather_recvs.at[0])
    frames = Gathering(ways, frames_ref, input_ref, gather_sends.at[1], gather_recvs.at[1])
    words.start()
    frames.start()
    lengths_copy = mail.send(lengths_ref, lengths_other_ref, ways.sibling)
    half = words_ref.shape[0] // 2
    for slot in range(2):
        words.arrived(slot)
    words_copy = mail.send(words_ref.at[:half], words_ref.at[half:], ways.sibling)
    loads[0].wait()
    loads[1].wait()
    words_copy.wait_recv()
    store(words_ref, words_out)
    projected = (dot(words_ref[...], proj_here[...]) + bias_ref[...]).astype(BF)
    projected_ref[...] = projected
    store(projected_ref, projected_out)
    text_pair_ref[...] = dot(projected, kv_here[...]).astype(BF)
    store(text_pair_ref, text_pair_out)
    loads[2].wait()
    width = input_ref.shape[1]
    block = input_ref.shape[0] // 2
    copies = []
    for slot in range(2):
        frames.arrived(slot)
        at = slice(slot * block, (slot + 1) * block)
        normed_ref[at] = layer_norm(input_ref[at].astype(F32), gain_ref[...], shift_ref[...])
        store(input_ref.at[at], input_out.at[at])
        store(normed_ref.at[at], normed_out.at[at])
        pair_ref[at] = dot(normed_ref[at], qkv_here[:, width:]).astype(BF)
        store(pair_ref.at[at], pair_out.at[at])
        copies.append(mail.send(pair_ref.at[at], pair_other_ref.at[at], ways.sibling))
    queries_ref[...] = dot(normed_ref[...], qkv_here[:, :width]).astype(BF)
    store(queries_ref, queries_out)
    lengths_copy.wait_recv()
    for copy in copies:
        copy.wait_recv()
    mail.finish()
    for gathering in (words, frames):
        gathering.finish()
    for copy in stores:
        copy.wait()


def entry(place, frames, text, lengths, gain, shift, qkv, proj, bias, kv):
    count, block, width = frames.shape
    tokens, words = count * block, 2 * count * text.shape[1]
    shape, vmem = jax.ShapeDtypeStruct, pltpu.VMEM
    return pl.pallas_call(
        functools.partial(entry_kernel, place.nz),
        in_specs=[ANY_SPEC] * 2 + [WHOLE_SPEC] * 3 + [ANY_SPEC] * 2 + [WHOLE_SPEC, ANY_SPEC],
        out_specs=[ANY_SPEC] * 8 + [WHOLE_SPEC],
        out_shape=[
            shape((tokens, width), BF),
            shape((tokens, width), BF),
            shape((tokens, width), BF),
            shape((tokens, 2 * width), BF),
            shape((tokens, 2 * width), BF),
            shape((words, text.shape[2]), BF),
            shape((words, width), BF),
            shape((words, 2 * width), BF),
            shape(lengths.shape, jnp.int32),
        ],
        scratch_shapes=[
            vmem((tokens, width), BF),
            vmem((tokens, width), BF),
            vmem((tokens, width), BF),
            vmem((tokens, 2 * width), BF),
            vmem((words, text.shape[2]), BF),
            vmem((words, width), BF),
            vmem((words, 2 * width), BF),
            pltpu.SemaphoreType.DMA((10,)),
            vmem(qkv.shape, BF),
            vmem(proj.shape, BF),
            vmem(kv.shape, BF),
            pltpu.SemaphoreType.DMA((3,)),
            pltpu.SemaphoreType.DMA((4,)),
            pltpu.SemaphoreType.DMA((4,)),
            pltpu.SemaphoreType.DMA((2, 2)),
            pltpu.SemaphoreType.DMA((2, 2)),
        ],
        compiler_params=pltpu.CompilerParams(
            collective_id=3, has_side_effects=True, vmem_limit_bytes=MOST_VMEM
        ),
        cost_estimate=pl.CostEstimate(
            flops=20 * tokens * width * width, bytes_accessed=20 << 20, transcendentals=0
        ),
    )(frames, text, lengths, gain[None], shift[None], qkv, proj, bias[None], kv)


def with_loads(kernel, count, late):
    def run(*refs):
        inputs, rest = list(refs[:count]), refs[count:]
        here, sems = rest[-len(late) - 1 : -1], rest[-1]
        copies = []
        for number, which in enumerate(late):
            copy = pltpu.make_async_copy(inputs[which], here[number], sems.at[number])
            copy.start()
            inputs[which] = here[number]
            copies.append(copy)
        open_copies = dict(zip(map(id, here), copies))

        def wait(*wanted):
            for ref in wanted:
                open_copies.pop(id(ref)).wait()

        kernel(wait, *inputs, *rest[: -len(late) - 1])

    return run


def load_scratch(operands, late):
    return [pltpu.VMEM(operands[n].shape, operands[n].dtype) for n in late] + [
        pltpu.SemaphoreType.DMA((len(late),))
    ]


def middle_kernel(
    shape,
    wait,
    mixed_ref,
    normed_ref,
    projected_ref,
    text_ref,
    self_ref,
    g_second_ref,
    g_query_ref,
    g_keys_ref,
    g_values_ref,
    g_projected_ref,
    g_first_ref,
    result_ref,
    result_away_ref,
    in_up_ref,
    in_up_got_ref,
    in_low_ref,
    in_low_got_ref,
    out_one_ref,
    out_one_got_ref,
    out_zero_ref,
    self_weight_ref,
    send_up_ref,
    send_low_ref,
    keep_up_ref,
    keep_low_ref,
    result_out,
    in_up_keep,
    in_up_next,
    in_low_keep,
    in_low_next,
    out_next,
    g_mix_ref,
    mixed_t,
    normed_t,
    projected_t,
    text_t,
    self_t,
    own_ref,
    away_ref,
    got_ref,
    result_got_ref,
    in_send_ref,
    out_send_ref,
    out_came_ref,
    send_sems,
    recv_sems,
    home_sends,
    home_recvs,
):
    nz, piece = shape
    ways = Ways(nz)
    ways.meet(ways.plane() + [ways.above, ways.below])
    mail = Mail(send_sems, recv_sems)
    result_copy = mail.send(result_away_ref, result_got_ref, ways.sibling)
    wait(out_one_ref, out_one_got_ref)
    out_send_ref[...] = out_one_ref[...] + out_one_got_ref[...]
    out_copy = mail.send(out_send_ref, out_came_ref, ways.above)
    wait(in_up_ref, in_up_got_ref, in_low_ref, in_low_got_ref)
    in_send_ref[0] = in_up_ref[0] + in_up_got_ref[0]
    in_send_ref[1] = in_low_ref[0] + in_low_got_ref[0]
    in_copies = [
        mail.send(in_send_ref.at[0], in_up_next, ways.across_y),
        mail.send(in_send_ref.at[1], in_low_next, ways.across_x),
    ]
    in_up_keep[...] = in_up_ref[1] + in_up_got_ref[1]
    in_low_keep[...] = in_low_ref[1] + in_low_got_ref[1]
    home = Home(ways, result_out, home_sends, home_recvs)
    for left, to in ((mixed_ref, mixed_t), (normed_ref, normed_t), (projected_ref, projected_t), (self_ref, self_t)):
        wait(left)
        to[...] = turned(left[...])
    wait(text_ref)
    turned_text = turned(text_ref[...])
    block = own_ref.shape[2]
    count = 2 * nz
    part = turned_text.shape[0] // count
    text_t[...] = jnp.zeros_like(text_t)
    for b in range(count):
        text_t[b * block : b * block + part] = turned_text[b * part : (b + 1) * part]
    half = block // 2
    up, low = slice(0, half), slice(half, block)
    homes = (
        (send_up_ref.at[0], send_low_ref.at[0]),
        (send_up_ref.at[1], keep_low_ref.at[0]),
        (keep_up_ref.at[0], send_low_ref.at[1]),
        (keep_up_ref.at[1], keep_low_ref.at[1]),
    )
    copies = []
    wait(g_second_ref, g_query_ref, g_keys_ref, g_values_ref, g_projected_ref, g_first_ref)

    def settle(q):
        copies[q].wait_recv()
        total = own_ref[q] + got_ref[q]
        homes[q][0][...] = total[:, up]
        homes[q][1][...] = total[:, low]

    for q in range(4):
        place = ways.place(q)
        columns = pl.ds(pl.multiple_of(place * piece, piece), piece)
        twice = pl.ds(pl.multiple_of(place % 2 * 2 * piece, piece), 2 * piece)
        pair = jnp.where(place < 2, g_keys_ref[:, twice], g_values_ref[:, twice])
        units = (
            (mixed_t, g_second_ref[:, columns]),
            (normed_t, g_query_ref[:, columns]),
            (projected_t, pair),
            (text_t, g_projected_ref[:, columns]),
            (self_t, g_first_ref[:, columns]),
        )
        for which, ref in ((1 - ways.core, away_ref), (ways.core, own_ref)):
            first = 0
            for left, right in units:
                to = slice(first, first + right.shape[1])
                first += right.shape[1]
                for k in range(nz):
                    ref[q, k, :, to] = dot(left[ways.rows(k, which, block)], right).astype(BF)
            if ref is away_ref:
                copies.append(mail.send(away_ref.at[q], got_ref.at[q], ways.sibling))
        if q == 0:
            wait(result_ref)
            result_copy.wait_recv()
            result_got_ref[...] = (result_ref[...] + result_got_ref[...].astype(F32)).astype(BF)
            slots = result_ref.shape[0] // 2
            for slot in range(2):
                home.send(result_got_ref.at[slot * slots : (slot + 1) * slots], slot)
        else:
            settle(q - 1)
    wait(self_weight_ref)
    g_mix_ref[...] = nt(g_first_ref[...], self_weight_ref[...]).astype(BF)
    settle(3)
    for copy in in_copies:
        copy.wait_recv()
    out_copy.wait_recv()
    wait(out_zero_ref)
    out_next[...] = out_zero_ref[...] + out_came_ref[...]
    mail.finish()
    home.finish()


def middle_parts(place, count, lefts, rights, result, result_away, feeds, weight):
    nz = place.nz
    depth, width = lefts[0].shape[1], rights[0].shape[1]
    piece, block = width // place.seq, depth // place.rows
    columns = piece * len(rights)
    out = jax.ShapeDtypeStruct((2, nz, block // 2, columns), BF)
    big = pltpu.VMEM((4, nz, block, columns), BF)
    operands = [*lefts, *rights, result, result_away, *feeds, weight]
    late = (17, 18, 13, 14, 15, 16, 0, 1, 2, 4, 3, 5, 6, 7, 8, 9, 10, 11, 20, 19)
    return pl.pallas_call(
        with_loads(functools.partial(middle_kernel, (nz, piece)), len(operands), late),
        in_specs=[ANY_SPEC] * len(operands),
        out_specs=[WHOLE_SPEC] * 4
        + [ANY_SPEC, WHOLE_SPEC, ANY_SPEC, WHOLE_SPEC, ANY_SPEC, WHOLE_SPEC, WHOLE_SPEC],
        out_shape=[out] * 4
        + [jax.ShapeDtypeStruct((count, result.shape[0] // count, width), BF)]
        + [jax.ShapeDtypeStruct(feeds[0].shape[1:], BF)] * 4
        + [jax.ShapeDtypeStruct(feeds[4].shape, BF), jax.ShapeDtypeStruct(result.shape, BF)],
        scratch_shapes=[pltpu.VMEM((depth, left.shape[0]), BF) for left in lefts]
        + [big] * 3
        + [pltpu.VMEM(result.shape, BF), pltpu.VMEM(feeds[0].shape, BF)]
        + [pltpu.VMEM(feeds[4].shape, BF)] * 2
        + [pltpu.SemaphoreType.DMA((8,))] * 2
        + [pltpu.SemaphoreType.DMA((2,))] * 2
        + load_scratch(operands, late),
        compiler_params=pltpu.CompilerParams(
            collective_id=2, has_side_effects=True, vmem_limit_bytes=63 * 1024 * 1024
        ),
        cost_estimate=pl.CostEstimate(
            flops=2 * 8 * 512 * depth * width, bytes_accessed=24 << 20, transcendentals=0
        ),
    )(*operands)


def final_kernel(nz, wait, *refs):
    (
        normed_ref,
        input_ref,
        first_ref,
        gain_ref,
        weight_ref,
        gq_ref,
        gk_ref,
        gv_ref,
        k_away_ref,
        v_away_ref,
        upper_ref,
        upper_got_ref,
        lower_ref,
        lower_got_ref,
        in_up_ref,
        in_up_got_ref,
        in_low_ref,
        in_low_got_ref,
        out_last_ref,
        out_got_ref,
        vector_ref,
        projected_ref,
        proj_ref,
    ) = refs[:23]
    (qkv_ref, middle_ref, feed_ref, sum_ref, frames_out, text_out) = refs[23:29]
    (
        out_ref,
        text_ref,
        packed_ref,
        k_got_ref,
        v_got_ref,
        acc_ref,
        turned_ref,
        own_ref,
        away_ref,
        got_ref,
        first_x_ref,
        first_y_ref,
        second_y_ref,
        second_x_ref,
        mid_up_ref,
        mid_low_ref,
        mid_ref,
        mid_ring_ref,
        qkv_ring_ref,
        feed_send_ref,
        feed_ring_ref,
        out_x_ref,
        out_own_ref,
        out_y_ref,
        feed_away_ref,
        feed_other_ref,
        vector_out_ref,
        vector_in_ref,
        text_away_ref,
        text_got_ref,
        send_sems,
        recv_sems,
        home_sends,
        home_recvs,
    ) = refs[29:]
    ways = Ways(nz)
    core, z = ways.core, ways.z
    sibling, across_x, across_y, above = ways.sibling, ways.across_x, ways.across_y, ways.above
    ways.meet(ways.plane() + [ways.above, ways.below])
    mail = Mail(send_sems, recv_sems)
    ring = ring_order(nz)
    half = upper_ref.shape[2]
    feed_half = feed_ring_ref.shape[1] // 2
    tokens, width = normed_ref.shape

    k_copy = mail.send(k_away_ref, k_got_ref, sibling)
    v_copy = mail.send(v_away_ref, v_got_ref, sibling)

    feed_copies, feed_last_copies = [], {}

    def feed_piece(t):
        at = slice(ring[t] * feed_half, (ring[t] + 1) * feed_half)
        return (
            in_up_ref[at].astype(F32) + in_up_got_ref[at].astype(F32),
            in_low_ref[at].astype(F32) + in_low_got_ref[at].astype(F32),
        )

    def feed_step(t):
        upper_part, lower_part = feed_piece(t)
        if t > 0:
            feed_copies[t - 1].wait_recv()
            upper_part += feed_ring_ref[t - 1, :feed_half].astype(F32)
            lower_part += feed_ring_ref[t - 1, feed_half:].astype(F32)
        if t == nz - 1:
            feed_finish(0, upper_part, lower_part)
            return
        feed_send_ref[t, :feed_half] = upper_part.astype(BF)
        feed_send_ref[t, feed_half:] = lower_part.astype(BF)
        feed_copies.append(mail.send(feed_send_ref.at[t], feed_ring_ref.at[t], above))

    wait(in_up_ref, in_up_got_ref, in_low_ref, in_low_got_ref)
    feed_step(0)

    mid_copies = {}
    wait(upper_ref, upper_got_ref, lower_ref, lower_got_ref)
    for k in ring:
        mid_ref[k, :half] = upper_ref[0, k] + upper_got_ref[0, k]
        mid_ref[k, half:] = lower_ref[0, k] + lower_got_ref[0, k]
        mid_copies[k] = (
            mail.send(mid_ref.at[k, :half], mid_up_ref.at[k], across_y),
            mail.send(mid_ref.at[k, half:], mid_low_ref.at[k], across_x),
        )
    wait(normed_ref, gq_ref, gk_ref, gv_ref)
    turned_ref[...] = turned(normed_ref[...])
    packed_ref[:, :width] = gq_ref[...]
    k_copy.wait_recv()
    packed_ref[:, width : 2 * width] = gk_ref[...] + k_got_ref[...]
    v_copy.wait_recv()
    packed_ref[:, 2 * width :] = gv_ref[...] + v_got_ref[...]

    block = own_ref.shape[2]
    columns = own_ref.shape[3]
    core_copies = []
    for q in range(4):
        right = packed_ref[:, pl.ds(pl.multiple_of(ways.place(q) * columns, columns), columns)]
        for which, ref in ((1 - core, away_ref), (core, own_ref)):
            for k in range(nz):
                ref[q, k] = dot(turned_ref[ways.rows(k, which, block)], right).astype(BF)
            if ref is away_ref:
                core_copies.append(mail.send(away_ref.at[q], got_ref.at[q], sibling))

    def out_step():
        for q in range(2):
            out_copies[q].wait_recv()
            out_own_ref[q] = out_ref[2 + q] + out_x_ref[q]
            if q == 0:
                out_copies.append(mail.send(out_own_ref.at[0], out_y_ref, across_y))

    def out_last():
        out_copies[2].wait_recv()
        total = out_own_ref[1].astype(F32) + out_y_ref[...].astype(F32)
        feed_finish(1, total[:feed_half], total[feed_half:])

    def feed_finish(kind, even, odd):
        away = jnp.where(core == 0, odd, even)
        own = jnp.where(core == 0, even, odd)
        across = own.shape[1]
        feed_away_ref[kind] = away
        feed_last_copies[kind] = mail.send(feed_away_ref.at[kind], feed_other_ref.at[kind], sibling)
        at = pl.ds(pl.multiple_of(core * across, across), across)
        feed_ref[kind, :, at] = own

    def feed_last(kind):
        feed_last_copies[kind].wait_recv()
        across = feed_other_ref.shape[2]
        at = pl.ds(pl.multiple_of((1 - core) * across, across), across)
        feed_ref[kind, :, at] = feed_other_ref[kind]

    wait(projected_ref, proj_ref)
    text_ref[...] = nt(projected_ref[...], proj_ref[...])
    text_rows = text_ref.shape[0] // 2
    text_away_ref[...] = text_ref[text_rows:].astype(BF)
    text_copy = mail.send(text_away_ref, text_got_ref, sibling)

    def core_step(q):
        core_copies[q].wait_recv()
        own_ref[q] = own_ref[q] + got_ref[q]

    mid_ring = {}

    def mid_send(t):
        k = ring[t]
        up, low = mid_copies[k]
        up.wait()
        low.wait()
        mid_ref[k, :half] = upper_ref[1, k] + upper_got_ref[1, k] + mid_up_ref[k]
        mid_ref[k, half:] = lower_ref[1, k] + lower_got_ref[1, k] + mid_low_ref[k]
        if t > 0:
            mid_ring[t - 1].wait_recv()
        if t == nz - 1:
            middle_ref[...] = mid_ref[k].astype(F32) + mid_ring_ref[t - 1].astype(F32)
            return
        if t > 0:
            mid_ref[k] = mid_ref[k] + mid_ring_ref[t - 1]
        mid_ring[t] = mail.send(mid_ref.at[k], mid_ring_ref.at[t], above)

    qkv_ring = {}

    def qkv_send(t):
        k = ring[t]
        second[k][0].wait_recv()
        own_ref[3, k, up] = own_ref[3, k, up] + second_y_ref[k]
        second[k][1].wait_recv()
        own_ref[3, k, low] = own_ref[3, k, low] + second_x_ref[k]
        if t > 0:
            qkv_ring[t - 1].wait_recv()
        if t == nz - 1:
            qkv_ref[...] = own_ref[3, k].astype(F32) + qkv_ring_ref[t - 1].astype(F32)
            return
        if t > 0:
            own_ref[3, k] = own_ref[3, k] + qkv_ring_ref[t - 1]
        qkv_ring[t] = mail.send(own_ref.at[3, k], qkv_ring_ref.at[t], above)

    up, low = slice(0, half), slice(half, 2 * half)
    core_step(0)
    upper_first = [mail.send(own_ref.at[0, :, up], first_x_ref.at[0], across_x)]
    lower_first = [mail.send(own_ref.at[0, :, low], first_y_ref.at[0], across_y)]
    core_step(1)
    upper_first.append(mail.send(own_ref.at[1, :, up], first_x_ref.at[1], across_x))
    core_step(2)
    lower_first.append(mail.send(own_ref.at[2, :, low], first_y_ref.at[1], across_y))
    core_step(3)
    wait(out_last_ref, out_got_ref)
    out_ref[...] = out_last_ref[...] + out_got_ref[...]
    out_copies = [mail.send(out_ref.at[q], out_x_ref.at[q], across_x) for q in range(2)]

    slots = tokens // 2
    text_copy.wait_recv()
    text_got_ref[...] = (text_ref[:text_rows] + text_got_ref[...].astype(F32)).astype(BF)
    text_home = Home(ways, text_out, home_sends.at[0], home_recvs.at[0])
    for slot in range(2):
        at = slice(slot * text_rows // 2, (slot + 1) * text_rows // 2)
        text_home.send(text_got_ref.at[at], slot)

    wait(weight_ref)
    acc_ref[...] = nt(packed_ref[:, :width], weight_ref[:, :width])
    acc_ref[...] += nt(packed_ref[:, width : 2 * width], weight_ref[:, width : 2 * width])
    mid_send(0)
    feed_step(1)
    acc_ref[...] += nt(packed_ref[:, 2 * width :], weight_ref[:, 2 * width :])
    wait(input_ref, first_ref, gain_ref)
    gain_sum = jnp.zeros((1, width), F32)
    shift_sum = jnp.zeros((1, width), F32)
    chunk = min(128, tokens)
    for m in range(tokens // chunk):
        at = slice(m * chunk, (m + 1) * chunk)
        grad, gain_part, shift_part = norm_backward(
            input_ref[at].astype(F32), gain_ref[...], acc_ref[at]
        )
        k_got_ref[at] = (first_ref[at] + grad).astype(BF)
        gain_sum += gain_part[None]
        shift_sum += shift_part[None]
    wait(vector_ref)
    vector_out_ref[0] = vector_ref[...]
    vector_out_ref[0, 0:1] = gain_sum
    vector_out_ref[0, 1:2] = shift_sum
    vector_copy = mail.send(vector_out_ref.at[0], vector_in_ref.at[0], sibling)
    mid_send(1)

    vector_copy.wait_recv()
    vector_out_ref[1] = vector_out_ref[0] + vector_in_ref[0]
    vector_copy = mail.send(vector_out_ref.at[1], vector_in_ref.at[1], across_x)
    for t in range(2, nz):
        feed_step(t)
        if t < nz - 1:
            mid_send(t)
    vector_copy.wait_recv()
    vector_out_ref[2] = vector_out_ref[1] + vector_in_ref[1]
    vector_copy = mail.send(vector_out_ref.at[2], vector_in_ref.at[2], across_y)

    upper_first[0].wait_recv()
    own_ref[2, :, up] = own_ref[2, :, up] + first_x_ref[0]
    lower_first[0].wait_recv()
    own_ref[1, :, low] = own_ref[1, :, low] + first_y_ref[0]
    second = {}
    for k in ring:
        second[k] = (
            mail.send(own_ref.at[2, k, up], second_y_ref.at[k], across_y),
            mail.send(own_ref.at[1, k, low], second_x_ref.at[k], across_x),
        )
    frames_home = Home(ways, frames_out, home_sends.at[1], home_recvs.at[1])
    for slot in range(2):
        frames_home.send(k_got_ref.at[slot * slots : (slot + 1) * slots], slot)
    vector_copy.wait_recv()
    vector_out_ref[3] = vector_out_ref[2] + vector_in_ref[2]
    vector_copy = mail.send(vector_out_ref.at[3], vector_in_ref.at[3], above)
    upper_first[1].wait_recv()
    own_ref[3, :, up] = own_ref[3, :, up] + first_x_ref[1]
    lower_first[1].wait_recv()
    own_ref[3, :, low] = own_ref[3, :, low] + first_y_ref[1]
    out_step()
    mid_send(nz - 1)
    feed_last(0)
    total = vector_out_ref[3]
    for t in range(nz - 1):
        vector_copy.wait_recv()
        total = total + vector_in_ref[3 + t]
        if t < nz - 2:
            vector_copy = mail.send(vector_in_ref.at[3 + t], vector_in_ref.at[4 + t], above)
    sum_ref[...] = total
    for t in range(nz):
        qkv_send(t)
    out_last()
    feed_last(1)
    text_home.finish()
    frames_home.finish()
    for number, copy in enumerate(mail.sent):
        if not any(copy is c for pair in mid_copies.values() for c in pair):
            copy.wait_send()


FINAL_LOADS = (14, 15, 16, 17, 10, 11, 12, 13, 0, 5, 6, 7, 18, 19, 21, 22, 4, 1, 2, 3, 20)


def final_sums(place, count, *operands):
    nz = place.nz
    normed, weight, upper, in_up = operands[0], operands[4], operands[10], operands[14]
    vectors, projected, proj = operands[20], operands[21], operands[22]
    words, text_width = projected.shape[0], proj.shape[0]
    tokens, width = normed.shape
    block, piece = width // place.rows, weight.shape[1] // place.seq
    half, middle = block // 2, upper.shape[3]
    feed_width = in_up.shape[1]
    feed_rows = width // nz
    copies = 2 + 3 + nz - 1 + 2 + 2 * nz + 1 + 4 + 3 + nz - 1 + 4 + 2 * nz + 2 * (nz - 1)
    vmem = pltpu.VMEM
    return pl.pallas_call(
        with_loads(functools.partial(final_kernel, nz), len(operands), FINAL_LOADS),
        in_specs=[ANY_SPEC] * len(operands),
        out_specs=[WHOLE_SPEC] * 4 + [ANY_SPEC] * 2,
        out_shape=[
            jax.ShapeDtypeStruct((block, piece), F32),
            jax.ShapeDtypeStruct((block, middle), F32),
            jax.ShapeDtypeStruct((2, block, 2 * feed_width), F32),
            jax.ShapeDtypeStruct(vectors.shape, F32),
            jax.ShapeDtypeStruct((count, tokens // count, width), BF),
            jax.ShapeDtypeStruct((count, words // 2 // count, text_width), BF),
        ],
        scratch_shapes=[
            vmem((4, feed_rows, feed_width), BF),
            vmem((words, text_width), F32),
            vmem((tokens, 3 * width), BF),
            vmem((tokens, width), BF),
            vmem((tokens, width), BF),
            vmem((tokens, width), F32),
            vmem((width, tokens), BF),
            vmem((4, nz, block, piece), BF),
            vmem((4, nz, block, piece), BF),
            vmem((4, nz, block, piece), BF),
            vmem((2, nz, half, piece), BF),
            vmem((2, nz, half, piece), BF),
            vmem((nz, half, piece), BF),
            vmem((nz, half, piece), BF),
            vmem((nz, half, middle), BF),
            vmem((nz, half, middle), BF),
            vmem((nz, block, middle), BF),
            vmem((nz - 1, block, middle), BF),
            vmem((nz - 1, block, piece), BF),
            vmem((nz - 1, feed_rows, feed_width), BF),
            vmem((nz - 1, feed_rows, feed_width), BF),
            vmem((2, feed_rows, feed_width), BF),
            vmem((2, feed_rows, feed_width), BF),
            vmem((feed_rows, feed_width), BF),
            vmem((2, feed_rows // 2, feed_width), F32),
            vmem((2, feed_rows // 2, feed_width), F32),
            vmem((4,) + vectors.shape, F32),
            vmem((2 + nz,) + vectors.shape, F32),
            vmem((words // 2, text_width), BF),
            vmem((words // 2, text_width), BF),
            pltpu.SemaphoreType.DMA((copies,)),
            pltpu.SemaphoreType.DMA((copies,)),
            pltpu.SemaphoreType.DMA((2, 2)),
            pltpu.SemaphoreType.DMA((2, 2)),
        ]
        + load_scratch(operands, FINAL_LOADS),
        compiler_params=pltpu.CompilerParams(
            collective_id=1, has_side_effects=True, vmem_limit_bytes=63 * 1024 * 1024
        ),
        cost_estimate=pl.CostEstimate(
            flops=60 * tokens * width * weight.shape[1], bytes_accessed=40 << 20, transcendentals=0
        ),
    )(*operands)


def last_kernel(padding, qkv_ref, middle_ref, feed_ref, frames_ref, text_ref, *outs):
    frames_out, text_out, qkv_out, self_out, query_out, proj_out, kv_out, cross_out, in_out, out_out = outs
    piece = self_out.shape[1]
    frames_out[...] = frames_ref[...].astype(F32)
    text_out[...] = text_ref[...].astype(F32)
    qkv_out[...] = qkv_ref[...]
    cross_out[...] = middle_ref[:, :piece]
    query_out[...] = middle_ref[:, piece : 2 * piece]
    kv_out[...] = middle_ref[:, 2 * piece : 4 * piece]
    proj_out[...] = middle_ref[: proj_out.shape[0], 4 * piece : 5 * piece]
    self_out[...] = middle_ref[:, 5 * piece :]
    in_out[...] = feed_ref[0]
    out_out[...] = jnp.swapaxes(feed_ref[1], 0, 1)


def last_step(padding, piece, qkv, middle, feed_sums, frames, text):
    block, across = qkv.shape[0], feed_sums.shape[2]
    shapes = [
        frames.shape,
        text.shape,
        qkv.shape,
        (block, piece),
        (block, piece),
        (block - padding, piece),
        (block, 2 * piece),
        (block, piece),
        (block, across),
        (across, block),
    ]
    return pl.pallas_call(
        functools.partial(last_kernel, padding),
        in_specs=[WHOLE_SPEC] * 5,
        out_specs=[WHOLE_SPEC] * len(shapes),
        out_shape=[jax.ShapeDtypeStruct(shape, F32) for shape in shapes],
        compiler_params=pltpu.CompilerParams(vmem_limit_bytes=MOST_VMEM),
    )(qkv, middle, feed_sums, frames, text)


def permuted_sums(place, meta, in_up, in_low, out_sum, lefts, rights, normed_self, backward_self):
    nx, ny, nz, seq = place.nx, place.ny, place.nz, place.seq
    width = normed_self.shape[1]
    block, piece = width // place.rows, width // seq
    middle_own, middle_away = weight_parts(
        place, meta, lefts[:3] + lefts[2:4], rights[:5]
    )
    out_own, out_away = weight_parts(place, meta, lefts[4:], rights[5:])
    middle_got = place.swap_core(middle_away)
    out_got = place.swap_core(out_away)
    grad_packed = backward_self(middle_got, out_got)
    in_up = ring_sum([lambda a=in_up[k]: a.astype(F32) for k in range(ny)], place.next_y)
    in_low = ring_sum([lambda a=in_low[k]: a.astype(F32) for k in range(nx)], place.next_x)
    in_both = jnp.stack([in_up, in_low]).astype(BF).reshape(2, nz, block, -1)
    in_both = ring_sum([lambda a=in_both[:, k]: a.astype(F32) for k in range(nz)], place.next_z)
    out_sum = out_sum.reshape((nx, ny) + out_sum.shape[1:])
    out_sum = ring_sum([lambda a=out_sum[k]: a.astype(F32) for k in range(nx)], place.next_x)
    out_sum = out_sum.astype(BF)
    out_sum = ring_sum([lambda a=out_sum[k]: a.astype(F32) for k in range(ny)], place.next_y)
    feed_own = jnp.stack([in_both, out_sum.reshape(2, block, -1)])
    feed_got = place.swap_core(pick(feed_own, 1 - place.core, 1))
    feed_own = pick(feed_own, place.core, 1)
    low = jnp.where(place.core == 0, feed_own, feed_got)
    high = jnp.where(place.core == 0, feed_got, feed_own)
    sum_feed = jnp.concatenate([low, high], axis=2)

    def middle_piece(k):
        at = slice(k * block, (k + 1) * block)
        return lambda: middle_own[:, at].astype(F32) + middle_got[:, at].astype(F32)

    middle = ring_sum([middle_piece(k) for k in range(nz)], place.next_z).astype(BF)
    spread = jnp.concatenate(
        [
            middle[0].reshape(block, seq, -1),
            middle[1].reshape(block, seq, -1),
            jnp.concatenate([middle[2], middle[3]], axis=1).reshape(block, seq, -1),
            middle[4].reshape(block, seq, -1),
        ],
        axis=2,
    ).reshape(block, ny, nx, -1)

    def shifted(array, index, number, length, axis):
        return lambda: pick(array, (index + 1 + number) % length, axis).astype(F32)

    spread = ring_sum([shifted(spread, place.x, k, nx, 2) for k in range(nx)], place.next_x).astype(BF)
    spread = ring_sum([shifted(spread, place.y, k, ny, 1) for k in range(ny)], place.next_y)
    relative_parts = place.relative_columns(grad_packed, True)
    qkv_own, qkv_away = weight_parts(place, meta, [normed_self], [relative_parts])
    qkv_got = place.swap_core(qkv_away)

    def columns(array):
        return array[0].reshape(array.shape[1], nx, ny, -1)

    def natural(array):
        return jnp.stack(
            [
                jnp.stack(
                    [
                        pick(array[0].reshape(array.shape[1], seq, -1), place.offset(i, j), 1)
                        for i in range(ny)
                    ],
                    axis=1,
                )
                for j in range(nx)
            ],
            axis=1,
        )

    last_own = jnp.concatenate([columns(qkv_own), natural(out_own)], axis=3)
    last_got = jnp.concatenate([columns(qkv_got), natural(out_got)], axis=3)
    last = (last_own.astype(F32) + last_got.astype(F32)).astype(BF)
    last = last.reshape(nz, 2, block // 2, nx, ny, -1)
    upper = ring_sum([lambda k=k: last[:, 0, :, k].astype(F32) for k in range(nx)], place.next_x).astype(BF)
    lower = ring_sum([lambda k=k: last[:, 1, :, :, k].astype(F32) for k in range(ny)], place.next_y).astype(BF)
    upper = ring_sum([lambda a=upper[:, :, k]: a.astype(F32) for k in range(ny)], place.next_y)
    lower = ring_sum([lambda a=lower[:, :, k]: a.astype(F32) for k in range(nx)], place.next_x)
    last = jnp.stack([upper, lower], axis=1).astype(BF)
    last = ring_sum([lambda a=last[k]: a.astype(F32) for k in range(nz)], place.next_z)
    last = last.reshape(block, -1)
    sum_self_qkv, sum_self_out = last[:, : 3 * piece], last[:, 3 * piece :]

    return sum_feed, spread, sum_self_qkv, sum_self_out, grad_packed


def shards(
    frames,
    text_states,
    clip_lengths,
    text_lengths,
    self_gain,
    self_shift,
    self_qkv,
    self_out,
    cross_gain,
    cross_shift,
    cross_query,
    text_proj,
    text_bias,
    cross_kv,
    cross_out,
    feed_gain,
    feed_shift,
    feed_in,
    feed_out,
    grad_out,
):
    place = Place()
    count = frames.shape[0]
    width = frames.shape[2]
    text_total = text_states.shape[1] * place.seq

    nx, ny, nz, seq = place.nx, place.ny, place.nz, place.seq
    block, piece = width // place.rows, width // seq
    kernels = nx == 2 and ny == 2 and nz == 4 and piece % 128 == 0
    lengths = jnp.concatenate([clip_lengths, text_lengths], axis=1)
    if kernels:
        padded = jnp.zeros((8, 128), jnp.int32).at[:count, : 2 * CLIPS].set(lengths)
        (
            layer_raw,
            normed_self,
            queries,
            pair,
            pair_other,
            text_input,
            projected,
            text_pair,
            lengths_other,
        ) = entry(
            place,
            frames,
            text_states,
            padded,
            self_gain,
            self_shift,
            self_qkv,
            text_proj,
            text_bias,
            cross_kv,
        )
        lengths_other = lengths_other[:count, : 2 * CLIPS]
        layer_input = layer_raw.astype(F32)
    else:
        lengths_other = place.swap_core(lengths)
        text_half = place.to_rows(text_states)
        layer_raw = place.to_rows(frames)
        text_input = jnp.concatenate([text_half, place.swap_core(text_half)], axis=0)
        cotangent = place.to_rows(grad_out)
        projected = (dot(text_input, text_proj) + text_bias).astype(BF)
        text_pair = dot(projected, cross_kv).astype(BF)
        layer_input = layer_raw.astype(F32)
        normed_self = layer_norm(layer_input, self_gain, self_shift)
        pair = dot(normed_self, self_qkv[:, width:]).astype(BF)
        pair_other = place.swap_core(pair)
        queries = dot(normed_self, self_qkv[:, :width]).astype(BF)
    mine = place.spot // count == place.core
    row_lengths = pick(jnp.where(mine, lengths, lengths_other), place.spot % count, 0)

    if kernels:
        self_mix, self_lse, cotangent = self_forward_and_gather(
            place, row_lengths, queries, pair, pair_other, grad_out
        )
    else:
        self_mix, self_lse, _ = self_forward(row_lengths, queries, pair, pair_other)
    cotangent_other = place.swap_core(cotangent)
    first = layer_input + dot(self_mix, self_out)
    normed_cross = layer_norm(first, cross_gain, cross_shift)
    cross_queries = dot(normed_cross, cross_query).astype(BF)
    cross_mix, cross_lse, _ = cross_forward(row_lengths, cross_queries, text_pair)
    second = first + dot(cross_mix, cross_out)
    normed_feed = layer_norm(second, feed_gain, feed_shift)

    meta = jnp.stack([place.core, place.x, place.y, place.z]).astype(jnp.int32)
    normed_other = place.swap_core(normed_feed)
    fed = feed(
        place, meta, normed_feed, normed_other, cotangent, cotangent_other, feed_in, feed_out
    )
    result, result_away, grad_normed_feed, grad_away = fed[:4]
    up_parts, low_parts, out_parts = fed[4 : 4 + nx], fed[4 + nx : 4 + nx + ny], fed[4 + nx + ny :]
    grad_normed_feed = grad_normed_feed + place.swap_core(grad_away).astype(F32)

    grad_part, grad_feed_gain, grad_feed_shift = norm_backward(second, feed_gain, grad_normed_feed)
    grad_second = cotangent.astype(F32) + grad_part
    grad_second_branch = grad_second.astype(BF)
    grad_cross_mix = dot(grad_second_branch, cross_out, 1, 1).astype(BF)
    grad_cross_queries, grad_text_keys, grad_text_values, _ = cross_backward(
        row_lengths,
        cross_queries,
        text_pair,
        grad_cross_mix,
        cross_mix,
        cross_lse,
    )
    grad_normed_cross = dot(grad_cross_queries, cross_query, 1, 1)
    grad_part, grad_cross_gain, grad_cross_shift = norm_backward(first, cross_gain, grad_normed_cross)
    grad_first = grad_second + grad_part
    grad_first_branch = grad_first.astype(BF)

    grad_pair = jnp.concatenate([grad_text_keys, grad_text_values], axis=1)
    grad_projected = dot(grad_pair, cross_kv, 1, 1).astype(BF)
    grad_text_bias = jnp.sum(grad_projected.astype(F32), axis=0)
    padding = block - text_input.shape[1] // place.rows
    lefts = [cross_mix, normed_cross, projected, text_input, self_mix]
    rights = [
        grad_second_branch,
        grad_cross_queries,
        grad_text_keys,
        grad_text_values,
        grad_projected,
        grad_first_branch,
    ]
    result = second + result

    def backward_self(grad_self_mix, *before):
        return self_backward(
            row_lengths,
            queries,
            pair,
            pair_other,
            grad_self_mix,
            self_mix,
            self_lse,
            before=before,
        )[:5]

    def vector_list(grad_gain, grad_shift):
        return jnp.stack(
            [
                grad_gain,
                grad_shift,
                grad_cross_gain,
                grad_cross_shift,
                grad_text_bias,
                grad_feed_gain,
                grad_feed_shift,
                jnp.zeros_like(grad_feed_shift),
            ]
        )

    if kernels:
        (
            send_up,
            send_low,
            keep_up,
            keep_low,
            result,
            in_up,
            in_up_got,
            in_low,
            in_low_got,
            out_sum,
            grad_self_mix,
        ) = middle_parts(
            place,
            count,
            lefts,
            rights,
            result,
            result_away,
            (
                up_parts[1],
                place.next_x(up_parts[0]),
                low_parts[1],
                place.next_y(low_parts[0]),
                out_parts[1],
                place.next_z(out_parts[2]),
                out_parts[0],
            ),
            self_out,
        )
        up_got, low_got = place.next_x(send_up), place.next_y(send_low)
        out_got = place.next_z(out_sum)
        grads = backward_self(grad_self_mix)
        nothing = jnp.zeros_like(grad_feed_shift)
        sum_self_qkv, spread, sum_feed, vectors, grad_frames, grad_text = final_sums(
            place,
            count,
            normed_self,
            layer_raw,
            grad_first,
            self_gain[None],
            self_qkv,
            *grads,
            keep_up,
            up_got,
            keep_low,
            low_got,
            in_up,
            in_up_got,
            in_low,
            in_low_got,
            out_parts[3],
            out_got,
            vector_list(nothing, nothing),
            grad_projected,
            text_proj,
        )
        (
            grad_frames,
            grad_text,
            sum_self_qkv,
            sum_self_out,
            sum_cross_query,
            sum_text_proj,
            sum_cross_kv,
            sum_cross_out,
            sum_feed_in,
            sum_feed_out,
        ) = last_step(padding, piece, sum_self_qkv, spread, sum_feed, grad_frames, grad_text)
    else:

        def packed_self(*before):
            grads = backward_self(dot(grad_first_branch, self_out, 1, 1).astype(BF), *before)
            keys = (grads[1].astype(F32) + place.swap_core(grads[3]).astype(F32)).astype(BF)
            values = (grads[2].astype(F32) + place.swap_core(grads[4]).astype(F32)).astype(BF)
            return jnp.concatenate([grads[0], keys, values], axis=1)

        in_up = ring_sum([lambda a=a: a.astype(F32) for a in up_parts], place.next_x).astype(BF)
        in_low = ring_sum([lambda a=a: a.astype(F32) for a in low_parts], place.next_y).astype(BF)
        out_sum = ring_sum([lambda a=a: a.astype(F32) for a in out_parts], place.next_z).astype(BF)
        grad_text = dot(grad_projected, text_proj, 1, 1)
        text_blocks = text_input.reshape(text_total, place.rows, -1)
        text_padded = jnp.pad(text_blocks, ((0, 0), (0, 0), (0, padding))).reshape(text_total, width)
        lefts[3] = text_padded
        sum_feed, spread, sum_self_qkv, sum_self_out, grad_packed = permuted_sums(
            place, meta, in_up, in_low, out_sum, lefts, rights, normed_self, packed_self
        )
        result = (result + place.swap_core(result_away).astype(F32)).astype(BF)
        result = place.from_rows(result, count)
        grad_normed_self = dot(grad_packed, self_qkv, 1, 1)
        grad_part, grad_gain, grad_shift = norm_backward(layer_input, self_gain, grad_normed_self)
        grad_frames = place.from_rows((grad_first + grad_part).astype(BF), count)
        half = grad_text.shape[0] // 2
        text_away = place.swap_core(grad_text[half:].astype(BF))
        grad_text = (grad_text[:half] + text_away.astype(F32)).astype(BF)
        grad_text = place.from_rows(grad_text, count)
        vectors = place.vector_sum(vector_list(grad_gain, grad_shift))
        sum_cross_out, sum_cross_query = spread[:, :piece], spread[:, piece : 2 * piece]
        sum_cross_kv, sum_text_proj = spread[:, 2 * piece : 4 * piece], spread[:, 4 * piece : 5 * piece]
        sum_text_proj = sum_text_proj[: block - padding]
        sum_feed_in, sum_feed_out = sum_feed[0], jnp.swapaxes(sum_feed[1], 0, 1)
        grad_frames, grad_text = grad_frames.astype(F32), grad_text.astype(F32)
    vectors = pick(vectors.reshape(8, seq, width // seq), place.spot, 1)
    return (
        result,
        grad_frames,
        grad_text,
        vectors[0],
        vectors[1],
        sum_self_qkv,
        sum_self_out,
        vectors[2],
        vectors[3],
        sum_cross_query,
        sum_text_proj,
        vectors[4],
        sum_cross_kv,
        sum_cross_out,
        vectors[5],
        vectors[6],
        sum_feed_in,
        sum_feed_out,
    )


def solution(mesh):
    split, copied, table = P(ROWS, SEQ, None), P(), P(ROWS, None)
    vector, matrix = P(SEQ), P(ROWS, SEQ)
    return jax.shard_map(
        shards,
        mesh=mesh,
        in_specs=(split, split, table, table) + (copied,) * 15 + (split,),
        out_specs=(
            (split,) * 3
            + (vector, vector, matrix, matrix)
            + (vector, vector, matrix, matrix)
            + (vector, matrix, matrix)
            + (vector, vector, matrix, P(SEQ, ROWS))
        ),
        check_vma=False,
    )
```

```python
import functools
import math

import jax
import jax.numpy as jnp
from jax import lax
from jax.experimental import pallas as pl
from jax.experimental.pallas import tpu as pltpu
from jax.sharding import PartitionSpec as P

HD = 64
PAIR = 2 * HD
EPSILON = 1e-05
MASKED = -1e30
CLIPS = 4
ROWS = "rows"
SEQ = "seq"
BF = jnp.bfloat16
F32 = jnp.float32
VMEM_LIMIT = 48 * 1024 * 1024
MOST_VMEM = 62 * 1024 * 1024


def dot(left, right, left_dim=1, right_dim=0):
    return lax.dot_general(
        left, right, (((left_dim,), (right_dim,)), ((), ())), preferred_element_type=F32
    )


def pick(array, index, axis):
    return lax.dynamic_index_in_dim(array, index, axis, keepdims=False)


def after(value, *others):
    return lax.optimization_barrier((value,) + others)[0]


class Place:
    def __init__(self):
        self.rows, self.seq = lax.axis_size(ROWS), lax.axis_size(SEQ)
        self.nz = self.rows // 2
        self.nx = math.isqrt(self.seq)
        self.ny = self.seq // self.nx
        row, self.spot = lax.axis_index(ROWS), lax.axis_index(SEQ)
        self.core, self.z = row % 2, row // 2
        self.x, self.y = self.spot % self.nx, self.spot // self.nx
        self.owner = [0 if 4 * s // self.seq in (0, 3) else 1 for s in range(self.seq)]
        self.members = [[s for s in range(self.seq) if self.owner[s] == c] for c in (0, 1)]
        self.rank = [self.members[self.owner[s]].index(s) for s in range(self.seq)]

    def permute(self, value, target):
        pairs = []
        for z in range(self.nz):
            for c in range(2):
                for s in range(self.seq):
                    tz, tc, ts = target(z, c, s)
                    pairs.append(((2 * z + c) * self.seq + s, (2 * tz + tc) * self.seq + ts))
        return lax.ppermute(value, (ROWS, SEQ), pairs)

    def swap_core(self, value):
        return self.permute(value, lambda z, c, s: (z, 1 - c, s))

    def next_z(self, value):
        return self.permute(value, lambda z, c, s: ((z + 1) % self.nz, c, s))

    def next_x(self, value):
        nx = self.nx
        return self.permute(value, lambda z, c, s: (z, c, s // nx * nx + (s % nx + 1) % nx))

    def next_y(self, value):
        return self.permute(value, lambda z, c, s: (z, c, (s + self.nx) % self.seq))

    def to_rows(self, value):
        count = value.shape[0]
        my_rank = jnp.array(self.rank, jnp.int32)[self.spot]
        got = []
        for t in range(count):

            def target(z, c, s, t=t):
                return z, self.owner[s], c * count + (t + self.rank[s]) % count

            got.append(self.permute(pick(value, (t + my_rank) % count, 0), target))
        stacked = jnp.stack(got)
        here = self.spot % count
        return jnp.concatenate([pick(stacked, (here - k) % count, 0) for k in range(count)], axis=0)

    def from_rows(self, value, count):
        my_rank = jnp.array(self.rank, jnp.int32)[self.spot]
        slots = value.reshape(count, value.shape[0] // count, value.shape[1])
        here = self.spot % count
        got = []
        for t in range(count):

            def target(z, c, s, t=t):
                return z, s // count, self.members[c][(s % count - t) % count]

            got.append(self.permute(pick(slots, (here - t) % count, 0), target))
        stacked = jnp.stack(got)
        return jnp.stack([pick(stacked, (i - my_rank) % count, 0) for i in range(count)])

    def positions(self, total, core):
        quarter = total // 4
        inner = jnp.arange(quarter, dtype=jnp.int32)
        return jnp.concatenate([inner + core * quarter, inner + (3 - core) * quarter])

    def offset(self, i, j):
        return (self.y + 1 + i) % self.ny * self.nx + (self.x + 1 + j) % self.nx

    def relative_columns(self, value, outer_x):
        blocks = value.reshape(value.shape[0], self.seq, -1)
        if outer_x:
            order = [self.offset(i, j) for j in range(self.nx) for i in range(self.ny)]
        else:
            order = [self.offset(i, j) for i in range(self.ny) for j in range(self.nx)]
        return jnp.concatenate([pick(blocks, place, 1) for place in order], axis=1)


    def vector_sum(self, value):
        bit = 1
        while bit < self.rows:
            value = value + self.permute(
                value,
                lambda z, c, s: ((2 * z + c ^ bit) // 2, (2 * z + c ^ bit) % 2, s),
            )
            bit *= 2
        bit = 1
        while bit < self.seq:
            value = value + self.permute(value, lambda z, c, s: (z, c, s ^ bit))
            bit *= 2
        return value


def ring_order(count):
    return list(range(count - 2, -1, -1)) + [count - 1]


def ring_sum(pieces, send):
    order = ring_order(len(pieces))
    value = pieces[order[0]]()
    for k in order[1:]:
        value = pieces[k]() + send(value.astype(BF)).astype(F32)
    return value


def normalize(values):
    centered = values - jnp.mean(values, axis=-1, keepdims=True)
    scale = lax.rsqrt(jnp.mean(centered * centered, axis=-1, keepdims=True) + EPSILON)
    return centered * scale, scale


def layer_norm(values, gain, shift):
    return (normalize(values)[0] * gain + shift).astype(BF)


def norm_backward(values, gain, cotangent):
    normal, scale = normalize(values)
    grown = cotangent * gain
    inner = jnp.mean(grown, axis=-1, keepdims=True)
    along = jnp.mean(grown * normal, axis=-1, keepdims=True)
    grad = scale * (grown - inner - normal * along)
    return grad, jnp.sum(cotangent * normal, axis=0), jnp.sum(cotangent, axis=0)


def nt(left, right):
    return dot(left, right, 1, 1)


def head_lanes(values, head):
    lane = lax.broadcasted_iota(jnp.int32, values.shape, 1)
    return jnp.where((lane < HD) == (head == 0), values, jnp.zeros_like(values))


def turned(values):
    return jnp.swapaxes(values.astype(F32), 0, 1).astype(BF)


def running(lengths_ref, first):
    ends, total = [], 0
    for c in range(CLIPS):
        total = total + lengths_ref[first + c]
        ends.append(total)
    return ends


def spans(start, length, axis, ends):
    shape = (length, 1) if axis == 0 else (1, length)
    positions = lax.broadcasted_iota(jnp.int32, shape, axis) + start
    return sum((positions >= end).astype(jnp.int32) for end in ends)


def segment_bias(key_segment, query_segment, causal):
    allowed = key_segment == query_segment
    if causal:
        key = lax.broadcasted_iota(jnp.int32, allowed.shape, 0)
        query = lax.broadcasted_iota(jnp.int32, allowed.shape, 1)
        allowed = allowed & (key <= query)
    return jnp.where(allowed, 0.0, MASKED).astype(F32)


def forward_heads(queries, blocks, lse_ref, at):
    parts = []
    for head in range(2):
        query = head_lanes(queries, head)
        scores = [nt(keys, query) + bias() for keys, _, bias in blocks]
        highest = functools.reduce(
            jnp.maximum, [jnp.max(s, axis=0, keepdims=True) for s in scores]
        )
        weights = [jnp.exp(s - highest) for s in scores]
        total = sum(jnp.sum(w, axis=0, keepdims=True) for w in weights)
        mixed = sum(
            dot(values[head * HD : (head + 1) * HD], w.astype(BF))
            for (_, values, _), w in zip(blocks, weights)
        )
        parts.append(mixed * (1.0 / total))
        lse_ref[0, head : head + 1, at] = highest + jnp.log(total)
    return jnp.swapaxes(jnp.concatenate(parts, axis=0), 0, 1).astype(BF)


def backward_heads(queries, grads, mixed, blocks, lse_ref, at):
    product = jnp.swapaxes(grads.astype(F32) * mixed.astype(F32), 0, 1)
    parts = []
    for head in range(2):
        query, grad = head_lanes(queries, head), head_lanes(grads, head)
        rows = slice(head * HD, (head + 1) * HD)
        inner = jnp.sum(product[rows], axis=0, keepdims=True)
        totals = lse_ref[0, head : head + 1, at]
        grad_query = None
        for keys, turned_keys, values, bias, sums in blocks:
            weights = jnp.exp(nt(keys, query) + bias() - totals)
            scores = (weights * (nt(values, grad) - inner)).astype(BF)
            add_to(sums, 0, dot(scores, query))
            add_to(sums, 1, dot(weights.astype(BF), grad))
            term = dot(turned_keys[rows], scores)
            grad_query = term if grad_query is None else grad_query + term
        parts.append(grad_query)
    return (jnp.swapaxes(jnp.concatenate(parts, axis=0), 0, 1) * HD**-0.5).astype(BF)


def add_to(sums, index, term):
    sums[index] = term if sums[index] is None else sums[index] + term


def scaled(values):
    return values * jnp.array(HD**-0.5, BF)


def self_plan(core):
    if core == 0:
        return [(0, 0, 0)], [(0, 0, 1), (0, 1, 2), (1, 0, 3), (1, 1, 4)]
    return [(0, 0, 0), (1, 0, 4)], [(0, 0, 1), (0, 1, 2), (1, 0, 3)]


def self_biases(core, lengths_ref, bias_ref):
    length = bias_ref.shape[1]
    ends = running(lengths_ref, 0)
    quarters = (core, 3 - core)
    keys = [spans(q * length, length, 0, ends) for q in quarters]
    queries = [spans(q * length, length, 1, ends) for q in quarters]
    others = [spans(q * length, length, 0, ends) for q in (1 - core, 2 + core)]
    bias_ref[0] = segment_bias(keys[0], queries[0], True)
    bias_ref[1] = segment_bias(keys[0], queries[1], False)
    bias_ref[2] = segment_bias(keys[1], queries[1], True)
    bias_ref[3] = segment_bias(others[0], queries[1], False)
    last_key = jnp.where(core == 0, others[1], others[0])
    last_query = jnp.where(core == 0, queries[1], queries[0])
    bias_ref[4] = segment_bias(last_key, last_query, False)


def cross_bias(lengths_ref, bias_ref):
    core = lax.axis_index(ROWS) % 2
    count, rows = bias_ref.shape
    for n, token in enumerate((core, 3 - core, 1 - core, 2 + core)):
        keys = spans(token * (count // 4), count // 4, 0, running(lengths_ref, CLIPS))
        for m, frame in enumerate((core, 3 - core)):
            queries = spans(frame * (rows // 2), rows // 2, 1, running(lengths_ref, 0))
            at = slice(n * (count // 4), (n + 1) * (count // 4))
            bias_ref[at, m * (rows // 2) : (m + 1) * (rows // 2)] = segment_bias(keys, queries, False)


def self_forward_kernel(
    lengths_ref, q_ref, k_ref, v_ref, ko_ref, vo_ref, o_ref, lse_ref, bias_ref, fresh=True
):
    core = lax.axis_index(ROWS) % 2
    length = bias_ref.shape[1]

    @pl.when((pl.program_id(0) == 0) & fresh)
    def _():
        self_biases(core, lengths_ref, bias_ref)

    keys, values = (k_ref, ko_ref), (v_ref, vo_ref)
    for which in range(2):

        @pl.when((core == 0) == (which == 0))
        def _(which=which):
            for half, plan in enumerate(self_plan(which)):
                at = slice(half * length, (half + 1) * length)
                blocks = []
                for source, part, number in plan:
                    where = slice(part * length, (part + 1) * length)
                    blocks.append(
                        (
                            keys[source][where],
                            turned(values[source][where]),
                            functools.partial(bias_ref.__getitem__, number),
                        )
                    )
                o_ref[at] = forward_heads(scaled(q_ref[at]), blocks, lse_ref, at)


def self_backward_kernel(
    lengths_ref,
    q_ref,
    k_ref,
    v_ref,
    ko_ref,
    vo_ref,
    g_ref,
    o_ref,
    lse_ref,
    dq_ref,
    dk_ref,
    dv_ref,
    dko_ref,
    dvo_ref,
    bias_ref,
    fresh=True,
):
    core = lax.axis_index(ROWS) % 2
    length = bias_ref.shape[1]

    @pl.when((pl.program_id(0) == 0) & fresh)
    def _():
        self_biases(core, lengths_ref, bias_ref)

    keys, values = (k_ref, ko_ref), (v_ref, vo_ref)
    for which in range(2):

        @pl.when((core == 0) == (which == 0))
        def _(which=which):
            sums = {(s, p): [None, None] for s in range(2) for p in range(2)}
            for half, plan in enumerate(self_plan(which)):
                at = slice(half * length, (half + 1) * length)
                blocks = []
                for source, part, number in plan:
                    where = slice(part * length, (part + 1) * length)
                    blocks.append(
                        (
                            keys[source][where],
                            turned(keys[source][where]),
                            values[source][where],
                            functools.partial(bias_ref.__getitem__, number),
                            sums[source, part],
                        )
                    )
                dq_ref[at] = backward_heads(
                    scaled(q_ref[at]), g_ref[at], o_ref[at], blocks, lse_ref, at
                )
            for (source, part), pair in sums.items():
                where = slice(part * length, (part + 1) * length)
                for ref, value in zip(((dk_ref, dv_ref), (dko_ref, dvo_ref))[source], pair):
                    if value is None:
                        ref[where] = jnp.zeros((length, PAIR), BF)
                    else:
                        ref[where] = value.astype(BF)


def cross_forward_kernel(lengths_ref, q_ref, k_ref, v_ref, o_ref, lse_ref, bias_ref, fresh=True):
    length = q_ref.shape[0] // 2

    @pl.when((pl.program_id(0) == 0) & fresh)
    def _():
        cross_bias(lengths_ref, bias_ref)

    turned_values = turned(v_ref[...])
    for half in range(2):
        at = slice(half * length, (half + 1) * length)
        blocks = [(k_ref[...], turned_values, lambda at=at: bias_ref[:, at])]
        o_ref[at] = forward_heads(scaled(q_ref[at]), blocks, lse_ref, at)


def cross_backward_kernel(
    lengths_ref,
    q_ref,
    k_ref,
    v_ref,
    g_ref,
    o_ref,
    lse_ref,
    dq_ref,
    dk_ref,
    dv_ref,
    bias_ref,
    fresh=True,
):
    length = q_ref.shape[0] // 2

    @pl.when((pl.program_id(0) == 0) & fresh)
    def _():
        cross_bias(lengths_ref, bias_ref)

    turned_keys = turned(k_ref[...])
    sums = [None, None]
    for half in range(2):
        at = slice(half * length, (half + 1) * length)
        blocks = [(k_ref[...], turned_keys, v_ref[...], lambda at=at: bias_ref[:, at], sums)]
        dq_ref[at] = backward_heads(scaled(q_ref[at]), g_ref[at], o_ref[at], blocks, lse_ref, at)
    dk_ref[...] = sums[0].astype(BF)
    dv_ref[...] = sums[1].astype(BF)


GROUP = 2


def column(rows, first=0):
    return pl.BlockSpec((rows, GROUP * PAIR), lambda i: (0, first // GROUP + i))


def grouped(kernel):
    def part(ref, pair):
        if len(ref.shape) == 2 and ref.shape[1] == GROUP * PAIR and ref.dtype == BF:
            return ref.at[:, pair * PAIR : (pair + 1) * PAIR]
        if len(ref.shape) == 3 and ref.shape[:2] == (GROUP, 8):
            return ref.at[pair : pair + 1]
        return ref

    def run(*refs):
        for pair in range(GROUP):
            kernel(*[part(ref, pair) for ref in refs], fresh=pair == 0)

    return run


SMEM_SPEC = pl.BlockSpec(memory_space=pltpu.SMEM)


def without(kernel, first, count):
    def run(*refs):
        kernel(*refs[:first], *refs[first + count :])

    return run


ANY_SPEC = pl.BlockSpec(memory_space=pl.ANY)
WHOLE_SPEC = pl.BlockSpec(memory_space=pltpu.VMEM)


MARK = jax.ShapeDtypeStruct((8, 128), F32)


def marked(kernel, at):
    def run(*refs):
        refs[at][...] = jnp.zeros((8, 128), F32)
        kernel(*refs[:at], *refs[at + 1 :])

    return run


def attention_call(
    kernel, heads, in_specs, outs, bias_shape, flops, arguments, before=(), limit=VMEM_LIMIT
):
    pairs = heads // 2
    kernel = marked(grouped(kernel), len(arguments) + len(outs))
    kernel = without(kernel, len(arguments), len(before))
    in_specs = list(in_specs) + [ANY_SPEC] * len(before)
    arguments = tuple(arguments) + tuple(before)
    out_shape, out_specs = [], []
    for rows in outs:
        if rows is None:
            queries = outs[0]
            out_shape.append(jax.ShapeDtypeStruct((pairs, 8, queries), F32))
            out_specs.append(lse_spec(queries))
        else:
            out_shape.append(jax.ShapeDtypeStruct((rows, pairs * PAIR), BF))
            out_specs.append(column(rows))
    out_shape.append(MARK)
    out_specs.append(pl.BlockSpec((8, 128), lambda i: (0, 0)))
    return pl.pallas_call(
        kernel,
        grid=(pairs // GROUP,),
        in_specs=in_specs,
        out_specs=out_specs,
        out_shape=out_shape,
        scratch_shapes=[pltpu.VMEM(bias_shape, F32)],
        compiler_params=pltpu.CompilerParams(vmem_limit_bytes=limit),
        cost_estimate=pl.CostEstimate(flops=flops, bytes_accessed=8 << 20, transcendentals=flops >> 8),
    )(*arguments)


def lse_spec(queries):
    return pl.BlockSpec((GROUP, 8, queries), lambda i: (i, 0, 0))


def self_forward(lengths, queries, pair, pair_other):
    rows, width = queries.shape
    heads = width // HD
    length = rows // 2
    half = heads // 2
    return attention_call(
        self_forward_kernel,
        heads,
        [
            SMEM_SPEC,
            column(rows),
            column(rows),
            column(rows, half),
            column(rows),
            column(rows, half),
        ],
        (rows, None),
        (5, length, length),
        heads * 5 * 4 * length * length * PAIR * 2,
        (lengths, queries, pair, pair, pair_other, pair_other),
    )


def self_backward(lengths, queries, pair, pair_other, grads, mixed, lse, before=()):
    rows, width = queries.shape
    heads = width // HD
    length = rows // 2
    half = heads // 2
    return attention_call(
        self_backward_kernel,
        heads,
        [
            SMEM_SPEC,
            column(rows),
            column(rows),
            column(rows, half),
            column(rows),
            column(rows, half),
            column(rows),
            column(rows),
            lse_spec(rows),
        ],
        (rows,) * 5,
        (5, length, length),
        heads * 5 * 10 * length * length * PAIR * 2,
        (lengths, queries, pair, pair, pair_other, pair_other, grads, mixed, lse),
        before,
        MOST_VMEM,
    )


def cross_forward(lengths, queries, pair):
    rows, width = queries.shape
    heads = width // HD
    count = pair.shape[0]
    return attention_call(
        cross_forward_kernel,
        heads,
        [SMEM_SPEC, column(rows), column(count), column(count, heads // 2)],
        (rows, None),
        (count, rows),
        heads * 4 * rows * count * PAIR * 2,
        (lengths, queries, pair, pair),
    )


def cross_backward(lengths, queries, pair, grads, mixed, lse, before=()):
    rows, width = queries.shape
    heads = width // HD
    count = pair.shape[0]
    return attention_call(
        cross_backward_kernel,
        heads,
        [
            SMEM_SPEC,
            column(rows),
            column(count),
            column(count, heads // 2),
            column(rows),
            column(rows),
            lse_spec(rows),
        ],
        (rows, count, count),
        (count, rows),
        heads * 10 * rows * count * PAIR * 2,
        (lengths, queries, pair, pair, grads, mixed, lse),
        before,
    )


def gelu_and_slope(values):
    inside = 0.5 * (1.0 + lax.erf(values * (0.5**0.5)))
    bell = jnp.exp(-0.5 * values * values) * ((2.0 * math.pi) ** -0.5)
    return values * inside, inside + values * bell


def feed_kernel(shape, meta_ref, own_in, other_in, gown_in, gother_in, win_ref, wout_ref, *refs):
    nx, ny, nz, chunk = shape
    res_out, res_other_out, grad_out, grad_other_out = refs[:4]
    up_refs, low_refs, gout_refs = refs[4 : 4 + nx], refs[4 + nx : 4 + nx + ny], refs[4 + nx + ny : 4 + nx + ny + nz]
    scratch = refs[4 + nx + ny + nz :]
    act_ref, pre_ref, own_ref, other_ref, gown_ref, gother_ref, res_acc, grad_acc = scratch[:8]
    res_ref, grad_ref, res_other_ref, grad_other_ref, load_sems, store_sems = scratch[8:]
    loads = [
        pltpu.make_async_copy(source, target, load_sems.at[number])
        for number, (source, target) in enumerate(
            (
                (own_in, own_ref),
                (gown_in, gown_ref),
                (other_in, other_ref),
                (gother_in, gother_ref),
            )
        )
    ]
    stores = [
        pltpu.make_async_copy(source, target, store_sems.at[number])
        for number, (source, target) in enumerate(
            (
                (res_ref, res_out),
                (res_other_ref, res_other_out),
                (grad_ref, grad_out),
                (grad_other_ref, grad_other_out),
            )
        )
    ]
    j, i = pl.program_id(0), pl.program_id(1)
    z = meta_ref[3]
    tokens = own_ref.shape[0]
    sources = ((own_ref, gown_ref, res_ref, grad_ref), (other_ref, gother_ref, res_acc, grad_acc))

    first = (i == 0) & (j == 0)

    @pl.when(first)
    def _():
        for load in loads:
            load.start()
        for _, _, res, grad in sources:
            res[...] = jnp.zeros_like(res)
            grad[...] = jnp.zeros_like(grad)

    for side, (values, grads, res, grad) in enumerate(sources):

        @pl.when(first)
        def _(side=side):
            loads[2 * side].wait()
            loads[2 * side + 1].wait()

        for m in range(tokens // chunk):
            at = slice(m * chunk, (m + 1) * chunk)
            activated, slope = gelu_and_slope(dot(values[at], win_ref[...]))
            activated = activated.astype(BF)
            before = (nt(grads[at], wout_ref[...]) * slope).astype(BF)
            to = slice(side * tokens + m * chunk, side * tokens + (m + 1) * chunk)
            act_ref[to] = activated
            pre_ref[to] = before
            res[at] += dot(activated, wout_ref[...])
            grad[at] += nt(before, win_ref[...])

    @pl.when((i == ny - 1) & (j == nx - 1))
    def _():
        res_other_ref[...] = res_acc[...].astype(BF)
        grad_other_ref[...] = grad_acc[...].astype(BF)
        for copy in stores:
            copy.start()

    rows = own_ref.shape[1] // nz
    half = rows // 2

    def both(one, two, right):
        low, high = right[:tokens], right[tokens:]
        return (dot(one, low, 0, 0) + dot(two, high, 0, 0)).astype(BF)

    for k in range(nz):
        at = pl.ds(pl.multiple_of((z + 1 + k) % nz * rows, rows), rows)
        gin = both(own_ref[:, at], other_ref[:, at], pre_ref)
        gout_refs[k][0] = both(gown_ref[:, at], gother_ref[:, at], act_ref)
        to = slice(k * half, (k + 1) * half)
        for number, ref in enumerate(up_refs):

            @pl.when(j == number)
            def _(ref=ref):
                ref[0, to] = gin[:half]

        for number, ref in enumerate(low_refs):

            @pl.when(i == number)
            def _(ref=ref):
                ref[0, to] = gin[half:]

    @pl.when((i == ny - 1) & (j == nx - 1))
    def _():
        for copy in stores:
            copy.wait()


def feed(place, meta, own, other, gown, gother, feed_in, feed_out):
    nx, ny, nz = place.nx, place.ny, place.nz
    tokens, width = own.shape
    part = feed_in.shape[1] // place.seq // 2
    chunk = min(256, tokens)

    def unit(j, i, meta):
        return 2 * ((meta[2] + 1 + i) % ny * nx + (meta[1] + 1 + j) % nx) + meta[0]

    def up_spec(number):
        def index(j, i, meta):
            return jnp.where(j == number, i, jnp.where(j < number, 0, ny - 1)), 0, 0

        return pl.BlockSpec((1, width // 2, part), index)

    low_spec = pl.BlockSpec((1, width // 2, part), lambda j, i, meta: (j, 0, 0))
    gout_spec = pl.BlockSpec((1, width // nz, part), lambda j, i, meta: (j * ny + i, 0, 0))
    total = 2 * tokens
    shape = jax.ShapeDtypeStruct
    return pl.pallas_call(
        functools.partial(feed_kernel, (nx, ny, nz, chunk)),
        grid_spec=pltpu.PrefetchScalarGridSpec(
            num_scalar_prefetch=1,
            grid=(nx, ny),
            in_specs=[ANY_SPEC] * 4
            + [
                pl.BlockSpec((width, part), lambda j, i, meta: (0, unit(j, i, meta))),
                pl.BlockSpec((part, width), lambda j, i, meta: (unit(j, i, meta), 0)),
            ],
            out_specs=[ANY_SPEC] * 4
            + [up_spec(n) for n in range(nx)]
            + [low_spec] * ny
            + [gout_spec] * nz,
            scratch_shapes=[
                pltpu.VMEM((total, part), BF),
                pltpu.VMEM((total, part), BF),
                pltpu.VMEM((tokens, width), BF),
                pltpu.VMEM((tokens, width), BF),
                pltpu.VMEM((tokens, width), BF),
                pltpu.VMEM((tokens, width), BF),
                pltpu.VMEM((tokens, width), F32),
                pltpu.VMEM((tokens, width), F32),
                pltpu.VMEM((tokens, width), F32),
                pltpu.VMEM((tokens, width), F32),
                pltpu.VMEM((tokens, width), BF),
                pltpu.VMEM((tokens, width), BF),
                pltpu.SemaphoreType.DMA((4,)),
                pltpu.SemaphoreType.DMA((4,)),
            ],
        ),
        out_shape=[
            shape((tokens, width), F32),
            shape((tokens, width), BF),
            shape((tokens, width), F32),
            shape((tokens, width), BF),
        ]
        + [shape((ny, width // 2, part), BF)] * nx
        + [shape((nx, width // 2, part), BF)] * ny
        + [shape((place.seq, width // nz, part), BF)] * nz,
        compiler_params=pltpu.CompilerParams(vmem_limit_bytes=60 * 1024 * 1024),
        cost_estimate=pl.CostEstimate(
            flops=12 * total * width * part * place.seq,
            bytes_accessed=40 << 20,
            transcendentals=2 * total * part * place.seq,
        ),
    )(meta, own, other, gown, gother, feed_in, feed_out)


def weight_kernel(shape, meta_ref, *refs):
    count, nz = shape
    lefts, rights = refs[:count], refs[count : 2 * count]
    own_ref, other_ref, turned_ref = refs[2 * count :]
    core, z = meta_ref[0], meta_ref[3]
    block = own_ref.shape[1] // nz
    for number in range(count):

        @pl.when(pl.program_id(0) == number)
        def _(left=lefts[number], right=rights[number]):
            tokens = left.shape[0]
            turned_ref[:, :tokens] = turned(left[...])
            for k in range(nz):
                start = (z + 1 + k) % nz * 2
                to = slice(k * block, (k + 1) * block)
                for which, ref in ((core, own_ref), (1 - core, other_ref)):
                    at = pl.ds(pl.multiple_of((start + which) * block, block), block)
                    ref[0, to] = dot(turned_ref[at, :tokens], right[...]).astype(BF)


def weight_parts(place, meta, lefts, rights, before=()):
    count = len(lefts)
    depth, width = lefts[0].shape[1], rights[0].shape[1]
    tokens = max(left.shape[0] for left in lefts)
    out = jax.ShapeDtypeStruct((count, depth // 2, width), BF)
    spec = pl.BlockSpec((1, depth // 2, width), lambda u: (u, 0, 0))
    return pl.pallas_call(
        without(functools.partial(weight_kernel, (count, place.nz)), 1 + 2 * count, len(before)),
        grid=(count,),
        in_specs=[SMEM_SPEC] + [WHOLE_SPEC] * (2 * count) + [ANY_SPEC] * len(before),
        out_specs=[spec, spec],
        out_shape=[out, out],
        scratch_shapes=[pltpu.VMEM((depth, tokens), BF)],
        compiler_params=pltpu.CompilerParams(vmem_limit_bytes=VMEM_LIMIT),
        cost_estimate=pl.CostEstimate(
            flops=2 * count * tokens * depth * width,
            bytes_accessed=count * depth * width * 4,
            transcendentals=0,
        ),
    )(meta, *lefts, *rights, *before)


MESH = pl.DeviceIdType.MESH


class Mail:
    def __init__(self, send_sems, recv_sems):
        self.send_sems, self.recv_sems, self.sent = send_sems, recv_sems, []

    def send(self, source, target, device):
        number = len(self.sent)
        copy = pltpu.make_async_remote_copy(
            src_ref=source,
            dst_ref=target,
            send_sem=self.send_sems.at[number],
            recv_sem=self.recv_sems.at[number],
            device_id=device,
            device_id_type=MESH,
        )
        copy.start()
        self.sent.append(copy)
        return copy

    def finish(self):
        for copy in self.sent:
            copy.wait_send()


class Ways:
    def __init__(self, nz):
        self.row, self.spot = lax.axis_index(ROWS), lax.axis_index(SEQ)
        self.core, self.z = self.row % 2, self.row // 2
        self.x, self.y = self.spot % 2, self.spot // 2
        self.nz = nz
        self.sibling = (self.row + 1 - 2 * self.core, self.spot)
        self.across_x = (self.row, self.spot + 1 - 2 * self.x)
        self.across_y = (self.row, self.y * -2 + 2 + self.x)
        self.above = ((self.row + 2) % (2 * nz), self.spot)
        self.below = ((self.row + 2 * nz - 2) % (2 * nz), self.spot)

    def plane(self):
        devices = []
        for other in range(2):
            row = self.row if other == 0 else self.sibling[0]
            devices += [(row, (self.spot + s) % 4) for s in range(4) if other or s]
        return devices

    def meet(self, devices):
        barrier = pltpu.get_barrier_semaphore()
        for device in devices:
            pl.semaphore_signal(barrier, inc=1, device_id=device, device_id_type=MESH)
        pl.semaphore_wait(barrier, len(devices))

    def place(self, q):
        return (self.y + 1 + q % 2) % 2 * 2 + (self.x + 1 + q // 2) % 2

    def rows(self, k, which, block):
        start = ((self.z + 1 + k) % self.nz * 2 + which) * block
        return pl.ds(pl.multiple_of(start, block), block)


class Home:
    def __init__(self, ways, out_ref, send_sems, recv_sems):
        self.ways, self.out_ref = ways, out_ref
        self.send_sems, self.recv_sems = send_sems, recv_sems
        self.started = []

    def send(self, source, slot):
        ways = self.ways
        spot = jnp.where(ways.core == 0, 3 * slot, 1 + slot)
        row = 2 * ways.z + ways.spot // 2
        stays = (spot == ways.spot) & (row == ways.row)
        to = self.out_ref.at[ways.spot % 2]
        copy = pltpu.make_async_remote_copy(
            src_ref=source,
            dst_ref=to,
            send_sem=self.send_sems.at[slot],
            recv_sem=self.recv_sems.at[ways.spot % 2],
            device_id=(row, spot),
            device_id_type=MESH,
        )
        local = pltpu.make_async_copy(source, to, self.recv_sems.at[ways.spot % 2])

        @pl.when(stays)
        def _():
            local.start()

        @pl.when(jnp.logical_not(stays))
        def _():
            copy.start()

        self.started.append((stays, copy))

    def finish(self):
        for r in range(2):
            to = self.out_ref.at[r]
            pltpu.make_async_copy(to, to, self.recv_sems.at[r]).wait()
        for stays, copy in self.started:

            @pl.when(jnp.logical_not(stays))
            def _(copy=copy):
                copy.wait_send()


class Gathering:
    def __init__(self, ways, source_ref, target_ref, send_sems, recv_sems):
        self.ways, self.source_ref, self.target_ref = ways, source_ref, target_ref
        self.send_sems, self.recv_sems = send_sems, recv_sems
        self.block = source_ref.shape[1]
        self.copies = []
        owner = jnp.where((ways.spot == 0) | (ways.spot == 3), 0, 1)
        slot = ways.spot // 2
        to = target_ref.at[pl.ds(pl.multiple_of(slot * self.block, self.block), self.block)]
        for r in range(2):
            row, spot = 2 * ways.z + owner, 2 * ways.core + r
            stays = (spot == ways.spot) & (row == ways.row)
            copy = pltpu.make_async_remote_copy(
                src_ref=source_ref.at[r],
                dst_ref=to,
                send_sem=send_sems.at[r],
                recv_sem=recv_sems.at[slot],
                device_id=(row, spot),
                device_id_type=MESH,
            )
            local = pltpu.make_async_copy(source_ref.at[r], to, recv_sems.at[slot])
            self.copies.append((stays, copy, local))

    def start(self):
        for stays, copy, local in self.copies:

            @pl.when(stays)
            def _(local=local):
                local.start()

            @pl.when(jnp.logical_not(stays))
            def _(copy=copy):
                copy.start()

    def arrived(self, slot):
        to = self.target_ref.at[slot * self.block : (slot + 1) * self.block]
        pltpu.make_async_copy(to, to, self.recv_sems.at[slot]).wait()

    def finish(self):
        for stays, copy, _ in self.copies:

            @pl.when(jnp.logical_not(stays))
            def _(copy=copy):
                copy.wait_send()


def self_forward_carrying(nz, lengths_ref, *refs):
    grads_ref, cotangent_ref = refs[5], refs[8]
    bias_ref, sends, recvs = refs[9:]
    gathering = Gathering(Ways(nz), grads_ref, cotangent_ref, sends, recvs)

    @pl.when(pl.program_id(0) == 0)
    def _():
        gathering.ways.meet(gathering.ways.plane())
        gathering.start()

    grouped(self_forward_kernel)(lengths_ref, *refs[:5], *refs[6:8], bias_ref)

    @pl.when(pl.program_id(0) == pl.num_programs(0) - 1)
    def _():
        for slot in range(2):
            gathering.arrived(slot)
        gathering.finish()


def self_forward_and_gather(place, lengths, queries, pair, pair_other, grads):
    rows, width = queries.shape
    half = width // HD // 2
    length = rows // 2
    return pl.pallas_call(
        functools.partial(self_forward_carrying, place.nz),
        grid=(half // GROUP,),
        in_specs=[
            SMEM_SPEC,
            column(rows),
            column(rows),
            column(rows, half),
            column(rows),
            column(rows, half),
            ANY_SPEC,
        ],
        out_specs=[column(rows), lse_spec(rows), ANY_SPEC],
        out_shape=[
            jax.ShapeDtypeStruct((rows, width), BF),
            jax.ShapeDtypeStruct((half, 8, rows), F32),
            jax.ShapeDtypeStruct((rows, width), BF),
        ],
        scratch_shapes=[pltpu.VMEM((5, length, length), F32)]
        + [pltpu.SemaphoreType.DMA((2,))] * 2,
        compiler_params=pltpu.CompilerParams(
            collective_id=4, has_side_effects=True, vmem_limit_bytes=VMEM_LIMIT
        ),
        cost_estimate=pl.CostEstimate(
            flops=40 * rows * length * width, bytes_accessed=8 << 20, transcendentals=0
        ),
    )(lengths, queries, pair, pair, pair_other, pair_other, grads)


def entry_kernel(
    nz,
    frames_ref,
    text_ref,
    lengths_ref,
    gain_ref,
    shift_ref,
    qkv_ref,
    proj_ref,
    bias_ref,
    kv_ref,
    input_out,
    normed_out,
    queries_out,
    pair_out,
    pair_other_ref,
    words_out,
    projected_out,
    text_pair_out,
    lengths_other_ref,
    input_ref,
    normed_ref,
    queries_ref,
    pair_ref,
    words_ref,
    projected_ref,
    text_pair_ref,
    store_sems,
    qkv_here,
    proj_here,
    kv_here,
    load_sems,
    send_sems,
    recv_sems,
    gather_sends,
    gather_recvs,
):
    loads = [
        pltpu.make_async_copy(source, target, load_sems.at[number])
        for number, (source, target) in enumerate(
            ((proj_ref, proj_here), (kv_ref, kv_here), (qkv_ref, qkv_here))
        )
    ]
    for load in loads:
        load.start()
    stores = []

    def store(source, target):
        copy = pltpu.make_async_copy(source, target, store_sems.at[len(stores)])
        copy.start()
        stores.append(copy)

    ways = Ways(nz)
    ways.meet(ways.plane())
    mail = Mail(send_sems, recv_sems)
    words = Gathering(ways, text_ref, words_ref, gather_sends.at[0], gather_recvs.at[0])
    frames = Gathering(ways, frames_ref, input_ref, gather_sends.at[1], gather_recvs.at[1])
    words.start()
    frames.start()
    lengths_copy = mail.send(lengths_ref, lengths_other_ref, ways.sibling)
    half = words_ref.shape[0] // 2
    for slot in range(2):
        words.arrived(slot)
    words_copy = mail.send(words_ref.at[:half], words_ref.at[half:], ways.sibling)
    loads[0].wait()
    loads[1].wait()
    words_copy.wait_recv()
    store(words_ref, words_out)
    projected = (dot(words_ref[...], proj_here[...]) + bias_ref[...]).astype(BF)
    projected_ref[...] = projected
    store(projected_ref, projected_out)
    text_pair_ref[...] = dot(projected, kv_here[...]).astype(BF)
    store(text_pair_ref, text_pair_out)
    loads[2].wait()
    width = input_ref.shape[1]
    block = input_ref.shape[0] // 2
    copies = []
    for slot in range(2):
        frames.arrived(slot)
        at = slice(slot * block, (slot + 1) * block)
        normed_ref[at] = layer_norm(input_ref[at].astype(F32), gain_ref[...], shift_ref[...])
        store(input_ref.at[at], input_out.at[at])
        store(normed_ref.at[at], normed_out.at[at])
        pair_ref[at] = dot(normed_ref[at], qkv_here[:, width:]).astype(BF)
        store(pair_ref.at[at], pair_out.at[at])
        copies.append(mail.send(pair_ref.at[at], pair_other_ref.at[at], ways.sibling))
    queries_ref[...] = dot(normed_ref[...], qkv_here[:, :width]).astype(BF)
    store(queries_ref, queries_out)
    lengths_copy.wait_recv()
    for copy in copies:
        copy.wait_recv()
    mail.finish()
    for gathering in (words, frames):
        gathering.finish()
    for copy in stores:
        copy.wait()


def entry(place, frames, text, lengths, gain, shift, qkv, proj, bias, kv):
    count, block, width = frames.shape
    tokens, words = count * block, 2 * count * text.shape[1]
    shape, vmem = jax.ShapeDtypeStruct, pltpu.VMEM
    return pl.pallas_call(
        functools.partial(entry_kernel, place.nz),
        in_specs=[ANY_SPEC] * 2 + [WHOLE_SPEC] * 3 + [ANY_SPEC] * 2 + [WHOLE_SPEC, ANY_SPEC],
        out_specs=[ANY_SPEC] * 8 + [WHOLE_SPEC],
        out_shape=[
            shape((tokens, width), BF),
            shape((tokens, width), BF),
            shape((tokens, width), BF),
            shape((tokens, 2 * width), BF),
            shape((tokens, 2 * width), BF),
            shape((words, text.shape[2]), BF),
            shape((words, width), BF),
            shape((words, 2 * width), BF),
            shape(lengths.shape, jnp.int32),
        ],
        scratch_shapes=[
            vmem((tokens, width), BF),
            vmem((tokens, width), BF),
            vmem((tokens, width), BF),
            vmem((tokens, 2 * width), BF),
            vmem((words, text.shape[2]), BF),
            vmem((words, width), BF),
            vmem((words, 2 * width), BF),
            pltpu.SemaphoreType.DMA((10,)),
            vmem(qkv.shape, BF),
            vmem(proj.shape, BF),
            vmem(kv.shape, BF),
            pltpu.SemaphoreType.DMA((3,)),
            pltpu.SemaphoreType.DMA((4,)),
            pltpu.SemaphoreType.DMA((4,)),
            pltpu.SemaphoreType.DMA((2, 2)),
            pltpu.SemaphoreType.DMA((2, 2)),
        ],
        compiler_params=pltpu.CompilerParams(
            collective_id=3, has_side_effects=True, vmem_limit_bytes=MOST_VMEM
        ),
        cost_estimate=pl.CostEstimate(
            flops=20 * tokens * width * width, bytes_accessed=20 << 20, transcendentals=0
        ),
    )(frames, text, lengths, gain[None], shift[None], qkv, proj, bias[None], kv)


def with_loads(kernel, count, late):
    def run(*refs):
        inputs, rest = list(refs[:count]), refs[count:]
        here, sems = rest[-len(late) - 1 : -1], rest[-1]
        copies = []
        for number, which in enumerate(late):
            copy = pltpu.make_async_copy(inputs[which], here[number], sems.at[number])
            copy.start()
            inputs[which] = here[number]
            copies.append(copy)
        open_copies = dict(zip(map(id, here), copies))

        def wait(*wanted):
            for ref in wanted:
                open_copies.pop(id(ref)).wait()

        kernel(wait, *inputs, *rest[: -len(late) - 1])

    return run


def load_scratch(operands, late):
    return [pltpu.VMEM(operands[n].shape, operands[n].dtype) for n in late] + [
        pltpu.SemaphoreType.DMA((len(late),))
    ]


def middle_kernel(
    shape,
    wait,
    mixed_ref,
    normed_ref,
    projected_ref,
    text_ref,
    self_ref,
    g_second_ref,
    g_query_ref,
    g_keys_ref,
    g_values_ref,
    g_projected_ref,
    g_first_ref,
    result_ref,
    result_away_ref,
    in_up_ref,
    in_up_got_ref,
    in_low_ref,
    in_low_got_ref,
    out_one_ref,
    out_one_got_ref,
    out_zero_ref,
    self_weight_ref,
    send_up_ref,
    send_low_ref,
    keep_up_ref,
    keep_low_ref,
    result_out,
    in_up_keep,
    in_up_next,
    in_low_keep,
    in_low_next,
    out_next,
    g_mix_ref,
    mixed_t,
    normed_t,
    projected_t,
    text_t,
    self_t,
    own_ref,
    away_ref,
    got_ref,
    result_got_ref,
    in_send_ref,
    out_send_ref,
    out_came_ref,
    send_sems,
    recv_sems,
    home_sends,
    home_recvs,
):
    nz, piece = shape
    ways = Ways(nz)
    ways.meet(ways.plane() + [ways.above, ways.below])
    mail = Mail(send_sems, recv_sems)
    result_copy = mail.send(result_away_ref, result_got_ref, ways.sibling)
    wait(out_one_ref, out_one_got_ref)
    out_send_ref[...] = out_one_ref[...] + out_one_got_ref[...]
    out_copy = mail.send(out_send_ref, out_came_ref, ways.above)
    wait(in_up_ref, in_up_got_ref, in_low_ref, in_low_got_ref)
    in_send_ref[0] = in_up_ref[0] + in_up_got_ref[0]
    in_send_ref[1] = in_low_ref[0] + in_low_got_ref[0]
    in_copies = [
        mail.send(in_send_ref.at[0], in_up_next, ways.across_y),
        mail.send(in_send_ref.at[1], in_low_next, ways.across_x),
    ]
    in_up_keep[...] = in_up_ref[1] + in_up_got_ref[1]
    in_low_keep[...] = in_low_ref[1] + in_low_got_ref[1]
    home = Home(ways, result_out, home_sends, home_recvs)
    for left, to in ((mixed_ref, mixed_t), (normed_ref, normed_t), (projected_ref, projected_t), (self_ref, self_t)):
        wait(left)
        to[...] = turned(left[...])
    wait(text_ref)
    turned_text = turned(text_ref[...])
    block = own_ref.shape[2]
    count = 2 * nz
    part = turned_text.shape[0] // count
    text_t[...] = jnp.zeros_like(text_t)
    for b in range(count):
        text_t[b * block : b * block + part] = turned_text[b * part : (b + 1) * part]
    half = block // 2
    up, low = slice(0, half), slice(half, block)
    homes = (
        (send_up_ref.at[0], send_low_ref.at[0]),
        (send_up_ref.at[1], keep_low_ref.at[0]),
        (keep_up_ref.at[0], send_low_ref.at[1]),
        (keep_up_ref.at[1], keep_low_ref.at[1]),
    )
    copies = []
    wait(g_second_ref, g_query_ref, g_keys_ref, g_values_ref, g_projected_ref, g_first_ref)

    def settle(q):
        copies[q].wait_recv()
        total = own_ref[q] + got_ref[q]
        homes[q][0][...] = total[:, up]
        homes[q][1][...] = total[:, low]

    for q in range(4):
        place = ways.place(q)
        columns = pl.ds(pl.multiple_of(place * piece, piece), piece)
        twice = pl.ds(pl.multiple_of(place % 2 * 2 * piece, piece), 2 * piece)
        pair = jnp.where(place < 2, g_keys_ref[:, twice], g_values_ref[:, twice])
        units = (
            (mixed_t, g_second_ref[:, columns]),
            (normed_t, g_query_ref[:, columns]),
            (projected_t, pair),
            (text_t, g_projected_ref[:, columns]),
            (self_t, g_first_ref[:, columns]),
        )
        for which, ref in ((1 - ways.core, away_ref), (ways.core, own_ref)):
            first = 0
            for left, right in units:
                to = slice(first, first + right.shape[1])
                first += right.shape[1]
                for k in range(nz):
                    ref[q, k, :, to] = dot(left[ways.rows(k, which, block)], right).astype(BF)
            if ref is away_ref:
                copies.append(mail.send(away_ref.at[q], got_ref.at[q], ways.sibling))
        if q == 0:
            wait(result_ref)
            result_copy.wait_recv()
            result_got_ref[...] = (result_ref[...] + result_got_ref[...].astype(F32)).astype(BF)
            slots = result_ref.shape[0] // 2
            for slot in range(2):
                home.send(result_got_ref.at[slot * slots : (slot + 1) * slots], slot)
        else:
            settle(q - 1)
    wait(self_weight_ref)
    g_mix_ref[...] = nt(g_first_ref[...], self_weight_ref[...]).astype(BF)
    settle(3)
    for copy in in_copies:
        copy.wait_recv()
    out_copy.wait_recv()
    wait(out_zero_ref)
    out_next[...] = out_zero_ref[...] + out_came_ref[...]
    mail.finish()
    home.finish()


def middle_parts(place, count, lefts, rights, result, result_away, feeds, weight):
    nz = place.nz
    depth, width = lefts[0].shape[1], rights[0].shape[1]
    piece, block = width // place.seq, depth // place.rows
    columns = piece * len(rights)
    out = jax.ShapeDtypeStruct((2, nz, block // 2, columns), BF)
    big = pltpu.VMEM((4, nz, block, columns), BF)
    operands = [*lefts, *rights, result, result_away, *feeds, weight]
    late = (17, 18, 13, 14, 15, 16, 0, 1, 2, 4, 3, 5, 6, 7, 8, 9, 10, 11, 20, 19)
    return pl.pallas_call(
        with_loads(functools.partial(middle_kernel, (nz, piece)), len(operands), late),
        in_specs=[ANY_SPEC] * len(operands),
        out_specs=[WHOLE_SPEC] * 4
        + [ANY_SPEC, WHOLE_SPEC, ANY_SPEC, WHOLE_SPEC, ANY_SPEC, WHOLE_SPEC, WHOLE_SPEC],
        out_shape=[out] * 4
        + [jax.ShapeDtypeStruct((count, result.shape[0] // count, width), BF)]
        + [jax.ShapeDtypeStruct(feeds[0].shape[1:], BF)] * 4
        + [jax.ShapeDtypeStruct(feeds[4].shape, BF), jax.ShapeDtypeStruct(result.shape, BF)],
        scratch_shapes=[pltpu.VMEM((depth, left.shape[0]), BF) for left in lefts]
        + [big] * 3
        + [pltpu.VMEM(result.shape, BF), pltpu.VMEM(feeds[0].shape, BF)]
        + [pltpu.VMEM(feeds[4].shape, BF)] * 2
        + [pltpu.SemaphoreType.DMA((8,))] * 2
        + [pltpu.SemaphoreType.DMA((2,))] * 2
        + load_scratch(operands, late),
        compiler_params=pltpu.CompilerParams(
            collective_id=2, has_side_effects=True, vmem_limit_bytes=63 * 1024 * 1024
        ),
        cost_estimate=pl.CostEstimate(
            flops=2 * 8 * 512 * depth * width, bytes_accessed=24 << 20, transcendentals=0
        ),
    )(*operands)


def final_kernel(nz, wait, *refs):
    (
        normed_ref,
        input_ref,
        first_ref,
        gain_ref,
        weight_ref,
        gq_ref,
        gk_ref,
        gv_ref,
        k_away_ref,
        v_away_ref,
        upper_ref,
        upper_got_ref,
        lower_ref,
        lower_got_ref,
        in_up_ref,
        in_up_got_ref,
        in_low_ref,
        in_low_got_ref,
        out_last_ref,
        out_got_ref,
        vector_ref,
        projected_ref,
        proj_ref,
    ) = refs[:23]
    (qkv_ref, middle_ref, feed_ref, sum_ref, frames_out, text_out) = refs[23:29]
    (
        out_ref,
        text_ref,
        packed_ref,
        k_got_ref,
        v_got_ref,
        acc_ref,
        turned_ref,
        own_ref,
        away_ref,
        got_ref,
        first_x_ref,
        first_y_ref,
        second_y_ref,
        second_x_ref,
        mid_up_ref,
        mid_low_ref,
        mid_ref,
        mid_ring_ref,
        qkv_ring_ref,
        feed_send_ref,
        feed_ring_ref,
        out_x_ref,
        out_own_ref,
        out_y_ref,
        feed_away_ref,
        feed_other_ref,
        vector_out_ref,
        vector_in_ref,
        text_away_ref,
        text_got_ref,
        send_sems,
        recv_sems,
        home_sends,
        home_recvs,
    ) = refs[29:]
    ways = Ways(nz)
    core, z = ways.core, ways.z
    sibling, across_x, across_y, above = ways.sibling, ways.across_x, ways.across_y, ways.above
    ways.meet(ways.plane() + [ways.above, ways.below])
    mail = Mail(send_sems, recv_sems)
    ring = ring_order(nz)
    half = upper_ref.shape[2]
    feed_half = feed_ring_ref.shape[1] // 2
    tokens, width = normed_ref.shape

    k_copy = mail.send(k_away_ref, k_got_ref, sibling)
    v_copy = mail.send(v_away_ref, v_got_ref, sibling)

    feed_copies, feed_last_copies = [], {}

    def feed_piece(t):
        at = slice(ring[t] * feed_half, (ring[t] + 1) * feed_half)
        return (
            in_up_ref[at].astype(F32) + in_up_got_ref[at].astype(F32),
            in_low_ref[at].astype(F32) + in_low_got_ref[at].astype(F32),
        )

    def feed_step(t):
        upper_part, lower_part = feed_piece(t)
        if t > 0:
            feed_copies[t - 1].wait_recv()
            upper_part += feed_ring_ref[t - 1, :feed_half].astype(F32)
            lower_part += feed_ring_ref[t - 1, feed_half:].astype(F32)
        if t == nz - 1:
            feed_finish(0, upper_part, lower_part)
            return
        feed_send_ref[t, :feed_half] = upper_part.astype(BF)
        feed_send_ref[t, feed_half:] = lower_part.astype(BF)
        feed_copies.append(mail.send(feed_send_ref.at[t], feed_ring_ref.at[t], above))

    wait(in_up_ref, in_up_got_ref, in_low_ref, in_low_got_ref)
    feed_step(0)

    mid_copies = {}
    wait(upper_ref, upper_got_ref, lower_ref, lower_got_ref)
    for k in ring:
        mid_ref[k, :half] = upper_ref[0, k] + upper_got_ref[0, k]
        mid_ref[k, half:] = lower_ref[0, k] + lower_got_ref[0, k]
        mid_copies[k] = (
            mail.send(mid_ref.at[k, :half], mid_up_ref.at[k], across_y),
            mail.send(mid_ref.at[k, half:], mid_low_ref.at[k], across_x),
        )
    wait(normed_ref, gq_ref, gk_ref, gv_ref)
    turned_ref[...] = turned(normed_ref[...])
    packed_ref[:, :width] = gq_ref[...]
    k_copy.wait_recv()
    packed_ref[:, width : 2 * width] = gk_ref[...] + k_got_ref[...]
    v_copy.wait_recv()
    packed_ref[:, 2 * width :] = gv_ref[...] + v_got_ref[...]

    block = own_ref.shape[2]
    columns = own_ref.shape[3]
    core_copies = []
    for q in range(4):
        right = packed_ref[:, pl.ds(pl.multiple_of(ways.place(q) * columns, columns), columns)]
        for which, ref in ((1 - core, away_ref), (core, own_ref)):
            for k in range(nz):
                ref[q, k] = dot(turned_ref[ways.rows(k, which, block)], right).astype(BF)
            if ref is away_ref:
                core_copies.append(mail.send(away_ref.at[q], got_ref.at[q], sibling))

    even_rows, odd_rows = slice(0, feed_half), slice(feed_half, 2 * feed_half)

    def out_first():
        for n in range(2):
            out_copies.append(
                (
                    mail.send(out_ref.at[n, even_rows], out_x_ref.at[n], across_x),
                    mail.send(out_ref.at[2 * n, odd_rows], out_y_ref.at[n], across_y),
                )
            )

    def out_step():
        for n in range(2):
            for copy in out_copies[n]:
                copy.wait_recv()
            out_own_ref[0, n] = out_ref[2 + n, even_rows] + out_x_ref[n]
            out_own_ref[1, n] = out_ref[1 + 2 * n, odd_rows] + out_y_ref[n]
            if n == 0:
                out_copies.append(
                    (
                        mail.send(out_own_ref.at[0, 0], out_x_ref.at[2], across_y),
                        mail.send(out_own_ref.at[1, 0], out_y_ref.at[2], across_x),
                    )
                )

    def out_last():
        for copy in out_copies[2]:
            copy.wait_recv()
        feed_finish(
            1,
            out_own_ref[0, 1].astype(F32) + out_x_ref[2].astype(F32),
            out_own_ref[1, 1].astype(F32) + out_y_ref[2].astype(F32),
        )

    def feed_finish(kind, even, odd):
        away = jnp.where(core == 0, odd, even)
        own = jnp.where(core == 0, even, odd)
        across = own.shape[1]
        feed_away_ref[kind] = away
        feed_last_copies[kind] = mail.send(feed_away_ref.at[kind], feed_other_ref.at[kind], sibling)
        at = pl.ds(pl.multiple_of(core * across, across), across)
        feed_ref[kind, :, at] = own

    def feed_last(kind):
        feed_last_copies[kind].wait_recv()
        across = feed_other_ref.shape[2]
        at = pl.ds(pl.multiple_of((1 - core) * across, across), across)
        feed_ref[kind, :, at] = feed_other_ref[kind]

    wait(projected_ref, proj_ref)
    text_ref[...] = nt(projected_ref[...], proj_ref[...])
    text_rows = text_ref.shape[0] // 2
    text_away_ref[...] = text_ref[text_rows:].astype(BF)
    text_copy = mail.send(text_away_ref, text_got_ref, sibling)

    def core_step(q):
        core_copies[q].wait_recv()
        own_ref[q] = own_ref[q] + got_ref[q]

    mid_ring = {}

    def mid_send(t):
        k = ring[t]
        up, low = mid_copies[k]
        up.wait()
        low.wait()
        mid_ref[k, :half] = upper_ref[1, k] + upper_got_ref[1, k] + mid_up_ref[k]
        mid_ref[k, half:] = lower_ref[1, k] + lower_got_ref[1, k] + mid_low_ref[k]
        if t > 0:
            mid_ring[t - 1].wait_recv()
        if t == nz - 1:
            middle_ref[...] = mid_ref[k].astype(F32) + mid_ring_ref[t - 1].astype(F32)
            return
        if t > 0:
            mid_ref[k] = mid_ref[k] + mid_ring_ref[t - 1]
        mid_ring[t] = mail.send(mid_ref.at[k], mid_ring_ref.at[t], above)

    qkv_ring = {}

    def qkv_send(t):
        k = ring[t]
        second[k][0].wait_recv()
        own_ref[3, k, up] = own_ref[3, k, up] + second_y_ref[k]
        second[k][1].wait_recv()
        own_ref[3, k, low] = own_ref[3, k, low] + second_x_ref[k]
        if t > 0:
            qkv_ring[t - 1].wait_recv()
        if t == nz - 1:
            qkv_ref[...] = own_ref[3, k].astype(F32) + qkv_ring_ref[t - 1].astype(F32)
            return
        if t > 0:
            own_ref[3, k] = own_ref[3, k] + qkv_ring_ref[t - 1]
        qkv_ring[t] = mail.send(own_ref.at[3, k], qkv_ring_ref.at[t], above)

    up, low = slice(0, half), slice(half, 2 * half)
    core_step(0)
    upper_first = [mail.send(own_ref.at[0, :, up], first_x_ref.at[0], across_x)]
    lower_first = [mail.send(own_ref.at[0, :, low], first_y_ref.at[0], across_y)]
    core_step(1)
    upper_first.append(mail.send(own_ref.at[1, :, up], first_x_ref.at[1], across_x))
    core_step(2)
    lower_first.append(mail.send(own_ref.at[2, :, low], first_y_ref.at[1], across_y))
    core_step(3)
    wait(out_last_ref, out_got_ref)
    out_ref[...] = out_last_ref[...] + out_got_ref[...]
    out_copies = []
    out_first()

    slots = tokens // 2
    text_copy.wait_recv()
    text_got_ref[...] = (text_ref[:text_rows] + text_got_ref[...].astype(F32)).astype(BF)
    text_home = Home(ways, text_out, home_sends.at[0], home_recvs.at[0])
    for slot in range(2):
        at = slice(slot * text_rows // 2, (slot + 1) * text_rows // 2)
        text_home.send(text_got_ref.at[at], slot)

    wait(weight_ref)
    acc_ref[...] = nt(packed_ref[:, :width], weight_ref[:, :width])
    acc_ref[...] += nt(packed_ref[:, width : 2 * width], weight_ref[:, width : 2 * width])
    mid_send(0)
    feed_step(1)
    acc_ref[...] += nt(packed_ref[:, 2 * width :], weight_ref[:, 2 * width :])
    wait(input_ref, first_ref, gain_ref)
    gain_sum = jnp.zeros((1, width), F32)
    shift_sum = jnp.zeros((1, width), F32)
    chunk = min(128, tokens)
    for m in range(tokens // chunk):
        at = slice(m * chunk, (m + 1) * chunk)
        grad, gain_part, shift_part = norm_backward(
            input_ref[at].astype(F32), gain_ref[...], acc_ref[at]
        )
        k_got_ref[at] = (first_ref[at] + grad).astype(BF)
        gain_sum += gain_part[None]
        shift_sum += shift_part[None]
    wait(vector_ref)
    vector_out_ref[0] = vector_ref[...]
    vector_out_ref[0, 0:1] = gain_sum
    vector_out_ref[0, 1:2] = shift_sum
    vector_copy = mail.send(vector_out_ref.at[0], vector_in_ref.at[0], sibling)
    mid_send(1)

    vector_copy.wait_recv()
    vector_out_ref[1] = vector_out_ref[0] + vector_in_ref[0]
    vector_copy = mail.send(vector_out_ref.at[1], vector_in_ref.at[1], across_x)
    for t in range(2, nz):
        feed_step(t)
        if t < nz - 1:
            mid_send(t)
    vector_copy.wait_recv()
    vector_out_ref[2] = vector_out_ref[1] + vector_in_ref[1]
    vector_copy = mail.send(vector_out_ref.at[2], vector_in_ref.at[2], across_y)

    upper_first[0].wait_recv()
    own_ref[2, :, up] = own_ref[2, :, up] + first_x_ref[0]
    lower_first[0].wait_recv()
    own_ref[1, :, low] = own_ref[1, :, low] + first_y_ref[0]
    second = {}
    for k in ring:
        second[k] = (
            mail.send(own_ref.at[2, k, up], second_y_ref.at[k], across_y),
            mail.send(own_ref.at[1, k, low], second_x_ref.at[k], across_x),
        )
    frames_home = Home(ways, frames_out, home_sends.at[1], home_recvs.at[1])
    for slot in range(2):
        frames_home.send(k_got_ref.at[slot * slots : (slot + 1) * slots], slot)
    vector_copy.wait_recv()
    vector_out_ref[3] = vector_out_ref[2] + vector_in_ref[2]
    vector_copy = mail.send(vector_out_ref.at[3], vector_in_ref.at[3], above)
    upper_first[1].wait_recv()
    own_ref[3, :, up] = own_ref[3, :, up] + first_x_ref[1]
    lower_first[1].wait_recv()
    own_ref[3, :, low] = own_ref[3, :, low] + first_y_ref[1]
    out_step()
    mid_send(nz - 1)
    feed_last(0)
    total = vector_out_ref[3]
    for t in range(nz - 1):
        vector_copy.wait_recv()
        total = total + vector_in_ref[3 + t]
        if t < nz - 2:
            vector_copy = mail.send(vector_in_ref.at[3 + t], vector_in_ref.at[4 + t], above)
    sum_ref[...] = total
    for t in range(nz):
        qkv_send(t)
    out_last()
    feed_last(1)
    text_home.finish()
    frames_home.finish()
    for number, copy in enumerate(mail.sent):
        if not any(copy is c for pair in mid_copies.values() for c in pair):
            copy.wait_send()


FINAL_LOADS = (14, 15, 16, 17, 10, 11, 12, 13, 0, 5, 6, 7, 18, 19, 21, 22, 4, 1, 2, 3, 20)


def final_sums(place, count, *operands):
    nz = place.nz
    normed, weight, upper, in_up = operands[0], operands[4], operands[10], operands[14]
    vectors, projected, proj = operands[20], operands[21], operands[22]
    words, text_width = projected.shape[0], proj.shape[0]
    tokens, width = normed.shape
    block, piece = width // place.rows, weight.shape[1] // place.seq
    half, middle = block // 2, upper.shape[3]
    feed_width = in_up.shape[1]
    feed_rows = width // nz
    copies = 2 + 6 + nz - 1 + 2 + 2 * nz + 1 + 4 + 3 + nz - 1 + 4 + 2 * nz + 2 * (nz - 1)
    vmem = pltpu.VMEM
    return pl.pallas_call(
        with_loads(functools.partial(final_kernel, nz), len(operands), FINAL_LOADS),
        in_specs=[ANY_SPEC] * len(operands),
        out_specs=[WHOLE_SPEC] * 4 + [ANY_SPEC] * 2,
        out_shape=[
            jax.ShapeDtypeStruct((block, piece), F32),
            jax.ShapeDtypeStruct((block, middle), F32),
            jax.ShapeDtypeStruct((2, block, 2 * feed_width), F32),
            jax.ShapeDtypeStruct(vectors.shape, F32),
            jax.ShapeDtypeStruct((count, tokens // count, width), BF),
            jax.ShapeDtypeStruct((count, words // 2 // count, text_width), BF),
        ],
        scratch_shapes=[
            vmem((4, feed_rows, feed_width), BF),
            vmem((words, text_width), F32),
            vmem((tokens, 3 * width), BF),
            vmem((tokens, width), BF),
            vmem((tokens, width), BF),
            vmem((tokens, width), F32),
            vmem((width, tokens), BF),
            vmem((4, nz, block, piece), BF),
            vmem((4, nz, block, piece), BF),
            vmem((4, nz, block, piece), BF),
            vmem((2, nz, half, piece), BF),
            vmem((2, nz, half, piece), BF),
            vmem((nz, half, piece), BF),
            vmem((nz, half, piece), BF),
            vmem((nz, half, middle), BF),
            vmem((nz, half, middle), BF),
            vmem((nz, block, middle), BF),
            vmem((nz - 1, block, middle), BF),
            vmem((nz - 1, block, piece), BF),
            vmem((nz - 1, feed_rows, feed_width), BF),
            vmem((nz - 1, feed_rows, feed_width), BF),
            vmem((3, feed_rows // 2, feed_width), BF),
            vmem((2, 2, feed_rows // 2, feed_width), BF),
            vmem((3, feed_rows // 2, feed_width), BF),
            vmem((2, feed_rows // 2, feed_width), F32),
            vmem((2, feed_rows // 2, feed_width), F32),
            vmem((4,) + vectors.shape, F32),
            vmem((2 + nz,) + vectors.shape, F32),
            vmem((words // 2, text_width), BF),
            vmem((words // 2, text_width), BF),
            pltpu.SemaphoreType.DMA((copies,)),
            pltpu.SemaphoreType.DMA((copies,)),
            pltpu.SemaphoreType.DMA((2, 2)),
            pltpu.SemaphoreType.DMA((2, 2)),
        ]
        + load_scratch(operands, FINAL_LOADS),
        compiler_params=pltpu.CompilerParams(
            collective_id=1, has_side_effects=True, vmem_limit_bytes=63 * 1024 * 1024
        ),
        cost_estimate=pl.CostEstimate(
            flops=60 * tokens * width * weight.shape[1], bytes_accessed=40 << 20, transcendentals=0
        ),
    )(*operands)


def last_kernel(padding, qkv_ref, middle_ref, feed_ref, frames_ref, text_ref, *outs):
    frames_out, text_out, qkv_out, self_out, query_out, proj_out, kv_out, cross_out, in_out, out_out = outs
    piece = self_out.shape[1]
    frames_out[...] = frames_ref[...].astype(F32)
    text_out[...] = text_ref[...].astype(F32)
    qkv_out[...] = qkv_ref[...]
    cross_out[...] = middle_ref[:, :piece]
    query_out[...] = middle_ref[:, piece : 2 * piece]
    kv_out[...] = middle_ref[:, 2 * piece : 4 * piece]
    proj_out[...] = middle_ref[: proj_out.shape[0], 4 * piece : 5 * piece]
    self_out[...] = middle_ref[:, 5 * piece :]
    in_out[...] = feed_ref[0]
    out_out[...] = jnp.swapaxes(feed_ref[1], 0, 1)


def last_step(padding, piece, qkv, middle, feed_sums, frames, text):
    block, across = qkv.shape[0], feed_sums.shape[2]
    shapes = [
        frames.shape,
        text.shape,
        qkv.shape,
        (block, piece),
        (block, piece),
        (block - padding, piece),
        (block, 2 * piece),
        (block, piece),
        (block, across),
        (across, block),
    ]
    return pl.pallas_call(
        functools.partial(last_kernel, padding),
        in_specs=[WHOLE_SPEC] * 5,
        out_specs=[WHOLE_SPEC] * len(shapes),
        out_shape=[jax.ShapeDtypeStruct(shape, F32) for shape in shapes],
        compiler_params=pltpu.CompilerParams(vmem_limit_bytes=MOST_VMEM),
    )(qkv, middle, feed_sums, frames, text)


def permuted_sums(place, meta, in_up, in_low, out_sum, lefts, rights, normed_self, backward_self):
    nx, ny, nz, seq = place.nx, place.ny, place.nz, place.seq
    width = normed_self.shape[1]
    block, piece = width // place.rows, width // seq
    middle_own, middle_away = weight_parts(
        place, meta, lefts[:3] + lefts[2:4], rights[:5]
    )
    out_own, out_away = weight_parts(place, meta, lefts[4:], rights[5:])
    middle_got = place.swap_core(middle_away)
    out_got = place.swap_core(out_away)
    grad_packed = backward_self(middle_got, out_got)
    in_up = ring_sum([lambda a=in_up[k]: a.astype(F32) for k in range(ny)], place.next_y)
    in_low = ring_sum([lambda a=in_low[k]: a.astype(F32) for k in range(nx)], place.next_x)
    in_both = jnp.stack([in_up, in_low]).astype(BF).reshape(2, nz, block, -1)
    in_both = ring_sum([lambda a=in_both[:, k]: a.astype(F32) for k in range(nz)], place.next_z)
    out_sum = out_sum.reshape((nx, ny) + out_sum.shape[1:])
    out_sum = ring_sum([lambda a=out_sum[k]: a.astype(F32) for k in range(nx)], place.next_x)
    out_sum = out_sum.astype(BF)
    out_sum = ring_sum([lambda a=out_sum[k]: a.astype(F32) for k in range(ny)], place.next_y)
    feed_own = jnp.stack([in_both, out_sum.reshape(2, block, -1)])
    feed_got = place.swap_core(pick(feed_own, 1 - place.core, 1))
    feed_own = pick(feed_own, place.core, 1)
    low = jnp.where(place.core == 0, feed_own, feed_got)
    high = jnp.where(place.core == 0, feed_got, feed_own)
    sum_feed = jnp.concatenate([low, high], axis=2)

    def middle_piece(k):
        at = slice(k * block, (k + 1) * block)
        return lambda: middle_own[:, at].astype(F32) + middle_got[:, at].astype(F32)

    middle = ring_sum([middle_piece(k) for k in range(nz)], place.next_z).astype(BF)
    spread = jnp.concatenate(
        [
            middle[0].reshape(block, seq, -1),
            middle[1].reshape(block, seq, -1),
            jnp.concatenate([middle[2], middle[3]], axis=1).reshape(block, seq, -1),
            middle[4].reshape(block, seq, -1),
        ],
        axis=2,
    ).reshape(block, ny, nx, -1)

    def shifted(array, index, number, length, axis):
        return lambda: pick(array, (index + 1 + number) % length, axis).astype(F32)

    spread = ring_sum([shifted(spread, place.x, k, nx, 2) for k in range(nx)], place.next_x).astype(BF)
    spread = ring_sum([shifted(spread, place.y, k, ny, 1) for k in range(ny)], place.next_y)
    relative_parts = place.relative_columns(grad_packed, True)
    qkv_own, qkv_away = weight_parts(place, meta, [normed_self], [relative_parts])
    qkv_got = place.swap_core(qkv_away)

    def columns(array):
        return array[0].reshape(array.shape[1], nx, ny, -1)

    def natural(array):
        return jnp.stack(
            [
                jnp.stack(
                    [
                        pick(array[0].reshape(array.shape[1], seq, -1), place.offset(i, j), 1)
                        for i in range(ny)
                    ],
                    axis=1,
                )
                for j in range(nx)
            ],
            axis=1,
        )

    last_own = jnp.concatenate([columns(qkv_own), natural(out_own)], axis=3)
    last_got = jnp.concatenate([columns(qkv_got), natural(out_got)], axis=3)
    last = (last_own.astype(F32) + last_got.astype(F32)).astype(BF)
    last = last.reshape(nz, 2, block // 2, nx, ny, -1)
    upper = ring_sum([lambda k=k: last[:, 0, :, k].astype(F32) for k in range(nx)], place.next_x).astype(BF)
    lower = ring_sum([lambda k=k: last[:, 1, :, :, k].astype(F32) for k in range(ny)], place.next_y).astype(BF)
    upper = ring_sum([lambda a=upper[:, :, k]: a.astype(F32) for k in range(ny)], place.next_y)
    lower = ring_sum([lambda a=lower[:, :, k]: a.astype(F32) for k in range(nx)], place.next_x)
    last = jnp.stack([upper, lower], axis=1).astype(BF)
    last = ring_sum([lambda a=last[k]: a.astype(F32) for k in range(nz)], place.next_z)
    last = last.reshape(block, -1)
    sum_self_qkv, sum_self_out = last[:, : 3 * piece], last[:, 3 * piece :]

    return sum_feed, spread, sum_self_qkv, sum_self_out, grad_packed


def shards(
    frames,
    text_states,
    clip_lengths,
    text_lengths,
    self_gain,
    self_shift,
    self_qkv,
    self_out,
    cross_gain,
    cross_shift,
    cross_query,
    text_proj,
    text_bias,
    cross_kv,
    cross_out,
    feed_gain,
    feed_shift,
    feed_in,
    feed_out,
    grad_out,
):
    place = Place()
    count = frames.shape[0]
    width = frames.shape[2]
    text_total = text_states.shape[1] * place.seq

    nx, ny, nz, seq = place.nx, place.ny, place.nz, place.seq
    block, piece = width // place.rows, width // seq
    kernels = nx == 2 and ny == 2 and nz == 4 and piece % 128 == 0
    lengths = jnp.concatenate([clip_lengths, text_lengths], axis=1)
    if kernels:
        padded = jnp.zeros((8, 128), jnp.int32).at[:count, : 2 * CLIPS].set(lengths)
        (
            layer_raw,
            normed_self,
            queries,
            pair,
            pair_other,
            text_input,
            projected,
            text_pair,
            lengths_other,
        ) = entry(
            place,
            frames,
            text_states,
            padded,
            self_gain,
            self_shift,
            self_qkv,
            text_proj,
            text_bias,
            cross_kv,
        )
        lengths_other = lengths_other[:count, : 2 * CLIPS]
        layer_input = layer_raw.astype(F32)
    else:
        lengths_other = place.swap_core(lengths)
        text_half = place.to_rows(text_states)
        layer_raw = place.to_rows(frames)
        text_input = jnp.concatenate([text_half, place.swap_core(text_half)], axis=0)
        cotangent = place.to_rows(grad_out)
        projected = (dot(text_input, text_proj) + text_bias).astype(BF)
        text_pair = dot(projected, cross_kv).astype(BF)
        layer_input = layer_raw.astype(F32)
        normed_self = layer_norm(layer_input, self_gain, self_shift)
        pair = dot(normed_self, self_qkv[:, width:]).astype(BF)
        pair_other = place.swap_core(pair)
        queries = dot(normed_self, self_qkv[:, :width]).astype(BF)
    mine = place.spot // count == place.core
    row_lengths = pick(jnp.where(mine, lengths, lengths_other), place.spot % count, 0)

    if kernels:
        self_mix, self_lse, cotangent = self_forward_and_gather(
            place, row_lengths, queries, pair, pair_other, grad_out
        )
    else:
        self_mix, self_lse, _ = self_forward(row_lengths, queries, pair, pair_other)
    cotangent_other = place.swap_core(cotangent)
    first = layer_input + dot(self_mix, self_out)
    normed_cross = layer_norm(first, cross_gain, cross_shift)
    cross_queries = dot(normed_cross, cross_query).astype(BF)
    cross_mix, cross_lse, _ = cross_forward(row_lengths, cross_queries, text_pair)
    second = first + dot(cross_mix, cross_out)
    normed_feed = layer_norm(second, feed_gain, feed_shift)

    meta = jnp.stack([place.core, place.x, place.y, place.z]).astype(jnp.int32)
    normed_other = place.swap_core(normed_feed)
    fed = feed(
        place, meta, normed_feed, normed_other, cotangent, cotangent_other, feed_in, feed_out
    )
    result, result_away, grad_normed_feed, grad_away = fed[:4]
    up_parts, low_parts, out_parts = fed[4 : 4 + nx], fed[4 + nx : 4 + nx + ny], fed[4 + nx + ny :]
    grad_normed_feed = grad_normed_feed + place.swap_core(grad_away).astype(F32)

    grad_part, grad_feed_gain, grad_feed_shift = norm_backward(second, feed_gain, grad_normed_feed)
    grad_second = cotangent.astype(F32) + grad_part
    grad_second_branch = grad_second.astype(BF)
    grad_cross_mix = dot(grad_second_branch, cross_out, 1, 1).astype(BF)
    grad_cross_queries, grad_text_keys, grad_text_values, _ = cross_backward(
        row_lengths,
        cross_queries,
        text_pair,
        grad_cross_mix,
        cross_mix,
        cross_lse,
    )
    grad_normed_cross = dot(grad_cross_queries, cross_query, 1, 1)
    grad_part, grad_cross_gain, grad_cross_shift = norm_backward(first, cross_gain, grad_normed_cross)
    grad_first = grad_second + grad_part
    grad_first_branch = grad_first.astype(BF)

    grad_pair = jnp.concatenate([grad_text_keys, grad_text_values], axis=1)
    grad_projected = dot(grad_pair, cross_kv, 1, 1).astype(BF)
    grad_text_bias = jnp.sum(grad_projected.astype(F32), axis=0)
    padding = block - text_input.shape[1] // place.rows
    lefts = [cross_mix, normed_cross, projected, text_input, self_mix]
    rights = [
        grad_second_branch,
        grad_cross_queries,
        grad_text_keys,
        grad_text_values,
        grad_projected,
        grad_first_branch,
    ]
    result = second + result

    def backward_self(grad_self_mix, *before):
        return self_backward(
            row_lengths,
            queries,
            pair,
            pair_other,
            grad_self_mix,
            self_mix,
            self_lse,
            before=before,
        )[:5]

    def vector_list(grad_gain, grad_shift):
        return jnp.stack(
            [
                grad_gain,
                grad_shift,
                grad_cross_gain,
                grad_cross_shift,
                grad_text_bias,
                grad_feed_gain,
                grad_feed_shift,
                jnp.zeros_like(grad_feed_shift),
            ]
        )

    if kernels:
        (
            send_up,
            send_low,
            keep_up,
            keep_low,
            result,
            in_up,
            in_up_got,
            in_low,
            in_low_got,
            out_sum,
            grad_self_mix,
        ) = middle_parts(
            place,
            count,
            lefts,
            rights,
            result,
            result_away,
            (
                up_parts[1],
                place.next_x(up_parts[0]),
                low_parts[1],
                place.next_y(low_parts[0]),
                out_parts[1],
                place.next_z(out_parts[2]),
                out_parts[0],
            ),
            self_out,
        )
        up_got, low_got = place.next_x(send_up), place.next_y(send_low)
        out_got = place.next_z(out_sum)
        grads = backward_self(grad_self_mix)
        nothing = jnp.zeros_like(grad_feed_shift)
        sum_self_qkv, spread, sum_feed, vectors, grad_frames, grad_text = final_sums(
            place,
            count,
            normed_self,
            layer_raw,
            grad_first,
            self_gain[None],
            self_qkv,
            *grads,
            keep_up,
            up_got,
            keep_low,
            low_got,
            in_up,
            in_up_got,
            in_low,
            in_low_got,
            out_parts[3],
            out_got,
            vector_list(nothing, nothing),
            grad_projected,
            text_proj,
        )
        (
            grad_frames,
            grad_text,
            sum_self_qkv,
            sum_self_out,
            sum_cross_query,
            sum_text_proj,
            sum_cross_kv,
            sum_cross_out,
            sum_feed_in,
            sum_feed_out,
        ) = last_step(padding, piece, sum_self_qkv, spread, sum_feed, grad_frames, grad_text)
    else:

        def packed_self(*before):
            grads = backward_self(dot(grad_first_branch, self_out, 1, 1).astype(BF), *before)
            keys = (grads[1].astype(F32) + place.swap_core(grads[3]).astype(F32)).astype(BF)
            values = (grads[2].astype(F32) + place.swap_core(grads[4]).astype(F32)).astype(BF)
            return jnp.concatenate([grads[0], keys, values], axis=1)

        in_up = ring_sum([lambda a=a: a.astype(F32) for a in up_parts], place.next_x).astype(BF)
        in_low = ring_sum([lambda a=a: a.astype(F32) for a in low_parts], place.next_y).astype(BF)
        out_sum = ring_sum([lambda a=a: a.astype(F32) for a in out_parts], place.next_z).astype(BF)
        grad_text = dot(grad_projected, text_proj, 1, 1)
        text_blocks = text_input.reshape(text_total, place.rows, -1)
        text_padded = jnp.pad(text_blocks, ((0, 0), (0, 0), (0, padding))).reshape(text_total, width)
        lefts[3] = text_padded
        sum_feed, spread, sum_self_qkv, sum_self_out, grad_packed = permuted_sums(
            place, meta, in_up, in_low, out_sum, lefts, rights, normed_self, packed_self
        )
        result = (result + place.swap_core(result_away).astype(F32)).astype(BF)
        result = place.from_rows(result, count)
        grad_normed_self = dot(grad_packed, self_qkv, 1, 1)
        grad_part, grad_gain, grad_shift = norm_backward(layer_input, self_gain, grad_normed_self)
        grad_frames = place.from_rows((grad_first + grad_part).astype(BF), count)
        half = grad_text.shape[0] // 2
        text_away = place.swap_core(grad_text[half:].astype(BF))
        grad_text = (grad_text[:half] + text_away.astype(F32)).astype(BF)
        grad_text = place.from_rows(grad_text, count)
        vectors = place.vector_sum(vector_list(grad_gain, grad_shift))
        sum_cross_out, sum_cross_query = spread[:, :piece], spread[:, piece : 2 * piece]
        sum_cross_kv, sum_text_proj = spread[:, 2 * piece : 4 * piece], spread[:, 4 * piece : 5 * piece]
        sum_text_proj = sum_text_proj[: block - padding]
        sum_feed_in, sum_feed_out = sum_feed[0], jnp.swapaxes(sum_feed[1], 0, 1)
        grad_frames, grad_text = grad_frames.astype(F32), grad_text.astype(F32)
    vectors = pick(vectors.reshape(8, seq, width // seq), place.spot, 1)
    return (
        result,
        grad_frames,
        grad_text,
        vectors[0],
        vectors[1],
        sum_self_qkv,
        sum_self_out,
        vectors[2],
        vectors[3],
        sum_cross_query,
        sum_text_proj,
        vectors[4],
        sum_cross_kv,
        sum_cross_out,
        vectors[5],
        vectors[6],
        sum_feed_in,
        sum_feed_out,
    )


def solution(mesh):
    split, copied, table = P(ROWS, SEQ, None), P(), P(ROWS, None)
    vector, matrix = P(SEQ), P(ROWS, SEQ)
    return jax.shard_map(
        shards,
        mesh=mesh,
        in_specs=(split, split, table, table) + (copied,) * 15 + (split,),
        out_specs=(
            (split,) * 3
            + (vector, vector, matrix, matrix)
            + (vector, vector, matrix, matrix)
            + (vector, matrix, matrix)
            + (vector, vector, matrix, P(SEQ, ROWS))
        ),
        check_vma=False,
    )
```

```python
import functools
import math

import jax
import jax.numpy as jnp
from jax import lax
from jax.experimental import pallas as pl
from jax.experimental.pallas import tpu as pltpu
from jax.sharding import PartitionSpec as P

HD = 64
PAIR = 2 * HD
EPSILON = 1e-05
MASKED = -1e30
CLIPS = 4
ROWS = "rows"
SEQ = "seq"
BF = jnp.bfloat16
F32 = jnp.float32
VMEM_LIMIT = 48 * 1024 * 1024
MOST_VMEM = 62 * 1024 * 1024


def dot(left, right, left_dim=1, right_dim=0):
    return lax.dot_general(
        left, right, (((left_dim,), (right_dim,)), ((), ())), preferred_element_type=F32
    )


def pick(array, index, axis):
    return lax.dynamic_index_in_dim(array, index, axis, keepdims=False)


def after(value, *others):
    return lax.optimization_barrier((value,) + others)[0]


class Place:
    def __init__(self):
        self.rows, self.seq = lax.axis_size(ROWS), lax.axis_size(SEQ)
        self.nz = self.rows // 2
        self.nx = math.isqrt(self.seq)
        self.ny = self.seq // self.nx
        row, self.spot = lax.axis_index(ROWS), lax.axis_index(SEQ)
        self.core, self.z = row % 2, row // 2
        self.x, self.y = self.spot % self.nx, self.spot // self.nx
        self.owner = [0 if 4 * s // self.seq in (0, 3) else 1 for s in range(self.seq)]
        self.members = [[s for s in range(self.seq) if self.owner[s] == c] for c in (0, 1)]
        self.rank = [self.members[self.owner[s]].index(s) for s in range(self.seq)]

    def permute(self, value, target):
        pairs = []
        for z in range(self.nz):
            for c in range(2):
                for s in range(self.seq):
                    tz, tc, ts = target(z, c, s)
                    pairs.append(((2 * z + c) * self.seq + s, (2 * tz + tc) * self.seq + ts))
        return lax.ppermute(value, (ROWS, SEQ), pairs)

    def swap_core(self, value):
        return self.permute(value, lambda z, c, s: (z, 1 - c, s))

    def next_z(self, value):
        return self.permute(value, lambda z, c, s: ((z + 1) % self.nz, c, s))

    def next_x(self, value):
        nx = self.nx
        return self.permute(value, lambda z, c, s: (z, c, s // nx * nx + (s % nx + 1) % nx))

    def next_y(self, value):
        return self.permute(value, lambda z, c, s: (z, c, (s + self.nx) % self.seq))

    def to_rows(self, value):
        count = value.shape[0]
        my_rank = jnp.array(self.rank, jnp.int32)[self.spot]
        got = []
        for t in range(count):

            def target(z, c, s, t=t):
                return z, self.owner[s], c * count + (t + self.rank[s]) % count

            got.append(self.permute(pick(value, (t + my_rank) % count, 0), target))
        stacked = jnp.stack(got)
        here = self.spot % count
        return jnp.concatenate([pick(stacked, (here - k) % count, 0) for k in range(count)], axis=0)

    def from_rows(self, value, count):
        my_rank = jnp.array(self.rank, jnp.int32)[self.spot]
        slots = value.reshape(count, value.shape[0] // count, value.shape[1])
        here = self.spot % count
        got = []
        for t in range(count):

            def target(z, c, s, t=t):
                return z, s // count, self.members[c][(s % count - t) % count]

            got.append(self.permute(pick(slots, (here - t) % count, 0), target))
        stacked = jnp.stack(got)
        return jnp.stack([pick(stacked, (i - my_rank) % count, 0) for i in range(count)])

    def positions(self, total, core):
        quarter = total // 4
        inner = jnp.arange(quarter, dtype=jnp.int32)
        return jnp.concatenate([inner + core * quarter, inner + (3 - core) * quarter])

    def offset(self, i, j):
        return (self.y + 1 + i) % self.ny * self.nx + (self.x + 1 + j) % self.nx

    def relative_columns(self, value, outer_x):
        blocks = value.reshape(value.shape[0], self.seq, -1)
        if outer_x:
            order = [self.offset(i, j) for j in range(self.nx) for i in range(self.ny)]
        else:
            order = [self.offset(i, j) for i in range(self.ny) for j in range(self.nx)]
        return jnp.concatenate([pick(blocks, place, 1) for place in order], axis=1)


    def vector_sum(self, value):
        bit = 1
        while bit < self.rows:
            value = value + self.permute(
                value,
                lambda z, c, s: ((2 * z + c ^ bit) // 2, (2 * z + c ^ bit) % 2, s),
            )
            bit *= 2
        bit = 1
        while bit < self.seq:
            value = value + self.permute(value, lambda z, c, s: (z, c, s ^ bit))
            bit *= 2
        return value


def ring_order(count):
    return list(range(count - 2, -1, -1)) + [count - 1]


def ring_sum(pieces, send):
    order = ring_order(len(pieces))
    value = pieces[order[0]]()
    for k in order[1:]:
        value = pieces[k]() + send(value.astype(BF)).astype(F32)
    return value


def normalize(values):
    centered = values - jnp.mean(values, axis=-1, keepdims=True)
    scale = lax.rsqrt(jnp.mean(centered * centered, axis=-1, keepdims=True) + EPSILON)
    return centered * scale, scale


def layer_norm(values, gain, shift):
    return (normalize(values)[0] * gain + shift).astype(BF)


def norm_backward(values, gain, cotangent):
    normal, scale = normalize(values)
    grown = cotangent * gain
    inner = jnp.mean(grown, axis=-1, keepdims=True)
    along = jnp.mean(grown * normal, axis=-1, keepdims=True)
    grad = scale * (grown - inner - normal * along)
    return grad, jnp.sum(cotangent * normal, axis=0), jnp.sum(cotangent, axis=0)


def nt(left, right):
    return dot(left, right, 1, 1)


def head_lanes(values, head):
    lane = lax.broadcasted_iota(jnp.int32, values.shape, 1)
    return jnp.where((lane < HD) == (head == 0), values, jnp.zeros_like(values))


def turned(values):
    return jnp.swapaxes(values.astype(F32), 0, 1).astype(BF)


def running(lengths_ref, first):
    ends, total = [], 0
    for c in range(CLIPS):
        total = total + lengths_ref[first + c]
        ends.append(total)
    return ends


def spans(start, length, axis, ends):
    shape = (length, 1) if axis == 0 else (1, length)
    positions = lax.broadcasted_iota(jnp.int32, shape, axis) + start
    return sum((positions >= end).astype(jnp.int32) for end in ends)


def segment_bias(key_segment, query_segment, causal):
    allowed = key_segment == query_segment
    if causal:
        key = lax.broadcasted_iota(jnp.int32, allowed.shape, 0)
        query = lax.broadcasted_iota(jnp.int32, allowed.shape, 1)
        allowed = allowed & (key <= query)
    return jnp.where(allowed, 0.0, MASKED).astype(F32)


def forward_heads(queries, blocks, lse_ref, at):
    parts = []
    for head in range(2):
        query = head_lanes(queries, head)
        scores = [nt(keys, query) + bias() for keys, _, bias in blocks]
        highest = functools.reduce(
            jnp.maximum, [jnp.max(s, axis=0, keepdims=True) for s in scores]
        )
        weights = [jnp.exp(s - highest) for s in scores]
        total = sum(jnp.sum(w, axis=0, keepdims=True) for w in weights)
        mixed = sum(
            dot(values[head * HD : (head + 1) * HD], w.astype(BF))
            for (_, values, _), w in zip(blocks, weights)
        )
        parts.append(mixed * (1.0 / total))
        lse_ref[0, head : head + 1, at] = highest + jnp.log(total)
    return jnp.swapaxes(jnp.concatenate(parts, axis=0), 0, 1).astype(BF)


def backward_heads(queries, grads, mixed, blocks, lse_ref, at):
    product = jnp.swapaxes(grads.astype(F32) * mixed.astype(F32), 0, 1)
    parts = []
    for head in range(2):
        query, grad = head_lanes(queries, head), head_lanes(grads, head)
        rows = slice(head * HD, (head + 1) * HD)
        inner = jnp.sum(product[rows], axis=0, keepdims=True)
        totals = lse_ref[0, head : head + 1, at]
        grad_query = None
        for keys, turned_keys, values, bias, sums in blocks:
            weights = jnp.exp(nt(keys, query) + bias() - totals)
            scores = (weights * (nt(values, grad) - inner)).astype(BF)
            add_to(sums, 0, dot(scores, query))
            add_to(sums, 1, dot(weights.astype(BF), grad))
            term = dot(turned_keys[rows], scores)
            grad_query = term if grad_query is None else grad_query + term
        parts.append(grad_query)
    return (jnp.swapaxes(jnp.concatenate(parts, axis=0), 0, 1) * HD**-0.5).astype(BF)


def add_to(sums, index, term):
    sums[index] = term if sums[index] is None else sums[index] + term


def scaled(values):
    return values * jnp.array(HD**-0.5, BF)


def self_plan(core):
    if core == 0:
        return [(0, 0, 0)], [(0, 0, 1), (0, 1, 2), (1, 0, 3), (1, 1, 4)]
    return [(0, 0, 0), (1, 0, 4)], [(0, 0, 1), (0, 1, 2), (1, 0, 3)]


def self_biases(core, lengths_ref, bias_ref):
    length = bias_ref.shape[1]
    ends = running(lengths_ref, 0)
    quarters = (core, 3 - core)
    keys = [spans(q * length, length, 0, ends) for q in quarters]
    queries = [spans(q * length, length, 1, ends) for q in quarters]
    others = [spans(q * length, length, 0, ends) for q in (1 - core, 2 + core)]
    bias_ref[0] = segment_bias(keys[0], queries[0], True)
    bias_ref[1] = segment_bias(keys[0], queries[1], False)
    bias_ref[2] = segment_bias(keys[1], queries[1], True)
    bias_ref[3] = segment_bias(others[0], queries[1], False)
    last_key = jnp.where(core == 0, others[1], others[0])
    last_query = jnp.where(core == 0, queries[1], queries[0])
    bias_ref[4] = segment_bias(last_key, last_query, False)


def cross_bias(lengths_ref, bias_ref):
    core = lax.axis_index(ROWS) % 2
    count, rows = bias_ref.shape
    for n, token in enumerate((core, 3 - core, 1 - core, 2 + core)):
        keys = spans(token * (count // 4), count // 4, 0, running(lengths_ref, CLIPS))
        for m, frame in enumerate((core, 3 - core)):
            queries = spans(frame * (rows // 2), rows // 2, 1, running(lengths_ref, 0))
            at = slice(n * (count // 4), (n + 1) * (count // 4))
            bias_ref[at, m * (rows // 2) : (m + 1) * (rows // 2)] = segment_bias(keys, queries, False)


def self_forward_kernel(
    lengths_ref, q_ref, k_ref, v_ref, ko_ref, vo_ref, o_ref, lse_ref, bias_ref, fresh=True
):
    core = lax.axis_index(ROWS) % 2
    length = bias_ref.shape[1]

    @pl.when((pl.program_id(0) == 0) & fresh)
    def _():
        self_biases(core, lengths_ref, bias_ref)

    keys, values = (k_ref, ko_ref), (v_ref, vo_ref)
    for which in range(2):

        @pl.when((core == 0) == (which == 0))
        def _(which=which):
            for half, plan in enumerate(self_plan(which)):
                at = slice(half * length, (half + 1) * length)
                blocks = []
                for source, part, number in plan:
                    where = slice(part * length, (part + 1) * length)
                    blocks.append(
                        (
                            keys[source][where],
                            turned(values[source][where]),
                            functools.partial(bias_ref.__getitem__, number),
                        )
                    )
                o_ref[at] = forward_heads(scaled(q_ref[at]), blocks, lse_ref, at)


def self_backward_kernel(
    lengths_ref,
    q_ref,
    k_ref,
    v_ref,
    ko_ref,
    vo_ref,
    g_ref,
    o_ref,
    lse_ref,
    dq_ref,
    dk_ref,
    dv_ref,
    dko_ref,
    dvo_ref,
    bias_ref,
    fresh=True,
):
    core = lax.axis_index(ROWS) % 2
    length = bias_ref.shape[1]

    @pl.when((pl.program_id(0) == 0) & fresh)
    def _():
        self_biases(core, lengths_ref, bias_ref)

    keys, values = (k_ref, ko_ref), (v_ref, vo_ref)
    for which in range(2):

        @pl.when((core == 0) == (which == 0))
        def _(which=which):
            sums = {(s, p): [None, None] for s in range(2) for p in range(2)}
            for half, plan in enumerate(self_plan(which)):
                at = slice(half * length, (half + 1) * length)
                blocks = []
                for source, part, number in plan:
                    where = slice(part * length, (part + 1) * length)
                    blocks.append(
                        (
                            keys[source][where],
                            turned(keys[source][where]),
                            values[source][where],
                            functools.partial(bias_ref.__getitem__, number),
                            sums[source, part],
                        )
                    )
                dq_ref[at] = backward_heads(
                    scaled(q_ref[at]), g_ref[at], o_ref[at], blocks, lse_ref, at
                )
            for (source, part), pair in sums.items():
                where = slice(part * length, (part + 1) * length)
                for ref, value in zip(((dk_ref, dv_ref), (dko_ref, dvo_ref))[source], pair):
                    if value is None:
                        ref[where] = jnp.zeros((length, PAIR), BF)
                    else:
                        ref[where] = value.astype(BF)


def cross_forward_kernel(lengths_ref, q_ref, k_ref, v_ref, o_ref, lse_ref, bias_ref, fresh=True):
    length = q_ref.shape[0] // 2

    @pl.when((pl.program_id(0) == 0) & fresh)
    def _():
        cross_bias(lengths_ref, bias_ref)

    turned_values = turned(v_ref[...])
    for half in range(2):
        at = slice(half * length, (half + 1) * length)
        blocks = [(k_ref[...], turned_values, lambda at=at: bias_ref[:, at])]
        o_ref[at] = forward_heads(scaled(q_ref[at]), blocks, lse_ref, at)


def cross_backward_kernel(
    lengths_ref,
    q_ref,
    k_ref,
    v_ref,
    g_ref,
    o_ref,
    lse_ref,
    dq_ref,
    dk_ref,
    dv_ref,
    bias_ref,
    fresh=True,
):
    length = q_ref.shape[0] // 2

    @pl.when((pl.program_id(0) == 0) & fresh)
    def _():
        cross_bias(lengths_ref, bias_ref)

    turned_keys = turned(k_ref[...])
    sums = [None, None]
    for half in range(2):
        at = slice(half * length, (half + 1) * length)
        blocks = [(k_ref[...], turned_keys, v_ref[...], lambda at=at: bias_ref[:, at], sums)]
        dq_ref[at] = backward_heads(scaled(q_ref[at]), g_ref[at], o_ref[at], blocks, lse_ref, at)
    dk_ref[...] = sums[0].astype(BF)
    dv_ref[...] = sums[1].astype(BF)


GROUP = 4


def column(rows, first=0):
    return pl.BlockSpec((rows, GROUP * PAIR), lambda i: (0, first // GROUP + i))


def grouped(kernel):
    def part(ref, pair):
        if len(ref.shape) == 2 and ref.shape[1] == GROUP * PAIR and ref.dtype == BF:
            return ref.at[:, pair * PAIR : (pair + 1) * PAIR]
        if len(ref.shape) == 3 and ref.shape[:2] == (GROUP, 8):
            return ref.at[pair : pair + 1]
        return ref

    def run(*refs):
        for pair in range(GROUP):
            kernel(*[part(ref, pair) for ref in refs], fresh=pair == 0)

    return run


SMEM_SPEC = pl.BlockSpec(memory_space=pltpu.SMEM)


def without(kernel, first, count):
    def run(*refs):
        kernel(*refs[:first], *refs[first + count :])

    return run


ANY_SPEC = pl.BlockSpec(memory_space=pl.ANY)
WHOLE_SPEC = pl.BlockSpec(memory_space=pltpu.VMEM)


MARK = jax.ShapeDtypeStruct((8, 128), F32)


def marked(kernel, at):
    def run(*refs):
        refs[at][...] = jnp.zeros((8, 128), F32)
        kernel(*refs[:at], *refs[at + 1 :])

    return run


def attention_call(
    kernel, heads, in_specs, outs, bias_shape, flops, arguments, before=(), limit=VMEM_LIMIT
):
    pairs = heads // 2
    kernel = marked(grouped(kernel), len(arguments) + len(outs))
    kernel = without(kernel, len(arguments), len(before))
    in_specs = list(in_specs) + [ANY_SPEC] * len(before)
    arguments = tuple(arguments) + tuple(before)
    out_shape, out_specs = [], []
    for rows in outs:
        if rows is None:
            queries = outs[0]
            out_shape.append(jax.ShapeDtypeStruct((pairs, 8, queries), F32))
            out_specs.append(lse_spec(queries))
        else:
            out_shape.append(jax.ShapeDtypeStruct((rows, pairs * PAIR), BF))
            out_specs.append(column(rows))
    out_shape.append(MARK)
    out_specs.append(pl.BlockSpec((8, 128), lambda i: (0, 0)))
    return pl.pallas_call(
        kernel,
        grid=(pairs // GROUP,),
        in_specs=in_specs,
        out_specs=out_specs,
        out_shape=out_shape,
        scratch_shapes=[pltpu.VMEM(bias_shape, F32)],
        compiler_params=pltpu.CompilerParams(vmem_limit_bytes=limit),
        cost_estimate=pl.CostEstimate(flops=flops, bytes_accessed=8 << 20, transcendentals=flops >> 8),
    )(*arguments)


def lse_spec(queries):
    return pl.BlockSpec((GROUP, 8, queries), lambda i: (i, 0, 0))


def self_forward(lengths, queries, pair, pair_other):
    rows, width = queries.shape
    heads = width // HD
    length = rows // 2
    half = heads // 2
    return attention_call(
        self_forward_kernel,
        heads,
        [
            SMEM_SPEC,
            column(rows),
            column(rows),
            column(rows, half),
            column(rows),
            column(rows, half),
        ],
        (rows, None),
        (5, length, length),
        heads * 5 * 4 * length * length * PAIR * 2,
        (lengths, queries, pair, pair, pair_other, pair_other),
    )


def self_backward(lengths, queries, pair, pair_other, grads, mixed, lse, before=()):
    rows, width = queries.shape
    heads = width // HD
    length = rows // 2
    half = heads // 2
    return attention_call(
        self_backward_kernel,
        heads,
        [
            SMEM_SPEC,
            column(rows),
            column(rows),
            column(rows, half),
            column(rows),
            column(rows, half),
            column(rows),
            column(rows),
            lse_spec(rows),
        ],
        (rows,) * 5,
        (5, length, length),
        heads * 5 * 10 * length * length * PAIR * 2,
        (lengths, queries, pair, pair, pair_other, pair_other, grads, mixed, lse),
        before,
        MOST_VMEM,
    )


def cross_forward(lengths, queries, pair):
    rows, width = queries.shape
    heads = width // HD
    count = pair.shape[0]
    return attention_call(
        cross_forward_kernel,
        heads,
        [SMEM_SPEC, column(rows), column(count), column(count, heads // 2)],
        (rows, None),
        (count, rows),
        heads * 4 * rows * count * PAIR * 2,
        (lengths, queries, pair, pair),
    )


def cross_backward(lengths, queries, pair, grads, mixed, lse, before=()):
    rows, width = queries.shape
    heads = width // HD
    count = pair.shape[0]
    return attention_call(
        cross_backward_kernel,
        heads,
        [
            SMEM_SPEC,
            column(rows),
            column(count),
            column(count, heads // 2),
            column(rows),
            column(rows),
            lse_spec(rows),
        ],
        (rows, count, count),
        (count, rows),
        heads * 10 * rows * count * PAIR * 2,
        (lengths, queries, pair, pair, grads, mixed, lse),
        before,
    )


def gelu_and_slope(values):
    inside = 0.5 * (1.0 + lax.erf(values * (0.5**0.5)))
    bell = jnp.exp(-0.5 * values * values) * ((2.0 * math.pi) ** -0.5)
    return values * inside, inside + values * bell


def feed_kernel(shape, meta_ref, own_in, other_in, gown_in, gother_in, win_ref, wout_ref, *refs):
    nx, ny, nz, chunk = shape
    res_out, res_other_out, grad_out, grad_other_out = refs[:4]
    up_refs, low_refs, gout_refs = refs[4 : 4 + nx], refs[4 + nx : 4 + nx + ny], refs[4 + nx + ny : 4 + nx + ny + nz]
    scratch = refs[4 + nx + ny + nz :]
    act_ref, pre_ref, own_ref, other_ref, gown_ref, gother_ref, res_acc, grad_acc = scratch[:8]
    res_ref, grad_ref, res_other_ref, grad_other_ref, load_sems, store_sems = scratch[8:]
    loads = [
        pltpu.make_async_copy(source, target, load_sems.at[number])
        for number, (source, target) in enumerate(
            (
                (own_in, own_ref),
                (gown_in, gown_ref),
                (other_in, other_ref),
                (gother_in, gother_ref),
            )
        )
    ]
    stores = [
        pltpu.make_async_copy(source, target, store_sems.at[number])
        for number, (source, target) in enumerate(
            (
                (res_ref, res_out),
                (res_other_ref, res_other_out),
                (grad_ref, grad_out),
                (grad_other_ref, grad_other_out),
            )
        )
    ]
    j, i = pl.program_id(0), pl.program_id(1)
    z = meta_ref[3]
    tokens = own_ref.shape[0]
    sources = ((own_ref, gown_ref, res_ref, grad_ref), (other_ref, gother_ref, res_acc, grad_acc))

    first = (i == 0) & (j == 0)

    @pl.when(first)
    def _():
        for load in loads:
            load.start()
        for _, _, res, grad in sources:
            res[...] = jnp.zeros_like(res)
            grad[...] = jnp.zeros_like(grad)

    for side, (values, grads, res, grad) in enumerate(sources):

        @pl.when(first)
        def _(side=side):
            loads[2 * side].wait()
            loads[2 * side + 1].wait()

        for m in range(tokens // chunk):
            at = slice(m * chunk, (m + 1) * chunk)
            activated, slope = gelu_and_slope(dot(values[at], win_ref[...]))
            activated = activated.astype(BF)
            before = (nt(grads[at], wout_ref[...]) * slope).astype(BF)
            to = slice(side * tokens + m * chunk, side * tokens + (m + 1) * chunk)
            act_ref[to] = activated
            pre_ref[to] = before
            res[at] += dot(activated, wout_ref[...])
            grad[at] += nt(before, win_ref[...])

    @pl.when((i == ny - 1) & (j == nx - 1))
    def _():
        res_other_ref[...] = res_acc[...].astype(BF)
        grad_other_ref[...] = grad_acc[...].astype(BF)
        for copy in stores:
            copy.start()

    rows = own_ref.shape[1] // nz
    half = rows // 2

    def both(one, two, right):
        low, high = right[:tokens], right[tokens:]
        return (dot(one, low, 0, 0) + dot(two, high, 0, 0)).astype(BF)

    for k in range(nz):
        at = pl.ds(pl.multiple_of((z + 1 + k) % nz * rows, rows), rows)
        gin = both(own_ref[:, at], other_ref[:, at], pre_ref)
        gout_refs[k][0] = both(gown_ref[:, at], gother_ref[:, at], act_ref)
        to = slice(k * half, (k + 1) * half)
        for number, ref in enumerate(up_refs):

            @pl.when(j == number)
            def _(ref=ref):
                ref[0, to] = gin[:half]

        for number, ref in enumerate(low_refs):

            @pl.when(i == number)
            def _(ref=ref):
                ref[0, to] = gin[half:]

    @pl.when((i == ny - 1) & (j == nx - 1))
    def _():
        for copy in stores:
            copy.wait()


def feed(place, meta, own, other, gown, gother, feed_in, feed_out):
    nx, ny, nz = place.nx, place.ny, place.nz
    tokens, width = own.shape
    part = feed_in.shape[1] // place.seq // 2
    chunk = min(256, tokens)

    def unit(j, i, meta):
        return 2 * ((meta[2] + 1 + i) % ny * nx + (meta[1] + 1 + j) % nx) + meta[0]

    def up_spec(number):
        def index(j, i, meta):
            return jnp.where(j == number, i, jnp.where(j < number, 0, ny - 1)), 0, 0

        return pl.BlockSpec((1, width // 2, part), index)

    low_spec = pl.BlockSpec((1, width // 2, part), lambda j, i, meta: (j, 0, 0))
    gout_spec = pl.BlockSpec((1, width // nz, part), lambda j, i, meta: (j * ny + i, 0, 0))
    total = 2 * tokens
    shape = jax.ShapeDtypeStruct
    return pl.pallas_call(
        functools.partial(feed_kernel, (nx, ny, nz, chunk)),
        grid_spec=pltpu.PrefetchScalarGridSpec(
            num_scalar_prefetch=1,
            grid=(nx, ny),
            in_specs=[ANY_SPEC] * 4
            + [
                pl.BlockSpec((width, part), lambda j, i, meta: (0, unit(j, i, meta))),
                pl.BlockSpec((part, width), lambda j, i, meta: (unit(j, i, meta), 0)),
            ],
            out_specs=[ANY_SPEC] * 4
            + [up_spec(n) for n in range(nx)]
            + [low_spec] * ny
            + [gout_spec] * nz,
            scratch_shapes=[
                pltpu.VMEM((total, part), BF),
                pltpu.VMEM((total, part), BF),
                pltpu.VMEM((tokens, width), BF),
                pltpu.VMEM((tokens, width), BF),
                pltpu.VMEM((tokens, width), BF),
                pltpu.VMEM((tokens, width), BF),
                pltpu.VMEM((tokens, width), F32),
                pltpu.VMEM((tokens, width), F32),
                pltpu.VMEM((tokens, width), F32),
                pltpu.VMEM((tokens, width), F32),
                pltpu.VMEM((tokens, width), BF),
                pltpu.VMEM((tokens, width), BF),
                pltpu.SemaphoreType.DMA((4,)),
                pltpu.SemaphoreType.DMA((4,)),
            ],
        ),
        out_shape=[
            shape((tokens, width), F32),
            shape((tokens, width), BF),
            shape((tokens, width), F32),
            shape((tokens, width), BF),
        ]
        + [shape((ny, width // 2, part), BF)] * nx
        + [shape((nx, width // 2, part), BF)] * ny
        + [shape((place.seq, width // nz, part), BF)] * nz,
        compiler_params=pltpu.CompilerParams(vmem_limit_bytes=60 * 1024 * 1024),
        cost_estimate=pl.CostEstimate(
            flops=12 * total * width * part * place.seq,
            bytes_accessed=40 << 20,
            transcendentals=2 * total * part * place.seq,
        ),
    )(meta, own, other, gown, gother, feed_in, feed_out)


def weight_kernel(shape, meta_ref, *refs):
    count, nz = shape
    lefts, rights = refs[:count], refs[count : 2 * count]
    own_ref, other_ref, turned_ref = refs[2 * count :]
    core, z = meta_ref[0], meta_ref[3]
    block = own_ref.shape[1] // nz
    for number in range(count):

        @pl.when(pl.program_id(0) == number)
        def _(left=lefts[number], right=rights[number]):
            tokens = left.shape[0]
            turned_ref[:, :tokens] = turned(left[...])
            for k in range(nz):
                start = (z + 1 + k) % nz * 2
                to = slice(k * block, (k + 1) * block)
                for which, ref in ((core, own_ref), (1 - core, other_ref)):
                    at = pl.ds(pl.multiple_of((start + which) * block, block), block)
                    ref[0, to] = dot(turned_ref[at, :tokens], right[...]).astype(BF)


def weight_parts(place, meta, lefts, rights, before=()):
    count = len(lefts)
    depth, width = lefts[0].shape[1], rights[0].shape[1]
    tokens = max(left.shape[0] for left in lefts)
    out = jax.ShapeDtypeStruct((count, depth // 2, width), BF)
    spec = pl.BlockSpec((1, depth // 2, width), lambda u: (u, 0, 0))
    return pl.pallas_call(
        without(functools.partial(weight_kernel, (count, place.nz)), 1 + 2 * count, len(before)),
        grid=(count,),
        in_specs=[SMEM_SPEC] + [WHOLE_SPEC] * (2 * count) + [ANY_SPEC] * len(before),
        out_specs=[spec, spec],
        out_shape=[out, out],
        scratch_shapes=[pltpu.VMEM((depth, tokens), BF)],
        compiler_params=pltpu.CompilerParams(vmem_limit_bytes=VMEM_LIMIT),
        cost_estimate=pl.CostEstimate(
            flops=2 * count * tokens * depth * width,
            bytes_accessed=count * depth * width * 4,
            transcendentals=0,
        ),
    )(meta, *lefts, *rights, *before)


MESH = pl.DeviceIdType.MESH


class Mail:
    def __init__(self, send_sems, recv_sems):
        self.send_sems, self.recv_sems, self.sent = send_sems, recv_sems, []

    def send(self, source, target, device):
        number = len(self.sent)
        copy = pltpu.make_async_remote_copy(
            src_ref=source,
            dst_ref=target,
            send_sem=self.send_sems.at[number],
            recv_sem=self.recv_sems.at[number],
            device_id=device,
            device_id_type=MESH,
        )
        copy.start()
        self.sent.append(copy)
        return copy

    def finish(self):
        for copy in self.sent:
            copy.wait_send()


class Ways:
    def __init__(self, nz):
        self.row, self.spot = lax.axis_index(ROWS), lax.axis_index(SEQ)
        self.core, self.z = self.row % 2, self.row // 2
        self.x, self.y = self.spot % 2, self.spot // 2
        self.nz = nz
        self.sibling = (self.row + 1 - 2 * self.core, self.spot)
        self.across_x = (self.row, self.spot + 1 - 2 * self.x)
        self.across_y = (self.row, self.y * -2 + 2 + self.x)
        self.above = ((self.row + 2) % (2 * nz), self.spot)
        self.below = ((self.row + 2 * nz - 2) % (2 * nz), self.spot)

    def plane(self):
        devices = []
        for other in range(2):
            row = self.row if other == 0 else self.sibling[0]
            devices += [(row, (self.spot + s) % 4) for s in range(4) if other or s]
        return devices

    def meet(self, devices):
        barrier = pltpu.get_barrier_semaphore()
        for device in devices:
            pl.semaphore_signal(barrier, inc=1, device_id=device, device_id_type=MESH)
        pl.semaphore_wait(barrier, len(devices))

    def place(self, q):
        return (self.y + 1 + q % 2) % 2 * 2 + (self.x + 1 + q // 2) % 2

    def rows(self, k, which, block):
        start = ((self.z + 1 + k) % self.nz * 2 + which) * block
        return pl.ds(pl.multiple_of(start, block), block)


class Home:
    def __init__(self, ways, out_ref, send_sems, recv_sems):
        self.ways, self.out_ref = ways, out_ref
        self.send_sems, self.recv_sems = send_sems, recv_sems
        self.started = []

    def send(self, source, slot):
        ways = self.ways
        spot = jnp.where(ways.core == 0, 3 * slot, 1 + slot)
        row = 2 * ways.z + ways.spot // 2
        stays = (spot == ways.spot) & (row == ways.row)
        to = self.out_ref.at[ways.spot % 2]
        copy = pltpu.make_async_remote_copy(
            src_ref=source,
            dst_ref=to,
            send_sem=self.send_sems.at[slot],
            recv_sem=self.recv_sems.at[ways.spot % 2],
            device_id=(row, spot),
            device_id_type=MESH,
        )
        local = pltpu.make_async_copy(source, to, self.recv_sems.at[ways.spot % 2])

        @pl.when(stays)
        def _():
            local.start()

        @pl.when(jnp.logical_not(stays))
        def _():
            copy.start()

        self.started.append((stays, copy))

    def finish(self):
        for r in range(2):
            to = self.out_ref.at[r]
            pltpu.make_async_copy(to, to, self.recv_sems.at[r]).wait()
        for stays, copy in self.started:

            @pl.when(jnp.logical_not(stays))
            def _(copy=copy):
                copy.wait_send()


class Gathering:
    def __init__(self, ways, source_ref, target_ref, send_sems, recv_sems):
        self.ways, self.source_ref, self.target_ref = ways, source_ref, target_ref
        self.send_sems, self.recv_sems = send_sems, recv_sems
        self.block = source_ref.shape[1]
        self.copies = []
        owner = jnp.where((ways.spot == 0) | (ways.spot == 3), 0, 1)
        slot = ways.spot // 2
        to = target_ref.at[pl.ds(pl.multiple_of(slot * self.block, self.block), self.block)]
        for r in range(2):
            row, spot = 2 * ways.z + owner, 2 * ways.core + r
            stays = (spot == ways.spot) & (row == ways.row)
            copy = pltpu.make_async_remote_copy(
                src_ref=source_ref.at[r],
                dst_ref=to,
                send_sem=send_sems.at[r],
                recv_sem=recv_sems.at[slot],
                device_id=(row, spot),
                device_id_type=MESH,
            )
            local = pltpu.make_async_copy(source_ref.at[r], to, recv_sems.at[slot])
            self.copies.append((stays, copy, local))

    def start(self):
        for stays, copy, local in self.copies:

            @pl.when(stays)
            def _(local=local):
                local.start()

            @pl.when(jnp.logical_not(stays))
            def _(copy=copy):
                copy.start()

    def arrived(self, slot):
        to = self.target_ref.at[slot * self.block : (slot + 1) * self.block]
        pltpu.make_async_copy(to, to, self.recv_sems.at[slot]).wait()

    def finish(self):
        for stays, copy, _ in self.copies:

            @pl.when(jnp.logical_not(stays))
            def _(copy=copy):
                copy.wait_send()


def self_forward_carrying(nz, lengths_ref, *refs):
    grads_ref, cotangent_ref = refs[5], refs[8]
    bias_ref, sends, recvs = refs[9:]
    gathering = Gathering(Ways(nz), grads_ref, cotangent_ref, sends, recvs)

    @pl.when(pl.program_id(0) == 0)
    def _():
        gathering.ways.meet(gathering.ways.plane())
        gathering.start()

    grouped(self_forward_kernel)(lengths_ref, *refs[:5], *refs[6:8], bias_ref)

    @pl.when(pl.program_id(0) == pl.num_programs(0) - 1)
    def _():
        for slot in range(2):
            gathering.arrived(slot)
        gathering.finish()


def self_forward_and_gather(place, lengths, queries, pair, pair_other, grads):
    rows, width = queries.shape
    half = width // HD // 2
    length = rows // 2
    return pl.pallas_call(
        functools.partial(self_forward_carrying, place.nz),
        grid=(half // GROUP,),
        in_specs=[
            SMEM_SPEC,
            column(rows),
            column(rows),
            column(rows, half),
            column(rows),
            column(rows, half),
            ANY_SPEC,
        ],
        out_specs=[column(rows), lse_spec(rows), ANY_SPEC],
        out_shape=[
            jax.ShapeDtypeStruct((rows, width), BF),
            jax.ShapeDtypeStruct((half, 8, rows), F32),
            jax.ShapeDtypeStruct((rows, width), BF),
        ],
        scratch_shapes=[pltpu.VMEM((5, length, length), F32)]
        + [pltpu.SemaphoreType.DMA((2,))] * 2,
        compiler_params=pltpu.CompilerParams(
            collective_id=4, has_side_effects=True, vmem_limit_bytes=VMEM_LIMIT
        ),
        cost_estimate=pl.CostEstimate(
            flops=40 * rows * length * width, bytes_accessed=8 << 20, transcendentals=0
        ),
    )(lengths, queries, pair, pair, pair_other, pair_other, grads)


def entry_kernel(
    nz,
    frames_ref,
    text_ref,
    lengths_ref,
    gain_ref,
    shift_ref,
    qkv_ref,
    proj_ref,
    bias_ref,
    kv_ref,
    input_out,
    normed_out,
    queries_out,
    pair_out,
    pair_other_ref,
    words_out,
    projected_out,
    text_pair_out,
    lengths_other_ref,
    input_ref,
    normed_ref,
    queries_ref,
    pair_ref,
    words_ref,
    projected_ref,
    text_pair_ref,
    store_sems,
    qkv_here,
    proj_here,
    kv_here,
    load_sems,
    send_sems,
    recv_sems,
    gather_sends,
    gather_recvs,
):
    loads = [
        pltpu.make_async_copy(source, target, load_sems.at[number])
        for number, (source, target) in enumerate(
            ((proj_ref, proj_here), (kv_ref, kv_here), (qkv_ref, qkv_here))
        )
    ]
    for load in loads:
        load.start()
    stores = []

    def store(source, target):
        copy = pltpu.make_async_copy(source, target, store_sems.at[len(stores)])
        copy.start()
        stores.append(copy)

    ways = Ways(nz)
    ways.meet(ways.plane())
    mail = Mail(send_sems, recv_sems)
    words = Gathering(ways, text_ref, words_ref, gather_sends.at[0], gather_recvs.at[0])
    frames = Gathering(ways, frames_ref, input_ref, gather_sends.at[1], gather_recvs.at[1])
    words.start()
    frames.start()
    lengths_copy = mail.send(lengths_ref, lengths_other_ref, ways.sibling)
    half = words_ref.shape[0] // 2
    for slot in range(2):
        words.arrived(slot)
    words_copy = mail.send(words_ref.at[:half], words_ref.at[half:], ways.sibling)
    loads[0].wait()
    loads[1].wait()
    words_copy.wait_recv()
    store(words_ref, words_out)
    projected = (dot(words_ref[...], proj_here[...]) + bias_ref[...]).astype(BF)
    projected_ref[...] = projected
    store(projected_ref, projected_out)
    text_pair_ref[...] = dot(projected, kv_here[...]).astype(BF)
    store(text_pair_ref, text_pair_out)
    loads[2].wait()
    width = input_ref.shape[1]
    block = input_ref.shape[0] // 2
    copies = []
    for slot in range(2):
        frames.arrived(slot)
        at = slice(slot * block, (slot + 1) * block)
        normed_ref[at] = layer_norm(input_ref[at].astype(F32), gain_ref[...], shift_ref[...])
        store(input_ref.at[at], input_out.at[at])
        store(normed_ref.at[at], normed_out.at[at])
        pair_ref[at] = dot(normed_ref[at], qkv_here[:, width:]).astype(BF)
        store(pair_ref.at[at], pair_out.at[at])
        copies.append(mail.send(pair_ref.at[at], pair_other_ref.at[at], ways.sibling))
    queries_ref[...] = dot(normed_ref[...], qkv_here[:, :width]).astype(BF)
    store(queries_ref, queries_out)
    lengths_copy.wait_recv()
    for copy in copies:
        copy.wait_recv()
    mail.finish()
    for gathering in (words, frames):
        gathering.finish()
    for copy in stores:
        copy.wait()


def entry(place, frames, text, lengths, gain, shift, qkv, proj, bias, kv):
    count, block, width = frames.shape
    tokens, words = count * block, 2 * count * text.shape[1]
    shape, vmem = jax.ShapeDtypeStruct, pltpu.VMEM
    return pl.pallas_call(
        functools.partial(entry_kernel, place.nz),
        in_specs=[ANY_SPEC] * 2 + [WHOLE_SPEC] * 3 + [ANY_SPEC] * 2 + [WHOLE_SPEC, ANY_SPEC],
        out_specs=[ANY_SPEC] * 8 + [WHOLE_SPEC],
        out_shape=[
            shape((tokens, width), BF),
            shape((tokens, width), BF),
            shape((tokens, width), BF),
            shape((tokens, 2 * width), BF),
            shape((tokens, 2 * width), BF),
            shape((words, text.shape[2]), BF),
            shape((words, width), BF),
            shape((words, 2 * width), BF),
            shape(lengths.shape, jnp.int32),
        ],
        scratch_shapes=[
            vmem((tokens, width), BF),
            vmem((tokens, width), BF),
            vmem((tokens, width), BF),
            vmem((tokens, 2 * width), BF),
            vmem((words, text.shape[2]), BF),
            vmem((words, width), BF),
            vmem((words, 2 * width), BF),
            pltpu.SemaphoreType.DMA((10,)),
            vmem(qkv.shape, BF),
            vmem(proj.shape, BF),
            vmem(kv.shape, BF),
            pltpu.SemaphoreType.DMA((3,)),
            pltpu.SemaphoreType.DMA((4,)),
            pltpu.SemaphoreType.DMA((4,)),
            pltpu.SemaphoreType.DMA((2, 2)),
            pltpu.SemaphoreType.DMA((2, 2)),
        ],
        compiler_params=pltpu.CompilerParams(
            collective_id=3, has_side_effects=True, vmem_limit_bytes=MOST_VMEM
        ),
        cost_estimate=pl.CostEstimate(
            flops=20 * tokens * width * width, bytes_accessed=20 << 20, transcendentals=0
        ),
    )(frames, text, lengths, gain[None], shift[None], qkv, proj, bias[None], kv)


def with_loads(kernel, count, late):
    def run(*refs):
        inputs, rest = list(refs[:count]), refs[count:]
        here, sems = rest[-len(late) - 1 : -1], rest[-1]
        copies = []
        for number, which in enumerate(late):
            copy = pltpu.make_async_copy(inputs[which], here[number], sems.at[number])
            copy.start()
            inputs[which] = here[number]
            copies.append(copy)
        open_copies = dict(zip(map(id, here), copies))

        def wait(*wanted):
            for ref in wanted:
                open_copies.pop(id(ref)).wait()

        kernel(wait, *inputs, *rest[: -len(late) - 1])

    return run


def load_scratch(operands, late):
    return [pltpu.VMEM(operands[n].shape, operands[n].dtype) for n in late] + [
        pltpu.SemaphoreType.DMA((len(late),))
    ]


def middle_kernel(
    shape,
    wait,
    mixed_ref,
    normed_ref,
    projected_ref,
    text_ref,
    self_ref,
    g_second_ref,
    g_query_ref,
    g_keys_ref,
    g_values_ref,
    g_projected_ref,
    g_first_ref,
    result_ref,
    result_away_ref,
    in_up_ref,
    in_up_got_ref,
    in_low_ref,
    in_low_got_ref,
    out_one_ref,
    out_one_got_ref,
    out_zero_ref,
    self_weight_ref,
    send_up_ref,
    send_low_ref,
    keep_up_ref,
    keep_low_ref,
    result_out,
    in_up_keep,
    in_up_next,
    in_low_keep,
    in_low_next,
    out_next,
    g_mix_ref,
    mixed_t,
    normed_t,
    projected_t,
    text_t,
    self_t,
    own_ref,
    away_ref,
    got_ref,
    result_got_ref,
    in_send_ref,
    out_send_ref,
    out_came_ref,
    send_sems,
    recv_sems,
    home_sends,
    home_recvs,
):
    nz, piece = shape
    ways = Ways(nz)
    ways.meet(ways.plane() + [ways.above, ways.below])
    mail = Mail(send_sems, recv_sems)
    result_copy = mail.send(result_away_ref, result_got_ref, ways.sibling)
    wait(out_one_ref, out_one_got_ref)
    out_send_ref[...] = out_one_ref[...] + out_one_got_ref[...]
    out_copy = mail.send(out_send_ref, out_came_ref, ways.above)
    wait(in_up_ref, in_up_got_ref, in_low_ref, in_low_got_ref)
    in_send_ref[0] = in_up_ref[0] + in_up_got_ref[0]
    in_send_ref[1] = in_low_ref[0] + in_low_got_ref[0]
    in_copies = [
        mail.send(in_send_ref.at[0], in_up_next, ways.across_y),
        mail.send(in_send_ref.at[1], in_low_next, ways.across_x),
    ]
    in_up_keep[...] = in_up_ref[1] + in_up_got_ref[1]
    in_low_keep[...] = in_low_ref[1] + in_low_got_ref[1]
    home = Home(ways, result_out, home_sends, home_recvs)
    for left, to in ((mixed_ref, mixed_t), (normed_ref, normed_t), (projected_ref, projected_t), (self_ref, self_t)):
        wait(left)
        to[...] = turned(left[...])
    wait(text_ref)
    turned_text = turned(text_ref[...])
    block = own_ref.shape[2]
    count = 2 * nz
    part = turned_text.shape[0] // count
    text_t[...] = jnp.zeros_like(text_t)
    for b in range(count):
        text_t[b * block : b * block + part] = turned_text[b * part : (b + 1) * part]
    half = block // 2
    up, low = slice(0, half), slice(half, block)
    homes = (
        (send_up_ref.at[0], send_low_ref.at[0]),
        (send_up_ref.at[1], keep_low_ref.at[0]),
        (keep_up_ref.at[0], send_low_ref.at[1]),
        (keep_up_ref.at[1], keep_low_ref.at[1]),
    )
    copies = []
    wait(g_second_ref, g_query_ref, g_keys_ref, g_values_ref, g_projected_ref, g_first_ref)

    def settle(q):
        copies[q].wait_recv()
        total = own_ref[q] + got_ref[q]
        homes[q][0][...] = total[:, up]
        homes[q][1][...] = total[:, low]

    for q in range(4):
        place = ways.place(q)
        columns = pl.ds(pl.multiple_of(place * piece, piece), piece)
        twice = pl.ds(pl.multiple_of(place % 2 * 2 * piece, piece), 2 * piece)
        pair = jnp.where(place < 2, g_keys_ref[:, twice], g_values_ref[:, twice])
        units = (
            (mixed_t, g_second_ref[:, columns]),
            (normed_t, g_query_ref[:, columns]),
            (projected_t, pair),
            (text_t, g_projected_ref[:, columns]),
            (self_t, g_first_ref[:, columns]),
        )
        for which, ref in ((1 - ways.core, away_ref), (ways.core, own_ref)):
            first = 0
            for left, right in units:
                to = slice(first, first + right.shape[1])
                first += right.shape[1]
                for k in range(nz):
                    ref[q, k, :, to] = dot(left[ways.rows(k, which, block)], right).astype(BF)
            if ref is away_ref:
                copies.append(mail.send(away_ref.at[q], got_ref.at[q], ways.sibling))
        if q == 0:
            wait(result_ref)
            result_copy.wait_recv()
            result_got_ref[...] = (result_ref[...] + result_got_ref[...].astype(F32)).astype(BF)
            slots = result_ref.shape[0] // 2
            for slot in range(2):
                home.send(result_got_ref.at[slot * slots : (slot + 1) * slots], slot)
        else:
            settle(q - 1)
    wait(self_weight_ref)
    g_mix_ref[...] = nt(g_first_ref[...], self_weight_ref[...]).astype(BF)
    settle(3)
    for copy in in_copies:
        copy.wait_recv()
    out_copy.wait_recv()
    wait(out_zero_ref)
    out_next[...] = out_zero_ref[...] + out_came_ref[...]
    mail.finish()
    home.finish()


def middle_parts(place, count, lefts, rights, result, result_away, feeds, weight):
    nz = place.nz
    depth, width = lefts[0].shape[1], rights[0].shape[1]
    piece, block = width // place.seq, depth // place.rows
    columns = piece * len(rights)
    out = jax.ShapeDtypeStruct((2, nz, block // 2, columns), BF)
    big = pltpu.VMEM((4, nz, block, columns), BF)
    operands = [*lefts, *rights, result, result_away, *feeds, weight]
    late = (17, 18, 13, 14, 15, 16, 0, 1, 2, 4, 3, 5, 6, 7, 8, 9, 10, 11, 20, 19)
    return pl.pallas_call(
        with_loads(functools.partial(middle_kernel, (nz, piece)), len(operands), late),
        in_specs=[ANY_SPEC] * len(operands),
        out_specs=[WHOLE_SPEC] * 4
        + [ANY_SPEC, WHOLE_SPEC, ANY_SPEC, WHOLE_SPEC, ANY_SPEC, WHOLE_SPEC, WHOLE_SPEC],
        out_shape=[out] * 4
        + [jax.ShapeDtypeStruct((count, result.shape[0] // count, width), BF)]
        + [jax.ShapeDtypeStruct(feeds[0].shape[1:], BF)] * 4
        + [jax.ShapeDtypeStruct(feeds[4].shape, BF), jax.ShapeDtypeStruct(result.shape, BF)],
        scratch_shapes=[pltpu.VMEM((depth, left.shape[0]), BF) for left in lefts]
        + [big] * 3
        + [pltpu.VMEM(result.shape, BF), pltpu.VMEM(feeds[0].shape, BF)]
        + [pltpu.VMEM(feeds[4].shape, BF)] * 2
        + [pltpu.SemaphoreType.DMA((8,))] * 2
        + [pltpu.SemaphoreType.DMA((2,))] * 2
        + load_scratch(operands, late),
        compiler_params=pltpu.CompilerParams(
            collective_id=2, has_side_effects=True, vmem_limit_bytes=63 * 1024 * 1024
        ),
        cost_estimate=pl.CostEstimate(
            flops=2 * 8 * 512 * depth * width, bytes_accessed=24 << 20, transcendentals=0
        ),
    )(*operands)


def final_kernel(nz, wait, *refs):
    (
        normed_ref,
        input_ref,
        first_ref,
        gain_ref,
        weight_ref,
        gq_ref,
        gk_ref,
        gv_ref,
        k_away_ref,
        v_away_ref,
        upper_ref,
        upper_got_ref,
        lower_ref,
        lower_got_ref,
        in_up_ref,
        in_up_got_ref,
        in_low_ref,
        in_low_got_ref,
        out_last_ref,
        out_got_ref,
        vector_ref,
        projected_ref,
        proj_ref,
    ) = refs[:23]
    (qkv_ref, middle_ref, feed_ref, sum_ref, frames_out, text_out) = refs[23:29]
    (
        out_ref,
        text_ref,
        packed_ref,
        k_got_ref,
        v_got_ref,
        acc_ref,
        turned_ref,
        own_ref,
        away_ref,
        got_ref,
        first_x_ref,
        first_y_ref,
        second_y_ref,
        second_x_ref,
        mid_up_ref,
        mid_low_ref,
        mid_ref,
        mid_ring_ref,
        qkv_ring_ref,
        feed_send_ref,
        feed_ring_ref,
        out_x_ref,
        out_own_ref,
        out_y_ref,
        feed_away_ref,
        feed_other_ref,
        vector_out_ref,
        vector_in_ref,
        text_away_ref,
        text_got_ref,
        send_sems,
        recv_sems,
        home_sends,
        home_recvs,
    ) = refs[29:]
    ways = Ways(nz)
    core, z = ways.core, ways.z
    sibling, across_x, across_y, above = ways.sibling, ways.across_x, ways.across_y, ways.above
    ways.meet(ways.plane() + [ways.above, ways.below])
    mail = Mail(send_sems, recv_sems)
    ring = ring_order(nz)
    half = upper_ref.shape[2]
    feed_half = feed_ring_ref.shape[1] // 2
    tokens, width = normed_ref.shape

    k_copy = mail.send(k_away_ref, k_got_ref, sibling)
    v_copy = mail.send(v_away_ref, v_got_ref, sibling)

    feed_copies, feed_last_copies = [], {}

    def feed_piece(t):
        at = slice(ring[t] * feed_half, (ring[t] + 1) * feed_half)
        return (
            in_up_ref[at].astype(F32) + in_up_got_ref[at].astype(F32),
            in_low_ref[at].astype(F32) + in_low_got_ref[at].astype(F32),
        )

    def feed_step(t):
        upper_part, lower_part = feed_piece(t)
        if t > 0:
            feed_copies[t - 1].wait_recv()
            upper_part += feed_ring_ref[t - 1, :feed_half].astype(F32)
            lower_part += feed_ring_ref[t - 1, feed_half:].astype(F32)
        if t == nz - 1:
            feed_finish(0, upper_part, lower_part)
            return
        feed_send_ref[t, :feed_half] = upper_part.astype(BF)
        feed_send_ref[t, feed_half:] = lower_part.astype(BF)
        feed_copies.append(mail.send(feed_send_ref.at[t], feed_ring_ref.at[t], above))

    wait(in_up_ref, in_up_got_ref, in_low_ref, in_low_got_ref)
    feed_step(0)

    mid_copies = {}
    wait(upper_ref, upper_got_ref, lower_ref, lower_got_ref)
    for k in ring:
        mid_ref[k, :half] = upper_ref[0, k] + upper_got_ref[0, k]
        mid_ref[k, half:] = lower_ref[0, k] + lower_got_ref[0, k]
        mid_copies[k] = (
            mail.send(mid_ref.at[k, :half], mid_up_ref.at[k], across_y),
            mail.send(mid_ref.at[k, half:], mid_low_ref.at[k], across_x),
        )
    wait(normed_ref, gq_ref, gk_ref, gv_ref)
    turned_ref[...] = turned(normed_ref[...])
    packed_ref[:, :width] = gq_ref[...]
    k_copy.wait_recv()
    packed_ref[:, width : 2 * width] = gk_ref[...] + k_got_ref[...]
    v_copy.wait_recv()
    packed_ref[:, 2 * width :] = gv_ref[...] + v_got_ref[...]

    block = own_ref.shape[2]
    columns = own_ref.shape[3]
    core_copies = []
    for q in range(4):
        right = packed_ref[:, pl.ds(pl.multiple_of(ways.place(q) * columns, columns), columns)]
        for which, ref in ((1 - core, away_ref), (core, own_ref)):
            for k in range(nz):
                ref[q, k] = dot(turned_ref[ways.rows(k, which, block)], right).astype(BF)
            if ref is away_ref:
                core_copies.append(mail.send(away_ref.at[q], got_ref.at[q], sibling))

    even_rows, odd_rows = slice(0, feed_half), slice(feed_half, 2 * feed_half)

    def out_first():
        for n in range(2):
            out_copies.append(
                (
                    mail.send(out_ref.at[n, even_rows], out_x_ref.at[n], across_x),
                    mail.send(out_ref.at[2 * n, odd_rows], out_y_ref.at[n], across_y),
                )
            )

    def out_step():
        for n in range(2):
            for copy in out_copies[n]:
                copy.wait_recv()
            out_own_ref[0, n] = out_ref[2 + n, even_rows] + out_x_ref[n]
            out_own_ref[1, n] = out_ref[1 + 2 * n, odd_rows] + out_y_ref[n]
            if n == 0:
                out_copies.append(
                    (
                        mail.send(out_own_ref.at[0, 0], out_x_ref.at[2], across_y),
                        mail.send(out_own_ref.at[1, 0], out_y_ref.at[2], across_x),
                    )
                )

    def out_last():
        for copy in out_copies[2]:
            copy.wait_recv()
        feed_finish(
            1,
            out_own_ref[0, 1].astype(F32) + out_x_ref[2].astype(F32),
            out_own_ref[1, 1].astype(F32) + out_y_ref[2].astype(F32),
        )

    def feed_finish(kind, even, odd):
        away = jnp.where(core == 0, odd, even)
        own = jnp.where(core == 0, even, odd)
        across = own.shape[1]
        feed_away_ref[kind] = away
        feed_last_copies[kind] = mail.send(feed_away_ref.at[kind], feed_other_ref.at[kind], sibling)
        at = pl.ds(pl.multiple_of(core * across, across), across)
        feed_ref[kind, :, at] = own

    def feed_last(kind):
        feed_last_copies[kind].wait_recv()
        across = feed_other_ref.shape[2]
        at = pl.ds(pl.multiple_of((1 - core) * across, across), across)
        feed_ref[kind, :, at] = feed_other_ref[kind]

    wait(projected_ref, proj_ref)
    text_ref[...] = nt(projected_ref[...], proj_ref[...])
    text_rows = text_ref.shape[0] // 2
    text_away_ref[...] = text_ref[text_rows:].astype(BF)
    text_copy = mail.send(text_away_ref, text_got_ref, sibling)

    def core_step(q):
        core_copies[q].wait_recv()
        own_ref[q] = own_ref[q] + got_ref[q]

    mid_ring = {}

    def mid_send(t):
        k = ring[t]
        up, low = mid_copies[k]
        up.wait()
        low.wait()
        mid_ref[k, :half] = upper_ref[1, k] + upper_got_ref[1, k] + mid_up_ref[k]
        mid_ref[k, half:] = lower_ref[1, k] + lower_got_ref[1, k] + mid_low_ref[k]
        if t > 0:
            mid_ring[t - 1].wait_recv()
        if t == nz - 1:
            middle_ref[...] = mid_ref[k].astype(F32) + mid_ring_ref[t - 1].astype(F32)
            return
        if t > 0:
            mid_ref[k] = mid_ref[k] + mid_ring_ref[t - 1]
        mid_ring[t] = mail.send(mid_ref.at[k], mid_ring_ref.at[t], above)

    qkv_ring = {}

    def qkv_send(t):
        k = ring[t]
        second[k][0].wait_recv()
        own_ref[3, k, up] = own_ref[3, k, up] + second_y_ref[k]
        second[k][1].wait_recv()
        own_ref[3, k, low] = own_ref[3, k, low] + second_x_ref[k]
        if t > 0:
            qkv_ring[t - 1].wait_recv()
        if t == nz - 1:
            qkv_ref[...] = own_ref[3, k].astype(F32) + qkv_ring_ref[t - 1].astype(F32)
            return
        if t > 0:
            own_ref[3, k] = own_ref[3, k] + qkv_ring_ref[t - 1]
        qkv_ring[t] = mail.send(own_ref.at[3, k], qkv_ring_ref.at[t], above)

    up, low = slice(0, half), slice(half, 2 * half)
    core_step(0)
    upper_first = [mail.send(own_ref.at[0, :, up], first_x_ref.at[0], across_x)]
    lower_first = [mail.send(own_ref.at[0, :, low], first_y_ref.at[0], across_y)]
    core_step(1)
    upper_first.append(mail.send(own_ref.at[1, :, up], first_x_ref.at[1], across_x))
    core_step(2)
    lower_first.append(mail.send(own_ref.at[2, :, low], first_y_ref.at[1], across_y))
    core_step(3)
    wait(out_last_ref, out_got_ref)
    out_ref[...] = out_last_ref[...] + out_got_ref[...]
    out_copies = []
    out_first()

    slots = tokens // 2
    text_copy.wait_recv()
    text_got_ref[...] = (text_ref[:text_rows] + text_got_ref[...].astype(F32)).astype(BF)
    text_home = Home(ways, text_out, home_sends.at[0], home_recvs.at[0])
    for slot in range(2):
        at = slice(slot * text_rows // 2, (slot + 1) * text_rows // 2)
        text_home.send(text_got_ref.at[at], slot)

    wait(weight_ref)
    acc_ref[...] = nt(packed_ref[:, :width], weight_ref[:, :width])
    acc_ref[...] += nt(packed_ref[:, width : 2 * width], weight_ref[:, width : 2 * width])
    mid_send(0)
    feed_step(1)
    acc_ref[...] += nt(packed_ref[:, 2 * width :], weight_ref[:, 2 * width :])
    wait(input_ref, first_ref, gain_ref)
    gain_sum = jnp.zeros((1, width), F32)
    shift_sum = jnp.zeros((1, width), F32)
    chunk = min(128, tokens)
    for m in range(tokens // chunk):
        at = slice(m * chunk, (m + 1) * chunk)
        grad, gain_part, shift_part = norm_backward(
            input_ref[at].astype(F32), gain_ref[...], acc_ref[at]
        )
        k_got_ref[at] = (first_ref[at] + grad).astype(BF)
        gain_sum += gain_part[None]
        shift_sum += shift_part[None]
    wait(vector_ref)
    vector_out_ref[0] = vector_ref[...]
    vector_out_ref[0, 0:1] = gain_sum
    vector_out_ref[0, 1:2] = shift_sum
    vector_copy = mail.send(vector_out_ref.at[0], vector_in_ref.at[0], sibling)
    mid_send(1)

    vector_copy.wait_recv()
    vector_out_ref[1] = vector_out_ref[0] + vector_in_ref[0]
    vector_copy = mail.send(vector_out_ref.at[1], vector_in_ref.at[1], across_x)
    for t in range(2, nz):
        feed_step(t)
        if t < nz - 1:
            mid_send(t)
    vector_copy.wait_recv()
    vector_out_ref[2] = vector_out_ref[1] + vector_in_ref[1]
    vector_copy = mail.send(vector_out_ref.at[2], vector_in_ref.at[2], across_y)

    upper_first[0].wait_recv()
    own_ref[2, :, up] = own_ref[2, :, up] + first_x_ref[0]
    lower_first[0].wait_recv()
    own_ref[1, :, low] = own_ref[1, :, low] + first_y_ref[0]
    second = {}
    for k in ring:
        second[k] = (
            mail.send(own_ref.at[2, k, up], second_y_ref.at[k], across_y),
            mail.send(own_ref.at[1, k, low], second_x_ref.at[k], across_x),
        )
    frames_home = Home(ways, frames_out, home_sends.at[1], home_recvs.at[1])
    for slot in range(2):
        frames_home.send(k_got_ref.at[slot * slots : (slot + 1) * slots], slot)
    vector_copy.wait_recv()
    vector_out_ref[3] = vector_out_ref[2] + vector_in_ref[2]
    vector_copy = mail.send(vector_out_ref.at[3], vector_in_ref.at[3], above)
    upper_first[1].wait_recv()
    own_ref[3, :, up] = own_ref[3, :, up] + first_x_ref[1]
    lower_first[1].wait_recv()
    own_ref[3, :, low] = own_ref[3, :, low] + first_y_ref[1]
    out_step()
    mid_send(nz - 1)
    feed_last(0)
    total = vector_out_ref[3]
    for t in range(nz - 1):
        vector_copy.wait_recv()
        total = total + vector_in_ref[3 + t]
        if t < nz - 2:
            vector_copy = mail.send(vector_in_ref.at[3 + t], vector_in_ref.at[4 + t], above)
    sum_ref[...] = total
    for t in range(nz):
        qkv_send(t)
    out_last()
    feed_last(1)
    text_home.finish()
    frames_home.finish()
    for number, copy in enumerate(mail.sent):
        if not any(copy is c for pair in mid_copies.values() for c in pair):
            copy.wait_send()


FINAL_LOADS = (14, 15, 16, 17, 10, 11, 12, 13, 0, 5, 6, 7, 18, 19, 21, 22, 4, 1, 2, 3, 20)


def final_sums(place, count, *operands):
    nz = place.nz
    normed, weight, upper, in_up = operands[0], operands[4], operands[10], operands[14]
    vectors, projected, proj = operands[20], operands[21], operands[22]
    words, text_width = projected.shape[0], proj.shape[0]
    tokens, width = normed.shape
    block, piece = width // place.rows, weight.shape[1] // place.seq
    half, middle = block // 2, upper.shape[3]
    feed_width = in_up.shape[1]
    feed_rows = width // nz
    copies = 2 + 6 + nz - 1 + 2 + 2 * nz + 1 + 4 + 3 + nz - 1 + 4 + 2 * nz + 2 * (nz - 1)
    vmem = pltpu.VMEM
    return pl.pallas_call(
        with_loads(functools.partial(final_kernel, nz), len(operands), FINAL_LOADS),
        in_specs=[ANY_SPEC] * len(operands),
        out_specs=[WHOLE_SPEC] * 4 + [ANY_SPEC] * 2,
        out_shape=[
            jax.ShapeDtypeStruct((block, piece), F32),
            jax.ShapeDtypeStruct((block, middle), F32),
            jax.ShapeDtypeStruct((2, block, 2 * feed_width), F32),
            jax.ShapeDtypeStruct(vectors.shape, F32),
            jax.ShapeDtypeStruct((count, tokens // count, width), BF),
            jax.ShapeDtypeStruct((count, words // 2 // count, text_width), BF),
        ],
        scratch_shapes=[
            vmem((4, feed_rows, feed_width), BF),
            vmem((words, text_width), F32),
            vmem((tokens, 3 * width), BF),
            vmem((tokens, width), BF),
            vmem((tokens, width), BF),
            vmem((tokens, width), F32),
            vmem((width, tokens), BF),
            vmem((4, nz, block, piece), BF),
            vmem((4, nz, block, piece), BF),
            vmem((4, nz, block, piece), BF),
            vmem((2, nz, half, piece), BF),
            vmem((2, nz, half, piece), BF),
            vmem((nz, half, piece), BF),
            vmem((nz, half, piece), BF),
            vmem((nz, half, middle), BF),
            vmem((nz, half, middle), BF),
            vmem((nz, block, middle), BF),
            vmem((nz - 1, block, middle), BF),
            vmem((nz - 1, block, piece), BF),
            vmem((nz - 1, feed_rows, feed_width), BF),
            vmem((nz - 1, feed_rows, feed_width), BF),
            vmem((3, feed_rows // 2, feed_width), BF),
            vmem((2, 2, feed_rows // 2, feed_width), BF),
            vmem((3, feed_rows // 2, feed_width), BF),
            vmem((2, feed_rows // 2, feed_width), F32),
            vmem((2, feed_rows // 2, feed_width), F32),
            vmem((4,) + vectors.shape, F32),
            vmem((2 + nz,) + vectors.shape, F32),
            vmem((words // 2, text_width), BF),
            vmem((words // 2, text_width), BF),
            pltpu.SemaphoreType.DMA((copies,)),
            pltpu.SemaphoreType.DMA((copies,)),
            pltpu.SemaphoreType.DMA((2, 2)),
            pltpu.SemaphoreType.DMA((2, 2)),
        ]
        + load_scratch(operands, FINAL_LOADS),
        compiler_params=pltpu.CompilerParams(
            collective_id=1, has_side_effects=True, vmem_limit_bytes=63 * 1024 * 1024
        ),
        cost_estimate=pl.CostEstimate(
            flops=60 * tokens * width * weight.shape[1], bytes_accessed=40 << 20, transcendentals=0
        ),
    )(*operands)


def last_kernel(padding, qkv_ref, middle_ref, feed_ref, frames_ref, text_ref, *outs):
    frames_out, text_out, qkv_out, self_out, query_out, proj_out, kv_out, cross_out, in_out, out_out = outs
    piece = self_out.shape[1]
    frames_out[...] = frames_ref[...].astype(F32)
    text_out[...] = text_ref[...].astype(F32)
    qkv_out[...] = qkv_ref[...]
    cross_out[...] = middle_ref[:, :piece]
    query_out[...] = middle_ref[:, piece : 2 * piece]
    kv_out[...] = middle_ref[:, 2 * piece : 4 * piece]
    proj_out[...] = middle_ref[: proj_out.shape[0], 4 * piece : 5 * piece]
    self_out[...] = middle_ref[:, 5 * piece :]
    in_out[...] = feed_ref[0]
    out_out[...] = jnp.swapaxes(feed_ref[1], 0, 1)


def last_step(padding, piece, qkv, middle, feed_sums, frames, text):
    block, across = qkv.shape[0], feed_sums.shape[2]
    shapes = [
        frames.shape,
        text.shape,
        qkv.shape,
        (block, piece),
        (block, piece),
        (block - padding, piece),
        (block, 2 * piece),
        (block, piece),
        (block, across),
        (across, block),
    ]
    return pl.pallas_call(
        functools.partial(last_kernel, padding),
        in_specs=[WHOLE_SPEC] * 5,
        out_specs=[WHOLE_SPEC] * len(shapes),
        out_shape=[jax.ShapeDtypeStruct(shape, F32) for shape in shapes],
        compiler_params=pltpu.CompilerParams(vmem_limit_bytes=MOST_VMEM),
    )(qkv, middle, feed_sums, frames, text)


def permuted_sums(place, meta, in_up, in_low, out_sum, lefts, rights, normed_self, backward_self):
    nx, ny, nz, seq = place.nx, place.ny, place.nz, place.seq
    width = normed_self.shape[1]
    block, piece = width // place.rows, width // seq
    middle_own, middle_away = weight_parts(
        place, meta, lefts[:3] + lefts[2:4], rights[:5]
    )
    out_own, out_away = weight_parts(place, meta, lefts[4:], rights[5:])
    middle_got = place.swap_core(middle_away)
    out_got = place.swap_core(out_away)
    grad_packed = backward_self(middle_got, out_got)
    in_up = ring_sum([lambda a=in_up[k]: a.astype(F32) for k in range(ny)], place.next_y)
    in_low = ring_sum([lambda a=in_low[k]: a.astype(F32) for k in range(nx)], place.next_x)
    in_both = jnp.stack([in_up, in_low]).astype(BF).reshape(2, nz, block, -1)
    in_both = ring_sum([lambda a=in_both[:, k]: a.astype(F32) for k in range(nz)], place.next_z)
    out_sum = out_sum.reshape((nx, ny) + out_sum.shape[1:])
    out_sum = ring_sum([lambda a=out_sum[k]: a.astype(F32) for k in range(nx)], place.next_x)
    out_sum = out_sum.astype(BF)
    out_sum = ring_sum([lambda a=out_sum[k]: a.astype(F32) for k in range(ny)], place.next_y)
    feed_own = jnp.stack([in_both, out_sum.reshape(2, block, -1)])
    feed_got = place.swap_core(pick(feed_own, 1 - place.core, 1))
    feed_own = pick(feed_own, place.core, 1)
    low = jnp.where(place.core == 0, feed_own, feed_got)
    high = jnp.where(place.core == 0, feed_got, feed_own)
    sum_feed = jnp.concatenate([low, high], axis=2)

    def middle_piece(k):
        at = slice(k * block, (k + 1) * block)
        return lambda: middle_own[:, at].astype(F32) + middle_got[:, at].astype(F32)

    middle = ring_sum([middle_piece(k) for k in range(nz)], place.next_z).astype(BF)
    spread = jnp.concatenate(
        [
            middle[0].reshape(block, seq, -1),
            middle[1].reshape(block, seq, -1),
            jnp.concatenate([middle[2], middle[3]], axis=1).reshape(block, seq, -1),
            middle[4].reshape(block, seq, -1),
        ],
        axis=2,
    ).reshape(block, ny, nx, -1)

    def shifted(array, index, number, length, axis):
        return lambda: pick(array, (index + 1 + number) % length, axis).astype(F32)

    spread = ring_sum([shifted(spread, place.x, k, nx, 2) for k in range(nx)], place.next_x).astype(BF)
    spread = ring_sum([shifted(spread, place.y, k, ny, 1) for k in range(ny)], place.next_y)
    relative_parts = place.relative_columns(grad_packed, True)
    qkv_own, qkv_away = weight_parts(place, meta, [normed_self], [relative_parts])
    qkv_got = place.swap_core(qkv_away)

    def columns(array):
        return array[0].reshape(array.shape[1], nx, ny, -1)

    def natural(array):
        return jnp.stack(
            [
                jnp.stack(
                    [
                        pick(array[0].reshape(array.shape[1], seq, -1), place.offset(i, j), 1)
                        for i in range(ny)
                    ],
                    axis=1,
                )
                for j in range(nx)
            ],
            axis=1,
        )

    last_own = jnp.concatenate([columns(qkv_own), natural(out_own)], axis=3)
    last_got = jnp.concatenate([columns(qkv_got), natural(out_got)], axis=3)
    last = (last_own.astype(F32) + last_got.astype(F32)).astype(BF)
    last = last.reshape(nz, 2, block // 2, nx, ny, -1)
    upper = ring_sum([lambda k=k: last[:, 0, :, k].astype(F32) for k in range(nx)], place.next_x).astype(BF)
    lower = ring_sum([lambda k=k: last[:, 1, :, :, k].astype(F32) for k in range(ny)], place.next_y).astype(BF)
    upper = ring_sum([lambda a=upper[:, :, k]: a.astype(F32) for k in range(ny)], place.next_y)
    lower = ring_sum([lambda a=lower[:, :, k]: a.astype(F32) for k in range(nx)], place.next_x)
    last = jnp.stack([upper, lower], axis=1).astype(BF)
    last = ring_sum([lambda a=last[k]: a.astype(F32) for k in range(nz)], place.next_z)
    last = last.reshape(block, -1)
    sum_self_qkv, sum_self_out = last[:, : 3 * piece], last[:, 3 * piece :]

    return sum_feed, spread, sum_self_qkv, sum_self_out, grad_packed


def shards(
    frames,
    text_states,
    clip_lengths,
    text_lengths,
    self_gain,
    self_shift,
    self_qkv,
    self_out,
    cross_gain,
    cross_shift,
    cross_query,
    text_proj,
    text_bias,
    cross_kv,
    cross_out,
    feed_gain,
    feed_shift,
    feed_in,
    feed_out,
    grad_out,
):
    place = Place()
    count = frames.shape[0]
    width = frames.shape[2]
    text_total = text_states.shape[1] * place.seq

    nx, ny, nz, seq = place.nx, place.ny, place.nz, place.seq
    block, piece = width // place.rows, width // seq
    kernels = nx == 2 and ny == 2 and nz == 4 and piece % 128 == 0
    lengths = jnp.concatenate([clip_lengths, text_lengths], axis=1)
    if kernels:
        padded = jnp.zeros((8, 128), jnp.int32).at[:count, : 2 * CLIPS].set(lengths)
        (
            layer_raw,
            normed_self,
            queries,
            pair,
            pair_other,
            text_input,
            projected,
            text_pair,
            lengths_other,
        ) = entry(
            place,
            frames,
            text_states,
            padded,
            self_gain,
            self_shift,
            self_qkv,
            text_proj,
            text_bias,
            cross_kv,
        )
        lengths_other = lengths_other[:count, : 2 * CLIPS]
        layer_input = layer_raw.astype(F32)
    else:
        lengths_other = place.swap_core(lengths)
        text_half = place.to_rows(text_states)
        layer_raw = place.to_rows(frames)
        text_input = jnp.concatenate([text_half, place.swap_core(text_half)], axis=0)
        cotangent = place.to_rows(grad_out)
        projected = (dot(text_input, text_proj) + text_bias).astype(BF)
        text_pair = dot(projected, cross_kv).astype(BF)
        layer_input = layer_raw.astype(F32)
        normed_self = layer_norm(layer_input, self_gain, self_shift)
        pair = dot(normed_self, self_qkv[:, width:]).astype(BF)
        pair_other = place.swap_core(pair)
        queries = dot(normed_self, self_qkv[:, :width]).astype(BF)
    mine = place.spot // count == place.core
    row_lengths = pick(jnp.where(mine, lengths, lengths_other), place.spot % count, 0)

    if kernels:
        self_mix, self_lse, cotangent = self_forward_and_gather(
            place, row_lengths, queries, pair, pair_other, grad_out
        )
    else:
        self_mix, self_lse, _ = self_forward(row_lengths, queries, pair, pair_other)
    cotangent_other = place.swap_core(cotangent)
    first = layer_input + dot(self_mix, self_out)
    normed_cross = layer_norm(first, cross_gain, cross_shift)
    cross_queries = dot(normed_cross, cross_query).astype(BF)
    cross_mix, cross_lse, _ = cross_forward(row_lengths, cross_queries, text_pair)
    second = first + dot(cross_mix, cross_out)
    normed_feed = layer_norm(second, feed_gain, feed_shift)

    meta = jnp.stack([place.core, place.x, place.y, place.z]).astype(jnp.int32)
    normed_other = place.swap_core(normed_feed)
    fed = feed(
        place, meta, normed_feed, normed_other, cotangent, cotangent_other, feed_in, feed_out
    )
    result, result_away, grad_normed_feed, grad_away = fed[:4]
    up_parts, low_parts, out_parts = fed[4 : 4 + nx], fed[4 + nx : 4 + nx + ny], fed[4 + nx + ny :]
    grad_normed_feed = grad_normed_feed + place.swap_core(grad_away).astype(F32)

    grad_part, grad_feed_gain, grad_feed_shift = norm_backward(second, feed_gain, grad_normed_feed)
    grad_second = cotangent.astype(F32) + grad_part
    grad_second_branch = grad_second.astype(BF)
    grad_cross_mix = dot(grad_second_branch, cross_out, 1, 1).astype(BF)
    grad_cross_queries, grad_text_keys, grad_text_values, _ = cross_backward(
        row_lengths,
        cross_queries,
        text_pair,
        grad_cross_mix,
        cross_mix,
        cross_lse,
    )
    grad_normed_cross = dot(grad_cross_queries, cross_query, 1, 1)
    grad_part, grad_cross_gain, grad_cross_shift = norm_backward(first, cross_gain, grad_normed_cross)
    grad_first = grad_second + grad_part
    grad_first_branch = grad_first.astype(BF)

    grad_pair = jnp.concatenate([grad_text_keys, grad_text_values], axis=1)
    grad_projected = dot(grad_pair, cross_kv, 1, 1).astype(BF)
    grad_text_bias = jnp.sum(grad_projected.astype(F32), axis=0)
    padding = block - text_input.shape[1] // place.rows
    lefts = [cross_mix, normed_cross, projected, text_input, self_mix]
    rights = [
        grad_second_branch,
        grad_cross_queries,
        grad_text_keys,
        grad_text_values,
        grad_projected,
        grad_first_branch,
    ]
    result = second + result

    def backward_self(grad_self_mix, *before):
        return self_backward(
            row_lengths,
            queries,
            pair,
            pair_other,
            grad_self_mix,
            self_mix,
            self_lse,
            before=before,
        )[:5]

    def vector_list(grad_gain, grad_shift):
        return jnp.stack(
            [
                grad_gain,
                grad_shift,
                grad_cross_gain,
                grad_cross_shift,
                grad_text_bias,
                grad_feed_gain,
                grad_feed_shift,
                jnp.zeros_like(grad_feed_shift),
            ]
        )

    if kernels:
        (
            send_up,
            send_low,
            keep_up,
            keep_low,
            result,
            in_up,
            in_up_got,
            in_low,
            in_low_got,
            out_sum,
            grad_self_mix,
        ) = middle_parts(
            place,
            count,
            lefts,
            rights,
            result,
            result_away,
            (
                up_parts[1],
                place.next_x(up_parts[0]),
                low_parts[1],
                place.next_y(low_parts[0]),
                out_parts[1],
                place.next_z(out_parts[2]),
                out_parts[0],
            ),
            self_out,
        )
        up_got, low_got = place.next_x(send_up), place.next_y(send_low)
        out_got = place.next_z(out_sum)
        grads = backward_self(grad_self_mix)
        nothing = jnp.zeros_like(grad_feed_shift)
        sum_self_qkv, spread, sum_feed, vectors, grad_frames, grad_text = final_sums(
            place,
            count,
            normed_self,
            layer_raw,
            grad_first,
            self_gain[None],
            self_qkv,
            *grads,
            keep_up,
            up_got,
            keep_low,
            low_got,
            in_up,
            in_up_got,
            in_low,
            in_low_got,
            out_parts[3],
            out_got,
            vector_list(nothing, nothing),
            grad_projected,
            text_proj,
        )
        (
            grad_frames,
            grad_text,
            sum_self_qkv,
            sum_self_out,
            sum_cross_query,
            sum_text_proj,
            sum_cross_kv,
            sum_cross_out,
            sum_feed_in,
            sum_feed_out,
        ) = last_step(padding, piece, sum_self_qkv, spread, sum_feed, grad_frames, grad_text)
    else:

        def packed_self(*before):
            grads = backward_self(dot(grad_first_branch, self_out, 1, 1).astype(BF), *before)
            keys = (grads[1].astype(F32) + place.swap_core(grads[3]).astype(F32)).astype(BF)
            values = (grads[2].astype(F32) + place.swap_core(grads[4]).astype(F32)).astype(BF)
            return jnp.concatenate([grads[0], keys, values], axis=1)

        in_up = ring_sum([lambda a=a: a.astype(F32) for a in up_parts], place.next_x).astype(BF)
        in_low = ring_sum([lambda a=a: a.astype(F32) for a in low_parts], place.next_y).astype(BF)
        out_sum = ring_sum([lambda a=a: a.astype(F32) for a in out_parts], place.next_z).astype(BF)
        grad_text = dot(grad_projected, text_proj, 1, 1)
        text_blocks = text_input.reshape(text_total, place.rows, -1)
        text_padded = jnp.pad(text_blocks, ((0, 0), (0, 0), (0, padding))).reshape(text_total, width)
        lefts[3] = text_padded
        sum_feed, spread, sum_self_qkv, sum_self_out, grad_packed = permuted_sums(
            place, meta, in_up, in_low, out_sum, lefts, rights, normed_self, packed_self
        )
        result = (result + place.swap_core(result_away).astype(F32)).astype(BF)
        result = place.from_rows(result, count)
        grad_normed_self = dot(grad_packed, self_qkv, 1, 1)
        grad_part, grad_gain, grad_shift = norm_backward(layer_input, self_gain, grad_normed_self)
        grad_frames = place.from_rows((grad_first + grad_part).astype(BF), count)
        half = grad_text.shape[0] // 2
        text_away = place.swap_core(grad_text[half:].astype(BF))
        grad_text = (grad_text[:half] + text_away.astype(F32)).astype(BF)
        grad_text = place.from_rows(grad_text, count)
        vectors = place.vector_sum(vector_list(grad_gain, grad_shift))
        sum_cross_out, sum_cross_query = spread[:, :piece], spread[:, piece : 2 * piece]
        sum_cross_kv, sum_text_proj = spread[:, 2 * piece : 4 * piece], spread[:, 4 * piece : 5 * piece]
        sum_text_proj = sum_text_proj[: block - padding]
        sum_feed_in, sum_feed_out = sum_feed[0], jnp.swapaxes(sum_feed[1], 0, 1)
        grad_frames, grad_text = grad_frames.astype(F32), grad_text.astype(F32)
    vectors = pick(vectors.reshape(8, seq, width // seq), place.spot, 1)
    return (
        result,
        grad_frames,
        grad_text,
        vectors[0],
        vectors[1],
        sum_self_qkv,
        sum_self_out,
        vectors[2],
        vectors[3],
        sum_cross_query,
        sum_text_proj,
        vectors[4],
        sum_cross_kv,
        sum_cross_out,
        vectors[5],
        vectors[6],
        sum_feed_in,
        sum_feed_out,
    )


def solution(mesh):
    split, copied, table = P(ROWS, SEQ, None), P(), P(ROWS, None)
    vector, matrix = P(SEQ), P(ROWS, SEQ)
    return jax.shard_map(
        shards,
        mesh=mesh,
        in_specs=(split, split, table, table) + (copied,) * 15 + (split,),
        out_specs=(
            (split,) * 3
            + (vector, vector, matrix, matrix)
            + (vector, vector, matrix, matrix)
            + (vector, matrix, matrix)
            + (vector, vector, matrix, P(SEQ, ROWS))
        ),
        check_vma=False,
    )
```
